32 devices in a mesh: path: 2 (over core), dp: 16 (over z, y, x).
Axes of the slice: x: 2, y: 2, z: 4, core: 2. Of those that a mesh axis runs over, the one named last changes fastest.
Arguments:
- acts: bfloat16 [2, 16, 16, 16, 4096], P('path', 'dp'), may hold values from -12 to 12
- cotangent: bfloat16 [2, 16, 16, 16, 4096], P('path', 'dp'), may hold values from -6 to 6
- clip_res: int32 [16], P('dp'), may hold values from 0 to 3, as said below
- w_slow_a: bfloat16 [1280, 256], replicated, may hold values from -0.15625 to 0.15625
- w_slow_b: bfloat16 [9, 256, 256], replicated, may hold values from -0.125 to 0.125
- w_slow_c: bfloat16 [256, 1024], replicated, may hold values from -0.375 to 0.375
- w_slow_proj: bfloat16 [1280, 1024], replicated, may hold values from -0.15625 to 0.15625
- slow_gain: float32 [2560], replicated, may hold values from 0.1 to 1.9
- slow_bias: float32 [2560], replicated, may hold values from -3 to 3
- w_fast_a: bfloat16 [3, 128, 32], replicated, may hold values from -0.3125 to 0.3125
- w_fast_b: bfloat16 [9, 32, 32], replicated, may hold values from -0.375 to 0.375
- w_fast_c: bfloat16 [32, 128], replicated, may hold values from -1 to 1
- w_lateral: bfloat16 [5, 128, 256], replicated, may hold values from -0.25 to 0.25
- fast_gain: float32 [192], replicated, may hold values from 0.1 to 1.9
- fast_bias: float32 [192], replicated, may hold values from -3 to 3
Outputs:
- out: bfloat16 [2, 16, 16, 16, 4096], P('path', 'dp')
- in_grad: bfloat16 [2, 16, 16, 16, 4096], P('path', 'dp')
- param_grads: float32 [2685312], P(('path', 'dp'))
The draws below stay inside these ranges and needn't reach their ends.
Inputs may be any that keep to these rules, and one draw needn't show every extreme that they name: `clip_res`: level of each clip slot: 0 an empty slot; 1, 2, 3 a clip whose valid pixels are the top-left square of side 16 * 5 // 8, 14 or 16.
All inputs are finite; a program needn't handle non-finite values.
Results may differ from the reference program's by a relative error of at most 0.0085.
Values may be sent and summed in bfloat16 or wider, within the bound.
No kernel may reach another device: no remote copies, remote signals or barrier semaphores. Data moves between devices by JAX's collectives and lax.ppermute only.
A program may use at most 256 MiB of HBM per device.

```python
import jax
import jax.numpy as jnp
from jax import lax

CLIPS_DEV = 1
GRID = 16
TS = 4
ALPHA = 8
CS = 1024
CS_MID = 256
CF = 128
CF_MID = 32
LAT = 256
TF = 32
CLIPS = 16
N_DP = 16


def draw_acts(key, part):
    key = jax.random.fold_in(key, 23)
    shape = (2, CLIPS, GRID, GRID, TS * CS)
    ramp = 1.0 + 2.0 * jnp.arange(CLIPS, dtype=jnp.float32) / max(CLIPS - 1, 1)
    ramp = ramp[None, :, None, None, None]
    values = jax.random.normal(key, shape, jnp.float32) * ramp
    return jnp.clip(values, -12.0, 12.0).astype(jnp.bfloat16)


def draw_clip_res(key, part):
    key = jax.random.fold_in(key, 11)
    group = jnp.arange(CLIPS, dtype=jnp.int32) // CLIPS_DEV
    base = jax.random.randint(key, (CLIPS,), -1, 2)
    levels = jnp.clip(base + 4 * group // N_DP, 0, 3).astype(jnp.int32)
    levels = levels.at[0].set(0)
    return levels.at[CLIPS - 1].set(3)


def block_levels(rng, extent, cuts, low, top_value):
    def one(axis_at, parts):
        heights = jax.random.uniform(jax.random.fold_in(jax.random.fold_in(rng, 6), axis_at), (parts,), jnp.float32, low / len(cuts), top_value / len(cuts))
        return jnp.repeat(jnp.exp(heights), extent[axis_at] // parts).reshape((-1,) + (1,) * (len(extent) - axis_at - 1))

    factor_of = one(*cuts[0])
    for cut in cuts[1:]:
        factor_of = factor_of * one(*cut)
    return factor_of


def gaussian(rng, dims, scale, limit, shards=(), kind=jnp.bfloat16):
    entries = scale * jax.random.normal(rng, dims, jnp.float32)
    if shards:
        entries = entries * block_levels(rng, dims, shards, -0.22, 0.18)
    return jnp.clip(entries, -limit, limit).astype(kind)


def setup_inputs(seed: int = 0) -> dict:
    key_list = jax.random.split(jax.random.key(seed), 16)
    return {
        "acts": draw_acts(jax.random.fold_in(key_list[15], 71), 0),
        "cotangent": gaussian(key_list[1], (2, CLIPS, GRID, GRID, TS * CS), 1.0, 6.0, ((0, 2), (1, 16))),
        "clip_res": draw_clip_res(jax.random.fold_in(key_list[15], 71), 0),
        "w_slow_a": gaussian(key_list[3], (CS + LAT, CS_MID), (CS + LAT) ** -0.5, 0.15625),
        "w_slow_b": gaussian(key_list[4], (9, CS_MID, CS_MID), (9 * CS_MID) ** -0.5, 0.125),
        "w_slow_c": gaussian(key_list[5], (CS_MID, CS), CS_MID ** -0.5, 0.375),
        "w_slow_proj": gaussian(key_list[6], (CS + LAT, CS), (CS + LAT) ** -0.5, 0.15625),
        "slow_gain": jnp.clip(1.0 + 0.18 * jax.random.normal(key_list[7], (2 * CS_MID + 2 * CS,), jnp.float32), 0.1, 1.9),
        "slow_bias": gaussian(key_list[8], (2 * CS_MID + 2 * CS,), 0.5, 3.0, (), jnp.float32),
        "w_fast_a": gaussian(key_list[9], (3, CF, CF_MID), (3 * CF) ** -0.5, 0.3125),
        "w_fast_b": gaussian(key_list[10], (9, CF_MID, CF_MID), (9 * CF_MID) ** -0.5, 0.375),
        "w_fast_c": gaussian(key_list[11], (CF_MID, CF), CF_MID ** -0.5, 1.0),
        "w_lateral": gaussian(key_list[12], (5, CF, LAT), (5 * CF) ** -0.5, 0.25),
        "fast_gain": jnp.clip(1.0 + 0.18 * jax.random.normal(key_list[13], (2 * CF_MID + CF,), jnp.float32), 0.1, 1.9),
        "fast_bias": gaussian(key_list[14], (2 * CF_MID + CF,), 0.5, 3.0, (), jnp.float32),
    }


epsilon = 1e-05

@jax.custom_vjp
def low(v):
    return lax.optimization_barrier(v.astype(jnp.bfloat16)).astype(jnp.float32)

@jax.custom_vjp
def low_back(v):
    return v

def low_keep(v):
    return (low(v), None)

def low_pass(kept, grad):
    return (grad,)

def back_keep(v):
    return (v, None)

def back_low(kept, grad):
    return (low(grad),)
low.defvjp(low_keep, low_pass)
low_back.defvjp(back_keep, back_low)

def region_mask(levels, grid):
    sides = jnp.where(levels == 1, grid * 5 // 8, jnp.where(levels == 2, grid * 7 // 8, jnp.where(levels == 3, grid, 0)))
    rows = lax.broadcasted_iota(jnp.int32, (levels.shape[0], grid, grid), 1)
    columns = lax.broadcasted_iota(jnp.int32, (levels.shape[0], grid, grid), 2)
    inside = jnp.logical_and(rows < sides[:, None, None], columns < sides[:, None, None])
    return jnp.where(inside, 1.0, 0.0).astype(jnp.float32)

def gelu_tanh(values):
    return jax.nn.gelu(values, approximate=True)

def point_conv(features, kernel):
    return jnp.einsum('chwti,io->chwto', features, kernel, precision=lax.Precision.HIGHEST)

def time_conv(features, kernel):
    frames = features.shape[3]
    padded = jnp.pad(features, ((0, 0), (0, 0), (0, 0), (1, 1), (0, 0)))
    running_total = point_conv(padded[:, :, :, 0:frames], kernel[0])
    for offset in range(1, 3):
        running_total = running_total + point_conv(padded[:, :, :, offset:offset + frames], kernel[offset])
    return running_total

def space_conv(features, kernel):
    height = features.shape[1]
    width = features.shape[2]
    padded = jnp.pad(features, ((0, 0), (1, 1), (1, 1), (0, 0), (0, 0)))
    running_total = point_conv(padded[:, 0:height, 0:width], kernel[0])
    for offset in range(1, 9):
        shift_rows = offset // 3
        shift_cols = offset % 3
        running_total = running_total + point_conv(padded[:, shift_rows:shift_rows + height, shift_cols:shift_cols + width], kernel[offset])
    return running_total

def lateral_conv(features, kernel):
    padded = jnp.pad(features, ((0, 0), (0, 0), (0, 0), (2, 2), (0, 0)))
    stacked = jnp.stack([padded[:, :, :, offset:offset + ALPHA * TS:ALPHA] for offset in range(5)], axis=4)
    return jnp.einsum('chwtki,kio->chwto', stacked, kernel, precision=lax.Precision.HIGHEST)

def normalize(values, valid_region, valid_count, norm_gain, shift):
    mean = lax.optimization_barrier(jnp.sum(values * valid_region, axis=(0, 1, 2, 3))) / valid_count
    centered = values - mean
    spread = lax.optimization_barrier(jnp.sum(centered * centered * valid_region, axis=(0, 1, 2, 3))) / valid_count
    return centered * lax.rsqrt(spread + epsilon) * norm_gain + shift

def reference(acts, cotangent, clip_res, w_slow_a, w_slow_b, w_slow_c, w_slow_proj, slow_gain, slow_bias, w_fast_a, w_fast_b, w_fast_c, w_lateral, fast_gain, fast_bias):
    clips = acts.shape[1]
    grid = acts.shape[2]
    valid_region = region_mask(clip_res, grid)[:, :, :, None, None]
    pixels = jnp.sum(valid_region)
    slow_count = pixels * TS
    fast_count = pixels * TF
    slow_in = acts[0].astype(jnp.float32).reshape(clips, grid, grid, TS, CS)
    fast_in = acts[1].astype(jnp.float32).reshape(clips, grid, grid, TF, CF)
    params = tuple((weight.astype(jnp.float32) for weight in (w_slow_a, w_slow_b, w_slow_c, w_slow_proj, slow_gain, slow_bias, w_fast_a, w_fast_b, w_fast_c, w_lateral, fast_gain, fast_bias)))

    def forward(slow_input, fast_input, weights):
        k_slow_a, k_slow_b, k_slow_c, k_slow_proj, g_slow, b_slow, k_fast_a, k_fast_b, k_fast_c, k_lateral, g_fast, b_fast = weights
        fast_a = low_back(time_conv(fast_input, k_fast_a))
        fast_h1 = low(gelu_tanh(normalize(fast_a, valid_region, fast_count, g_fast[0:CF_MID], b_fast[0:CF_MID])) * valid_region)
        fast_b = low_back(space_conv(fast_h1, k_fast_b))
        fast_h2 = low(gelu_tanh(normalize(fast_b, valid_region, fast_count, g_fast[CF_MID:2 * CF_MID], b_fast[CF_MID:2 * CF_MID])) * valid_region)
        fast_c = low_back(point_conv(fast_h2, k_fast_c))
        fast_out = gelu_tanh(normalize(fast_c, valid_region, fast_count, g_fast[2 * CF_MID:], b_fast[2 * CF_MID:]) + fast_input) * valid_region
        lateral = low(low_back(lateral_conv(low(fast_out), k_lateral)))
        joined = jnp.concatenate([slow_input, lateral], axis=4)
        slow_a = low_back(point_conv(joined, k_slow_a))
        slow_h1 = low(gelu_tanh(normalize(slow_a, valid_region, slow_count, g_slow[0:CS_MID], b_slow[0:CS_MID])) * valid_region)
        slow_b = low_back(space_conv(slow_h1, k_slow_b))
        slow_h2 = low(gelu_tanh(normalize(slow_b, valid_region, slow_count, g_slow[CS_MID:2 * CS_MID], b_slow[CS_MID:2 * CS_MID])) * valid_region)
        slow_c = low_back(point_conv(slow_h2, k_slow_c))
        slow_p = low_back(point_conv(joined, k_slow_proj))
        main_norm = normalize(slow_c, valid_region, slow_count, g_slow[2 * CS_MID:2 * CS_MID + CS], b_slow[2 * CS_MID:2 * CS_MID + CS])
        short_norm = normalize(slow_p, valid_region, slow_count, g_slow[2 * CS_MID + CS:], b_slow[2 * CS_MID + CS:])
        slow_out = gelu_tanh(main_norm + short_norm) * valid_region
        return (slow_out, fast_out)
    (slow_out, fast_out), pullback = jax.vjp(forward, slow_in, fast_in, params)
    slow_cot = cotangent[0].astype(jnp.float32).reshape(clips, grid, grid, TS, CS)
    fast_cot = cotangent[1].astype(jnp.float32).reshape(clips, grid, grid, TF, CF)
    slow_grad, fast_grad, weight_grads = pullback((slow_cot, fast_cot))
    out = jnp.stack([slow_out.reshape(clips, grid, grid, TS * CS), fast_out.reshape(clips, grid, grid, TF * CF)]).astype(jnp.bfloat16)
    in_grad = jnp.stack([slow_grad.reshape(clips, grid, grid, TS * CS), fast_grad.reshape(clips, grid, grid, TF * CF)]).astype(jnp.bfloat16)
    param_grads = jnp.concatenate([gradient.reshape(-1) for gradient in weight_grads])
    return (out, in_grad, param_grads)
```

```python
import functools

import jax
import jax.numpy as jnp
from jax import lax
from jax.experimental import pallas as pl
from jax.experimental.pallas import tpu as pltpu
from jax.sharding import PartitionSpec as P

TS = 4
ALPHA = 8
CS = 1024
CS_MID = 256
CF = 128
CF_MID = 32
LAT = 256
TF = 32
LN = 128
EPS = 1e-05
GELU_C = 0.7978845608028654
GELU_A = 0.044715

F32 = jnp.float32
BF16 = jnp.bfloat16
SWAP = [(0, 1), (1, 0)]

ROW_SA = 0
ROW_SB = ROW_SA + (CS + LAT) * CS_MID // LN
ROW_SC = ROW_SB + 9 * CS_MID * CS_MID // LN
ROW_SP = ROW_SC + CS_MID * CS // LN
ROW_SG = ROW_SP + (CS + LAT) * CS // LN
SLOW_VEC = (2 * CS_MID + 2 * CS) // LN
ROW_FA = ROW_SG + 2 * SLOW_VEC
ROW_LAT = ROW_FA + (3 * CF * CF_MID + 9 * CF_MID * CF_MID + CF_MID * CF) // LN
ROW_FG = ROW_LAT + 5 * CF * LAT // LN
ROWS = ROW_FG + 3


def dot(a, b):
    return lax.dot_general(a, b, (((1,), (0,)), ((), ())), preferred_element_type=F32)


def dot_t(a, b):
    return lax.dot_general(a, b, (((1,), (1,)), ((), ())), preferred_element_type=F32)


def call(body, outs, scratch, *args, smem=1, limit=48):
    one = not isinstance(outs, list)
    shapes = [jax.ShapeDtypeStruct(s, d) for s, d in ([outs] if one else outs)]
    specs = [pl.BlockSpec(memory_space=pltpu.SMEM)] * smem
    specs += [pl.BlockSpec(memory_space=pltpu.VMEM)] * (len(args) - smem)
    res = pl.pallas_call(
        body,
        out_shape=shapes,
        in_specs=specs,
        out_specs=[pl.BlockSpec(memory_space=pltpu.VMEM)] * len(shapes),
        scratch_shapes=scratch,
        compiler_params=pltpu.CompilerParams(vmem_limit_bytes=limit * 1024 * 1024),
    )(*args)
    return res[0] if one else res


def empty(shape, dtype):
    def body(out_ref):
        pass

    return pl.pallas_call(
        body,
        out_shape=jax.ShapeDtypeStruct(shape, dtype),
        out_specs=pl.BlockSpec(memory_space=pl.ANY),
    )()


def lanes(index):
    if isinstance(index, int):
        return slice(index * LN, (index + 1) * LN)
    return pl.ds(pl.multiple_of(index * LN, LN), LN)


def region(side, px, grid):
    bits = grid.bit_length() - 1
    r = lax.broadcasted_iota(jnp.int32, (px, LN), 0)
    inside = jnp.logical_and((r >> bits) < side, (r & (grid - 1)) < side)
    return jnp.where(inside, 1.0, 0.0).astype(F32)


def rows8(x):
    return x.reshape(x.shape[0] // 8, 8, LN).sum(axis=0)


def total(acc, fold):
    if fold:
        acc = acc + pltpu.roll(acc, 32, 1)
        acc = acc + pltpu.roll(acc, 64, 1)
    return acc.sum(axis=0, keepdims=True)


def gelu_parts(v):
    v2 = v * v
    t = jnp.tanh(v * (GELU_C + (GELU_C * GELU_A) * v2))
    return v2, t


def gelu(v):
    _, t = gelu_parts(v)
    h = 0.5 * v
    return h + h * t


def gelu_both(v):
    v2, t = gelu_parts(v)
    h = 0.5 * v
    slope = 0.5 + 0.5 * t + h * ((1.0 - t * t) * (GELU_C + (3.0 * GELU_C * GELU_A) * v2))
    return h + h * t, slope


def gelu_slope(v):
    return gelu_both(v)[1]


def loop(n, body, init, unroll=False):
    if unroll:
        for i in range(n):
            init = body(i, init)
        return init
    return lax.fori_loop(0, n, body, init)


def moments(ref, out, row, blocks, params, fold, mask, count):
    inv = 1.0 / jnp.maximum(count, 1.0)
    for p in range(params):
        n = blocks // params

        def first(i, acc):
            return acc + rows8(ref[:, lanes(p + i * params)] * mask)

        zero = jnp.zeros((8, LN), F32)
        s = total(loop(n, first, zero, n <= 4), fold)
        mean = s * inv

        def second(i, acc):
            d = (ref[:, lanes(p + i * params)] - mean) * mask
            return acc + rows8(d * d)

        m2 = total(loop(n, second, zero, n <= 4), fold)
        out[row + p : row + p + 1, :] = s
        out[row + params + p : row + params + p + 1, :] = m2


def send(pay_ref, rows_ref):
    value = rows_ref[...]
    for d in range(pay_ref.shape[0]):
        pay_ref[d] = value


def combine(recv_ref, row, params, count_row, cst_ref, at):
    n = recv_ref[:, count_row : count_row + 1, :]
    s = recv_ref[:, row : row + params, :]
    m2 = recv_ref[:, row + params : row + 2 * params, :]
    k = n.sum(axis=0)
    mean = s.sum(axis=0) / k
    off = s / jnp.maximum(n, 1.0) - mean[None]
    var = (m2 + n * off * off).sum(axis=0) / k
    cst_ref[at : at + params, :] = mean
    cst_ref[at + params : at + 2 * params, :] = lax.rsqrt(var + EPS)
    return k


def pack3(pad, b, mid, left, right, px, grid):
    g, half = b // 2, b % 2
    for slot, value in enumerate((left, mid, right)):
        at = g * 768 + slot * 256 + half * 128
        pad[grid : grid + px, at : at + LN] = value.astype(BF16)


def neighbours(h, px, grid):
    col = lax.broadcasted_iota(jnp.int32, (px, LN), 0) & (grid - 1)
    before = jnp.where(col == 0, 0.0, pltpu.roll(h, 1, 0))
    after = jnp.where(col == grid - 1, 0.0, pltpu.roll(h, px - 1, 0))
    return before, after


def clear_edges(pad, px, grid):
    zero = jnp.zeros((grid, pad.shape[1]), BF16)
    pad[0:grid, :] = zero
    pad[grid + px : grid + px + grid, :] = zero


def put_count(rows_ref, row, count):
    rows_ref[row : row + 1, :] = jnp.zeros((1, LN), F32) + count


def side_sq(side, frames):
    s = side.astype(F32)
    return s * s * frames


class Net:
    def __init__(self, ndp, grid):
        self.ndp = ndp
        self.grid = grid
        self.px = grid * grid

    def fast_first(self, side, xf, wa):
        px, grid, ndp = self.px, self.grid, self.ndp

        def body(side_ref, xf_ref, wa_ref, fa_ref, band_ref, pay_ref, row_ref):
            pick = jnp.where(
                (lax.broadcasted_iota(jnp.int32, (CF_MID, 256), 1) & (CF_MID - 1))
                == lax.broadcasted_iota(jnp.int32, (CF_MID, 256), 0),
                1.0,
                0.0,
            ).astype(BF16)
            wide = [dot(wa_ref[k], pick) for k in range(3)]
            group = lax.broadcasted_iota(jnp.int32, (CF, 256), 1) >> 5
            for j in range(10):
                acc = jnp.zeros((CF, 256), F32)
                for k in range(3):
                    if 0 <= j - k < 8:
                        acc = jnp.where(group == j - k, wide[k], acc)
                band_ref[j * CF : (j + 1) * CF, :] = acc.astype(BF16)
            for g in range(4):
                lo, hi = max(8 * g - 1, 0), min(8 * g + 9, TF)
                k0 = lo - (8 * g - 1)
                fa_ref[:, g * 256 : (g + 1) * 256] = dot(
                    xf_ref[:, lo * CF : hi * CF], band_ref[k0 * CF : (k0 + hi - lo) * CF, :]
                )
            side_v = side_ref[0]
            count = side_sq(side_v, TF)
            moments(fa_ref, row_ref, 0, 8, 1, True, region(side_v, px, grid), count)
            put_count(row_ref, 2, count)
            send(pay_ref, row_ref)

        return call(
            body,
            [((px, 1024), F32), ((10 * CF, 256), BF16), ((ndp, 8, LN), F32)],
            [pltpu.VMEM((8, LN), F32)],
            side, xf, wa,
        )

    def fast_weights(self, wb, wbt, wc):
        def body(wb_ref, wbt_ref, wc_ref, b_ref, bt_ref, c_ref):
            pick = jnp.where(
                (lax.broadcasted_iota(jnp.int32, (CF_MID, 256), 1) & (CF_MID - 1))
                == lax.broadcasted_iota(jnp.int32, (CF_MID, 256), 0),
                1.0,
                0.0,
            ).astype(BF16)
            same = (lax.broadcasted_iota(jnp.int32, (256, 256), 0) >> 5) == (
                lax.broadcasted_iota(jnp.int32, (256, 256), 1) >> 5
            )
            for source, target in ((wb_ref, b_ref), (wbt_ref, bt_ref)):
                for tap in range(9):
                    tiled = jnp.concatenate([dot(source[tap], pick)] * 8, axis=0)
                    target[tap // 3, (tap % 3) * 256 : (tap % 3 + 1) * 256, :] = jnp.where(
                        same, tiled, 0.0
                    ).astype(BF16)
            c_ref[...] = jnp.zeros_like(c_ref)
            for i in range(8):
                c_ref[i * CF_MID : (i + 1) * CF_MID, i * CF : (i + 1) * CF] = wc_ref[...]

        return call(
            body,
            [((3, 768, 256), BF16), ((3, 768, 256), BF16), ((256, 1024), BF16)],
            [],
            wb, wbt, wc, smem=0,
        )

    def conv_stage(self, side, recv, row, crow, x, par, w, params, frames):
        px, grid, ndp = self.px, self.grid, self.ndp
        fold = params == 1

        def body(side_ref, recv_ref, x_ref, par_ref, w_ref, h_ref, y_ref, cst_ref, pay_ref, row_ref, pad):
            side_v = side_ref[0]
            mask = region(side_v, px, grid)
            combine(recv_ref, row, params, crow, cst_ref, 0)
            mean, rs = cst_ref[0:params, :], cst_ref[params : 2 * params, :]
            scale = par_ref[0:params, :] * rs
            shift = par_ref[params : 2 * params, :] - mean * scale
            clear_edges(pad, px, grid)
            for b in range(8):
                p = b % params
                v = x_ref[:, lanes(b)] * scale[p : p + 1] + shift[p : p + 1]
                h = gelu(v) * mask
                h_ref[:, lanes(b)] = h.astype(BF16)
                before, after = neighbours(h, px, grid)
                pack3(pad, b, h, before, after, px, grid)
            for g in range(4):
                acc = None
                for i in range(3):
                    part = dot(pad[grid * i : grid * i + px, g * 768 : (g + 1) * 768], w_ref[i])
                    acc = part if acc is None else acc + part
                y_ref[:, g * 256 : (g + 1) * 256] = acc
            count = side_sq(side_v, frames)
            moments(y_ref, row_ref, 0, 8, params, fold, mask, count)
            put_count(row_ref, 2 * params, count)
            send(pay_ref, row_ref)

        return call(
            body,
            [((px, 1024), BF16), ((px, 1024), F32), ((8, LN), F32), ((ndp, 8, LN), F32)],
            [pltpu.VMEM((8, LN), F32), pltpu.VMEM((px + 2 * grid, 4 * 768), BF16)],
            side, recv, x, par, w,
        )

    def expand_stage(self, side, recv, y, par, w, params, wide, frames):
        px, grid, ndp = self.px, self.grid, self.ndp
        rows = -(-(2 * wide + 1) // 8) * 8

        def body(side_ref, recv_ref, y_ref, par_ref, w_ref, h_ref, cst_ref, pay_ref, row_ref, c_ref):
            side_v = side_ref[0]
            mask = region(side_v, px, grid)
            combine(recv_ref, 0, params, 2 * params, cst_ref, 0)
            mean, rs = cst_ref[0:params, :], cst_ref[params : 2 * params, :]
            scale = par_ref[0:params, :] * rs
            shift = par_ref[params : 2 * params, :] - mean * scale
            for b in range(8):
                p = b % params
                v = y_ref[:, lanes(b)] * scale[p : p + 1] + shift[p : p + 1]
                h_ref[:, lanes(b)] = (gelu(v) * mask).astype(BF16)
            for g in range(4):
                c_ref[:, g * 1024 : (g + 1) * 1024] = dot(h_ref[:, g * 256 : (g + 1) * 256], w_ref[...])
            count = side_sq(side_v, frames)
            moments(c_ref, row_ref, 0, 32, wide, False, mask, count)
            put_count(row_ref, 2 * wide, count)
            send(pay_ref, row_ref)

        return call(
            body,
            [((px, 1024), BF16), ((8, LN), F32), ((ndp, rows, LN), F32)],
            [pltpu.VMEM((rows, LN), F32), pltpu.VMEM((px, 4096), F32)],
            side, recv, y, par, w,
        )

    def fast_finish(self, side, recv, h2, w, xf, par, wlat):
        px, grid = self.px, self.grid

        def body(side_ref, recv_ref, h_ref, w_ref, xf_ref, par_ref, wl_ref, out_ref, lat_ref, cst_ref, c_ref):
            mask = region(side_ref[0], px, grid)
            combine(recv_ref, 0, 1, 2, cst_ref, 0)
            scale = par_ref[0:1, :] * cst_ref[1:2, :]
            shift = par_ref[1:2, :] - cst_ref[0:1, :] * scale
            for g in range(4):
                c_ref[...] = dot(h_ref[:, g * 256 : (g + 1) * 256], w_ref[...])

                def step(i, carry):
                    f = g * 8 + i
                    v = c_ref[:, lanes(i)] * scale + shift + xf_ref[:, lanes(f)].astype(F32)
                    out_ref[:, lanes(f)] = (gelu(v) * mask).astype(BF16)
                    return carry

                loop(8, step, 0)
            for t in range(TS):
                lo = max(ALPHA * t - 2, 0)
                k0 = lo - (ALPHA * t - 2)
                lat_ref[:, t * LAT : (t + 1) * LAT] = dot(
                    out_ref[:, lo * CF : (ALPHA * t + 3) * CF], wl_ref[k0 * CF :, :]
                ).astype(BF16)

        return call(
            body,
            [((px, 4096), BF16), ((px, 1024), BF16), ((8, LN), F32)],
            [pltpu.VMEM((px, 1024), F32)],
            side, recv, h2, w, xf, par, wlat,
        )

    def fast_slope(self, side, h2, w, xf, par, cst):
        px, grid = self.px, self.grid

        def body(side_ref, h_ref, w_ref, xf_ref, par_ref, cst_ref, gp_ref, c_ref):
            mask = region(side_ref[0], px, grid)
            scale = par_ref[0:1, :] * cst_ref[1:2, :]
            shift = par_ref[1:2, :] - cst_ref[0:1, :] * scale
            for g in range(4):
                c_ref[...] = dot(h_ref[:, g * 256 : (g + 1) * 256], w_ref[...])

                def step(i, carry):
                    f = g * 8 + i
                    v = c_ref[:, lanes(i)] * scale + shift + xf_ref[:, lanes(f)].astype(F32)
                    gp_ref[:, lanes(f)] = gelu_slope(v) * mask
                    return carry

                loop(8, step, 0)

        return call(body, ((px, 4096), F32), [pltpu.VMEM((px, 1024), F32)], side, h2, w, xf, par, cst)

    def slow_start(self, xs, wa, wp):
        px = self.px

        def body(x_ref, wa_ref, wp_ref, a_ref, p_ref):
            for t in range(TS):
                x = x_ref[:, t * CS : (t + 1) * CS]
                a_ref[:, t * CS_MID : (t + 1) * CS_MID] = dot(x, wa_ref[0:CS, :])
                p_ref[:, t * CS : (t + 1) * CS] = dot(x, wp_ref[0:CS, :])

        return call(body, [((px, 1024), F32), ((px, 4096), F32)], [], xs, wa, wp, smem=0)

    def slow_first(self, side, pa, pp, lat, wa, wp):
        px, grid, ndp = self.px, self.grid, self.ndp

        def body(side_ref, pa_ref, pp_ref, lat_ref, wa_ref, wp_ref, sa_ref, sp_ref, pay_ref, row_ref):
            side_v = side_ref[0]
            mask = region(side_v, px, grid)
            for t in range(TS):
                x = lat_ref[:, t * LAT : (t + 1) * LAT]
                a, p = slice(t * CS_MID, (t + 1) * CS_MID), slice(t * CS, (t + 1) * CS)
                sa_ref[:, a] = pa_ref[:, a] + dot(x, wa_ref[...])
                sp_ref[:, p] = pp_ref[:, p] + dot(x, wp_ref[...])
            count = side_sq(side_v, TS)
            moments(sa_ref, row_ref, 0, 8, 2, False, mask, count)
            moments(sp_ref, row_ref, 4, 32, 8, False, mask, count)
            put_count(row_ref, 20, count)
            send(pay_ref, row_ref)

        return call(
            body,
            [((px, 1024), F32), ((px, 4096), F32), ((ndp, 24, LN), F32)],
            [pltpu.VMEM((24, LN), F32)],
            side, pa, pp, lat, wa, wp,
        )

    def slow_top(self, side, recv3, recv1, h2, w, sp, gs, parc, parp):
        px, grid, ndp = self.px, self.grid, self.ndp

        def body(
            side_ref, r3_ref, r1_ref, h_ref, w_ref, sp_ref, gs_ref, pc_ref, pp_ref,
            ys_ref, ds_ref, cc_ref, cp_ref, pay_ref, row_ref, c_ref, acc_ref,
        ):
            mask = region(side_ref[0], px, grid)
            combine(r3_ref, 0, 8, 16, cc_ref, 0)
            combine(r1_ref, 4, 8, 20, cp_ref, 0)
            acc_ref[...] = jnp.zeros_like(acc_ref)
            for t in range(TS):
                c_ref[...] = dot(h_ref[:, t * 256 : (t + 1) * 256], w_ref[...])

                def step(b, carry):
                    at = lanes(t * 8 + b)
                    one = pl.ds(b, 1)
                    up = pl.ds(b + 8, 1)
                    xc = (c_ref[:, lanes(b)] - cc_ref[one, :]) * cc_ref[up, :]
                    xp = (sp_ref[:, at] - cp_ref[one, :]) * cp_ref[up, :]
                    v = (
                        xc * pc_ref[one, :]
                        + xp * pp_ref[one, :]
                        + (pc_ref[up, :] + pp_ref[up, :])
                    )
                    y, slope = gelu_both(v)
                    ys_ref[:, at] = (y * mask).astype(BF16)
                    d = gs_ref[:, at].astype(F32) * slope * mask
                    ds_ref[:, at] = d
                    acc_ref[b] += rows8(d)
                    acc_ref[8 + b] += rows8(d * xc)
                    acc_ref[16 + b] += rows8(d * xp)
                    return carry

                loop(8, step, 0)
            row_ref[...] = acc_ref[...].sum(axis=1)
            send(pay_ref, row_ref)

        return call(
            body,
            [
                ((px, 4096), BF16), ((px, 4096), F32), ((16, LN), F32), ((16, LN), F32),
                ((ndp, 24, LN), F32),
            ],
            [pltpu.VMEM((24, LN), F32), pltpu.VMEM((px, 1024), F32), pltpu.VMEM((24, 8, LN), F32)],
            side, recv3, recv1, h2, w, sp, gs, parc, parp,
        )

    def fast_top(self, dlat, wlat, gf, gp, h2, w, cst):
        px, ndp = self.px, self.ndp

        def body(dl_ref, wl_ref, gf_ref, gp_ref, h_ref, w_ref, cst_ref, ds_ref, pay_ref, row_ref, lt_ref, c_ref, acc_ref):
            for t in range(TS):
                lt_ref[:, t * 640 : (t + 1) * 640] = dot_t(dl_ref[:, t * LAT : (t + 1) * LAT], wl_ref[...])
            lt_ref[:, TS * 640 : TS * 640 + 256] = jnp.zeros((px, 256), F32)
            acc_ref[...] = jnp.zeros_like(acc_ref)
            mean, rs = cst_ref[0:1, :], cst_ref[1:2, :]
            for g in range(4):
                c_ref[...] = dot(h_ref[:, g * 256 : (g + 1) * 256], w_ref[...])
                for i in range(8):
                    at = lanes(g * 8 + i)
                    d = gf_ref[:, at].astype(F32)
                    if i < 3:
                        d = d + lt_ref[:, lanes(g * 5 + i + 2)]
                    elif i >= 6:
                        d = d + lt_ref[:, lanes((g + 1) * 5 + i - 6)]
                    d = d * gp_ref[:, at]
                    ds_ref[:, at] = d
                    xh = (c_ref[:, lanes(i)] - mean) * rs
                    acc_ref[0] += rows8(d)
                    acc_ref[1] += rows8(d * xh)
            row_ref[...] = jnp.zeros_like(row_ref)
            row_ref[0:2, :] = acc_ref[...].sum(axis=1)
            send(pay_ref, row_ref)

        return call(
            body,
            [((px, 4096), F32), ((ndp, 8, LN), F32)],
            [
                pltpu.VMEM((8, LN), F32), pltpu.VMEM((px, TS * 640 + 256), F32),
                pltpu.VMEM((px, 1024), F32), pltpu.VMEM((2, 8, LN), F32),
            ],
            dlat, wlat, gf, gp, h2, w, cst, smem=0,
        )

    def expand_back(self, side, kcount, recv, ds, h2, w, cstw, parw, y, cst, par, params, wide, shortcut=None):
        px, grid, ndp = self.px, self.grid, self.ndp
        fold = params == 1
        both = shortcut is not None
        srows = 3 * wide if both else 8

        def body(*refs):
            side_ref, k_ref, recv_ref, ds_ref, h_ref, w_ref, cw_ref, pw_ref, y_ref, cs_ref, par_ref = refs[:11]
            refs = refs[11:]
            if both:
                sp_ref, cp_ref, pp_ref = refs[:3]
                refs = refs[3:]
                dp_ref = refs[0]
                refs = refs[1:]
            dc_ref, dn_ref, sum_ref, pay_ref, row_ref, c_ref, k3_ref = refs
            mask = region(side_ref[0], px, grid)
            inv_k = 1.0 / k_ref[0]
            sums = recv_ref[...].sum(axis=0)
            sum_ref[...] = sums
            a = pw_ref[0:wide, :] * cw_ref[wide : 2 * wide, :]
            k3_ref[0:wide, :] = a
            k3_ref[wide : 2 * wide, :] = a * inv_k * sums[0:wide]
            k3_ref[2 * wide : 3 * wide, :] = a * inv_k * cw_ref[wide : 2 * wide, :] * sums[wide : 2 * wide]
            if both:
                a = pp_ref[0:wide, :] * cp_ref[wide : 2 * wide, :]
                k3_ref[3 * wide : 4 * wide, :] = a
                k3_ref[4 * wide : 5 * wide, :] = a * inv_k * sums[0:wide]
                k3_ref[5 * wide : 6 * wide, :] = (
                    a * inv_k * cp_ref[wide : 2 * wide, :] * sums[2 * wide : 3 * wide]
                )
            mean, rs = cs_ref[0:params, :], cs_ref[params : 2 * params, :]
            accs = [[jnp.zeros((8, LN), F32) for _ in range(params)] for _ in range(2)]
            for g in range(4):
                c_ref[...] = dot(h_ref[:, g * 256 : (g + 1) * 256], w_ref[...])

                def step(b, carry):
                    at = lanes(g * 8 + b)
                    p = b if wide == 8 else 0
                    d = ds_ref[:, at]
                    e = (c_ref[:, lanes(b)] - cw_ref[pl.ds(p, 1), :]) * k3_ref[pl.ds(2 * wide + p, 1), :]
                    e = d * k3_ref[pl.ds(p, 1), :] - k3_ref[pl.ds(wide + p, 1), :] - e
                    dc_ref[:, at] = (e * mask).astype(BF16)
                    if both:
                        e = (sp_ref[:, at] - cp_ref[pl.ds(p, 1), :]) * k3_ref[pl.ds(5 * wide + p, 1), :]
                        e = d * k3_ref[pl.ds(3 * wide + p, 1), :] - k3_ref[pl.ds(4 * wide + p, 1), :] - e
                        dp_ref[:, at] = (e * mask).astype(BF16)
                    return carry

                loop(8, step, 0)
                dh = dot_t(dc_ref[:, g * 1024 : (g + 1) * 1024], w_ref[...])
                for half in range(2):
                    b = g * 2 + half
                    p = b % params
                    xh = (y_ref[:, lanes(b)] - mean[p : p + 1]) * rs[p : p + 1]
                    v = xh * par_ref[p : p + 1, :] + par_ref[params + p : params + p + 1, :]
                    d = dh[:, half * LN : (half + 1) * LN] * gelu_slope(v) * mask
                    dn_ref[:, lanes(b)] = d
                    accs[0][p] = accs[0][p] + rows8(d)
                    accs[1][p] = accs[1][p] + rows8(d * xh)
            row_ref[...] = jnp.zeros_like(row_ref)
            for q in range(2):
                for p in range(params):
                    row_ref[q * params + p : q * params + p + 1, :] = total(accs[q][p], fold)
            send(pay_ref, row_ref)

        outs = [((px, 4096), BF16)] if both else []
        outs += [((px, 4096), BF16), ((px, 1024), F32), ((srows, LN), F32), ((ndp, 8, LN), F32)]
        extra = list(shortcut) if both else []
        return call(
            body,
            outs,
            [pltpu.VMEM((8, LN), F32), pltpu.VMEM((px, 1024), F32), pltpu.VMEM((max(6 * wide, 8), LN), F32)],
            side, kcount, recv, ds, h2, w, cstw, parw, y, cst, par, *extra, smem=2,
        )

    def conv_back(self, side, kcount, recv, dn, y, cst2, par2, wt, x, cst1, par1, params):
        px, grid, ndp = self.px, self.grid, self.ndp
        fold = params == 1

        def body(
            side_ref, k_ref, recv_ref, dn_ref, y_ref, c2_ref, p2_ref, w_ref, x_ref, c1_ref, p1_ref,
            db_ref, dn1_ref, sum_ref, pay_ref, row_ref, pad,
        ):
            mask = region(side_ref[0], px, grid)
            inv_k = 1.0 / k_ref[0]
            sums = recv_ref[...].sum(axis=0)
            sum_ref[...] = sums
            mean2, rs2 = c2_ref[0:params, :], c2_ref[params : 2 * params, :]
            a = p2_ref[0:params, :] * rs2
            b0 = a * inv_k * sums[0:params]
            c0 = a * inv_k * rs2 * sums[params : 2 * params]
            clear_edges(pad, px, grid)
            for b in range(8):
                p = b % params
                e = (y_ref[:, lanes(b)] - mean2[p : p + 1]) * c0[p : p + 1]
                e = (dn_ref[:, lanes(b)] * a[p : p + 1] - b0[p : p + 1] - e) * mask
                db_ref[:, lanes(b)] = e.astype(BF16)
                before, after = neighbours(e, px, grid)
                pack3(pad, b, e, after, before, px, grid)
            mean, rs = c1_ref[0:params, :], c1_ref[params : 2 * params, :]
            accs = [[jnp.zeros((8, LN), F32) for _ in range(params)] for _ in range(2)]
            for g in range(4):
                dh = None
                for i in range(3):
                    part = dot(pad[grid * i : grid * i + px, g * 768 : (g + 1) * 768], w_ref[2 - i])
                    dh = part if dh is None else dh + part
                for half in range(2):
                    b = g * 2 + half
                    p = b % params
                    xh = (x_ref[:, lanes(b)] - mean[p : p + 1]) * rs[p : p + 1]
                    v = xh * p1_ref[p : p + 1, :] + p1_ref[params + p : params + p + 1, :]
                    d = dh[:, half * LN : (half + 1) * LN] * gelu_slope(v) * mask
                    dn1_ref[:, lanes(b)] = d
                    accs[0][p] = accs[0][p] + rows8(d)
                    accs[1][p] = accs[1][p] + rows8(d * xh)
            row_ref[...] = jnp.zeros_like(row_ref)
            for q in range(2):
                for p in range(params):
                    row_ref[q * params + p : q * params + p + 1, :] = total(accs[q][p], fold)
            send(pay_ref, row_ref)

        return call(
            body,
            [((px, 1024), BF16), ((px, 1024), F32), ((8, LN), F32), ((ndp, 8, LN), F32)],
            [pltpu.VMEM((8, LN), F32), pltpu.VMEM((px + 2 * grid, 4 * 768), BF16)],
            side, kcount, recv, dn, y, cst2, par2, wt, x, cst1, par1, smem=2,
        )

    def slow_last(self, side, kcount, recv, dn, x, cst, par, dp, wa, wp):
        px, grid = self.px, self.grid

        def body(side_ref, k_ref, recv_ref, dn_ref, x_ref, cst_ref, par_ref, dp_ref, wa_ref, wp_ref, da_ref, dl_ref, sum_ref):
            mask = region(side_ref[0], px, grid)
            inv_k = 1.0 / k_ref[0]
            sums = recv_ref[...].sum(axis=0)
            sum_ref[...] = sums
            mean, rs = cst_ref[0:2, :], cst_ref[2:4, :]
            a = par_ref[0:2, :] * rs
            b0 = a * inv_k * sums[0:2]
            c0 = a * inv_k * rs * sums[2:4]
            for b in range(8):
                p = b % 2
                e = (x_ref[:, lanes(b)] - mean[p : p + 1]) * c0[p : p + 1]
                e = (dn_ref[:, lanes(b)] * a[p : p + 1] - b0[p : p + 1] - e) * mask
                da_ref[:, lanes(b)] = e.astype(BF16)
            for t in range(TS):
                h = slice(t * CS_MID, (t + 1) * CS_MID)
                dl_ref[:, t * LAT : (t + 1) * LAT] = (
                    dot_t(da_ref[:, h], wa_ref[...])
                    + dot_t(dp_ref[:, t * CS : (t + 1) * CS], wp_ref[...])
                ).astype(BF16)

        return call(
            body,
            [((px, 1024), BF16), ((px, 1024), BF16), ((8, LN), F32)],
            [],
            side, kcount, recv, dn, x, cst, par, dp, wa, wp, smem=2,
        )

    def slow_input_grad(self, da, dp, wa, wp):
        px = self.px

        def body(da_ref, dp_ref, wa_ref, wp_ref, dx_ref):
            for t in range(TS):
                dx_ref[:, t * CS : (t + 1) * CS] = (
                    dot_t(da_ref[:, t * CS_MID : (t + 1) * CS_MID], wa_ref[0:CS, :])
                    + dot_t(dp_ref[:, t * CS : (t + 1) * CS], wp_ref[0:CS, :])
                ).astype(BF16)

        return call(body, ((px, 4096), BF16), [], da, dp, wa, wp, smem=0)

    def fast_last(self, side, kcount, recv, dn, x, cst, par, ds, band):
        px, grid = self.px, self.grid

        def body(side_ref, k_ref, recv_ref, dn_ref, x_ref, cst_ref, par_ref, ds_ref, band_ref, da_ref, dx_ref, sum_ref, acc_ref):
            mask = region(side_ref[0], px, grid)
            inv_k = 1.0 / k_ref[0]
            sums = recv_ref[...].sum(axis=0)
            sum_ref[...] = sums
            mean, rs = cst_ref[0:1, :], cst_ref[1:2, :]
            a = par_ref[0:1, :] * rs
            b0 = a * inv_k * sums[0:1]
            c0 = a * inv_k * rs * sums[1:2]
            for b in range(8):
                e = (x_ref[:, lanes(b)] - mean) * c0
                e = (dn_ref[:, lanes(b)] * a - b0 - e) * mask
                da_ref[:, lanes(b)] = e.astype(BF16)
            for g in range(4):
                part = dot_t(da_ref[:, g * 256 : (g + 1) * 256], band_ref[...])
                base = 8 * g * CF
                if g == 0:
                    acc_ref[:, 0 : 10 * CF] = part
                else:
                    acc_ref[:, base : base + 2 * CF] += part[:, 0 : 2 * CF]
                    acc_ref[:, base + 2 * CF : base + 10 * CF] = part[:, 2 * CF :]

            def step(f, carry):
                dx_ref[:, lanes(f)] = (ds_ref[:, lanes(f)] + acc_ref[:, lanes(f + 1)]).astype(BF16)
                return carry

            loop(TF, step, 0)

        return call(
            body,
            [((px, 1024), BF16), ((px, 4096), BF16), ((8, LN), F32)],
            [pltpu.VMEM((px, 34 * CF), F32)],
            side, kcount, recv, dn, x, cst, par, ds, band, smem=2,
        )

    def fast_kernel_grads(self, xf, da, h1, db, h2, dc):
        px, grid = self.px, self.grid

        def body(x_ref, da_ref, h1_ref, db_ref, h2_ref, dc_ref, ga_ref, gb_ref, gc_ref, pad):
            group = lax.broadcasted_iota(jnp.int32, (CF, 256), 1) >> 5

            def fold(v):
                v = v[:, 0:LN] + v[:, LN:256]
                v = v + pltpu.roll(v, 32, 1)
                v = v + pltpu.roll(v, 64, 1)
                return v[:, 0:CF_MID]

            accs = [jnp.zeros((CF, 256), F32) for _ in range(3)]
            for g in range(4):
                lo, hi = max(8 * g - 1, 0), min(8 * g + 9, TF)
                k0 = lo - (8 * g - 1)
                d = da_ref[:, g * 256 : (g + 1) * 256]
                for j in range(k0, k0 + hi - lo):
                    f = 8 * g - 1 + j
                    part = dot(x_ref[:, f * CF : (f + 1) * CF].T, d)
                    for k in range(3):
                        if 0 <= j - k < 8:
                            accs[k] = accs[k] + jnp.where(group == j - k, part, 0.0)
            for k in range(3):
                ga_ref[k] = fold(accs[k])
            clear_edges(pad, px, grid)
            for b in range(8):
                h = h1_ref[:, lanes(b)].astype(F32)
                before, after = neighbours(h, px, grid)
                pack3(pad, b, h, before, after, px, grid)
            same = (lax.broadcasted_iota(jnp.int32, (256, 256), 0) >> 5) == (
                lax.broadcasted_iota(jnp.int32, (256, 256), 1) >> 5
            )
            for i in range(3):
                for s in range(3):
                    acc = jnp.zeros((256, 256), F32)
                    for g in range(4):
                        at = g * 768 + s * 256
                        acc = acc + dot(
                            pad[grid * i : grid * i + px, at : at + 256].T,
                            db_ref[:, g * 256 : (g + 1) * 256],
                        )
                    acc = jnp.where(same, acc, 0.0).reshape(8, CF_MID, 256).sum(axis=0)
                    gb_ref[3 * i + s] = fold(acc)
            acc = jnp.zeros((256, 1024), F32)
            for g in range(4):
                acc = acc + dot(h2_ref[:, g * 256 : (g + 1) * 256].T, dc_ref[:, g * 1024 : (g + 1) * 1024])
            out = None
            for i in range(8):
                part = acc[i * CF_MID : (i + 1) * CF_MID, i * CF : (i + 1) * CF]
                out = part if out is None else out + part
            gc_ref[...] = out

        return call(
            body,
            [((3, CF, CF_MID), F32), ((9, CF_MID, CF_MID), F32), ((CF_MID, CF), F32)],
            [pltpu.VMEM((px + 2 * grid, 4 * 768), BF16)],
            xf, da, h1, db, h2, dc, smem=0,
        )

    def slow_kernel_grads(self, plan, xs, lat, da, dp, h1, db, h2, dc, yf, dlat, pay1, pay2, pay3):
        px, grid = self.px, self.grid
        inner, outer, first, chunk = plan.inner, plan.outer, plan.first, plan.chunk
        ndp = self.ndp

        def body(
            x_ref, lat_ref, da_ref, dp_ref, h1_ref, db_ref, h2_ref, dc_ref, yf_ref, dl_ref,
            p1_ref, p2_ref, p3_ref, out_ref, buf, pad, xt,
        ):
            def put(base, value, wide):
                n = value.shape[0]
                for j in range(wide):
                    buf[pl.ds(base + j, n, stride=wide), :] = value[:, j * LN : (j + 1) * LN]

            for c in range((CS + LAT) // 256):
                acc_a = acc_p = None
                for t in range(TS):
                    if c < CS // 256:
                        x = x_ref[:, t * CS + c * 256 : t * CS + (c + 1) * 256]
                    else:
                        x = lat_ref[:, t * LAT : (t + 1) * LAT]
                    xt[:, t * px : (t + 1) * px] = x.T
                for t in range(TS):
                    part = dot(xt[:, t * px : (t + 1) * px], da_ref[:, t * CS_MID : (t + 1) * CS_MID])
                    acc_a = part if acc_a is None else acc_a + part
                put(ROW_SA + c * 512, acc_a, 2)
                for q in range(4):
                    acc_p = None
                    for t in range(TS):
                        at = t * CS + q * 256
                        part = dot(xt[:, t * px : (t + 1) * px], dp_ref[:, at : at + 256])
                        acc_p = part if acc_p is None else acc_p + part
                    for j in range(2):
                        buf[pl.ds(ROW_SP + c * 2048 + 2 * q + j, 256, stride=8), :] = acc_p[:, j * LN : (j + 1) * LN]
            for t in range(TS):
                xt[:, t * px : (t + 1) * px] = h2_ref[:, t * 256 : (t + 1) * 256].T
            for q in range(4):
                acc_p = None
                for t in range(TS):
                    at = t * CS + q * 256
                    part = dot(xt[:, t * px : (t + 1) * px], dc_ref[:, at : at + 256])
                    acc_p = part if acc_p is None else acc_p + part
                for j in range(2):
                    buf[pl.ds(ROW_SC + 2 * q + j, 256, stride=8), :] = acc_p[:, j * LN : (j + 1) * LN]
            clear_edges(pad, px, grid)
            for b in range(8):
                h = h1_ref[:, lanes(b)].astype(F32)
                before, after = neighbours(h, px, grid)
                pack3(pad, b, h, before, after, px, grid)
            for i in range(3):
                for s in range(3):
                    acc = None
                    for t in range(TS):
                        at = t * 768 + s * 256
                        part = dot(
                            pad[grid * i : grid * i + px, at : at + 256].T,
                            db_ref[:, t * 256 : (t + 1) * 256],
                        )
                        acc = part if acc is None else acc + part
                    put(ROW_SB + (3 * i + s) * 512, acc, 2)
            for k in range(5):
                acc = jnp.zeros((CF, LAT), F32)
                for t in range(TS):
                    f = ALPHA * t - 2 + k
                    if f >= 0:
                        acc = acc + dot(yf_ref[:, f * CF : (f + 1) * CF].T, dl_ref[:, t * LAT : (t + 1) * LAT])
                put(ROW_LAT + k * 256, acc, 2)
            for gain, base in ((1, ROW_SG), (0, ROW_SG + SLOW_VEC)):
                buf[base : base + 2, :] = p1_ref[0, 2 * gain : 2 * gain + 2, :]
                buf[base + 2 : base + 4, :] = p2_ref[0, 2 * gain : 2 * gain + 2, :]
                buf[base + 4 : base + 12, :] = p3_ref[0, 8 * gain : 8 * gain + 8, :]
                buf[base + 12 : base + 20, :] = p3_ref[0, 16 * gain : 16 * gain + 8, :]
            buf[ROW_FA:ROW_LAT, :] = jnp.zeros((ROW_LAT - ROW_FA, LN), F32)
            buf[ROW_FG:, :] = jnp.zeros((buf.shape[0] - ROW_FG, LN), F32)
            for path in range(2):
                for dp_at in range(ndp):
                    r0 = first[path * ndp + dp_at]
                    out_ref[dp_at % inner, dp_at // inner, path] = buf[r0 : r0 + chunk, :].astype(BF16)

        return call(
            body,
            ((inner, outer, 2, chunk, LN), BF16),
            [
                pltpu.VMEM((plan.rows, LN), F32),
                pltpu.VMEM((px + 2 * grid, 4 * 768), BF16),
                pltpu.VMEM((256, TS * px), BF16),
            ],
            xs, lat, da, dp, h1, db, h2, dc, yf, dlat, pay1, pay2, pay3, smem=0, limit=56,
        )

    def window(self, plan, ints, mine, theirs, small, tail):
        chunk, out_rows = plan.chunk, plan.out_rows
        pad = small.shape[0] + 8

        def body(int_ref, mine_ref, theirs_ref, small_ref, tail_ref, out_ref, a_ref):
            fast = int_ref[0]
            r0 = int_ref[1]
            row = int_ref[2]
            lane = int_ref[3]
            a_ref[...] = jnp.zeros_like(a_ref)
            ns = small_ref.shape[0]
            for ref, start in ((small_ref, ROW_FA), (tail_ref, ROW_FG)):
                at = jnp.clip(start - r0, -ref.shape[0], chunk) + pad
                a_ref[pl.ds(at, ref.shape[0]), :] = ref[...]
            body_rows = a_ref[pad : pad + chunk, :]
            body_rows = jnp.where(fast == 1, theirs_ref[...] + body_rows, mine_ref[...])
            a_ref[pad : pad + chunk, :] = body_rows
            one = a_ref[pl.ds(pad + row, out_rows), :]
            two = a_ref[pl.ds(pad + row + 1, out_rows), :]
            shift = (LN - lane) & (LN - 1)
            one = pltpu.roll(one, shift, 1)
            two = pltpu.roll(two, shift, 1)
            at = lax.broadcasted_iota(jnp.int32, (out_rows, LN), 1)
            out_ref[...] = jnp.where(at < LN - lane, one, two)

        return call(
            body,
            ((out_rows, LN), F32),
            [pltpu.VMEM((chunk + 2 * pad + 8, LN), F32)],
            ints, mine, theirs, small, tail,
        )


class Plan:
    def __init__(self, ndp):
        n = 2 * ndp
        total_values = 2685312
        self.share = total_values // n
        self.first = [self.share * d // LN // 16 * 16 for d in range(n)]
        ends = [-(-self.share * (d + 1) // LN) for d in range(n)]
        self.chunk = -(-max(e - f for e, f in zip(ends, self.first)) // 16) * 16
        self.rows = -(-max(max(f + self.chunk for f in self.first), ROWS) // 16) * 16
        self.out_rows = -(-self.share // LN)
        self.outer = 4 if ndp % 4 == 0 else 1
        self.inner = ndp // self.outer
        self.near = [[o * self.inner + i for i in range(self.inner)] for o in range(self.outer)]
        self.far = [[o * self.inner + i for o in range(self.outer)] for i in range(self.inner)]


def exchange(x, groups=None):
    return lax.all_to_all(x, "dp", 0, 0, axis_index_groups=groups)


def local(
    acts, cotangent, clip_res, w_slow_a, w_slow_b, w_slow_c, w_slow_proj, slow_gain, slow_bias,
    w_fast_a, w_fast_b, w_fast_c, w_lateral, fast_gain, fast_bias,
):
    grid = acts.shape[2]
    px = grid * grid
    ndp = lax.axis_size("dp")
    net = Net(ndp, grid)
    plan = Plan(ndp)
    is_fast = lax.axis_index("path") == 1
    level = clip_res[0]
    side = jnp.where(
        level == 1, grid * 5 // 8, jnp.where(level == 2, grid * 7 // 8, jnp.where(level == 3, grid, 0))
    ).astype(jnp.int32).reshape(1)
    x = acts.reshape(px, 4096)
    cot = cotangent.reshape(px, 4096)

    sg, sb_ = slow_gain.reshape(SLOW_VEC, LN), slow_bias.reshape(SLOW_VEC, LN)

    def slow_par(a, b):
        return jnp.concatenate([sg[a:b], sb_[a:b]], axis=0)

    def fast_par(a, b):
        one = jnp.stack([fast_gain[a:b], fast_bias[a:b]])
        return jnp.tile(one, (1, LN // (b - a)))

    wlat = w_lateral.reshape(5 * CF, LAT)
    wa_lat, wp_lat = w_slow_a[CS:], w_slow_proj[CS:]

    def fast_forward(x):
        p1, p2, p3 = fast_par(0, 32), fast_par(32, 64), fast_par(64, 192)
        wb, wbt, wc = net.fast_weights(w_fast_b, w_fast_b.transpose(0, 2, 1), w_fast_c)
        fa, band, pay = net.fast_first(side, x, w_fast_a)
        r1 = exchange(pay)
        h1, fb, c1, pay = net.conv_stage(side, r1, 0, 2, fa, p1, wb, 1, TF)
        r2 = exchange(pay)
        h2, c2, pay = net.expand_stage(side, r2, fb, p2, wc, 1, 1, TF)
        r3 = exchange(pay)
        out, lat, c3 = net.fast_finish(side, r3, h2, wc, x, p3, wlat)
        pixels = r1[:, 2, 0].sum().reshape(1)
        return fa, h1, fb, h2, out, lat, empty((px, 4096), F32), band, wbt, wc, c1, c2, c3, pixels

    def slow_forward(x):
        pa, pp = net.slow_start(x, w_slow_a, w_slow_proj)
        wt = w_slow_b.transpose(0, 2, 1).reshape(3, 768, 256)
        e = empty
        return (
            pa, e((px, 1024), BF16), e((px, 1024), F32), e((px, 1024), BF16), e((px, 4096), BF16),
            e((px, 1024), BF16), pp, e((10 * CF, 256), BF16), wt, e((256, 1024), BF16),
            e((8, LN), F32), e((8, LN), F32), e((8, LN), F32), e((1,), F32),
        )

    first, h1, second, h2, out_f, lat, pp, band, wt, wc, c1, c2, c3, kf = lax.cond(
        is_fast, fast_forward, slow_forward, x
    )
    lat_s = lax.ppermute(lat, "path", SWAP)
    yf_s = lax.ppermute(out_f, "path", SWAP)

    def slow_middle(args):
        lat_s, pa, pp, wt = args[:4]
        p1, p2, p3, pp3 = slow_par(0, 2), slow_par(2, 4), slow_par(4, 12), slow_par(12, 20)
        sa, sp, pay = net.slow_first(side, pa, pp, lat_s, wa_lat, wp_lat)
        r1 = exchange(pay)
        h1, sb, c1, pay = net.conv_stage(side, r1, 0, 20, sa, p1, w_slow_b.reshape(3, 768, 256), 2, TS)
        r2 = exchange(pay)
        h2, c2, pay = net.expand_stage(side, r2, sb, p2, w_slow_c, 2, 8, TS)
        r3 = exchange(pay)
        ks = r3[:, 16, 0].sum().reshape(1)
        ys, ds, cc, cp, pay3 = net.slow_top(side, r3, r1, h2, w_slow_c, sp, cot, p3, pp3)
        r = exchange(pay3)
        dp, dc, dn2, _, pay2 = net.expand_back(
            side, ks, r, ds, h2, w_slow_c, cc, p3, sb, c2, p2, 2, 8, (sp, cp, pp3)
        )
        r = exchange(pay2)
        db, dn1, _, pay1 = net.conv_back(side, ks, r, dn2, sb, c2, p2, wt, sa, c1, p1, 2)
        r = exchange(pay1)
        da, dlat, _ = net.slow_last(side, ks, r, dn1, sa, c1, p1, dp, wa_lat, wp_lat)
        return (
            ys, dlat, da, dp, dc, db, h1, h2, pay1, pay2, pay3, empty((px, 4096), F32),
        )

    def fast_middle(args):
        x, h2, wc, c3, out_f = args[4:]
        gp = net.fast_slope(side, h2, wc, x, fast_par(64, 192), c3)
        e = empty
        return (
            out_f, e((px, 1024), BF16), e((px, 1024), BF16), e((px, 4096), BF16), e((px, 4096), BF16),
            e((px, 1024), BF16), e((px, 1024), BF16), e((px, 1024), BF16), e((ndp, 8, LN), F32),
            e((ndp, 8, LN), F32), e((ndp, 24, LN), F32), gp,
        )

    out, dlat, da_s, dp_s, dc_s, db_s, h1_s, h2_s, pay1, pay2, pay3, gp = lax.cond(
        is_fast, fast_middle, slow_middle, (lat_s, first, pp, wt, x, h2, wc, c3, out_f)
    )
    dlat_f = lax.ppermute(dlat, "path", SWAP)

    def fast_backward(args):
        dlat, gp, x, fa, h1, fb, h2, wbt, wc, band, c1, c2, c3, kf = args[:14]
        p1, p2, p3 = fast_par(0, 32), fast_par(32, 64), fast_par(64, 192)
        ds, pay = net.fast_top(dlat, wlat, cot, gp, h2, wc, c3)
        r = exchange(pay)
        dc, dn2, s3, pay = net.expand_back(side, kf, r, ds, h2, wc, c3, p3, fb, c2, p2, 1, 1)
        r = exchange(pay)
        db, dn1, s2, pay = net.conv_back(side, kf, r, dn2, fb, c2, p2, wbt, fa, c1, p1, 1)
        r = exchange(pay)
        da, dx, s1 = net.fast_last(side, kf, r, dn1, fa, c1, p1, ds, band)
        ga, gb, gc = net.fast_kernel_grads(x, da, h1, db, h2, dc)
        rows = jnp.concatenate([v.reshape(-1, LN) for v in (ga, gb, gc)], axis=0)
        rows = jnp.pad(rows, ((0, -rows.shape[0] % 16), (0, 0))).astype(BF16)
        small = exchange(jnp.broadcast_to(rows[None], (ndp,) + rows.shape)).astype(F32).sum(axis=0)
        tail = jnp.concatenate(
            [s1[1, :32], s2[1, :32], s3[1], s1[0, :32], s2[0, :32], s3[0]]
        ).reshape(3, LN)
        tail = jnp.pad(tail, ((0, 5), (0, 0)))
        return dx, empty((2, plan.chunk, LN), F32), small, tail

    def slow_backward(args):
        x, yf, lat, dlat, da, dp, dc, db, h1, h2, pay1, pay2, pay3 = args[14:]
        parts = net.slow_kernel_grads(plan, x, lat, da, dp, h1, db, h2, dc, yf, dlat, pay1, pay2, pay3)
        near = exchange(parts, plan.near).astype(F32).sum(axis=0).astype(BF16)
        far = exchange(near, plan.far).astype(F32).sum(axis=0)
        dx = net.slow_input_grad(da, dp, w_slow_a, w_slow_proj)
        return dx, far, jnp.zeros((208, LN), F32), jnp.zeros((8, LN), F32)

    dx, far, small, tail = lax.cond(
        is_fast,
        fast_backward,
        slow_backward,
        (
            dlat_f, gp, x, first, h1, second, h2, wt, wc, band, c1, c2, c3, kf,
            x, yf_s, lat_s, dlat, da_s, dp_s, dc_s, db_s, h1_s, h2_s, pay1, pay2, pay3,
        ),
    )
    theirs = lax.ppermute(far[1], "path", SWAP)
    device = lax.axis_index("path") * ndp + lax.axis_index("dp")
    start = device * plan.share
    r0 = start // LN // 16 * 16
    off = start - r0 * LN
    ints = jnp.stack([is_fast.astype(jnp.int32), r0, off // LN, off % LN]).astype(jnp.int32)
    flat = net.window(plan, ints, far[0], theirs, small, tail).reshape(-1)[: plan.share]
    return (out.reshape(acts.shape), dx.reshape(acts.shape), flat)


def solution(mesh):
    data = P("path", "dp", None, None, None)
    in_specs = (data, data, P("dp")) + (P(),) * 12
    out_specs = (data, data, P(("path", "dp")))
    return jax.shard_map(local, mesh=mesh, in_specs=in_specs, out_specs=out_specs, check_vma=False)
```

```python
import functools

import jax
import jax.numpy as jnp
from jax import lax
from jax.experimental import pallas as pl
from jax.experimental.pallas import tpu as pltpu
from jax.sharding import PartitionSpec as P

TS = 4
ALPHA = 8
CS = 1024
CS_MID = 256
CF = 128
CF_MID = 32
LAT = 256
TF = 32
LN = 128
EPS = 1e-05
GELU_C = 0.7978845608028654
GELU_A = 0.044715

F32 = jnp.float32
BF16 = jnp.bfloat16
SWAP = [(0, 1), (1, 0)]

ROW_SA = 0
ROW_SB = ROW_SA + (CS + LAT) * CS_MID // LN
ROW_SC = ROW_SB + 9 * CS_MID * CS_MID // LN
ROW_SP = ROW_SC + CS_MID * CS // LN
ROW_SG = ROW_SP + (CS + LAT) * CS // LN
SLOW_VEC = (2 * CS_MID + 2 * CS) // LN
ROW_FA = ROW_SG + 2 * SLOW_VEC
ROW_LAT = ROW_FA + (3 * CF * CF_MID + 9 * CF_MID * CF_MID + CF_MID * CF) // LN
ROW_FG = ROW_LAT + 5 * CF * LAT // LN
VALUES = 2685312


def dot(a, b):
    return lax.dot_general(a, b, (((1,), (0,)), ((), ())), preferred_element_type=F32)


def dot_t(a, b):
    return lax.dot_general(a, b, (((1,), (1,)), ((), ())), preferred_element_type=F32)


class Near:
    def __init__(self, array):
        self.array = array


class Far:
    def __init__(self, array, block=None, index=None):
        self.array = pltpu.with_memory_space_constraint(array, pltpu.HBM)
        self.block, self.index = block, index


class Manual(Far):
    def __init__(self, array, pinned=True):
        if isinstance(array, Near):
            self.array = pltpu.with_memory_space_constraint(array.array, pltpu.HBM)
        else:
            self.array = pltpu.with_memory_space_constraint(array, pltpu.HBM) if pinned else array
        self.block = None


def dot_l(a, b):
    return lax.dot_general(a, b, (((0,), (0,)), ((), ())), preferred_element_type=F32)


def call(body, outs, scratch, *args, smem=1, limit=20, us=2.0, after=(), token=False, through=()):
    one = not isinstance(outs, list)
    shapes, out_specs, specs, operands = [], [], [], []
    vmem, anywhere = pl.BlockSpec(memory_space=pltpu.VMEM), pl.BlockSpec(memory_space=pl.ANY)
    for out in [outs] if one else outs:
        place = out[2] if len(out) > 2 else "near"
        shapes.append(pltpu.HBM(out[0], out[1]))
        out_specs.append(anywhere if place == "manual" else vmem)
    if token:
        shapes.append(pltpu.HBM((8, LN), F32))
        out_specs.append(anywhere)
    for k, a in enumerate(args):
        if k < smem:
            specs.append(pl.BlockSpec(memory_space=pltpu.SMEM))
        elif isinstance(a, Manual):
            specs.append(anywhere)
        elif isinstance(a, Far) and a.block is not None:
            index = a.index
            specs.append(pl.BlockSpec(a.block, lambda i, index=index: index))
        else:
            specs.append(vmem)
        if isinstance(a, Near):
            a = pltpu.with_memory_space_constraint(a.array, pltpu.HBM)
        operands.append(a.array if isinstance(a, Far) else a)
    for a in after:
        specs.append(anywhere)
        operands.append(pltpu.with_memory_space_constraint(a, pltpu.HBM))
    aliases = {}
    for a in through:
        aliases[len(operands)] = len(shapes)
        specs.append(anywhere)
        operands.append(pltpu.with_memory_space_constraint(a, pltpu.HBM))
        shapes.append(pltpu.HBM(a.shape, a.dtype))
        out_specs.append(anywhere)
    n_in, n_out = len(args), len(shapes) - token - len(through)
    cut = any(isinstance(a, Far) and a.block is not None for a in args)

    def wrapped(*refs):
        rest = refs[n_in + len(after) + len(through) :]
        body(*refs[:n_in], *rest[:n_out], *rest[n_out + token + len(through) :])

    res = pl.pallas_call(
        wrapped,
        out_shape=shapes,
        grid=(1,) if cut else (),
        in_specs=specs,
        out_specs=out_specs,
        scratch_shapes=scratch,
        input_output_aliases=aliases,
        cost_estimate=pl.CostEstimate(flops=int(us * 1e9), bytes_accessed=0, transcendentals=0),
        compiler_params=pltpu.CompilerParams(vmem_limit_bytes=limit * 1024 * 1024),
    )(*operands)
    got = [
        Near(r) if len(out) == 2 else r for r, out in zip(res, [outs] if one else outs)
    ]
    got = got[0] if one else got
    if through:
        return got, list(res[n_out + token :])
    return (got, res[n_out]) if token else got


def lanes(index):
    if isinstance(index, int):
        return slice(index * LN, (index + 1) * LN)
    return pl.ds(pl.multiple_of(index * LN, LN), LN)


def region(side, px, grid):
    bits = grid.bit_length() - 1
    r = lax.broadcasted_iota(jnp.int32, (px, LN), 0)
    inside = jnp.logical_and((r >> bits) < side, (r & (grid - 1)) < side)
    return jnp.where(inside, 1.0, 0.0).astype(F32)


def rows8(x):
    return x.reshape(x.shape[0] // 8, 8, LN).sum(axis=0)


def total(acc, fold):
    if fold:
        acc = acc + pltpu.roll(acc, 32, 1)
        acc = acc + pltpu.roll(acc, 64, 1)
    return acc.sum(axis=0, keepdims=True)


def gelu(v, half_mask):
    t = jnp.tanh(v * (GELU_C + (GELU_C * GELU_A) * (v * v)))
    return v * (half_mask + half_mask * t)


def gelu_both(v, half_mask):
    w = GELU_C + (GELU_C * GELU_A) * (v * v)
    t = jnp.tanh(v * w)
    q = half_mask + half_mask * t
    return v * q, q * (1.0 + (v - v * t) * (3.0 * w - 2.0 * GELU_C))


def loop(n, body, init, unroll=False):
    if unroll:
        for i in range(n):
            init = body(i, init)
        return init
    return lax.fori_loop(0, n, body, init)


def moments(ref, out, row, blocks, params, fold, mask, count):
    inv = 1.0 / jnp.maximum(count, 1.0)
    for p in range(params):
        n = blocks // params

        def first(i, acc):
            return acc + rows8(ref[:, lanes(p + i * params)] * mask)

        zero = jnp.zeros((8, LN), F32)
        s = total(loop(n, first, zero, n <= 4), fold)
        mean = s * inv

        def second(i, acc):
            d = (ref[:, lanes(p + i * params)] - mean) * mask
            return acc + rows8(d * d)

        m2 = total(loop(n, second, zero, n <= 4), fold)
        out[row + p : row + p + 1, :] = s
        out[row + params + p : row + params + p + 1, :] = m2


def send(pay_ref, rows_ref):
    value = rows_ref[...].astype(pay_ref.dtype)
    for d in range(pay_ref.shape[0]):
        pay_ref[d] = value


def combine(recv, row, params, n, cst_ref):
    s = recv[:, row : row + params, :]
    m2 = recv[:, row + params : row + 2 * params, :]
    k = n.sum(axis=0)
    mean = s.sum(axis=0) / k
    off = s / jnp.maximum(n, 1.0) - mean[None]
    cst_ref[0:params, :] = mean
    cst_ref[params : 2 * params, :] = lax.rsqrt((m2 + n * off * off).sum(axis=0) / k + EPS)


def pick_half(int_ref, other_ref, ref, b):
    if other_ref is None:
        return ref[:, lanes(b)]
    return jnp.where(int_ref[1] == 0, other_ref[:, lanes(b)], ref[:, lanes(b)])


def fold32(v):
    v = v[:, 0:LN] + v[:, LN:256]
    v = v + pltpu.roll(v, 32, 1)
    v = v + pltpu.roll(v, 64, 1)
    return v[:, 0:CF_MID]


def pack3(pad, b, mid, left, right, px, grid):
    g, half = b // 2, b % 2
    for slot, value in enumerate((left, mid, right)):
        at = g * 768 + slot * 256 + half * 128
        pad[grid : grid + px, at : at + LN] = value.astype(BF16)


def neighbours(h, px, grid):
    col = lax.broadcasted_iota(jnp.int32, (px, LN), 0) & (grid - 1)
    before = jnp.where(col == 0, 0.0, pltpu.roll(h, 1, 0))
    after = jnp.where(col == grid - 1, 0.0, pltpu.roll(h, px - 1, 0))
    return before, after


def clear_edges(pad, px, grid):
    zero = jnp.zeros((grid, pad.shape[1]), BF16)
    pad[0:grid, :] = zero
    pad[grid + px : grid + px + grid, :] = zero


def put_count(rows_ref, row, count):
    rows_ref[row : row + 1, :] = jnp.zeros((1, LN), F32) + count


def side_sq(side, frames):
    s = side.astype(F32)
    return s * s * frames


class Net:
    def __init__(self, ndp, grid):
        self.ndp = ndp
        self.n = 2 * ndp
        self.grid = grid
        self.px = grid * grid

    def fast_first(self, ints, xf, wa, **kw):
        px, grid, n = self.px, self.grid, self.n

        def body(int_ref, xf_ref, wa_ref, lo_ref, hi_ref, band_ref, pay_ref, row_ref, fa_ref):
            side = int_ref[0]
            row_ref[...] = jnp.zeros_like(row_ref)

            @pl.when(int_ref[1] == 1)
            def _():
                pick = jnp.where(
                    (lax.broadcasted_iota(jnp.int32, (CF_MID, 256), 1) & (CF_MID - 1))
                    == lax.broadcasted_iota(jnp.int32, (CF_MID, 256), 0),
                    1.0,
                    0.0,
                ).astype(BF16)
                wide = [dot_l(wa_ref[k], pick) for k in range(3)]
                group = lax.broadcasted_iota(jnp.int32, (CF, 256), 1) >> 5
                for j in range(10):
                    acc = jnp.zeros((CF, 256), F32)
                    for k in range(3):
                        if 0 <= j - k < 8:
                            acc = jnp.where(group == j - k, wide[k], acc)
                    band_ref[j * CF : (j + 1) * CF, :] = acc.astype(BF16)
                for g in range(4):
                    lo, hi = max(8 * g - 1, 0), min(8 * g + 9, TF)
                    k0 = lo - (8 * g - 1)
                    out = dot(
                        xf_ref[:, lo * CF : hi * CF], band_ref[k0 * CF : (k0 + hi - lo) * CF, :]
                    )
                    fa_ref[:, g * 256 : (g + 1) * 256] = out
                    target = lo_ref if g < 2 else hi_ref
                    target[:, (g % 2) * 256 : (g % 2 + 1) * 256] = out
                moments(fa_ref, row_ref, 0, 8, 1, True, region(side, px, grid), side_sq(side, TF))

            put_count(row_ref, 2, side_sq(side, 1))
            send(pay_ref, row_ref)

        return call(
            body,
            [((px, 512), F32, "far"), ((px, 512), F32), ((10 * CF, 256), BF16), ((n, 4, LN), F32, "far")],
            [pltpu.VMEM((4, LN), F32), pltpu.VMEM((px, 1024), F32)],
            ints, xf, wa,
            **kw,
        )

    def fast_weights(self, wb, wbt, wc, **kw):
        def body(wb_ref, wbt_ref, wc_ref, b_ref, bt_ref, c_ref):
            pick = jnp.where(
                (lax.broadcasted_iota(jnp.int32, (CF_MID, 256), 1) & (CF_MID - 1))
                == lax.broadcasted_iota(jnp.int32, (CF_MID, 256), 0),
                1.0,
                0.0,
            ).astype(BF16)
            same = (lax.broadcasted_iota(jnp.int32, (256, 256), 0) >> 5) == (
                lax.broadcasted_iota(jnp.int32, (256, 256), 1) >> 5
            )
            for source, target in ((wb_ref, b_ref), (wbt_ref, bt_ref)):
                for tap in range(9):
                    tiled = jnp.concatenate([dot(source[tap], pick)] * 8, axis=0)
                    target[tap // 3, (tap % 3) * 256 : (tap % 3 + 1) * 256, :] = jnp.where(
                        same, tiled, 0.0
                    ).astype(BF16)
            c_ref[...] = jnp.zeros_like(c_ref)
            for i in range(8):
                c_ref[i * CF_MID : (i + 1) * CF_MID, i * CF : (i + 1) * CF] = wc_ref[...]

        return call(
            body,
            [((3, 768, 256), BF16), ((3, 768, 256), BF16), ((256, 1024), BF16)],
            [],
            wb, wbt, wc, smem=0,
            **kw,
        )

    def conv_stage(self, ints, recv, counts, x, par, w, params, frames, other=None, more=None, **kw):
        px, grid, n, ndp = self.px, self.grid, self.n, self.ndp
        fold = params == 1
        two = other is not None
        rows = 4 + (0 if more is None else more.shape[0])

        def body(int_ref, recv_ref, n_ref, x_ref, par_ref, w_ref, *refs):
            o_ref = None
            if two:
                o_ref, refs = refs[0], refs[1:]
            if more is not None:
                m_ref, refs = refs[0], refs[1:]
            h_ref, y_ref, cst_ref, pay_ref = refs[:4]
            row_ref, pad = refs[-2:]
            if two:
                refs[4][...] = recv_ref[...]
            side = int_ref[0]
            mask = region(side, px, grid)
            half_mask = 0.5 * mask
            if two:
                stats, count = recv_ref[ndp:], n_ref[ndp:, 2:3, :] * float(TF)
            else:
                stats, count = recv_ref[...], n_ref[:, 2:3, :] * float(frames)
            combine(stats, 0, params, count, cst_ref)
            mean, rs = cst_ref[0:params, :], cst_ref[params : 2 * params, :]
            scale = par_ref[0:params, :] * rs
            shift = par_ref[params : 2 * params, :] - mean * scale
            clear_edges(pad, px, grid)
            for b in range(4):
                p = b % params
                v = pick_half(int_ref, o_ref, x_ref, b) * scale[p : p + 1] + shift[p : p + 1]
                h = gelu(v, half_mask)
                h_ref[:, lanes(b)] = h.astype(BF16)
                before, after = neighbours(h, px, grid)
                pack3(pad, b, h, before, after, px, grid)
            for g in range(2):
                acc = None
                for i in range(3):
                    part = dot(pad[grid * i : grid * i + px, g * 768 : (g + 1) * 768], w_ref[i])
                    acc = part if acc is None else acc + part
                y_ref[:, g * 256 : (g + 1) * 256] = acc
            moments(y_ref, row_ref, 0, 4, params, fold, mask, side_sq(side, frames))
            if more is not None:
                row_ref[4:rows, :] = m_ref[...]
            send(pay_ref, row_ref)

        extra = [other] if two else []
        extra += [] if more is None else [more]
        return call(
            body,
            [((px, 512), BF16), ((px, 512), F32), ((8, LN), F32), ((n, rows, LN), F32, "far")]
            + ([((n, 4, LN), F32)] if two else []),
            [pltpu.VMEM((rows, LN), F32), pltpu.VMEM((px + 2 * grid, 2 * 768), BF16)],
            ints, recv, counts, x, par, w, *extra,
            **kw,
        )

    def expand_stage(self, ints, recv, counts, y, par, w, params, wide, frames, edge=False, **kw):
        px, grid, n = self.px, self.grid, self.n
        rows = max(2 * wide, 4)

        def body(int_ref, recv_ref, n_ref, y_ref, par_ref, w_ref, h_ref, cst_ref, pay_ref, *refs):
            row_ref, c_ref = refs[-2:]
            side = int_ref[0]
            mask = region(side, px, grid)
            half_mask = 0.5 * mask
            combine(recv_ref[...], 0, params, n_ref[:, 2:3, :] * float(frames), cst_ref)
            mean, rs = cst_ref[0:params, :], cst_ref[params : 2 * params, :]
            scale = par_ref[0:params, :] * rs
            shift = par_ref[params : 2 * params, :] - mean * scale
            for b in range(4):
                p = b % params
                v = y_ref[:, lanes(b)] * scale[p : p + 1] + shift[p : p + 1]
                h_ref[:, lanes(b)] = gelu(v, half_mask).astype(BF16)
            if edge:
                refs[0][...] = h_ref[:, lanes(3)]
            for g in range(2):
                c_ref[:, g * 1024 : (g + 1) * 1024] = dot(h_ref[:, g * 256 : (g + 1) * 256], w_ref[...])
            moments(c_ref, row_ref, 0, 16, wide, False, mask, side_sq(side, frames))
            send(pay_ref, row_ref)

        return call(
            body,
            [((px, 512), BF16), ((8, LN), F32), ((n, rows, LN), F32, "far")]
            + ([((px, LN), BF16, "far")] if edge else []),
            [pltpu.VMEM((rows, LN), F32), pltpu.VMEM((px, 2048), F32)],
            ints, recv, counts, y, par, w,
            **kw,
        )

    def fast_finish(self, ints, recv, counts, h2, h2_other, w, xf, par, wlat, **kw):
        px, grid = self.px, self.grid

        def body(
            int_ref, recv_ref, n_ref, h_ref, ho_ref, w_ref, xf_ref, par_ref, wl_ref,
            y_ref, lat_ref, cst_ref, c_ref,
        ):
            half_mask = 0.5 * region(int_ref[0], px, grid)
            combine(recv_ref[...], 0, 1, n_ref[:, 2:3, :] * float(TF // 2), cst_ref)
            scale = par_ref[0:1, :] * cst_ref[1:2, :]
            shift = par_ref[1:2, :] - cst_ref[0:1, :] * scale
            c_ref[:, 0:256] = dot(ho_ref[...], w_ref[0:LN, 256:512])
            edge = half_mask * int_ref[1].astype(F32)
            for f in range(2):
                v = c_ref[:, lanes(f)] * scale + shift + xf_ref[:, lanes(f)].astype(F32)
                y_ref[:, lanes(f)] = jnp.where(int_ref[1] == 1, gelu(v, edge), 0.0).astype(BF16)
            for g in range(2):
                c_ref[...] = dot(h_ref[:, g * 256 : (g + 1) * 256], w_ref[...])

                def step(i, carry):
                    f = 2 + g * 8 + i
                    v = c_ref[:, lanes(i)] * scale + shift + xf_ref[:, lanes(f)].astype(F32)
                    y_ref[:, lanes(f)] = gelu(v, half_mask).astype(BF16)
                    return carry

                loop(8, step, 0)
            for t in range(2):
                at = ALPHA * t * CF
                lat_ref[:, t * LAT : (t + 1) * LAT] = dot(y_ref[:, at : at + 5 * CF], wl_ref[...]).astype(BF16)

        return call(
            body,
            [((px, 18 * CF), BF16), ((px, 512), BF16), ((8, LN), F32)],
            [pltpu.VMEM((px, 1024), F32)],
            ints, recv, counts, h2, h2_other, w, xf, par, wlat,
            **kw,
        )

    def fast_slope(self, ints, h2, w, xf, par, cst, **kw):
        px, grid = self.px, self.grid

        def body(int_ref, h_ref, w_ref, xf_ref, par_ref, cst_ref, gp_ref, c_ref):
            half_mask = 0.5 * region(int_ref[0], px, grid)
            scale = par_ref[0:1, :] * cst_ref[1:2, :]
            shift = par_ref[1:2, :] - cst_ref[0:1, :] * scale
            for g in range(2):
                c_ref[...] = dot(h_ref[:, g * 256 : (g + 1) * 256], w_ref[...])

                def step(i, carry):
                    f = g * 8 + i
                    v = c_ref[:, lanes(i)] * scale + shift + xf_ref[:, lanes(f + 2)].astype(F32)
                    gp_ref[:, lanes(f)] = gelu_both(v, half_mask)[1]
                    return carry

                loop(8, step, 0)

        return call(body, ((px, 2048), F32), [pltpu.VMEM((px, 1024), F32)], ints, h2, w, xf, par, cst, **kw)

    def slow_start(self, xs, wa, wp, **kw):
        px = self.px

        def body(x_ref, wa_ref, wp_ref, a_ref, p_ref):
            for t in range(2):
                x = x_ref[:, t * CS : (t + 1) * CS]
                a_ref[:, t * CS_MID : (t + 1) * CS_MID] = dot(x, wa_ref[0:CS, :])
                p_ref[:, t * CS : (t + 1) * CS] = dot(x, wp_ref[0:CS, :])

        return call(body, [((px, 512), F32), ((px, 2048), F32)], [], xs, wa, wp, smem=0, **kw)

    def slow_join(self, ints, part, lat, w, params, alone=True, **kw):
        px, grid, n = self.px, self.grid, self.n
        width = params * LN
        rows = max(2 * params, 4)

        def body(int_ref, part_ref, lat_ref, w_ref, out_ref, pay_ref, *refs):
            row_ref = refs[0] if alone else pay_ref
            side = int_ref[0]
            for t in range(2):
                at = slice(t * width, (t + 1) * width)
                out_ref[:, at] = part_ref[:, at] + dot(lat_ref[:, t * LAT : (t + 1) * LAT], w_ref[...])
            moments(
                out_ref, row_ref, 0, 2 * params, params, False, region(side, px, grid), side_sq(side, TS // 2)
            )
            if alone:
                send(pay_ref, row_ref)

        return call(
            body,
            [((px, 2 * width), F32), ((n, rows, LN) if alone else (rows, LN), F32, "far")],
            [pltpu.VMEM((rows, LN), F32)] if alone else [],
            ints, part, lat, w,
            **kw,
        )

    def slow_top(self, ints, recv3, recvp, counts, h2, w, sp, gs, parc, parp, **kw):
        px, grid, n = self.px, self.grid, self.n

        def body(
            int_ref, r3_ref, rp_ref, n_ref, h_ref, w_ref, sp_ref, gs_ref, pc_ref, pp_ref,
            ys_ref, ds_ref, cc_ref, cp_ref, pay_ref, row_ref, c_ref, acc_ref, k_ref,
        ):
            half_mask = 0.5 * region(int_ref[0], px, grid)
            count = n_ref[:, 2:3, :] * float(TS // 2)
            combine(r3_ref[...], 0, 8, count, cc_ref)
            combine(rp_ref[...], 4, 8, count, cp_ref)
            k_ref[0:8, :] = pc_ref[0:8, :] * cc_ref[8:16, :]
            k_ref[8:16, :] = pp_ref[0:8, :] * cp_ref[8:16, :]
            k_ref[16:24, :] = pc_ref[8:16, :] + pp_ref[8:16, :]
            acc_ref[...] = jnp.zeros_like(acc_ref)
            for t in range(2):
                c_ref[...] = dot(h_ref[:, t * 256 : (t + 1) * 256], w_ref[...])

                def step(b, carry):
                    at = lanes(t * 8 + b)
                    one = pl.ds(b, 1)
                    xc = c_ref[:, lanes(b)] - cc_ref[one, :]
                    xp = sp_ref[:, at] - cp_ref[one, :]
                    v = xc * k_ref[one, :] + (xp * k_ref[pl.ds(b + 8, 1), :] + k_ref[pl.ds(b + 16, 1), :])
                    y, slope = gelu_both(v, half_mask)
                    ys_ref[:, at] = y.astype(BF16)
                    d = gs_ref[:, at].astype(F32) * slope
                    ds_ref[:, at] = d
                    acc_ref[b] += rows8(d)
                    acc_ref[8 + b] += rows8(d * xc)
                    acc_ref[16 + b] += rows8(d * xp)
                    return carry

                loop(8, step, 0)
            row_ref[...] = acc_ref[...].sum(axis=1)
            row_ref[8:16, :] = row_ref[8:16, :] * cc_ref[8:16, :]
            row_ref[16:24, :] = row_ref[16:24, :] * cp_ref[8:16, :]
            send(pay_ref, row_ref)

        return call(
            body,
            [
                ((px, 2048), BF16), ((px, 2048), F32), ((16, LN), F32), ((16, LN), F32),
                ((n, 24, LN), BF16, "far"),
            ],
            [
                pltpu.VMEM((24, LN), F32), pltpu.VMEM((px, 1024), F32),
                pltpu.VMEM((24, 8, LN), F32), pltpu.VMEM((24, LN), F32),
            ],
            ints, recv3, recvp, counts, h2, w, sp, gs, parc, parp,
            **kw,
        )

    def fast_top(self, ints, dl0, dl1, dl_other, wlat, gf, gp, h2, w, cst, **kw):
        px, n = self.px, self.n

        def body(
            int_ref, d0_ref, d1_ref, do_ref, wl_ref, gf_ref, gp_ref, h_ref, w_ref, cst_ref,
            ds_ref, pay_ref, row_ref, lt_ref, c_ref, acc_ref,
        ):
            first = (1 - int_ref[1]).astype(F32)
            lt_ref[:, 0 : 3 * CF] = dot_t(d0_ref[...], wl_ref[2 * CF :, :])
            lt_ref[:, 3 * CF : 8 * CF] = dot_t(d1_ref[...], wl_ref[...])
            edge = dot_t(do_ref[...], wl_ref[0 : 2 * CF, :])
            lt_ref[:, 8 * CF : 10 * CF] = jnp.where(int_ref[1] == 0, edge, 0.0)
            acc_ref[...] = jnp.zeros_like(acc_ref)
            mean, rs = cst_ref[0:1, :], cst_ref[1:2, :]
            where = {0: 0, 1: 1, 2: 2, 6: 3, 7: 4, 8: 5, 9: 6, 10: 7, 14: 8, 15: 9}
            for g in range(2):
                c_ref[...] = dot(h_ref[:, g * 256 : (g + 1) * 256], w_ref[...])
                for i in range(8):
                    f = g * 8 + i
                    d = gf_ref[:, lanes(f)].astype(F32)
                    if f in where:
                        d = d + lt_ref[:, lanes(where[f])]
                    d = d * gp_ref[:, lanes(f)]
                    ds_ref[:, lanes(f)] = d
                    acc_ref[0] += rows8(d)
                    acc_ref[1] += rows8(d * (c_ref[:, lanes(i)] - mean))
            row_ref[...] = jnp.zeros_like(row_ref)
            row_ref[0:1, :] = acc_ref[0].sum(axis=0, keepdims=True)
            row_ref[1:2, :] = acc_ref[1].sum(axis=0, keepdims=True) * rs
            send(pay_ref, row_ref)

        return call(
            body,
            [((px, 2048), F32), ((n, 4, LN), F32, "far")],
            [
                pltpu.VMEM((4, LN), F32), pltpu.VMEM((px, 10 * CF), F32),
                pltpu.VMEM((px, 1024), F32), pltpu.VMEM((2, 8, LN), F32),
            ],
            ints, dl0, dl1, dl_other, wlat, gf, gp, h2, w, cst,
            **kw,
        )

    def expand_back(self, ints, counts, recv, ds, h2, w, cstw, parw, y, cst, par, params, wide, frames, shortcut=None, **kw):
        px, grid, n = self.px, self.grid, self.n
        fold = params == 1
        both = shortcut is not None
        srows = 3 * wide if both else 4

        def body(*refs):
            int_ref, n_ref, recv_ref, ds_ref, h_ref, w_ref, cw_ref, pw_ref, y_ref, cs_ref, par_ref = refs[:11]
            refs = refs[11:]
            if both:
                sp_ref, cp_ref, pp_ref, dp_ref = refs[:4]
                refs = refs[4:]
            dc_ref, dn_ref, sum_ref, pay_ref, row_ref, c_ref, k3_ref = refs
            mask = region(int_ref[0], px, grid)
            half_mask = 0.5 * mask
            inv_k = 1.0 / (n_ref[:, 2:3, :].sum(axis=0) * float(frames))
            sums = recv_ref[...].astype(F32).sum(axis=0)
            sum_ref[...] = sums
            a = pw_ref[0:wide, :] * cw_ref[wide : 2 * wide, :]
            k3_ref[0:wide, :] = a
            k3_ref[wide : 2 * wide, :] = a * inv_k * sums[0:wide]
            k3_ref[2 * wide : 3 * wide, :] = a * inv_k * cw_ref[wide : 2 * wide, :] * sums[wide : 2 * wide]
            if both:
                a = pp_ref[0:wide, :] * cp_ref[wide : 2 * wide, :]
                k3_ref[3 * wide : 4 * wide, :] = a
                k3_ref[4 * wide : 5 * wide, :] = a * inv_k * sums[0:wide]
                k3_ref[5 * wide : 6 * wide, :] = (
                    a * inv_k * cp_ref[wide : 2 * wide, :] * sums[2 * wide : 3 * wide]
                )
            mean, rs = cs_ref[0:params, :], cs_ref[params : 2 * params, :]
            accs = [[jnp.zeros((8, LN), F32) for _ in range(params)] for _ in range(2)]
            for g in range(2):
                c_ref[...] = dot(h_ref[:, g * 256 : (g + 1) * 256], w_ref[...])

                def step(b, carry):
                    at = lanes(g * 8 + b)
                    p = b if wide == 8 else 0
                    d = ds_ref[:, at]
                    e = (c_ref[:, lanes(b)] - cw_ref[pl.ds(p, 1), :]) * k3_ref[pl.ds(2 * wide + p, 1), :]
                    e = d * k3_ref[pl.ds(p, 1), :] - k3_ref[pl.ds(wide + p, 1), :] - e
                    dc_ref[:, at] = (e * mask).astype(BF16)
                    if both:
                        e = (sp_ref[:, at] - cp_ref[pl.ds(p, 1), :]) * k3_ref[pl.ds(5 * wide + p, 1), :]
                        e = d * k3_ref[pl.ds(3 * wide + p, 1), :] - k3_ref[pl.ds(4 * wide + p, 1), :] - e
                        dp_ref[:, at] = (e * mask).astype(BF16)
                    return carry

                loop(8, step, 0)
                dh = dot_t(dc_ref[:, g * 1024 : (g + 1) * 1024], w_ref[...])
                for half in range(2):
                    b = g * 2 + half
                    p = b % params
                    xh = (y_ref[:, lanes(b)] - mean[p : p + 1]) * rs[p : p + 1]
                    v = xh * par_ref[p : p + 1, :] + par_ref[params + p : params + p + 1, :]
                    d = dh[:, half * LN : (half + 1) * LN] * gelu_both(v, half_mask)[1]
                    dn_ref[:, lanes(b)] = d
                    accs[0][p] = accs[0][p] + rows8(d)
                    accs[1][p] = accs[1][p] + rows8(d * xh)
            row_ref[...] = jnp.zeros_like(row_ref)
            for q in range(2):
                for p in range(params):
                    row_ref[q * params + p : q * params + p + 1, :] = total(accs[q][p], fold)
            send(pay_ref, row_ref)

        outs = [((px, 2048), BF16)] if both else []
        outs += [((px, 2048), BF16), ((px, 512), F32), ((srows, LN), F32, "far"), ((n, 4, LN), F32, "far")]
        extra = list(shortcut) if both else []
        return call(
            body,
            outs,
            [pltpu.VMEM((4, LN), F32), pltpu.VMEM((px, 1024), F32), pltpu.VMEM((max(6 * wide, 8), LN), F32)],
            ints, counts, recv, ds, h2, w, cstw, parw, y, cst, par, *extra,
            **kw,
        )

    def conv_back(self, ints, counts, recv, dn, y, cst2, par2, wt, x, cst1, par1, params, frames, other=None, **kw):
        px, grid, n = self.px, self.grid, self.n
        fold = params == 1
        two = other is not None

        def body(int_ref, n_ref, recv_ref, dn_ref, y_ref, c2_ref, p2_ref, w_ref, x_ref, c1_ref, p1_ref, *refs):
            o_ref = None
            if two:
                o_ref, refs = refs[0], refs[1:]
            db_ref, dn1_ref, sum_ref, pay_ref, row_ref, pad = refs
            mask = region(int_ref[0], px, grid)
            half_mask = 0.5 * mask
            inv_k = 1.0 / (n_ref[:, 2:3, :].sum(axis=0) * float(frames))
            sums = recv_ref[...].astype(F32).sum(axis=0)
            sum_ref[...] = sums
            mean2, rs2 = c2_ref[0:params, :], c2_ref[params : 2 * params, :]
            a = p2_ref[0:params, :] * rs2
            b0 = a * inv_k * sums[0:params]
            c0 = a * inv_k * rs2 * sums[params : 2 * params]
            clear_edges(pad, px, grid)
            for b in range(4):
                p = b % params
                e = (y_ref[:, lanes(b)] - mean2[p : p + 1]) * c0[p : p + 1]
                e = (dn_ref[:, lanes(b)] * a[p : p + 1] - b0[p : p + 1] - e) * mask
                db_ref[:, lanes(b)] = e.astype(BF16)
                before, after = neighbours(e, px, grid)
                pack3(pad, b, e, after, before, px, grid)
            mean, rs = c1_ref[0:params, :], c1_ref[params : 2 * params, :]
            accs = [[jnp.zeros((8, LN), F32) for _ in range(params)] for _ in range(2)]
            for g in range(2):
                dh = None
                for i in range(3):
                    part = dot(pad[grid * i : grid * i + px, g * 768 : (g + 1) * 768], w_ref[2 - i])
                    dh = part if dh is None else dh + part
                for half in range(2):
                    b = g * 2 + half
                    p = b % params
                    xh = (pick_half(int_ref, o_ref, x_ref, b) - mean[p : p + 1]) * rs[p : p + 1]
                    v = xh * p1_ref[p : p + 1, :] + p1_ref[params + p : params + p + 1, :]
                    d = dh[:, half * LN : (half + 1) * LN] * gelu_both(v, half_mask)[1]
                    dn1_ref[:, lanes(b)] = d
                    accs[0][p] = accs[0][p] + rows8(d)
                    accs[1][p] = accs[1][p] + rows8(d * xh)
            row_ref[...] = jnp.zeros_like(row_ref)
            for q in range(2):
                for p in range(params):
                    row_ref[q * params + p : q * params + p + 1, :] = total(accs[q][p], fold)
            send(pay_ref, row_ref)

        extra = [other] if two else []
        return call(
            body,
            [((px, 512), BF16), ((px, 512), F32), ((4, LN), F32, "far"), ((n, 4, LN), F32, "far")],
            [pltpu.VMEM((4, LN), F32), pltpu.VMEM((px + 2 * grid, 2 * 768), BF16)],
            ints, counts, recv, dn, y, cst2, par2, wt, x, cst1, par1, *extra,
            **kw,
        )

    def slow_last(self, ints, counts, recv, dn, x, cst, par, dp, wa, wp, **kw):
        px, grid = self.px, self.grid

        def body(
            int_ref, n_ref, recv_ref, dn_ref, x_ref, cst_ref, par_ref, dp_ref, wa_ref, wp_ref,
            da_ref, d0_ref, d1_ref, sum_ref,
        ):
            mask = region(int_ref[0], px, grid)
            inv_k = 1.0 / (n_ref[:, 2:3, :].sum(axis=0) * float(TS // 2))
            sums = recv_ref[...].astype(F32).sum(axis=0)
            sum_ref[...] = sums
            mean, rs = cst_ref[0:2, :], cst_ref[2:4, :]
            a = par_ref[0:2, :] * rs
            b0 = a * inv_k * sums[0:2]
            c0 = a * inv_k * rs * sums[2:4]
            for b in range(4):
                p = b % 2
                e = (x_ref[:, lanes(b)] - mean[p : p + 1]) * c0[p : p + 1]
                e = (dn_ref[:, lanes(b)] * a[p : p + 1] - b0[p : p + 1] - e) * mask
                da_ref[:, lanes(b)] = e.astype(BF16)
            for t, out in ((0, d0_ref), (1, d1_ref)):
                out[...] = (
                    dot_t(da_ref[:, t * CS_MID : (t + 1) * CS_MID], wa_ref[...])
                    + dot_t(dp_ref[:, t * CS : (t + 1) * CS], wp_ref[...])
                ).astype(BF16)

        return call(
            body,
            [((px, 512), BF16), ((px, LAT), BF16), ((px, LAT), BF16), ((4, LN), F32, "far")],
            [],
            ints, counts, recv, dn, x, cst, par, dp, wa, wp,
            **kw,
        )

    def slow_input_grad(self, da, dp, wa, wp, **kw):
        px = self.px

        def body(da_ref, dp_ref, wa_ref, wp_ref, dx_ref):
            for t in range(2):
                dx_ref[:, t * CS : (t + 1) * CS] = (
                    dot_t(da_ref[:, t * CS_MID : (t + 1) * CS_MID], wa_ref[0:CS, :])
                    + dot_t(dp_ref[:, t * CS : (t + 1) * CS], wp_ref[0:CS, :])
                ).astype(BF16)

        return call(body, ((px, 2048), BF16, "far"), [], da, dp, wa, wp, smem=0, **kw)

    def fast_first_back(self, ints, counts, recv, dn_lo, dn_hi, fa_lo, fa_hi, cst, par, xf, bc, bc_other, **kw):
        px, grid, ndp = self.px, self.grid, self.ndp
        rows = bc.shape[0]

        def body(
            int_ref, n_ref, recv_ref, dl_ref, dh_ref, xl_ref, xh_ref, cst_ref, par_ref, x_ref, b0_ref, b1_ref,
            da_ref, sum_ref, pay_ref, row_ref,
        ):
            sums = recv_ref[...].sum(axis=0)
            sum_ref[...] = sums
            row_ref[...] = b0_ref[...] + b1_ref[...]

            @pl.when(int_ref[1] == 1)
            def _():
                mask = region(int_ref[0], px, grid)
                inv_k = 1.0 / (n_ref[:, 2:3, :].sum(axis=0) * float(TF // 2))
                mean, rs = cst_ref[0:1, :], cst_ref[1:2, :]
                a = par_ref[0:1, :] * rs
                b0 = a * inv_k * sums[0:1]
                c0 = a * inv_k * rs * sums[1:2]
                for dn_ref, h_ref, base in ((dl_ref, xl_ref, 0), (dh_ref, xh_ref, 4)):
                    for b in range(4):
                        e = (h_ref[:, lanes(b)] - mean) * c0
                        e = (dn_ref[:, lanes(b)] * a - b0 - e) * mask
                        da_ref[:, lanes(base + b)] = e.astype(BF16)
                accs = [None] * 3
                for g in range(4):
                    lo, hi = max(8 * g - 1, 0), min(8 * g + 9, TF)
                    k0 = lo - (8 * g - 1)
                    d = dot(da_ref[:, g * 256 : (g + 1) * 256].T, x_ref[:, lo * CF : hi * CF])
                    for k in range(3):
                        for i in range(8):
                            j = i + k - k0
                            if 0 <= j < hi - lo:
                                part = d[i * CF_MID : (i + 1) * CF_MID, j * CF : (j + 1) * CF]
                                accs[k] = part if accs[k] is None else accs[k] + part
                for k in range(3):
                    row_ref[k * CF_MID : (k + 1) * CF_MID, :] = accs[k]

            send(pay_ref, row_ref)

        return call(
            body,
            [((px, 1024), BF16), ((4, LN), F32, "far"), ((ndp, rows, LN), BF16, "far")],
            [pltpu.VMEM((rows, LN), F32)],
            ints, counts, recv, dn_lo, dn_hi, fa_lo, fa_hi, cst, par, xf, bc, bc_other,
            **kw,
        )

    def last(self, ints, da, ds_lo, ds_hi, band, dxs0, dxs1, **kw):
        px = self.px

        def body(int_ref, da_ref, sl_ref, sh_ref, band_ref, x0_ref, x1_ref, dx_ref, acc_ref, out_ref, sem):
            def part(g):
                at = slice(g * 1024, (g + 1) * 1024)
                return pltpu.make_async_copy(out_ref.at[:, at], dx_ref.at[:, at], sem.at[g])

            def half(ref, g):
                return pltpu.make_async_copy(ref, out_ref.at[:, g * 2048 : (g + 1) * 2048], sem.at[g])

            @pl.when(int_ref[1] == 0)
            def _():
                half(x0_ref, 0).start()
                half(x1_ref, 1).start()
                half(x0_ref, 0).wait()
                half(x1_ref, 1).wait()
                for g in range(4):
                    part(g).start()
                for g in range(4):
                    part(g).wait()

            @pl.when(int_ref[1] == 1)
            def _():
                acc_ref[:, 0 : 10 * CF] = dot_t(da_ref[:, 0:256], band_ref[...])
                for g in range(4):
                    if g < 3:
                        p = dot_t(da_ref[:, (g + 1) * 256 : (g + 2) * 256], band_ref[...])
                        base = 8 * (g + 1) * CF
                        acc_ref[:, base : base + 2 * CF] += p[:, 0 : 2 * CF]
                        acc_ref[:, base + 2 * CF : base + 10 * CF] = p[:, 2 * CF :]
                    s_ref = sl_ref if g < 2 else sh_ref
                    for i in range(8):
                        f = 8 * g + i
                        s = s_ref[:, lanes(f % 16)] + acc_ref[:, lanes(f + 1)]
                        out_ref[:, lanes(f)] = s.astype(BF16)
                    part(g).start()
                for g in range(4):
                    part(g).wait()

        return call(
            body,
            ((px, 4096), BF16, "manual"),
            [pltpu.VMEM((px, 34 * CF), F32), pltpu.VMEM((px, 4096), BF16), pltpu.SemaphoreType.DMA((4,))],
            ints, da, ds_lo, ds_hi, band, Manual(dxs0), Manual(dxs1),
            **kw,
        )

    def halves(self, ints, x, x_other, cot, cot_other, **kw):
        px = self.px

        def body(int_ref, x_ref, xo_ref, c_ref, co_ref, xs_ref, xf_ref, gs_ref, gf_ref, sem):
            def run(pairs):
                copies = [pltpu.make_async_copy(a, b, sem.at[k]) for k, (a, b) in enumerate(pairs)]
                for c in copies:
                    c.start()
                for c in copies:
                    c.wait()

            lo, hi = slice(0, 2048), slice(2048, 4096)

            @pl.when(int_ref[1] == 0)
            def _():
                xf_ref[:, 0 : 2 * CF] = jnp.zeros((px, 2 * CF), BF16)
                run([
                    (x_ref.at[:, lo], xs_ref), (xo_ref.at[:, lo], xf_ref.at[:, 2 * CF : 18 * CF]),
                    (c_ref.at[:, lo], gs_ref), (co_ref.at[:, lo], gf_ref),
                ])

            @pl.when(int_ref[1] == 1)
            def _():
                run([
                    (xo_ref.at[:, hi], xs_ref), (x_ref.at[:, 14 * CF :], xf_ref),
                    (co_ref.at[:, hi], gs_ref), (c_ref.at[:, hi], gf_ref),
                ])

        wide = ((px, 2048), BF16)
        return call(
            body,
            [wide, ((px, 18 * CF), BF16), wide, wide],
            [pltpu.SemaphoreType.DMA((4,))],
            ints, Manual(x), Manual(x_other), Manual(cot), Manual(cot_other),
            **kw,
        )

    def out_send(self, ints, ys, yf, **kw):
        px = self.px

        def body(int_ref, ys_ref, yf_ref, out_ref):
            for path, ref, at in ((0, yf_ref, 2 * CF), (1, ys_ref, 0)):

                @pl.when(int_ref[1] == path)
                def _():
                    out_ref[...] = ref[:, at : at + 2048]

        return call(body, ((px, 2048), BF16, "far"), [], ints, ys, yf, **kw)

    def out_join(self, ints, ys, yf, other, **kw):
        px = self.px

        def body(int_ref, ys_ref, yf_ref, o_ref, out_ref):
            for path, ref, at in ((0, ys_ref, 0), (1, yf_ref, 2 * CF)):

                @pl.when(int_ref[1] == path)
                def _():
                    mine, far = path * 2048, (1 - path) * 2048
                    out_ref[:, mine : mine + 2048] = ref[:, at : at + 2048]
                    out_ref[:, far : far + 2048] = o_ref[...]

        return call(body, ((px, 4096), BF16, "far"), [], ints, ys, yf, Far(other), **kw)

    def fast_grads_bc(self, h1, db, h2, dc, **kw):
        px, grid = self.px, self.grid

        def body(h1_ref, db_ref, h2_ref, dc_ref, gb_ref, gc_ref, pad):
            clear_edges(pad, px, grid)
            for b in range(4):
                h = h1_ref[:, lanes(b)].astype(F32)
                before, after = neighbours(h, px, grid)
                pack3(pad, b, h, before, after, px, grid)
            same = (lax.broadcasted_iota(jnp.int32, (256, 256), 0) >> 5) == (
                lax.broadcasted_iota(jnp.int32, (256, 256), 1) >> 5
            )
            for i in range(3):
                for s in range(3):
                    acc = jnp.zeros((256, 256), F32)
                    for g in range(2):
                        at = g * 768 + s * 256
                        acc = acc + dot(
                            pad[grid * i : grid * i + px, at : at + 256].T,
                            db_ref[:, g * 256 : (g + 1) * 256],
                        )
                    acc = jnp.where(same, acc, 0.0).reshape(8, CF_MID, 256).sum(axis=0)
                    gb_ref[3 * i + s] = fold32(acc)
            acc = jnp.zeros((256, 1024), F32)
            for g in range(2):
                acc = acc + dot(h2_ref[:, g * 256 : (g + 1) * 256].T, dc_ref[:, g * 1024 : (g + 1) * 1024])
            out = None
            for i in range(8):
                part = acc[i * CF_MID : (i + 1) * CF_MID, i * CF : (i + 1) * CF]
                out = part if out is None else out + part
            gc_ref[...] = out

        return call(
            body,
            [((9, CF_MID, CF_MID), F32, "far"), ((CF_MID, CF), F32, "far")],
            [pltpu.VMEM((px + 2 * grid, 2 * 768), BF16)],
            h1, db, h2, dc, smem=0,
            **kw,
        )

    def grads_early(self, plan, ints, xs, lat, dp, h2, dc, **kw):
        px = self.px
        rows = plan.early

        def body(int_ref, x_ref, lat_ref, dp_ref, h2_ref, dc_ref, keep_ref, send_ref, buf, xt):
            def put(base, q, acc):
                for j in range(2):
                    buf[pl.ds(base + 2 * q + j, 256, stride=8), :] = acc[:, j * LN : (j + 1) * LN]

            for c in range(6):
                for t in range(2):
                    if c == 5:
                        x = h2_ref[:, t * 256 : (t + 1) * 256]
                    elif c == 4:
                        x = lat_ref[:, t * LAT : (t + 1) * LAT]
                    else:
                        x = x_ref[:, t * CS + c * 256 : t * CS + (c + 1) * 256]
                    xt[:, t * px : (t + 1) * px] = x.T
                source = dc_ref if c == 5 else dp_ref
                base = (ROW_SC if c == 5 else ROW_SP + c * 2048) - ROW_SC
                for q in range(4):
                    acc = None
                    for t in range(2):
                        at = t * CS + q * 256
                        part = dot(xt[:, t * px : (t + 1) * px], source[:, at : at + 256])
                        acc = part if acc is None else acc + part
                    put(base, q, acc)
            lo = 0
            hi = plan.base[1] - ROW_SC
            mine = pl.multiple_of(jnp.where(int_ref[1] == 0, lo, hi), 16)
            other = pl.multiple_of(jnp.where(int_ref[1] == 0, hi, lo), 16)
            keep_ref[...] = buf[pl.ds(mine, rows), :].astype(BF16)
            send_ref[...] = buf[pl.ds(other, rows), :].astype(BF16)

        return call(
            body,
            [((rows, LN), BF16, "far"), ((rows, LN), BF16, "far")],
            [pltpu.VMEM((ROW_SG - ROW_SC, LN), F32), pltpu.VMEM((256, 2 * px), BF16)],
            ints, xs, lat, dp, h2, dc,
            **kw,
        )

    def grads_conv(self, h1, db, **kw):
        px, grid = self.px, self.grid

        def body(h1_ref, db_ref, out_ref, buf, pad):
            clear_edges(pad, px, grid)
            for b in range(4):
                h = h1_ref[:, lanes(b)].astype(F32)
                before, after = neighbours(h, px, grid)
                pack3(pad, b, h, before, after, px, grid)
            for i in range(3):
                for s in range(3):
                    acc = None
                    for t in range(2):
                        at = t * 768 + s * 256
                        part = dot(
                            pad[grid * i : grid * i + px, at : at + 256].T,
                            db_ref[:, t * 256 : (t + 1) * 256],
                        )
                        acc = part if acc is None else acc + part
                    for j in range(2):
                        buf[pl.ds((3 * i + s) * 512 + j, 256, stride=2), :] = acc[:, j * LN : (j + 1) * LN]
            out_ref[...] = buf[...].astype(BF16)

        return call(
            body,
            ((ROW_SC - ROW_SB, LN), BF16, "far"),
            [pltpu.VMEM((ROW_SC - ROW_SB, LN), F32), pltpu.VMEM((px + 2 * grid, 2 * 768), BF16)],
            h1, db, smem=0,
            **kw,
        )

    def grads_late(self, ints, xs, lat, da, yf, dl0, dl1, **kw):
        px = self.px
        rows = ROW_SB - ROW_SA
        lat_rows = ROW_FG - ROW_LAT

        def body(int_ref, x_ref, lat_ref, da_ref, yf_ref, d0_ref, d1_ref, keep_ref, send_ref, buf):
            for c in range(5):
                acc = None
                for t in range(2):
                    if c == 4:
                        x = lat_ref[:, t * LAT : (t + 1) * LAT]
                    else:
                        x = x_ref[:, t * CS + c * 256 : t * CS + (c + 1) * 256]
                    part = dot(x.T, da_ref[:, t * CS_MID : (t + 1) * CS_MID])
                    acc = part if acc is None else acc + part
                for j in range(2):
                    buf[pl.ds(c * 512 + j, 256, stride=2), :] = acc[:, j * LN : (j + 1) * LN]
            for k in range(5):
                acc = dot(yf_ref[:, lanes(k)].T, d0_ref[...]) + dot(yf_ref[:, lanes(8 + k)].T, d1_ref[...])
                for j in range(2):
                    buf[pl.ds(rows + k * 256 + j, CF, stride=2), :] = acc[:, j * LN : (j + 1) * LN]
            mine = pl.multiple_of(jnp.where(int_ref[1] == 0, 0, rows), 16)
            other = pl.multiple_of(jnp.where(int_ref[1] == 0, rows, 0), 16)
            keep_ref[...] = buf[pl.ds(mine, rows), :].astype(BF16)
            send_ref[...] = buf[pl.ds(other, rows), :].astype(BF16)

        return call(
            body,
            [((rows, LN), BF16, "far"), ((rows, LN), BF16, "far")],
            [pltpu.VMEM((2 * rows, LN), F32)],
            ints, xs, lat, da, yf, dl0, dl1,
            **kw,
        )

    def windows(self, plan, ints, early, conv, late, **kw):
        ndp, chunk, half = self.ndp, plan.chunk, self.ndp // 2

        def body(int_ref, e0_ref, e1_ref, c0_ref, c1_ref, l0_ref, l1_ref, keep_ref, send_ref, buf):
            def add(a, b, rows):
                return a[0:rows, :].astype(F32) + b[0:rows, :].astype(F32)

            for path in range(2):

                @pl.when(int_ref[1] == path)
                def _():
                    buf[...] = jnp.zeros_like(buf)
                    base = plan.base[path]
                    if path == 0:
                        buf[ROW_SA:ROW_SB, :] = add(l0_ref, l1_ref, ROW_SB - ROW_SA)
                        buf[ROW_SB:ROW_SC, :] = add(c0_ref, c1_ref, ROW_SC - ROW_SB)
                        rest = min(plan.length - ROW_SC, plan.early)
                        buf[ROW_SC : ROW_SC + rest, :] = add(e0_ref, e1_ref, rest)
                    else:
                        rest = ROW_SG - base
                        buf[0:rest, :] = add(e0_ref, e1_ref, rest)
                        at = ROW_LAT - base
                        buf[at : at + ROW_FG - ROW_LAT, :] = add(l0_ref, l1_ref, ROW_FG - ROW_LAT)

            path = int_ref[1]
            base = jnp.where(path == 0, plan.base[0], plan.base[1])

            def stretch(place):
                j = 0
                for step in range(plan.bits):
                    bit = (place >> (plan.bits - 1 - step)) & 1
                    j = j + jnp.where(
                        path == 0, bit << plan.order[0][step], bit << plan.order[1][step]
                    )
                at = ((path * ndp + j) * plan.share) // (16 * LN) * 16 - base
                return buf[pl.ds(pl.multiple_of(at, 16), chunk), :].astype(BF16)

            def step(q, carry):
                bit = int_ref[5]
                keep_ref[q] = stretch(bit * half + q)
                send_ref[q] = stretch((1 - bit) * half + q)
                return carry

            loop(half, step, 0)

        return call(
            body,
            [((half, chunk, LN), BF16, "far")] * 2,
            [pltpu.VMEM((plan.length, LN), F32)],
            ints, *early, *conv, *late,
            **kw,
        )

    def halve(self, plan, ints, step, keep, came, **kw):
        half = keep.shape[0] // 2

        def body(int_ref, a_ref, b_ref, keep_ref, send_ref):
            bit = int_ref[5 + step]

            def one(q, carry):
                for out, at in ((keep_ref, bit * half + q), (send_ref, (1 - bit) * half + q)):
                    out[q] = (a_ref[at].astype(F32) + b_ref[at].astype(F32)).astype(BF16)
                return carry

            loop(half, one, 0)

        return call(
            body,
            [((half, plan.chunk, LN), BF16, "far")] * 2,
            [],
            ints, Far(keep), came,
            **kw,
        )

    def window(self, plan, ints, keep, came, vectors, small, tail, **kw):
        chunk, out_rows = plan.chunk, plan.out_rows
        pad = small.shape[0] + 8

        def body(int_ref, keep_ref, came_ref, vec_ref, small_ref, tail_ref, out_ref, a_ref):
            r0 = int_ref[2]
            row = int_ref[3]
            lane = int_ref[4]
            a_ref[...] = jnp.zeros_like(a_ref)
            for ref, start, n in (
                (vec_ref, ROW_SG, 2 * SLOW_VEC), (small_ref, ROW_FA, ROW_LAT - ROW_FA), (tail_ref, ROW_FG, 3)
            ):
                at = jnp.clip(start - r0, -n, chunk) + pad
                a_ref[pl.ds(at, n), :] += ref[0:n, :]
            a_ref[pad : pad + chunk, :] += keep_ref[0].astype(F32) + came_ref[0].astype(F32)
            one = a_ref[pl.ds(pad + row, out_rows), :]
            two = a_ref[pl.ds(pad + row + 1, out_rows), :]
            shift = (LN - lane) & (LN - 1)
            one = pltpu.roll(one, shift, 1)
            two = pltpu.roll(two, shift, 1)
            at = lax.broadcasted_iota(jnp.int32, (out_rows, LN), 1)
            out_ref[...] = jnp.where(at < LN - lane, one, two)

        return call(
            body,
            ((out_rows, LN), F32, "far"),
            [pltpu.VMEM((chunk + 2 * pad + 8, LN), F32)],
            ints, keep, came, vectors, small, tail,
            **kw,
        )


class Plan:
    def __init__(self, ndp):
        n = 2 * ndp
        self.ndp = ndp
        self.share = VALUES // n
        self.first = [self.share * d // LN // 16 * 16 for d in range(n)]
        ends = [-(-self.share * (d + 1) // LN) for d in range(n)]
        self.chunk = -(-max(e - f for e, f in zip(ends, self.first)) // 16) * 16
        self.base = [self.first[0], self.first[ndp]]
        self.length = max(
            self.first[q * ndp + ndp - 1] + self.chunk - self.base[q] for q in range(2)
        )
        self.early = ROW_SG - self.base[1]
        self.out_rows = -(-self.share // LN)
        self.bits = ndp.bit_length() - 1
        one = list(range(self.bits))
        two = [b ^ 1 if (b ^ 1) < self.bits else b for b in one]
        self.order = [one, two]

    def place(self, path, j):
        at = 0
        for b in self.order[path]:
            at = 2 * at + ((j >> b) & 1)
        return at

    def pairs(self, step):
        out = []
        for q in range(2):
            b = self.order[q][step]
            out += [(q * self.ndp + j, q * self.ndp + (j ^ (1 << b))) for j in range(self.ndp)]
        return out


def exchange(x):
    return lax.all_to_all(x, ("path", "dp"), 0, 0)


def swap(x):
    x = x.array if isinstance(x, Near) else x
    return lax.ppermute(x, "path", SWAP)


def local(
    acts, cotangent, clip_res, w_slow_a, w_slow_b, w_slow_c, w_slow_proj, slow_gain, slow_bias,
    w_fast_a, w_fast_b, w_fast_c, w_lateral, fast_gain, fast_bias,
):
    grid = acts.shape[2]
    px = grid * grid
    ndp = lax.axis_size("dp")
    net = Net(ndp, grid)
    plan = Plan(ndp)
    path, chip = lax.axis_index("path"), lax.axis_index("dp")
    core0 = path == 0
    level = clip_res[0]
    side = jnp.where(
        level == 1, grid * 5 // 8, jnp.where(level == 2, grid * 7 // 8, jnp.where(level == 3, grid, 0))
    )
    start = (path * ndp + chip) * plan.share
    r0 = start // LN // 16 * 16
    off = start - r0 * LN
    bits = [
        jnp.where(core0, chip >> plan.order[0][s], chip >> plan.order[1][s]) & 1 for s in range(plan.bits)
    ]
    ints = jnp.stack([side, path, r0, off // LN, off % LN] + bits).astype(jnp.int32)
    x = acts.reshape(px, 4096)
    cot = cotangent.reshape(px, 4096)
    sg, sb_ = slow_gain.reshape(SLOW_VEC, LN), slow_bias.reshape(SLOW_VEC, LN)

    def slow_par(a, b):
        return jnp.concatenate([sg[a:b], sb_[a:b]], axis=0)

    def fast_par(a, b):
        one = jnp.stack([fast_gain[a:b], fast_bias[a:b]])
        return jnp.tile(one, (1, LN // (b - a)))

    wlat = w_lateral.reshape(5 * CF, LAT)
    wa_lat = Far(w_slow_a, (LAT, CS_MID), (CS // LAT, 0))
    wp_lat = Far(w_slow_proj, (LAT, CS), (CS // LAT, 0))
    f1, f2, f3 = fast_par(0, 32), fast_par(32, 64), fast_par(64, 192)
    s1, s2, s3, s4 = slow_par(0, 2), slow_par(2, 4), slow_par(4, 12), slow_par(12, 20)
    wb3 = w_slow_b.reshape(3, 768, 256)
    wbt3 = w_slow_b.transpose(0, 2, 1).reshape(3, 768, 256)
    half = TF // 2

    x_other = swap(x)
    cot_other = swap(cot)

    fa_lo, fa_hi, band, pay = net.fast_first(ints, x, w_fast_a.transpose(0, 2, 1), us=3.5)
    (fb_w, fbt_w, fc_w), tok = net.fast_weights(
        w_fast_b, w_fast_b.transpose(0, 2, 1), w_fast_c, us=1.0, after=[pay], token=True
    )
    fa_other = swap(fa_lo)
    r1 = exchange(pay)
    fh1, fb, fc1, pay, r1 = net.conv_stage(
        ints, r1, r1, fa_hi, f1, fb_w, 1, half, fa_other, us=2.7, after=[tok]
    )
    (xs, xf, gs, gf), tok = net.halves(ints, x, x_other, cot, cot_other, us=2.5, after=[pay], token=True)
    r = exchange(pay)
    fh2, fc2, pay, fh2_edge = net.expand_stage(
        ints, r, r1, fb, f2, fc_w, 1, 1, half, True, us=2.6, after=[tok]
    )
    fh2_other = swap(fh2_edge)
    (pa, pp), tok = net.slow_start(xs, w_slow_a, w_slow_proj, us=3.5, after=[pay], token=True)
    r = exchange(pay)
    yf, lat, fc3 = net.fast_finish(
        ints, r, r1, fh2, fh2_other, fc_w, xf, f3, wlat, us=3.0, after=[tok]
    )

    sa, pay = net.slow_join(ints, pa, lat, wa_lat, 2, us=2.0)
    (sp, sp_rows), tok = net.slow_join(ints, pp, lat, wp_lat, 8, False, us=3.0, after=[pay], token=True)
    r = exchange(pay)
    sh1, sb, sc1, pay = net.conv_stage(
        ints, r, r1, sa, s1, wb3, 2, TS // 2, more=sp_rows, us=3.0, after=[tok]
    )
    rp = exchange(pay)
    gp, tok = net.fast_slope(ints, fh2, fc_w, xf, f3, fc3, us=4.0, after=[pay], token=True)
    sh2, sc2, pay = net.expand_stage(ints, rp, r1, sb, s2, w_slow_c, 2, 8, TS // 2, us=3.0, after=[tok])
    r = exchange(pay)
    ys, ds, scc, scp, pay = net.slow_top(ints, r, rp, r1, sh2, w_slow_c, sp, gs, s3, s4, us=6.0)

    sent, tok = net.out_send(ints, ys, yf, us=2.0, after=[pay], token=True)
    r = exchange(pay)
    (dp, dc, dn, t3, pay), (sent,) = net.expand_back(
        ints, r1, r, ds, sh2, w_slow_c, scc, s3, sb, sc2, s2, 2, 8, TS // 2, (sp, scp, s4),
        us=6.0, after=[tok], through=[sent],
    )
    theirs = swap(sent)
    (early, early_out), tok = net.grads_early(
        plan, ints, xs, lat, dp, sh2, dc, us=6.0, after=[pay], token=True
    )
    r = exchange(pay)
    (db, dn, t2, pay), (early_out,) = net.conv_back(
        ints, r1, r, dn, sb, sc2, s2, wbt3, sa, sc1, s1, 2, TS // 2, us=3.0, after=[tok], through=[early_out]
    )
    early_in = swap(early_out)
    conv, tok = net.grads_conv(sh1, db, us=3.0, after=[pay], token=True)
    r = exchange(pay)
    (da, dl0, dl1, t1), (conv_out,) = net.slow_last(
        ints, r1, r, dn, sa, sc1, s1, dp, wa_lat, wp_lat, us=3.0, after=[tok], through=[conv]
    )
    dl_other = swap(dl0)

    (fds, pay), (conv_out,) = net.fast_top(
        ints, dl0, dl1, dl_other, wlat, gf, gp, fh2, fc_w, fc3, us=4.0, through=[conv_out]
    )
    conv_in = swap(conv_out)
    fds_lo = swap(fds)
    (late, late_out), tok = net.grads_late(ints, xs, lat, da, yf, dl0, dl1, us=4.0, after=[pay], token=True)
    dxs, tok2 = net.slow_input_grad(da, dp, w_slow_a, w_slow_proj, us=4.0, after=[tok], token=True)
    r = exchange(pay)
    (fdc, dn, u3, pay), (late_out, dxs_out) = net.expand_back(
        ints, r1, r, fds, fh2, fc_w, fc3, f3, fb, fc2, f2, 1, 1, half,
        us=4.0, after=[tok2], through=[late_out, dxs],
    )
    late_in = swap(late_out)
    (keep, there), tok = net.windows(
        plan, ints, (Far(early), Far(early_in)), (Far(conv_out), Far(conv_in)), (Far(late), late_in),
        us=6.0, after=[pay], token=True,
    )
    r = exchange(pay)
    (fdb, dn, u2, pay), (there, dxs_out) = net.conv_back(
        ints, r1, r, dn, fb, fc2, f2, fbt_w, fa_hi, fc1, f1, 1, half, fa_other,
        us=3.5, after=[tok], through=[there, dxs_out],
    )
    dn_lo = swap(dn)
    here = lax.ppermute(there, ("path", "dp"), plan.pairs(0))
    gb, gc = net.fast_grads_bc(fh1, fdb, fh2, fdc, us=3.5, after=[pay])
    bc = jnp.concatenate([gb.reshape(-1, LN), gc], axis=0)
    bc = jnp.pad(bc, ((0, -bc.shape[0] % 16), (0, 0)))
    bc_other = swap(bc)
    r = exchange(pay)
    fda, u1, pay = net.fast_first_back(
        ints, r1, r, dn_lo, dn, Far(fa_lo), fa_hi, fc1, f1, x, bc, bc_other, us=3.5
    )
    dxs_other = swap(dxs_out)
    dx = net.last(ints, fda, Far(fds_lo), fds, band, dxs_out, dxs_other, us=4.5, after=[pay])

    out = net.out_join(ints, ys, yf, theirs, us=3.0)

    for step in range(1, plan.bits):
        keep, there = net.halve(plan, ints, step, keep, here, us=1.5)
        here = lax.ppermute(there, ("path", "dp"), plan.pairs(step))
    small = lax.all_to_all(pay, "dp", 0, 0).astype(F32).sum(axis=0)
    bc = swap(small)
    ga = small[: 3 * CF_MID].reshape(3, CF_MID, CF).transpose(0, 2, 1).reshape(-1, LN)
    small = jnp.where(core0, 0.0, jnp.concatenate([ga, bc], axis=0))
    vectors = jnp.concatenate([t1[2:4], t2[2:4], t3[8:24], t1[0:2], t2[0:2], t3[0:8], t3[0:8]], axis=0)
    tail = jnp.concatenate([u1[1, :32], u2[1, :32], u3[1], u1[0, :32], u2[0, :32], u3[0]]).reshape(3, LN)
    tail = jnp.pad(tail, ((0, 5), (0, 0)))
    flat = net.window(plan, ints, keep, here, vectors, small, tail).reshape(-1)[: plan.share]
    return (out.reshape(acts.shape), dx.reshape(acts.shape), flat)


def solution(mesh):
    data = P("path", "dp", None, None, None)
    in_specs = (data, data, P("dp")) + (P(),) * 12
    out_specs = (data, data, P(("path", "dp")))
    return jax.shard_map(local, mesh=mesh, in_specs=in_specs, out_specs=out_specs, check_vma=False)
```

```python
import functools

import jax
import jax.numpy as jnp
from jax import lax
from jax.experimental import pallas as pl
from jax.experimental.pallas import tpu as pltpu
from jax.sharding import PartitionSpec as P

TS = 4
ALPHA = 8
CS = 1024
CS_MID = 256
CF = 128
CF_MID = 32
LAT = 256
TF = 32
LN = 128
EPS = 1e-05
GELU_C = 0.7978845608028654
GELU_A = 0.044715

F32 = jnp.float32
BF16 = jnp.bfloat16
SWAP = [(0, 1), (1, 0)]

ROW_SA = 0
ROW_SB = ROW_SA + (CS + LAT) * CS_MID // LN
ROW_SC = ROW_SB + 9 * CS_MID * CS_MID // LN
ROW_SP = ROW_SC + CS_MID * CS // LN
ROW_SG = ROW_SP + (CS + LAT) * CS // LN
SLOW_VEC = (2 * CS_MID + 2 * CS) // LN
ROW_FA = ROW_SG + 2 * SLOW_VEC
ROW_LAT = ROW_FA + (3 * CF * CF_MID + 9 * CF_MID * CF_MID + CF_MID * CF) // LN
ROW_FG = ROW_LAT + 5 * CF * LAT // LN
VALUES = 2685312


def dot(a, b):
    return lax.dot_general(a, b, (((1,), (0,)), ((), ())), preferred_element_type=F32)


def dot_t(a, b):
    return lax.dot_general(a, b, (((1,), (1,)), ((), ())), preferred_element_type=F32)


class Near:
    def __init__(self, array):
        self.array = array


class Far:
    def __init__(self, array, block=None, index=None):
        self.array = pltpu.with_memory_space_constraint(array, pltpu.HBM)
        self.block, self.index = block, index


class Manual(Far):
    def __init__(self, array, pinned=True):
        if isinstance(array, Near):
            self.array = pltpu.with_memory_space_constraint(array.array, pltpu.HBM)
        else:
            self.array = pltpu.with_memory_space_constraint(array, pltpu.HBM) if pinned else array
        self.block = None


def dot_l(a, b):
    return lax.dot_general(a, b, (((0,), (0,)), ((), ())), preferred_element_type=F32)


def call(body, outs, scratch, *args, smem=1, limit=20, us=2.0, after=(), token=False, through=()):
    one = not isinstance(outs, list)
    shapes, out_specs, specs, operands = [], [], [], []
    vmem, anywhere = pl.BlockSpec(memory_space=pltpu.VMEM), pl.BlockSpec(memory_space=pl.ANY)
    for out in [outs] if one else outs:
        place = out[2] if len(out) > 2 else "near"
        shapes.append(pltpu.HBM(out[0], out[1]))
        out_specs.append(anywhere if place == "manual" else vmem)
    if token:
        shapes.append(pltpu.HBM((8, LN), F32))
        out_specs.append(anywhere)
    for k, a in enumerate(args):
        if k < smem:
            specs.append(pl.BlockSpec(memory_space=pltpu.SMEM))
        elif isinstance(a, Manual):
            specs.append(anywhere)
        elif isinstance(a, Far) and a.block is not None:
            index = a.index
            specs.append(pl.BlockSpec(a.block, lambda i, index=index: index))
        else:
            specs.append(vmem)
        if isinstance(a, Near):
            a = pltpu.with_memory_space_constraint(a.array, pltpu.HBM)
        operands.append(a.array if isinstance(a, Far) else a)
    for a in after:
        specs.append(anywhere)
        operands.append(pltpu.with_memory_space_constraint(a, pltpu.HBM))
    aliases = {}
    for a in through:
        aliases[len(operands)] = len(shapes)
        specs.append(anywhere)
        operands.append(pltpu.with_memory_space_constraint(a, pltpu.HBM))
        shapes.append(pltpu.HBM(a.shape, a.dtype))
        out_specs.append(anywhere)
    n_in, n_out = len(args), len(shapes) - token - len(through)
    cut = any(isinstance(a, Far) and a.block is not None for a in args)

    def wrapped(*refs):
        rest = refs[n_in + len(after) + len(through) :]
        body(*refs[:n_in], *rest[:n_out], *rest[n_out + token + len(through) :])

    res = pl.pallas_call(
        wrapped,
        out_shape=shapes,
        grid=(1,) if cut else (),
        in_specs=specs,
        out_specs=out_specs,
        scratch_shapes=scratch,
        input_output_aliases=aliases,
        cost_estimate=pl.CostEstimate(flops=int(us * 1e9), bytes_accessed=0, transcendentals=0),
        compiler_params=pltpu.CompilerParams(vmem_limit_bytes=limit * 1024 * 1024),
    )(*operands)
    got = [
        Near(r) if len(out) == 2 else r for r, out in zip(res, [outs] if one else outs)
    ]
    got = got[0] if one else got
    if through:
        return got, list(res[n_out + token :])
    return (got, res[n_out]) if token else got


def lanes(index):
    if isinstance(index, int):
        return slice(index * LN, (index + 1) * LN)
    return pl.ds(pl.multiple_of(index * LN, LN), LN)


def region(side, px, grid):
    bits = grid.bit_length() - 1
    r = lax.broadcasted_iota(jnp.int32, (px, LN), 0)
    inside = jnp.logical_and((r >> bits) < side, (r & (grid - 1)) < side)
    return jnp.where(inside, 1.0, 0.0).astype(F32)


def rows8(x):
    return x.reshape(x.shape[0] // 8, 8, LN).sum(axis=0)


def total(acc, fold):
    if fold:
        acc = acc + pltpu.roll(acc, 32, 1)
        acc = acc + pltpu.roll(acc, 64, 1)
    return acc.sum(axis=0, keepdims=True)


def gelu(v, half_mask):
    t = jnp.tanh(v * (GELU_C + (GELU_C * GELU_A) * (v * v)))
    return v * (half_mask + half_mask * t)


def gelu_both(v, half_mask):
    w = GELU_C + (GELU_C * GELU_A) * (v * v)
    t = jnp.tanh(v * w)
    q = half_mask + half_mask * t
    return v * q, q * (1.0 + (v - v * t) * (3.0 * w - 2.0 * GELU_C))


def loop(n, body, init, unroll=False):
    if unroll:
        for i in range(n):
            init = body(i, init)
        return init
    return lax.fori_loop(0, n, body, init)


def moments(ref, out, row, blocks, params, fold, mask, count):
    inv = 1.0 / jnp.maximum(count, 1.0)
    for p in range(params):
        n = blocks // params

        def first(i, acc):
            return acc + rows8(ref[:, lanes(p + i * params)] * mask)

        zero = jnp.zeros((8, LN), F32)
        s = total(loop(n, first, zero, n <= 4), fold)
        mean = s * inv

        def second(i, acc):
            d = (ref[:, lanes(p + i * params)] - mean) * mask
            return acc + rows8(d * d)

        m2 = total(loop(n, second, zero, n <= 4), fold)
        out[row + p : row + p + 1, :] = s
        out[row + params + p : row + params + p + 1, :] = m2


def send(pay_ref, rows_ref):
    value = rows_ref[...].astype(pay_ref.dtype)
    for d in range(pay_ref.shape[0]):
        pay_ref[d] = value


def split(v):
    high = v.astype(BF16).astype(F32)
    return high, v - high


def encode(code_ref, rows_ref, narrow, wide):
    at = 0
    if narrow:
        high, low = split(rows_ref[0:narrow, :])
        code_ref[0:narrow, :] = high
        code_ref[narrow : 2 * narrow, :] = low
        at = 2 * narrow
    if wide:
        high, low = split(rows_ref[narrow : narrow + wide, :])
        code_ref[at : at + wide, :] = high
        code_ref[at + wide : at + 2 * wide, :] = low
        code_ref[at + 2 * wide : at + 3 * wide, :] = rows_ref[narrow + wide : narrow + 2 * wide, :]


def combine(recv, row, params, n, cst_ref):
    combine_sums(recv[:, row : row + params, :], recv[:, row + params : row + 2 * params, :], n, params, cst_ref)


def combine_coded(recv, row, params, n, cst_ref, narrow=False):
    v = recv.astype(F32)
    if narrow:
        v = v[:, 0 : 2 * params] + v[:, 2 * params : 4 * params]
        combine_sums(v[:, 0:params], v[:, params:], n, params, cst_ref)
        return
    s = v[:, row : row + params] + v[:, row + params : row + 2 * params]
    combine_sums(s, v[:, row + 2 * params : row + 3 * params], n, params, cst_ref)


def combine_sums(s, m2, n, params, cst_ref):
    k = n.sum(axis=0)
    mean = s.sum(axis=0) / k
    off = s / jnp.maximum(n, 1.0) - mean[None]
    cst_ref[0:params, :] = mean
    cst_ref[params : 2 * params, :] = lax.rsqrt((m2 + n * off * off).sum(axis=0) / k + EPS)


def pick_half(int_ref, other_ref, ref, b):
    if other_ref is None:
        return ref[:, lanes(b)]
    return jnp.where(int_ref[1] == 0, other_ref[:, lanes(b)], ref[:, lanes(b)])


def fold32(v):
    v = v[:, 0:LN] + v[:, LN:256]
    v = v + pltpu.roll(v, 32, 1)
    return v + pltpu.roll(v, 64, 1)


def tiled_rows(scratch, tiled):
    c = tiled.shape[0]
    scratch[0:c, :] = tiled
    group = lax.broadcasted_iota(jnp.int32, (c // 4, LN), 1) >> 5
    out = jnp.zeros((c // 4, LN), F32)
    for q in range(4):
        out = jnp.where(group == q, scratch[pl.ds(q, c // 4, stride=4), :], out)
    return out


def pack3(pad, b, mid, left, right, px, grid):
    g, half = b // 2, b % 2
    for slot, value in enumerate((left, mid, right)):
        at = g * 768 + slot * 256 + half * 128
        pad[grid : grid + px, at : at + LN] = value.astype(BF16)


def neighbours(h, px, grid):
    col = lax.broadcasted_iota(jnp.int32, (px, LN), 0) & (grid - 1)
    before = jnp.where(col == 0, 0.0, pltpu.roll(h, 1, 0))
    after = jnp.where(col == grid - 1, 0.0, pltpu.roll(h, px - 1, 0))
    return before, after


def clear_edges(pad, px, grid):
    zero = jnp.zeros((grid, pad.shape[1]), BF16)
    pad[0:grid, :] = zero
    pad[grid + px : grid + px + grid, :] = zero


def put_count(rows_ref, row, count):
    rows_ref[row : row + 1, :] = jnp.zeros((1, LN), F32) + count


def side_sq(side, frames):
    s = side.astype(F32)
    return s * s * frames


class Net:
    def __init__(self, ndp, grid):
        self.ndp = ndp
        self.n = 2 * ndp
        self.grid = grid
        self.px = grid * grid

    def fast_first(self, ints, xf, wa, **kw):
        px, grid, n = self.px, self.grid, self.n

        def body(int_ref, xf_ref, wa_ref, lo_ref, hi_ref, band_ref, pay_ref, row_ref, fa_ref):
            side = int_ref[0]
            row_ref[...] = jnp.zeros_like(row_ref)

            @pl.when(int_ref[1] == 1)
            def _():
                pick = jnp.where(
                    (lax.broadcasted_iota(jnp.int32, (CF_MID, 256), 1) & (CF_MID - 1))
                    == lax.broadcasted_iota(jnp.int32, (CF_MID, 256), 0),
                    1.0,
                    0.0,
                ).astype(BF16)
                wide = [dot_l(wa_ref[k], pick) for k in range(3)]
                group = lax.broadcasted_iota(jnp.int32, (CF, 256), 1) >> 5
                for j in range(10):
                    acc = jnp.zeros((CF, 256), F32)
                    for k in range(3):
                        if 0 <= j - k < 8:
                            acc = jnp.where(group == j - k, wide[k], acc)
                    band_ref[j * CF : (j + 1) * CF, :] = acc.astype(BF16)
                for g in range(4):
                    lo, hi = max(8 * g - 1, 0), min(8 * g + 9, TF)
                    k0 = lo - (8 * g - 1)
                    out = dot(
                        xf_ref[:, lo * CF : hi * CF], band_ref[k0 * CF : (k0 + hi - lo) * CF, :]
                    )
                    fa_ref[:, g * 256 : (g + 1) * 256] = out
                    target = lo_ref if g < 2 else hi_ref
                    target[:, (g % 2) * 256 : (g % 2 + 1) * 256] = out
                moments(fa_ref, row_ref, 0, 8, 1, True, region(side, px, grid), side_sq(side, TF))

            put_count(row_ref, 2, side_sq(side, 1))
            send(pay_ref, row_ref)

        return call(
            body,
            [((px, 512), F32, "far"), ((px, 512), F32), ((10 * CF, 256), BF16), ((n, 4, LN), F32, "far")],
            [pltpu.VMEM((4, LN), F32), pltpu.VMEM((px, 1024), F32)],
            ints, xf, wa,
            **kw,
        )

    def fast_weights(self, wb, wbt, wc, **kw):
        def body(wb_ref, wbt_ref, wc_ref, b_ref, bt_ref, c_ref):
            pick = jnp.where(
                (lax.broadcasted_iota(jnp.int32, (CF_MID, 256), 1) & (CF_MID - 1))
                == lax.broadcasted_iota(jnp.int32, (CF_MID, 256), 0),
                1.0,
                0.0,
            ).astype(BF16)
            same = (lax.broadcasted_iota(jnp.int32, (256, 256), 0) >> 5) == (
                lax.broadcasted_iota(jnp.int32, (256, 256), 1) >> 5
            )
            for source, target in ((wb_ref, b_ref), (wbt_ref, bt_ref)):
                for tap in range(9):
                    tiled = jnp.concatenate([dot(source[tap], pick)] * 8, axis=0)
                    target[tap // 3, (tap % 3) * 256 : (tap % 3 + 1) * 256, :] = jnp.where(
                        same, tiled, 0.0
                    ).astype(BF16)
            c_ref[...] = jnp.zeros_like(c_ref)
            for i in range(8):
                c_ref[i * CF_MID : (i + 1) * CF_MID, i * CF : (i + 1) * CF] = wc_ref[...]

        return call(
            body,
            [((3, 768, 256), BF16), ((3, 768, 256), BF16), ((256, 1024), BF16)],
            [],
            wb, wbt, wc, smem=0,
            **kw,
        )

    def conv_stage(self, ints, recv, counts, x, par, w, params, frames, other=None, more=None, **kw):
        px, grid, n, ndp = self.px, self.grid, self.n, self.ndp
        fold = params == 1
        two = other is not None
        rows = 4 + (0 if more is None else more.array.shape[0])
        coded = 8 + 3 * (rows - 4) // 2

        def body(int_ref, recv_ref, n_ref, x_ref, par_ref, w_ref, *refs):
            o_ref = None
            if two:
                o_ref, refs = refs[0], refs[1:]
            if more is not None:
                m_ref, refs = refs[0], refs[1:]
            h_ref, y_ref, cst_ref, pay_ref = refs[:4]
            row_ref, pad = refs[4 + two : 6 + two]
            code_ref = refs[-1]
            if two:
                refs[4][...] = recv_ref[...]
            side = int_ref[0]
            mask = region(side, px, grid)
            half_mask = 0.5 * mask
            if two:
                stats, count = recv_ref[ndp:], n_ref[ndp:, 2:3, :] * float(TF)
            else:
                stats, count = recv_ref[...], n_ref[:, 2:3, :] * float(frames)
            combine(stats, 0, params, count, cst_ref)
            mean, rs = cst_ref[0:params, :], cst_ref[params : 2 * params, :]
            scale = par_ref[0:params, :] * rs
            shift = par_ref[params : 2 * params, :] - mean * scale
            clear_edges(pad, px, grid)
            for b in range(4):
                p = b % params
                v = pick_half(int_ref, o_ref, x_ref, b) * scale[p : p + 1] + shift[p : p + 1]
                h = gelu(v, half_mask)
                h_ref[:, lanes(b)] = h.astype(BF16)
                before, after = neighbours(h, px, grid)
                pack3(pad, b, h, before, after, px, grid)
            for g in range(2):
                acc = None
                for i in range(3):
                    part = dot(pad[grid * i : grid * i + px, g * 768 : (g + 1) * 768], w_ref[i])
                    acc = part if acc is None else acc + part
                y_ref[:, g * 256 : (g + 1) * 256] = acc
            moments(y_ref, row_ref, 0, 4, params, fold, mask, side_sq(side, frames))
            if more is None:
                send(pay_ref, row_ref)
            else:
                row_ref[4:rows, :] = m_ref[...]
                encode(code_ref, row_ref, 4, rows // 2 - 2)
                send(pay_ref, code_ref)

        extra = [other] if two else []
        extra += [] if more is None else [more]
        return call(
            body,
            [((px, 512), BF16), ((px, 512), F32), ((8, LN), F32), ((n, rows, LN), F32, "far") if more is None else ((n, coded, LN), BF16, "far")]
            + ([((n, 4, LN), F32)] if two else []),
            [pltpu.VMEM((rows, LN), F32), pltpu.VMEM((px + 2 * grid, 2 * 768), BF16)]
            + ([] if more is None else [pltpu.VMEM((coded, LN), F32)]),
            ints, recv, counts, x, par, w, *extra,
            **kw,
        )

    def expand_stage(self, ints, recv, counts, y, par, w, params, wide, frames, edge=False, **kw):
        px, grid, n = self.px, self.grid, self.n
        rows = max(2 * wide, 4)
        code = wide > 1
        coded = 3 * wide

        def body(int_ref, recv_ref, n_ref, y_ref, par_ref, w_ref, h_ref, cst_ref, pay_ref, *refs):
            row_ref, c_ref = refs[edge : edge + 2]
            code_ref = refs[-1]
            side = int_ref[0]
            mask = region(side, px, grid)
            half_mask = 0.5 * mask
            count = n_ref[:, 2:3, :] * float(frames)
            if code:
                combine_coded(recv_ref[...], 0, params, count, cst_ref, True)
            else:
                combine(recv_ref[...], 0, params, count, cst_ref)
            mean, rs = cst_ref[0:params, :], cst_ref[params : 2 * params, :]
            scale = par_ref[0:params, :] * rs
            shift = par_ref[params : 2 * params, :] - mean * scale
            for b in range(4):
                p = b % params
                v = y_ref[:, lanes(b)] * scale[p : p + 1] + shift[p : p + 1]
                h_ref[:, lanes(b)] = gelu(v, half_mask).astype(BF16)
            if edge:
                refs[0][...] = h_ref[:, lanes(3)]
            for g in range(2):
                c_ref[:, g * 1024 : (g + 1) * 1024] = dot(h_ref[:, g * 256 : (g + 1) * 256], w_ref[...])
            moments(c_ref, row_ref, 0, 16, wide, False, mask, side_sq(side, frames))
            if code:
                encode(code_ref, row_ref, 0, wide)
            send(pay_ref, code_ref if code else row_ref)

        return call(
            body,
            [((px, 512), BF16), ((8, LN), F32), ((n, coded, LN), BF16, "far") if code else ((n, rows, LN), F32, "far")]
            + ([((px, LN), BF16, "far")] if edge else []),
            [pltpu.VMEM((rows, LN), F32), pltpu.VMEM((px, 2048), F32)]
            + ([pltpu.VMEM((coded, LN), F32)] if code else []),
            ints, recv, counts, y, par, w,
            **kw,
        )

    def fast_finish(self, ints, recv, counts, h2, h2_other, w, xf, par, wlat, pa, wa, **kw):
        px, grid, n = self.px, self.grid, self.n

        def body(
            int_ref, recv_ref, n_ref, h_ref, ho_ref, w_ref, xf_ref, par_ref, wl_ref, pa_ref, wa_ref,
            y_ref, lat_ref, cst_ref, sa_ref, pay_ref, c_ref, row_ref,
        ):
            half_mask = 0.5 * region(int_ref[0], px, grid)
            combine(recv_ref[...], 0, 1, n_ref[:, 2:3, :] * float(TF // 2), cst_ref)
            scale = par_ref[0:1, :] * cst_ref[1:2, :]
            shift = par_ref[1:2, :] - cst_ref[0:1, :] * scale
            c_ref[:, 0:256] = dot(ho_ref[...], w_ref[0:LN, 256:512])
            edge = half_mask * int_ref[1].astype(F32)
            for f in range(2):
                v = c_ref[:, lanes(f)] * scale + shift + xf_ref[:, lanes(f)].astype(F32)
                y_ref[:, lanes(f)] = jnp.where(int_ref[1] == 1, gelu(v, edge), 0.0).astype(BF16)
            for g in range(2):
                c_ref[...] = dot(h_ref[:, g * 256 : (g + 1) * 256], w_ref[...])

                def step(i, carry):
                    f = 2 + g * 8 + i
                    v = c_ref[:, lanes(i)] * scale + shift + xf_ref[:, lanes(f)].astype(F32)
                    y_ref[:, lanes(f)] = gelu(v, half_mask).astype(BF16)
                    return carry

                loop(8, step, 0)
            for t in range(2):
                at = ALPHA * t * CF
                lat_ref[:, t * LAT : (t + 1) * LAT] = dot(y_ref[:, at : at + 5 * CF], wl_ref[...]).astype(BF16)
                a = slice(t * CS_MID, (t + 1) * CS_MID)
                sa_ref[:, a] = pa_ref[:, a] + dot(lat_ref[:, t * LAT : (t + 1) * LAT], wa_ref[...])
            side = int_ref[0]
            moments(sa_ref, row_ref, 0, 4, 2, False, region(side, px, grid), side_sq(side, TS // 2))
            send(pay_ref, row_ref)

        return call(
            body,
            [((px, 18 * CF), BF16), ((px, 512), BF16), ((8, LN), F32), ((px, 512), F32), ((n, 4, LN), F32, "far")],
            [pltpu.VMEM((px, 1024), F32), pltpu.VMEM((4, LN), F32)],
            ints, recv, counts, h2, h2_other, w, xf, par, wlat, pa, wa,
            **kw,
        )

    def fast_slope(self, ints, h2, w, xf, par, cst, **kw):
        px, grid = self.px, self.grid

        def body(int_ref, h_ref, w_ref, xf_ref, par_ref, cst_ref, gp_ref, c_ref):
            half_mask = 0.5 * region(int_ref[0], px, grid)
            scale = par_ref[0:1, :] * cst_ref[1:2, :]
            shift = par_ref[1:2, :] - cst_ref[0:1, :] * scale
            for g in range(2):
                c_ref[...] = dot(h_ref[:, g * 256 : (g + 1) * 256], w_ref[...])

                def step(i, carry):
                    f = g * 8 + i
                    v = c_ref[:, lanes(i)] * scale + shift + xf_ref[:, lanes(f + 2)].astype(F32)
                    gp_ref[:, lanes(f)] = gelu_both(v, half_mask)[1]
                    return carry

                loop(8, step, 0)

        return call(body, ((px, 2048), F32), [pltpu.VMEM((px, 1024), F32)], ints, h2, w, xf, par, cst, **kw)

    def slow_start(self, xs, wa, wp, **kw):
        px = self.px

        def body(x_ref, wa_ref, wp_ref, a_ref, p_ref):
            for t in range(2):
                x = x_ref[:, t * CS : (t + 1) * CS]
                a_ref[:, t * CS_MID : (t + 1) * CS_MID] = dot(x, wa_ref[0:CS, :])
                p_ref[:, t * CS : (t + 1) * CS] = dot(x, wp_ref[0:CS, :])

        return call(body, [((px, 512), F32), ((px, 2048), F32)], [], xs, wa, wp, smem=0, **kw)

    def slow_join(self, ints, part, lat, w, params, **kw):
        px, grid = self.px, self.grid
        width = params * LN

        def body(int_ref, part_ref, lat_ref, w_ref, out_ref, row_ref):
            side = int_ref[0]
            for t in range(2):
                at = slice(t * width, (t + 1) * width)
                out_ref[:, at] = part_ref[:, at] + dot(lat_ref[:, t * LAT : (t + 1) * LAT], w_ref[...])
            moments(
                out_ref, row_ref, 0, 2 * params, params, False, region(side, px, grid), side_sq(side, TS // 2)
            )

        return call(
            body, [((px, 2 * width), F32), ((2 * params, LN), F32)], [], ints, part, lat, w, **kw
        )

    def slow_top(self, ints, recv3, recvp, counts, h2, w, sp, gs, parc, parp, **kw):
        px, grid, n = self.px, self.grid, self.n

        def body(
            int_ref, r3_ref, rp_ref, n_ref, h_ref, w_ref, sp_ref, gs_ref, pc_ref, pp_ref,
            ys_ref, ds_ref, cc_ref, cp_ref, pay_ref, row_ref, c_ref, acc_ref, k_ref,
        ):
            half_mask = 0.5 * region(int_ref[0], px, grid)
            count = n_ref[:, 2:3, :] * float(TS // 2)
            combine_coded(r3_ref[...], 0, 8, count, cc_ref)
            combine_coded(rp_ref[...], 8, 8, count, cp_ref)
            k_ref[0:8, :] = pc_ref[0:8, :] * cc_ref[8:16, :]
            k_ref[8:16, :] = pp_ref[0:8, :] * cp_ref[8:16, :]
            k_ref[16:24, :] = pc_ref[8:16, :] + pp_ref[8:16, :]
            acc_ref[...] = jnp.zeros_like(acc_ref)
            for t in range(2):
                c_ref[...] = dot(h_ref[:, t * 256 : (t + 1) * 256], w_ref[...])

                def step(b, carry):
                    at = lanes(t * 8 + b)
                    one = pl.ds(b, 1)
                    xc = c_ref[:, lanes(b)] - cc_ref[one, :]
                    xp = sp_ref[:, at] - cp_ref[one, :]
                    v = xc * k_ref[one, :] + (xp * k_ref[pl.ds(b + 8, 1), :] + k_ref[pl.ds(b + 16, 1), :])
                    y, slope = gelu_both(v, half_mask)
                    ys_ref[:, at] = y.astype(BF16)
                    d = gs_ref[:, at].astype(F32) * slope
                    ds_ref[:, at] = d
                    acc_ref[b] += rows8(d)
                    acc_ref[8 + b] += rows8(d * xc)
                    acc_ref[16 + b] += rows8(d * xp)
                    return carry

                loop(8, step, 0)
            row_ref[...] = acc_ref[...].sum(axis=1)
            row_ref[8:16, :] = row_ref[8:16, :] * cc_ref[8:16, :]
            row_ref[16:24, :] = row_ref[16:24, :] * cp_ref[8:16, :]
            send(pay_ref, row_ref)

        return call(
            body,
            [
                ((px, 2048), BF16), ((px, 2048), F32), ((16, LN), F32), ((16, LN), F32),
                ((n, 24, LN), BF16, "far"),
            ],
            [
                pltpu.VMEM((24, LN), F32), pltpu.VMEM((px, 1024), F32),
                pltpu.VMEM((24, 8, LN), F32), pltpu.VMEM((24, LN), F32),
            ],
            ints, recv3, recvp, counts, h2, w, sp, gs, parc, parp,
            **kw,
        )

    def fast_top(self, ints, dl0, dl1, dl_other, wlat, gf, gp, h2, w, cst, **kw):
        px, n = self.px, self.n

        def body(
            int_ref, d0_ref, d1_ref, do_ref, wl_ref, gf_ref, gp_ref, h_ref, w_ref, cst_ref,
            ds_ref, pay_ref, row_ref, lt_ref, c_ref, acc_ref,
        ):
            first = (1 - int_ref[1]).astype(F32)
            lt_ref[:, 0 : 3 * CF] = dot_t(d0_ref[...], wl_ref[2 * CF :, :])
            lt_ref[:, 3 * CF : 8 * CF] = dot_t(d1_ref[...], wl_ref[...])
            edge = dot_t(do_ref[...], wl_ref[0 : 2 * CF, :])
            lt_ref[:, 8 * CF : 10 * CF] = jnp.where(int_ref[1] == 0, edge, 0.0)
            acc_ref[...] = jnp.zeros_like(acc_ref)
            mean, rs = cst_ref[0:1, :], cst_ref[1:2, :]
            where = {0: 0, 1: 1, 2: 2, 6: 3, 7: 4, 8: 5, 9: 6, 10: 7, 14: 8, 15: 9}
            for g in range(2):
                c_ref[...] = dot(h_ref[:, g * 256 : (g + 1) * 256], w_ref[...])
                for i in range(8):
                    f = g * 8 + i
                    d = gf_ref[:, lanes(f)].astype(F32)
                    if f in where:
                        d = d + lt_ref[:, lanes(where[f])]
                    d = d * gp_ref[:, lanes(f)]
                    ds_ref[:, lanes(f)] = d
                    acc_ref[0] += rows8(d)
                    acc_ref[1] += rows8(d * (c_ref[:, lanes(i)] - mean))
            row_ref[...] = jnp.zeros_like(row_ref)
            row_ref[0:1, :] = acc_ref[0].sum(axis=0, keepdims=True)
            row_ref[1:2, :] = acc_ref[1].sum(axis=0, keepdims=True) * rs
            send(pay_ref, row_ref)

        return call(
            body,
            [((px, 2048), F32), ((n, 4, LN), F32, "far")],
            [
                pltpu.VMEM((4, LN), F32), pltpu.VMEM((px, 10 * CF), F32),
                pltpu.VMEM((px, 1024), F32), pltpu.VMEM((2, 8, LN), F32),
            ],
            ints, dl0, dl1, dl_other, wlat, gf, gp, h2, w, cst,
            **kw,
        )

    def expand_back(self, ints, counts, recv, ds, h2, w, cstw, parw, y, cst, par, params, wide, frames, shortcut=None, **kw):
        px, grid, n = self.px, self.grid, self.n
        fold = params == 1
        both = shortcut is not None
        srows = 3 * wide if both else 4

        def body(*refs):
            int_ref, n_ref, recv_ref, ds_ref, h_ref, w_ref, cw_ref, pw_ref, y_ref, cs_ref, par_ref = refs[:11]
            refs = refs[11:]
            if both:
                sp_ref, cp_ref, pp_ref, dp_ref = refs[:4]
                refs = refs[4:]
            dc_ref, dn_ref, sum_ref, pay_ref, row_ref, c_ref, k3_ref = refs
            mask = region(int_ref[0], px, grid)
            half_mask = 0.5 * mask
            inv_k = 1.0 / (n_ref[:, 2:3, :].sum(axis=0) * float(frames))
            sums = recv_ref[...].astype(F32).sum(axis=0)
            sum_ref[...] = sums
            a = pw_ref[0:wide, :] * cw_ref[wide : 2 * wide, :]
            k3_ref[0:wide, :] = a
            k3_ref[wide : 2 * wide, :] = a * inv_k * sums[0:wide]
            k3_ref[2 * wide : 3 * wide, :] = a * inv_k * cw_ref[wide : 2 * wide, :] * sums[wide : 2 * wide]
            if both:
                a = pp_ref[0:wide, :] * cp_ref[wide : 2 * wide, :]
                k3_ref[3 * wide : 4 * wide, :] = a
                k3_ref[4 * wide : 5 * wide, :] = a * inv_k * sums[0:wide]
                k3_ref[5 * wide : 6 * wide, :] = (
                    a * inv_k * cp_ref[wide : 2 * wide, :] * sums[2 * wide : 3 * wide]
                )
            mean, rs = cs_ref[0:params, :], cs_ref[params : 2 * params, :]
            accs = [[jnp.zeros((8, LN), F32) for _ in range(params)] for _ in range(2)]
            for g in range(2):
                c_ref[...] = dot(h_ref[:, g * 256 : (g + 1) * 256], w_ref[...])

                def step(b, carry):
                    at = lanes(g * 8 + b)
                    p = b if wide == 8 else 0
                    d = ds_ref[:, at]
                    e = (c_ref[:, lanes(b)] - cw_ref[pl.ds(p, 1), :]) * k3_ref[pl.ds(2 * wide + p, 1), :]
                    e = d * k3_ref[pl.ds(p, 1), :] - k3_ref[pl.ds(wide + p, 1), :] - e
                    dc_ref[:, at] = (e * mask).astype(BF16)
                    if both:
                        e = (sp_ref[:, at] - cp_ref[pl.ds(p, 1), :]) * k3_ref[pl.ds(5 * wide + p, 1), :]
                        e = d * k3_ref[pl.ds(3 * wide + p, 1), :] - k3_ref[pl.ds(4 * wide + p, 1), :] - e
                        dp_ref[:, at] = (e * mask).astype(BF16)
                    return carry

                loop(8, step, 0)
                dh = dot_t(dc_ref[:, g * 1024 : (g + 1) * 1024], w_ref[...])
                for half in range(2):
                    b = g * 2 + half
                    p = b % params
                    xh = (y_ref[:, lanes(b)] - mean[p : p + 1]) * rs[p : p + 1]
                    v = xh * par_ref[p : p + 1, :] + par_ref[params + p : params + p + 1, :]
                    d = dh[:, half * LN : (half + 1) * LN] * gelu_both(v, half_mask)[1]
                    dn_ref[:, lanes(b)] = d
                    accs[0][p] = accs[0][p] + rows8(d)
                    accs[1][p] = accs[1][p] + rows8(d * xh)
            row_ref[...] = jnp.zeros_like(row_ref)
            for q in range(2):
                for p in range(params):
                    row_ref[q * params + p : q * params + p + 1, :] = total(accs[q][p], fold)
            send(pay_ref, row_ref)

        outs = [((px, 2048), BF16)] if both else []
        outs += [((px, 2048), BF16), ((px, 512), F32), ((srows, LN), F32, "far"), ((n, 4, LN), F32, "far")]
        extra = list(shortcut) if both else []
        return call(
            body,
            outs,
            [pltpu.VMEM((4, LN), F32), pltpu.VMEM((px, 1024), F32), pltpu.VMEM((max(6 * wide, 8), LN), F32)],
            ints, counts, recv, ds, h2, w, cstw, parw, y, cst, par, *extra,
            **kw,
        )

    def conv_back(self, ints, counts, recv, dn, y, cst2, par2, wt, x, cst1, par1, params, frames, other=None, **kw):
        px, grid, n = self.px, self.grid, self.n
        fold = params == 1
        two = other is not None

        def body(int_ref, n_ref, recv_ref, dn_ref, y_ref, c2_ref, p2_ref, w_ref, x_ref, c1_ref, p1_ref, *refs):
            o_ref = None
            if two:
                o_ref, refs = refs[0], refs[1:]
            db_ref, dn1_ref, sum_ref, pay_ref, row_ref, pad = refs
            mask = region(int_ref[0], px, grid)
            half_mask = 0.5 * mask
            inv_k = 1.0 / (n_ref[:, 2:3, :].sum(axis=0) * float(frames))
            sums = recv_ref[...].astype(F32).sum(axis=0)
            sum_ref[...] = sums
            mean2, rs2 = c2_ref[0:params, :], c2_ref[params : 2 * params, :]
            a = p2_ref[0:params, :] * rs2
            b0 = a * inv_k * sums[0:params]
            c0 = a * inv_k * rs2 * sums[params : 2 * params]
            clear_edges(pad, px, grid)
            for b in range(4):
                p = b % params
                e = (y_ref[:, lanes(b)] - mean2[p : p + 1]) * c0[p : p + 1]
                e = (dn_ref[:, lanes(b)] * a[p : p + 1] - b0[p : p + 1] - e) * mask
                db_ref[:, lanes(b)] = e.astype(BF16)
                before, after = neighbours(e, px, grid)
                pack3(pad, b, e, after, before, px, grid)
            mean, rs = c1_ref[0:params, :], c1_ref[params : 2 * params, :]
            accs = [[jnp.zeros((8, LN), F32) for _ in range(params)] for _ in range(2)]
            for g in range(2):
                dh = None
                for i in range(3):
                    part = dot(pad[grid * i : grid * i + px, g * 768 : (g + 1) * 768], w_ref[2 - i])
                    dh = part if dh is None else dh + part
                for half in range(2):
                    b = g * 2 + half
                    p = b % params
                    xh = (pick_half(int_ref, o_ref, x_ref, b) - mean[p : p + 1]) * rs[p : p + 1]
                    v = xh * p1_ref[p : p + 1, :] + p1_ref[params + p : params + p + 1, :]
                    d = dh[:, half * LN : (half + 1) * LN] * gelu_both(v, half_mask)[1]
                    dn1_ref[:, lanes(b)] = d
                    accs[0][p] = accs[0][p] + rows8(d)
                    accs[1][p] = accs[1][p] + rows8(d * xh)
            row_ref[...] = jnp.zeros_like(row_ref)
            for q in range(2):
                for p in range(params):
                    row_ref[q * params + p : q * params + p + 1, :] = total(accs[q][p], fold)
            send(pay_ref, row_ref)

        extra = [other] if two else []
        return call(
            body,
            [((px, 512), BF16), ((px, 512), F32), ((4, LN), F32, "far"), ((n, 4, LN), F32, "far")],
            [pltpu.VMEM((4, LN), F32), pltpu.VMEM((px + 2 * grid, 2 * 768), BF16)],
            ints, counts, recv, dn, y, cst2, par2, wt, x, cst1, par1, *extra,
            **kw,
        )

    def slow_last(self, ints, counts, recv, dn, x, cst, par, dp, wa, wp, **kw):
        px, grid = self.px, self.grid

        def body(
            int_ref, n_ref, recv_ref, dn_ref, x_ref, cst_ref, par_ref, dp_ref, wa_ref, wp_ref,
            da_ref, d0_ref, d1_ref, sum_ref,
        ):
            mask = region(int_ref[0], px, grid)
            inv_k = 1.0 / (n_ref[:, 2:3, :].sum(axis=0) * float(TS // 2))
            sums = recv_ref[...].astype(F32).sum(axis=0)
            sum_ref[...] = sums
            mean, rs = cst_ref[0:2, :], cst_ref[2:4, :]
            a = par_ref[0:2, :] * rs
            b0 = a * inv_k * sums[0:2]
            c0 = a * inv_k * rs * sums[2:4]
            for b in range(4):
                p = b % 2
                e = (x_ref[:, lanes(b)] - mean[p : p + 1]) * c0[p : p + 1]
                e = (dn_ref[:, lanes(b)] * a[p : p + 1] - b0[p : p + 1] - e) * mask
                da_ref[:, lanes(b)] = e.astype(BF16)
            for t, out in ((0, d0_ref), (1, d1_ref)):
                out[...] = (
                    dot_t(da_ref[:, t * CS_MID : (t + 1) * CS_MID], wa_ref[...])
                    + dot_t(dp_ref[:, t * CS : (t + 1) * CS], wp_ref[...])
                ).astype(BF16)

        return call(
            body,
            [((px, 512), BF16), ((px, LAT), BF16), ((px, LAT), BF16), ((4, LN), F32, "far")],
            [],
            ints, counts, recv, dn, x, cst, par, dp, wa, wp,
            **kw,
        )

    def slow_input_grad(self, da, dp, wa, wp, **kw):
        px = self.px

        def body(da_ref, dp_ref, wa_ref, wp_ref, dx_ref):
            for t in range(2):
                dx_ref[:, t * CS : (t + 1) * CS] = (
                    dot_t(da_ref[:, t * CS_MID : (t + 1) * CS_MID], wa_ref[0:CS, :])
                    + dot_t(dp_ref[:, t * CS : (t + 1) * CS], wp_ref[0:CS, :])
                ).astype(BF16)

        return call(body, ((px, 2048), BF16, "far"), [], da, dp, wa, wp, smem=0, **kw)

    def fast_first_back(self, ints, counts, recv, dn_lo, dn_hi, fa_lo, fa_hi, cst, par, **kw):
        px, grid = self.px, self.grid

        def body(int_ref, n_ref, recv_ref, dl_ref, dh_ref, xl_ref, xh_ref, cst_ref, par_ref, da_ref, sum_ref):
            sums = recv_ref[...].sum(axis=0)
            sum_ref[...] = sums

            @pl.when(int_ref[1] == 1)
            def _():
                mask = region(int_ref[0], px, grid)
                inv_k = 1.0 / (n_ref[:, 2:3, :].sum(axis=0) * float(TF // 2))
                mean, rs = cst_ref[0:1, :], cst_ref[1:2, :]
                a = par_ref[0:1, :] * rs
                b0 = a * inv_k * sums[0:1]
                c0 = a * inv_k * rs * sums[1:2]
                for dn_ref, h_ref, base in ((dl_ref, xl_ref, 0), (dh_ref, xh_ref, 4)):
                    for b in range(4):
                        e = (h_ref[:, lanes(b)] - mean) * c0
                        e = (dn_ref[:, lanes(b)] * a - b0 - e) * mask
                        da_ref[:, lanes(base + b)] = e.astype(BF16)

        return call(
            body,
            [((px, 1024), BF16), ((4, LN), F32, "far")],
            [],
            ints, counts, recv, dn_lo, dn_hi, fa_lo, fa_hi, cst, par,
            **kw,
        )

    def fast_small(self, ints, da, xf, bc, bc_other, **kw):
        first = 3 * CF_MID
        rows = first + bc.shape[0]

        def body(int_ref, da_ref, x_ref, b0_ref, b1_ref, out_ref, row_ref, scratch):
            row_ref[0:first, :] = jnp.zeros((first, LN), F32)
            row_ref[first:rows, :] = b0_ref[...] + b1_ref[...]

            @pl.when(int_ref[1] == 1)
            def _():
                accs = [None] * 3
                for g in range(4):
                    lo, hi = max(8 * g - 1, 0), min(8 * g + 9, TF)
                    k0 = lo - (8 * g - 1)
                    d = dot(da_ref[:, g * 256 : (g + 1) * 256].T, x_ref[:, lo * CF : hi * CF])
                    for k in range(3):
                        for i in range(8):
                            j = i + k - k0
                            if 0 <= j < hi - lo:
                                part = d[i * CF_MID : (i + 1) * CF_MID, j * CF : (j + 1) * CF]
                                accs[k] = part if accs[k] is None else accs[k] + part
                for k in range(3):
                    tiled = jnp.concatenate([accs[k]] * 4, axis=0).T
                    row_ref[k * CF_MID : (k + 1) * CF_MID, :] = tiled_rows(scratch, tiled)

            out_ref[...] = row_ref[...].astype(BF16)

        return call(
            body,
            ((rows, LN), BF16, "far"),
            [pltpu.VMEM((rows, LN), F32), pltpu.VMEM((LN, LN), F32)],
            ints, da, xf, bc, bc_other,
            **kw,
        )

    def last(self, ints, da, ds_lo, ds_hi, band, dxs0, dxs1, **kw):
        px = self.px

        def body(int_ref, da_ref, sl_ref, sh_ref, band_ref, x0_ref, x1_ref, dx_ref, acc_ref, out_ref, sem):
            def part(g):
                at = slice(g * 1024, (g + 1) * 1024)
                return pltpu.make_async_copy(out_ref.at[:, at], dx_ref.at[:, at], sem.at[g])

            def half(ref, g):
                return pltpu.make_async_copy(ref, out_ref.at[:, g * 2048 : (g + 1) * 2048], sem.at[g])

            @pl.when(int_ref[1] == 0)
            def _():
                half(x0_ref, 0).start()
                half(x1_ref, 1).start()
                half(x0_ref, 0).wait()
                half(x1_ref, 1).wait()
                for g in range(4):
                    part(g).start()
                for g in range(4):
                    part(g).wait()

            @pl.when(int_ref[1] == 1)
            def _():
                acc_ref[:, 0 : 10 * CF] = dot_t(da_ref[:, 0:256], band_ref[...])
                for g in range(4):
                    if g < 3:
                        p = dot_t(da_ref[:, (g + 1) * 256 : (g + 2) * 256], band_ref[...])
                        base = 8 * (g + 1) * CF
                        acc_ref[:, base : base + 2 * CF] += p[:, 0 : 2 * CF]
                        acc_ref[:, base + 2 * CF : base + 10 * CF] = p[:, 2 * CF :]
                    s_ref = sl_ref if g < 2 else sh_ref
                    for i in range(8):
                        f = 8 * g + i
                        s = s_ref[:, lanes(f % 16)] + acc_ref[:, lanes(f + 1)]
                        out_ref[:, lanes(f)] = s.astype(BF16)
                    part(g).start()
                for g in range(4):
                    part(g).wait()

        return call(
            body,
            ((px, 4096), BF16, "manual"),
            [pltpu.VMEM((px, 34 * CF), F32), pltpu.VMEM((px, 4096), BF16), pltpu.SemaphoreType.DMA((4,))],
            ints, da, ds_lo, ds_hi, band, Manual(dxs0), Manual(dxs1),
            **kw,
        )

    def halves(self, ints, x, x_other, cot, cot_other, **kw):
        px = self.px

        def body(int_ref, x_ref, xo_ref, c_ref, co_ref, xs_ref, xf_ref, gs_ref, gf_ref, sem):
            def run(pairs):
                copies = [pltpu.make_async_copy(a, b, sem.at[k]) for k, (a, b) in enumerate(pairs)]
                for c in copies:
                    c.start()
                for c in copies:
                    c.wait()

            lo, hi = slice(0, 2048), slice(2048, 4096)

            @pl.when(int_ref[1] == 0)
            def _():
                xf_ref[:, 0 : 2 * CF] = jnp.zeros((px, 2 * CF), BF16)
                run([
                    (x_ref.at[:, lo], xs_ref), (xo_ref.at[:, lo], xf_ref.at[:, 2 * CF : 18 * CF]),
                    (c_ref.at[:, lo], gs_ref), (co_ref.at[:, lo], gf_ref),
                ])

            @pl.when(int_ref[1] == 1)
            def _():
                run([
                    (xo_ref.at[:, hi], xs_ref), (x_ref.at[:, 14 * CF :], xf_ref),
                    (co_ref.at[:, hi], gs_ref), (c_ref.at[:, hi], gf_ref),
                ])

        wide = ((px, 2048), BF16)
        return call(
            body,
            [wide, ((px, 18 * CF), BF16), wide, wide],
            [pltpu.SemaphoreType.DMA((4,))],
            ints, Manual(x), Manual(x_other), Manual(cot), Manual(cot_other),
            **kw,
        )

    def out_send(self, ints, ys, yf, **kw):
        px = self.px

        def body(int_ref, ys_ref, yf_ref, out_ref):
            for path, ref, at in ((0, yf_ref, 2 * CF), (1, ys_ref, 0)):

                @pl.when(int_ref[1] == path)
                def _():
                    out_ref[...] = ref[:, at : at + 2048]

        return call(body, ((px, 2048), BF16, "far"), [], ints, ys, yf, **kw)

    def out_join(self, ints, ys, yf, other, **kw):
        px = self.px

        def body(int_ref, ys_ref, yf_ref, o_ref, out_ref):
            for path, ref, at in ((0, ys_ref, 0), (1, yf_ref, 2 * CF)):

                @pl.when(int_ref[1] == path)
                def _():
                    mine, far = path * 2048, (1 - path) * 2048
                    out_ref[:, mine : mine + 2048] = ref[:, at : at + 2048]
                    out_ref[:, far : far + 2048] = o_ref[...]

        return call(body, ((px, 4096), BF16, "far"), [], ints, ys, yf, Far(other), **kw)

    def fast_grads_bc(self, h1, db, h2, dc, **kw):
        px, grid = self.px, self.grid

        def body(h1_ref, db_ref, h2_ref, dc_ref, out_ref, pad, scratch):
            clear_edges(pad, px, grid)
            for b in range(4):
                h = h1_ref[:, lanes(b)].astype(F32)
                before, after = neighbours(h, px, grid)
                pack3(pad, b, h, before, after, px, grid)
            same = (lax.broadcasted_iota(jnp.int32, (256, 256), 0) >> 5) == (
                lax.broadcasted_iota(jnp.int32, (256, 256), 1) >> 5
            )
            for i in range(3):
                for s in range(3):
                    acc = jnp.zeros((256, 256), F32)
                    for g in range(2):
                        at = g * 768 + s * 256
                        acc = acc + dot(
                            pad[grid * i : grid * i + px, at : at + 256].T,
                            db_ref[:, g * 256 : (g + 1) * 256],
                        )
                    acc = jnp.where(same, acc, 0.0).reshape(8, CF_MID, 256).sum(axis=0)
                    at = (3 * i + s) * 8
                    out_ref[at : at + 8, :] = tiled_rows(scratch, fold32(acc))
            acc = jnp.zeros((256, 1024), F32)
            for g in range(2):
                acc = acc + dot(h2_ref[:, g * 256 : (g + 1) * 256].T, dc_ref[:, g * 1024 : (g + 1) * 1024])
            out = None
            for i in range(8):
                part = acc[i * CF_MID : (i + 1) * CF_MID, i * CF : (i + 1) * CF]
                out = part if out is None else out + part
            out_ref[72:104, :] = out
            out_ref[104:, :] = jnp.zeros((8, LN), F32)

        return call(
            body,
            ((112, LN), F32, "far"),
            [pltpu.VMEM((px + 2 * grid, 2 * 768), BF16), pltpu.VMEM((CF_MID, LN), F32)],
            h1, db, h2, dc, smem=0,
            **kw,
        )

    def grads_early(self, plan, ints, xs, lat, dp, h2, dc, **kw):
        px = self.px
        rows = plan.early

        def body(int_ref, x_ref, lat_ref, dp_ref, h2_ref, dc_ref, keep_ref, send_ref, buf, xt):
            def put(base, q, acc):
                for j in range(2):
                    buf[pl.ds(base + 2 * q + j, 256, stride=8), :] = acc[:, j * LN : (j + 1) * LN]

            for c in range(6):
                for t in range(2):
                    if c == 5:
                        x = h2_ref[:, t * 256 : (t + 1) * 256]
                    elif c == 4:
                        x = lat_ref[:, t * LAT : (t + 1) * LAT]
                    else:
                        x = x_ref[:, t * CS + c * 256 : t * CS + (c + 1) * 256]
                    xt[:, t * px : (t + 1) * px] = x.T
                source = dc_ref if c == 5 else dp_ref
                base = (ROW_SC if c == 5 else ROW_SP + c * 2048) - ROW_SC
                for q in range(4):
                    acc = None
                    for t in range(2):
                        at = t * CS + q * 256
                        part = dot(xt[:, t * px : (t + 1) * px], source[:, at : at + 256])
                        acc = part if acc is None else acc + part
                    put(base, q, acc)
            lo = 0
            hi = plan.base[1] - ROW_SC
            mine = pl.multiple_of(jnp.where(int_ref[1] == 0, lo, hi), 16)
            other = pl.multiple_of(jnp.where(int_ref[1] == 0, hi, lo), 16)
            keep_ref[...] = buf[pl.ds(mine, rows), :].astype(BF16)
            send_ref[...] = buf[pl.ds(other, rows), :].astype(BF16)

        return call(
            body,
            [((rows, LN), BF16, "far"), ((rows, LN), BF16, "far")],
            [pltpu.VMEM((ROW_SG - ROW_SC, LN), F32), pltpu.VMEM((256, 2 * px), BF16)],
            ints, xs, lat, dp, h2, dc,
            **kw,
        )

    def grads_conv(self, h1, db, **kw):
        px, grid = self.px, self.grid

        def body(h1_ref, db_ref, out_ref, buf, pad):
            clear_edges(pad, px, grid)
            for b in range(4):
                h = h1_ref[:, lanes(b)].astype(F32)
                before, after = neighbours(h, px, grid)
                pack3(pad, b, h, before, after, px, grid)
            for i in range(3):
                for s in range(3):
                    acc = None
                    for t in range(2):
                        at = t * 768 + s * 256
                        part = dot(
                            pad[grid * i : grid * i + px, at : at + 256].T,
                            db_ref[:, t * 256 : (t + 1) * 256],
                        )
                        acc = part if acc is None else acc + part
                    for j in range(2):
                        buf[pl.ds((3 * i + s) * 512 + j, 256, stride=2), :] = acc[:, j * LN : (j + 1) * LN]
            out_ref[...] = buf[...].astype(BF16)

        return call(
            body,
            ((ROW_SC - ROW_SB, LN), BF16, "far"),
            [pltpu.VMEM((ROW_SC - ROW_SB, LN), F32), pltpu.VMEM((px + 2 * grid, 2 * 768), BF16)],
            h1, db, smem=0,
            **kw,
        )

    def grads_late(self, ints, xs, lat, da, yf, dl0, dl1, **kw):
        px = self.px
        rows = ROW_SB - ROW_SA
        lat_rows = ROW_FG - ROW_LAT

        def body(int_ref, x_ref, lat_ref, da_ref, yf_ref, d0_ref, d1_ref, keep_ref, send_ref, buf):
            for c in range(5):
                acc = None
                for t in range(2):
                    if c == 4:
                        x = lat_ref[:, t * LAT : (t + 1) * LAT]
                    else:
                        x = x_ref[:, t * CS + c * 256 : t * CS + (c + 1) * 256]
                    part = dot(x.T, da_ref[:, t * CS_MID : (t + 1) * CS_MID])
                    acc = part if acc is None else acc + part
                for j in range(2):
                    buf[pl.ds(c * 512 + j, 256, stride=2), :] = acc[:, j * LN : (j + 1) * LN]
            for k in range(5):
                acc = dot(yf_ref[:, lanes(k)].T, d0_ref[...]) + dot(yf_ref[:, lanes(8 + k)].T, d1_ref[...])
                for j in range(2):
                    buf[pl.ds(rows + k * 256 + j, CF, stride=2), :] = acc[:, j * LN : (j + 1) * LN]
            mine = pl.multiple_of(jnp.where(int_ref[1] == 0, 0, rows), 16)
            other = pl.multiple_of(jnp.where(int_ref[1] == 0, rows, 0), 16)
            keep_ref[...] = buf[pl.ds(mine, rows), :].astype(BF16)
            send_ref[...] = buf[pl.ds(other, rows), :].astype(BF16)

        return call(
            body,
            [((rows, LN), BF16, "far"), ((rows, LN), BF16, "far")],
            [pltpu.VMEM((2 * rows, LN), F32)],
            ints, xs, lat, da, yf, dl0, dl1,
            **kw,
        )

    def windows(self, plan, ints, early, conv, late, **kw):
        ndp, chunk, half = self.ndp, plan.chunk, self.ndp // 2

        def body(int_ref, e0_ref, e1_ref, c0_ref, c1_ref, l0_ref, l1_ref, keep_ref, send_ref, buf):
            def add(a, b, rows):
                return a[0:rows, :].astype(F32) + b[0:rows, :].astype(F32)

            for path in range(2):

                @pl.when(int_ref[1] == path)
                def _():
                    buf[...] = jnp.zeros_like(buf)
                    base = plan.base[path]
                    if path == 0:
                        buf[ROW_SA:ROW_SB, :] = add(l0_ref, l1_ref, ROW_SB - ROW_SA)
                        buf[ROW_SB:ROW_SC, :] = add(c0_ref, c1_ref, ROW_SC - ROW_SB)
                        rest = min(plan.length - ROW_SC, plan.early)
                        buf[ROW_SC : ROW_SC + rest, :] = add(e0_ref, e1_ref, rest)
                    else:
                        rest = ROW_SG - base
                        buf[0:rest, :] = add(e0_ref, e1_ref, rest)
                        at = ROW_LAT - base
                        buf[at : at + ROW_FG - ROW_LAT, :] = add(l0_ref, l1_ref, ROW_FG - ROW_LAT)

            path = int_ref[1]
            base = jnp.where(path == 0, plan.base[0], plan.base[1])

            def stretch(place):
                j = 0
                for step in range(plan.bits):
                    bit = (place >> (plan.bits - 1 - step)) & 1
                    j = j + jnp.where(
                        path == 0, bit << plan.order[0][step], bit << plan.order[1][step]
                    )
                at = ((path * ndp + j) * plan.share) // (16 * LN) * 16 - base
                return buf[pl.ds(pl.multiple_of(at, 16), chunk), :].astype(BF16)

            def step(q, carry):
                bit = int_ref[5]
                keep_ref[q] = stretch(bit * half + q)
                send_ref[q] = stretch((1 - bit) * half + q)
                return carry

            loop(half, step, 0)

        return call(
            body,
            [((half, chunk, LN), BF16, "far")] * 2,
            [pltpu.VMEM((plan.length, LN), F32)],
            ints, *early, *conv, *late,
            **kw,
        )

    def halve(self, plan, ints, step, keep, came, **kw):
        half = keep.shape[0] // 2

        def body(int_ref, a_ref, b_ref, keep_ref, send_ref):
            bit = int_ref[5 + step]

            def one(q, carry):
                for out, at in ((keep_ref, bit * half + q), (send_ref, (1 - bit) * half + q)):
                    out[q] = (a_ref[at].astype(F32) + b_ref[at].astype(F32)).astype(BF16)
                return carry

            loop(half, one, 0)

        return call(
            body,
            [((half, plan.chunk, LN), BF16, "far")] * 2,
            [],
            ints, Far(keep), came,
            **kw,
        )

    def window(self, plan, ints, keep, came, small, small_other, vectors, tail, **kw):
        chunk, out_rows = plan.chunk, plan.out_rows
        extra = small.shape[0]
        pad = extra + 8

        def body(int_ref, keep_ref, came_ref, s0_ref, s1_ref, vec_ref, tail_ref, out_ref, a_ref, small_ref):
            r0 = int_ref[2]
            row = int_ref[3]
            lane = int_ref[4]
            a_ref[...] = jnp.zeros_like(a_ref)
            total = s0_ref[...].astype(F32) + s1_ref[...].astype(F32)
            small_ref[...] = jnp.where(int_ref[1] == 1, total, 0.0)
            for ref, start, n in (
                (vec_ref, ROW_SG, 2 * SLOW_VEC), (small_ref, ROW_FA, ROW_LAT - ROW_FA), (tail_ref, ROW_FG, 3)
            ):
                at = jnp.clip(start - r0, -n, chunk) + pad
                a_ref[pl.ds(at, n), :] += ref[0:n, :]
            a_ref[pad : pad + chunk, :] += keep_ref[0].astype(F32) + came_ref[0].astype(F32)
            one = a_ref[pl.ds(pad + row, out_rows), :]
            two = a_ref[pl.ds(pad + row + 1, out_rows), :]
            shift = (LN - lane) & (LN - 1)
            one = pltpu.roll(one, shift, 1)
            two = pltpu.roll(two, shift, 1)
            at = lax.broadcasted_iota(jnp.int32, (out_rows, LN), 1)
            out_ref[...] = jnp.where(at < LN - lane, one, two)

        return call(
            body,
            ((out_rows, LN), F32, "far"),
            [pltpu.VMEM((chunk + 2 * pad + 8, LN), F32), pltpu.VMEM((extra, LN), F32)],
            ints, keep, came, small, small_other, vectors, tail,
            **kw,
        )


class Plan:
    def __init__(self, ndp):
        n = 2 * ndp
        self.ndp = ndp
        self.share = VALUES // n
        self.first = [self.share * d // LN // 16 * 16 for d in range(n)]
        ends = [-(-self.share * (d + 1) // LN) for d in range(n)]
        self.chunk = -(-max(e - f for e, f in zip(ends, self.first)) // 16) * 16
        self.base = [self.first[0], self.first[ndp]]
        self.length = max(
            self.first[q * ndp + ndp - 1] + self.chunk - self.base[q] for q in range(2)
        )
        self.early = ROW_SG - self.base[1]
        self.out_rows = -(-self.share // LN)
        self.bits = ndp.bit_length() - 1
        one = list(range(self.bits))
        two = one if self.bits < 3 else [1, 2, 0] + one[3:]
        self.order = [one, two]

    def place(self, path, j):
        at = 0
        for b in self.order[path]:
            at = 2 * at + ((j >> b) & 1)
        return at

    def pairs(self, step):
        out = []
        for q in range(2):
            b = self.order[q][step]
            out += [(q * self.ndp + j, q * self.ndp + (j ^ (1 << b))) for j in range(self.ndp)]
        return out


def exchange(x):
    return lax.all_to_all(x, ("path", "dp"), 0, 0)


def swap(x):
    x = x.array if isinstance(x, Near) else x
    return lax.ppermute(x, "path", SWAP)


def local(
    acts, cotangent, clip_res, w_slow_a, w_slow_b, w_slow_c, w_slow_proj, slow_gain, slow_bias,
    w_fast_a, w_fast_b, w_fast_c, w_lateral, fast_gain, fast_bias,
):
    grid = acts.shape[2]
    px = grid * grid
    ndp = lax.axis_size("dp")
    net = Net(ndp, grid)
    plan = Plan(ndp)
    path, chip = lax.axis_index("path"), lax.axis_index("dp")
    core0 = path == 0
    level = clip_res[0]
    side = jnp.where(
        level == 1, grid * 5 // 8, jnp.where(level == 2, grid * 7 // 8, jnp.where(level == 3, grid, 0))
    )
    start = (path * ndp + chip) * plan.share
    r0 = start // LN // 16 * 16
    off = start - r0 * LN
    bits = [
        jnp.where(core0, chip >> plan.order[0][s], chip >> plan.order[1][s]) & 1 for s in range(plan.bits)
    ]
    ints = jnp.stack([side, path, r0, off // LN, off % LN] + bits).astype(jnp.int32)
    x = acts.reshape(px, 4096)
    cot = cotangent.reshape(px, 4096)
    sg, sb_ = slow_gain.reshape(SLOW_VEC, LN), slow_bias.reshape(SLOW_VEC, LN)

    def slow_par(a, b):
        return jnp.concatenate([sg[a:b], sb_[a:b]], axis=0)

    def fast_par(a, b):
        one = jnp.stack([fast_gain[a:b], fast_bias[a:b]])
        return jnp.tile(one, (1, LN // (b - a)))

    wlat = w_lateral.reshape(5 * CF, LAT)
    wa_lat = Far(w_slow_a, (LAT, CS_MID), (CS // LAT, 0))
    wp_lat = Far(w_slow_proj, (LAT, CS), (CS // LAT, 0))
    f1, f2, f3 = fast_par(0, 32), fast_par(32, 64), fast_par(64, 192)
    s1, s2, s3, s4 = slow_par(0, 2), slow_par(2, 4), slow_par(4, 12), slow_par(12, 20)
    wb3 = w_slow_b.reshape(3, 768, 256)
    wbt3 = w_slow_b.transpose(0, 2, 1).reshape(3, 768, 256)
    half = TF // 2

    x_other = swap(x)
    cot_other = swap(cot)

    fa_lo, fa_hi, band, pay = net.fast_first(ints, x, w_fast_a.transpose(0, 2, 1), us=3.5)
    (fb_w, fbt_w, fc_w), tok = net.fast_weights(
        w_fast_b, w_fast_b.transpose(0, 2, 1), w_fast_c, us=1.0, after=[pay], token=True
    )
    fa_other = swap(fa_lo)
    r1 = exchange(pay)
    fh1, fb, fc1, pay, r1 = net.conv_stage(
        ints, r1, r1, fa_hi, f1, fb_w, 1, half, fa_other, us=2.7, after=[tok]
    )
    (xs, xf, gs, gf), tok = net.halves(ints, x, x_other, cot, cot_other, us=2.5, after=[pay], token=True)
    r = exchange(pay)
    fh2, fc2, pay, fh2_edge = net.expand_stage(
        ints, r, r1, fb, f2, fc_w, 1, 1, half, True, us=2.6, after=[tok]
    )
    fh2_other = swap(fh2_edge)
    (pa, pp), tok = net.slow_start(xs, w_slow_a, w_slow_proj, us=3.5, after=[pay], token=True)
    r = exchange(pay)
    yf, lat, fc3, sa, pay = net.fast_finish(
        ints, r, r1, fh2, fh2_other, fc_w, xf, f3, wlat, pa, wa_lat, us=5.0, after=[tok]
    )

    (sp, sp_rows), tok = net.slow_join(ints, pp, lat, wp_lat, 8, us=3.0, after=[pay], token=True)
    r = exchange(pay)
    sh1, sb, sc1, pay = net.conv_stage(
        ints, r, r1, sa, s1, wb3, 2, TS // 2, more=sp_rows, us=3.0, after=[tok]
    )
    rp = exchange(pay)
    gp, tok = net.fast_slope(ints, fh2, fc_w, xf, f3, fc3, us=4.0, after=[pay], token=True)
    sh2, sc2, pay = net.expand_stage(ints, rp, r1, sb, s2, w_slow_c, 2, 8, TS // 2, us=3.0, after=[tok])
    r = exchange(pay)
    ys, ds, scc, scp, pay = net.slow_top(ints, r, rp, r1, sh2, w_slow_c, sp, gs, s3, s4, us=6.0)

    sent, tok = net.out_send(ints, ys, yf, us=2.0, after=[pay], token=True)
    r = exchange(pay)
    (dp, dc, dn, t3, pay), (sent,) = net.expand_back(
        ints, r1, r, ds, sh2, w_slow_c, scc, s3, sb, sc2, s2, 2, 8, TS // 2, (sp, scp, s4),
        us=6.0, after=[tok], through=[sent],
    )
    theirs = swap(sent)
    (early, early_out), tok = net.grads_early(
        plan, ints, xs, lat, dp, sh2, dc, us=6.0, after=[pay], token=True
    )
    r = exchange(pay)
    (db, dn, t2, pay), (early_out,) = net.conv_back(
        ints, r1, r, dn, sb, sc2, s2, wbt3, sa, sc1, s1, 2, TS // 2, us=3.0, after=[tok], through=[early_out]
    )
    early_in = swap(early_out)
    conv, tok = net.grads_conv(sh1, db, us=3.0, after=[pay], token=True)
    r = exchange(pay)
    (da, dl0, dl1, t1), (conv_out,) = net.slow_last(
        ints, r1, r, dn, sa, sc1, s1, dp, wa_lat, wp_lat, us=3.0, after=[tok], through=[conv]
    )
    dl_other = swap(dl0)
    (late, late_out), tok = net.grads_late(ints, xs, lat, da, yf, dl0, dl1, us=4.0, token=True)

    (fds, pay), (conv_out, late_out) = net.fast_top(
        ints, dl0, dl1, dl_other, wlat, gf, gp, fh2, fc_w, fc3, us=4.0, through=[conv_out, late_out]
    )
    conv_in = swap(conv_out)
    late_in = swap(late_out)
    fds_lo = swap(fds)
    (keep, there), tok = net.windows(
        plan, ints, (Far(early), early_in), (Far(conv_out), conv_in), (Far(late), late_in),
        us=6.0, after=[pay], token=True,
    )
    r = exchange(pay)
    (fdc, dn, u3, pay), (there,) = net.expand_back(
        ints, r1, r, fds, fh2, fc_w, fc3, f3, fb, fc2, f2, 1, 1, half,
        us=5.0, after=[tok], through=[there],
    )
    here = lax.ppermute(there, ("path", "dp"), plan.pairs(0))
    dxs, tok = net.slow_input_grad(da, dp, w_slow_a, w_slow_proj, us=4.0, after=[pay], token=True)
    r = exchange(pay)
    (fdb, dn, u2, pay), (dxs_out,) = net.conv_back(
        ints, r1, r, dn, fb, fc2, f2, fbt_w, fa_hi, fc1, f1, 1, half, fa_other,
        us=4.0, after=[tok], through=[dxs],
    )
    dn_lo = swap(dn)
    bc, tok = net.fast_grads_bc(fh1, fdb, fh2, fdc, us=4.0, after=[pay], token=True)
    got, tok = net.halve(plan, ints, 1, keep, here, us=3.0, after=[tok], token=True)
    r = exchange(pay)
    (fda, u1), (bc, *there) = net.fast_first_back(
        ints, r1, r, dn_lo, dn, Far(fa_lo), fa_hi, fc1, f1, us=2.5, after=[tok], through=[bc] + got[1:]
    )
    bc_other = swap(bc)
    small = net.fast_small(ints, fda, x, bc, bc_other, us=3.0)
    dxs_other = swap(dxs_out)
    keep = got[0]
    first = small
    for step in range(plan.bits):
        small_other = lax.ppermute(small, ("path", "dp"), plan.pairs(step))
        if step < plan.bits - 1:
            small = (small.astype(F32) + small_other.astype(F32)).astype(BF16)
    here = lax.ppermute(there[0], ("path", "dp"), plan.pairs(1))
    for step in range(2, plan.bits):
        keep, there = net.halve(plan, ints, step, keep, here, us=2.5, after=[first])
        here = lax.ppermute(there, ("path", "dp"), plan.pairs(step))
    dx = net.last(ints, fda, Far(fds_lo), fds, band, dxs_out, dxs_other, us=4.5, after=[first])

    out = net.out_join(ints, ys, yf, theirs, us=3.0, after=[first])

    vectors = jnp.concatenate([t1[2:4], t2[2:4], t3[8:24], t1[0:2], t2[0:2], t3[0:8], t3[0:8]], axis=0)
    tail = jnp.concatenate([u1[1, :32], u2[1, :32], u3[1], u1[0, :32], u2[0, :32], u3[0]]).reshape(3, LN)
    tail = jnp.pad(tail, ((0, 5), (0, 0)))
    flat = net.window(plan, ints, keep, here, small, small_other, vectors, tail).reshape(-1)[: plan.share]
    return (out.reshape(acts.shape), dx.reshape(acts.shape), flat)


def solution(mesh):
    data = P("path", "dp", None, None, None)
    in_specs = (data, data, P("dp")) + (P(),) * 12
    out_specs = (data, data, P(("path", "dp")))
    return jax.shard_map(local, mesh=mesh, in_specs=in_specs, out_specs=out_specs, check_vma=False)
```

```python
import functools

import jax
import jax.numpy as jnp
from jax import lax
from jax.experimental import pallas as pl
from jax.experimental.pallas import tpu as pltpu
from jax.sharding import PartitionSpec as P

TS = 4
ALPHA = 8
CS = 1024
CS_MID = 256
CF = 128
CF_MID = 32
LAT = 256
TF = 32
LN = 128
EPS = 1e-05
GELU_C = 0.7978845608028654
GELU_A = 0.044715

F32 = jnp.float32
BF16 = jnp.bfloat16
SWAP = [(0, 1), (1, 0)]

ROW_SA = 0
ROW_SB = ROW_SA + (CS + LAT) * CS_MID // LN
ROW_SC = ROW_SB + 9 * CS_MID * CS_MID // LN
ROW_SP = ROW_SC + CS_MID * CS // LN
ROW_SG = ROW_SP + (CS + LAT) * CS // LN
SLOW_VEC = (2 * CS_MID + 2 * CS) // LN
ROW_FA = ROW_SG + 2 * SLOW_VEC
ROW_LAT = ROW_FA + (3 * CF * CF_MID + 9 * CF_MID * CF_MID + CF_MID * CF) // LN
ROW_FG = ROW_LAT + 5 * CF * LAT // LN
VALUES = 2685312


def dot(a, b):
    return lax.dot_general(a, b, (((1,), (0,)), ((), ())), preferred_element_type=F32)


def dot_t(a, b):
    return lax.dot_general(a, b, (((1,), (1,)), ((), ())), preferred_element_type=F32)


class Near:
    def __init__(self, array):
        self.array = array


class Far:
    def __init__(self, array, block=None, index=None):
        self.array = pltpu.with_memory_space_constraint(array, pltpu.HBM)
        self.block, self.index = block, index


class Manual(Far):
    def __init__(self, array, pinned=True):
        if isinstance(array, Near):
            self.array = pltpu.with_memory_space_constraint(array.array, pltpu.HBM)
        else:
            self.array = pltpu.with_memory_space_constraint(array, pltpu.HBM) if pinned else array
        self.block = None


def dot_l(a, b):
    return lax.dot_general(a, b, (((0,), (0,)), ((), ())), preferred_element_type=F32)


def call(body, outs, scratch, *args, smem=1, limit=20, us=2.0, after=(), token=False, through=()):
    one = not isinstance(outs, list)
    shapes, out_specs, specs, operands = [], [], [], []
    vmem, anywhere = pl.BlockSpec(memory_space=pltpu.VMEM), pl.BlockSpec(memory_space=pl.ANY)
    for out in [outs] if one else outs:
        place = out[2] if len(out) > 2 else "near"
        shapes.append(pltpu.HBM(out[0], out[1]))
        out_specs.append(anywhere if place == "manual" else vmem)
    if token:
        shapes.append(pltpu.HBM((8, LN), F32))
        out_specs.append(anywhere)
    for k, a in enumerate(args):
        if k < smem:
            specs.append(pl.BlockSpec(memory_space=pltpu.SMEM))
        elif isinstance(a, Manual):
            specs.append(anywhere)
        elif isinstance(a, Far) and a.block is not None:
            index = a.index
            specs.append(pl.BlockSpec(a.block, lambda i, index=index: index))
        else:
            specs.append(vmem)
        if isinstance(a, Near):
            a = pltpu.with_memory_space_constraint(a.array, pltpu.HBM)
        operands.append(a.array if isinstance(a, Far) else a)
    for a in after:
        specs.append(anywhere)
        operands.append(pltpu.with_memory_space_constraint(a, pltpu.HBM))
    aliases = {}
    for a in through:
        aliases[len(operands)] = len(shapes)
        specs.append(anywhere)
        operands.append(pltpu.with_memory_space_constraint(a, pltpu.HBM))
        shapes.append(pltpu.HBM(a.shape, a.dtype))
        out_specs.append(anywhere)
    n_in, n_out = len(args), len(shapes) - token - len(through)
    cut = any(isinstance(a, Far) and a.block is not None for a in args)

    def wrapped(*refs):
        rest = refs[n_in + len(after) + len(through) :]
        body(*refs[:n_in], *rest[:n_out], *rest[n_out + token + len(through) :])

    res = pl.pallas_call(
        wrapped,
        out_shape=shapes,
        grid=(1,) if cut else (),
        in_specs=specs,
        out_specs=out_specs,
        scratch_shapes=scratch,
        input_output_aliases=aliases,
        cost_estimate=pl.CostEstimate(flops=int(us * 1e9), bytes_accessed=0, transcendentals=0),
        compiler_params=pltpu.CompilerParams(vmem_limit_bytes=limit * 1024 * 1024),
    )(*operands)
    got = [
        Near(r) if len(out) == 2 else r for r, out in zip(res, [outs] if one else outs)
    ]
    got = got[0] if one else got
    if through:
        return got, list(res[n_out + token :])
    return (got, res[n_out]) if token else got


def lanes(index):
    if isinstance(index, int):
        return slice(index * LN, (index + 1) * LN)
    return pl.ds(pl.multiple_of(index * LN, LN), LN)


def region(side, px, grid):
    bits = grid.bit_length() - 1
    r = lax.broadcasted_iota(jnp.int32, (px, LN), 0)
    inside = jnp.logical_and((r >> bits) < side, (r & (grid - 1)) < side)
    return jnp.where(inside, 1.0, 0.0).astype(F32)


def rows8(x):
    return x.reshape(x.shape[0] // 8, 8, LN).sum(axis=0)


def total(acc, fold):
    if fold:
        acc = acc + pltpu.roll(acc, 32, 1)
        acc = acc + pltpu.roll(acc, 64, 1)
    return acc.sum(axis=0, keepdims=True)


def gelu(v, half_mask):
    t = jnp.tanh(v * (GELU_C + (GELU_C * GELU_A) * (v * v)))
    return v * (half_mask + half_mask * t)


def gelu_both(v, half_mask):
    w = GELU_C + (GELU_C * GELU_A) * (v * v)
    t = jnp.tanh(v * w)
    q = half_mask + half_mask * t
    return v * q, q * (1.0 + (v - v * t) * (3.0 * w - 2.0 * GELU_C))


def loop(n, body, init, unroll=False):
    if unroll:
        for i in range(n):
            init = body(i, init)
        return init
    return lax.fori_loop(0, n, body, init)


def moments(ref, out, row, blocks, params, fold, mask, count):
    inv = 1.0 / jnp.maximum(count, 1.0)
    for p in range(params):
        n = blocks // params

        def first(i, acc):
            return acc + rows8(ref[:, lanes(p + i * params)] * mask)

        zero = jnp.zeros((8, LN), F32)
        s = total(loop(n, first, zero, n <= 4), fold)
        mean = s * inv

        def second(i, acc):
            d = (ref[:, lanes(p + i * params)] - mean) * mask
            return acc + rows8(d * d)

        m2 = total(loop(n, second, zero, n <= 4), fold)
        out[row + p : row + p + 1, :] = s
        out[row + params + p : row + params + p + 1, :] = m2


def send(pay_ref, rows_ref):
    value = rows_ref[...].astype(pay_ref.dtype)
    for d in range(pay_ref.shape[0]):
        pay_ref[d] = value


def split(v):
    high = v.astype(BF16).astype(F32)
    return high, v - high


def encode(code_ref, rows_ref, narrow, wide):
    at = 0
    if narrow:
        high, low = split(rows_ref[0:narrow, :])
        code_ref[0:narrow, :] = high
        code_ref[narrow : 2 * narrow, :] = low
        at = 2 * narrow
    if wide:
        high, low = split(rows_ref[narrow : narrow + wide, :])
        code_ref[at : at + wide, :] = high
        code_ref[at + wide : at + 2 * wide, :] = low
        code_ref[at + 2 * wide : at + 3 * wide, :] = rows_ref[narrow + wide : narrow + 2 * wide, :]


def combine(recv, row, params, n, cst_ref):
    combine_sums(recv[:, row : row + params, :], recv[:, row + params : row + 2 * params, :], n, params, cst_ref)


def combine_coded(recv, row, params, n, cst_ref, narrow=False):
    v = recv.astype(F32)
    if narrow:
        v = v[:, 0 : 2 * params] + v[:, 2 * params : 4 * params]
        combine_sums(v[:, 0:params], v[:, params:], n, params, cst_ref)
        return
    s = v[:, row : row + params] + v[:, row + params : row + 2 * params]
    combine_sums(s, v[:, row + 2 * params : row + 3 * params], n, params, cst_ref)


def combine_sums(s, m2, n, params, cst_ref):
    k = n.sum(axis=0)
    mean = s.sum(axis=0) / k
    off = s / jnp.maximum(n, 1.0) - mean[None]
    cst_ref[0:params, :] = mean
    cst_ref[params : 2 * params, :] = lax.rsqrt((m2 + n * off * off).sum(axis=0) / k + EPS)


def pick_half(int_ref, other_ref, ref, b):
    if other_ref is None:
        return ref[:, lanes(b)]
    return jnp.where(int_ref[1] == 0, other_ref[:, lanes(b)], ref[:, lanes(b)])


def fold32(v):
    v = v[:, 0:LN] + v[:, LN:256]
    v = v + pltpu.roll(v, 32, 1)
    return v + pltpu.roll(v, 64, 1)


def tiled_rows(scratch, tiled):
    c = tiled.shape[0]
    scratch[0:c, :] = tiled
    group = lax.broadcasted_iota(jnp.int32, (c // 4, LN), 1) >> 5
    out = jnp.zeros((c // 4, LN), F32)
    for q in range(4):
        out = jnp.where(group == q, scratch[pl.ds(q, c // 4, stride=4), :], out)
    return out


def pack3(pad, b, mid, left, right, px, grid):
    g, half = b // 2, b % 2
    for slot, value in enumerate((left, mid, right)):
        at = g * 768 + slot * 256 + half * 128
        pad[grid : grid + px, at : at + LN] = value.astype(BF16)


def neighbours(h, px, grid):
    col = lax.broadcasted_iota(jnp.int32, (px, LN), 0) & (grid - 1)
    before = jnp.where(col == 0, 0.0, pltpu.roll(h, 1, 0))
    after = jnp.where(col == grid - 1, 0.0, pltpu.roll(h, px - 1, 0))
    return before, after


def clear_edges(pad, px, grid):
    zero = jnp.zeros((grid, pad.shape[1]), BF16)
    pad[0:grid, :] = zero
    pad[grid + px : grid + px + grid, :] = zero


def put_count(rows_ref, row, count):
    rows_ref[row : row + 1, :] = jnp.zeros((1, LN), F32) + count


def side_sq(side, frames):
    s = side.astype(F32)
    return s * s * frames


class Net:
    def __init__(self, ndp, grid):
        self.ndp = ndp
        self.n = 2 * ndp
        self.grid = grid
        self.px = grid * grid

    def fast_first(self, ints, xf, wa, **kw):
        px, grid, n = self.px, self.grid, self.n

        def body(int_ref, xf_ref, wa_ref, lo_ref, hi_ref, band_ref, pay_ref, row_ref, fa_ref):
            side = int_ref[0]
            row_ref[...] = jnp.zeros_like(row_ref)

            @pl.when(int_ref[1] == 1)
            def _():
                pick = jnp.where(
                    (lax.broadcasted_iota(jnp.int32, (CF_MID, 256), 1) & (CF_MID - 1))
                    == lax.broadcasted_iota(jnp.int32, (CF_MID, 256), 0),
                    1.0,
                    0.0,
                ).astype(BF16)
                wide = [dot_l(wa_ref[k], pick) for k in range(3)]
                group = lax.broadcasted_iota(jnp.int32, (CF, 256), 1) >> 5
                for j in range(10):
                    acc = jnp.zeros((CF, 256), F32)
                    for k in range(3):
                        if 0 <= j - k < 8:
                            acc = jnp.where(group == j - k, wide[k], acc)
                    band_ref[j * CF : (j + 1) * CF, :] = acc.astype(BF16)
                for g in range(4):
                    lo, hi = max(8 * g - 1, 0), min(8 * g + 9, TF)
                    k0 = lo - (8 * g - 1)
                    out = dot(
                        xf_ref[:, lo * CF : hi * CF], band_ref[k0 * CF : (k0 + hi - lo) * CF, :]
                    )
                    fa_ref[:, g * 256 : (g + 1) * 256] = out
                    target = lo_ref if g < 2 else hi_ref
                    target[:, (g % 2) * 256 : (g % 2 + 1) * 256] = out
                moments(fa_ref, row_ref, 0, 8, 1, True, region(side, px, grid), side_sq(side, TF))

            put_count(row_ref, 2, side_sq(side, 1))
            send(pay_ref, row_ref)

        return call(
            body,
            [((px, 512), F32, "far"), ((px, 512), F32), ((10 * CF, 256), BF16), ((n, 4, LN), F32, "far")],
            [pltpu.VMEM((4, LN), F32), pltpu.VMEM((px, 1024), F32)],
            ints, xf, wa,
            **kw,
        )

    def fast_weights(self, wb, wbt, wc, **kw):
        def body(wb_ref, wbt_ref, wc_ref, b_ref, bt_ref, c_ref):
            pick = jnp.where(
                (lax.broadcasted_iota(jnp.int32, (CF_MID, 256), 1) & (CF_MID - 1))
                == lax.broadcasted_iota(jnp.int32, (CF_MID, 256), 0),
                1.0,
                0.0,
            ).astype(BF16)
            same = (lax.broadcasted_iota(jnp.int32, (256, 256), 0) >> 5) == (
                lax.broadcasted_iota(jnp.int32, (256, 256), 1) >> 5
            )
            for source, target in ((wb_ref, b_ref), (wbt_ref, bt_ref)):
                for tap in range(9):
                    tiled = jnp.concatenate([dot(source[tap], pick)] * 8, axis=0)
                    target[tap // 3, (tap % 3) * 256 : (tap % 3 + 1) * 256, :] = jnp.where(
                        same, tiled, 0.0
                    ).astype(BF16)
            c_ref[...] = jnp.zeros_like(c_ref)
            for i in range(8):
                c_ref[i * CF_MID : (i + 1) * CF_MID, i * CF : (i + 1) * CF] = wc_ref[...]

        return call(
            body,
            [((3, 768, 256), BF16), ((3, 768, 256), BF16), ((256, 1024), BF16)],
            [],
            wb, wbt, wc, smem=0,
            **kw,
        )

    def conv_stage(self, ints, recv, counts, x, par, w, params, frames, other=None, more=None, **kw):
        px, grid, n, ndp = self.px, self.grid, self.n, self.ndp
        fold = params == 1
        two = other is not None
        rows = 4 + (0 if more is None else more.array.shape[0])
        coded = 8 + 3 * (rows - 4) // 2

        def body(int_ref, recv_ref, n_ref, x_ref, par_ref, w_ref, *refs):
            o_ref = None
            if two:
                o_ref, refs = refs[0], refs[1:]
            if more is not None:
                m_ref, refs = refs[0], refs[1:]
            h_ref, y_ref, cst_ref, pay_ref = refs[:4]
            row_ref, pad = refs[4 + two : 6 + two]
            code_ref = refs[-1]
            if two:
                refs[4][...] = recv_ref[...]
            side = int_ref[0]
            mask = region(side, px, grid)
            half_mask = 0.5 * mask
            if two:
                stats, count = recv_ref[ndp:], n_ref[ndp:, 2:3, :] * float(TF)
            else:
                stats, count = recv_ref[...], n_ref[:, 2:3, :] * float(frames)
            combine(stats, 0, params, count, cst_ref)
            mean, rs = cst_ref[0:params, :], cst_ref[params : 2 * params, :]
            scale = par_ref[0:params, :] * rs
            shift = par_ref[params : 2 * params, :] - mean * scale
            clear_edges(pad, px, grid)
            for b in range(4):
                p = b % params
                v = pick_half(int_ref, o_ref, x_ref, b) * scale[p : p + 1] + shift[p : p + 1]
                h = gelu(v, half_mask)
                h_ref[:, lanes(b)] = h.astype(BF16)
                before, after = neighbours(h, px, grid)
                pack3(pad, b, h, before, after, px, grid)
            for g in range(2):
                acc = None
                for i in range(3):
                    part = dot(pad[grid * i : grid * i + px, g * 768 : (g + 1) * 768], w_ref[i])
                    acc = part if acc is None else acc + part
                y_ref[:, g * 256 : (g + 1) * 256] = acc
            moments(y_ref, row_ref, 0, 4, params, fold, mask, side_sq(side, frames))
            if more is None:
                send(pay_ref, row_ref)
            else:
                row_ref[4:rows, :] = m_ref[...]
                encode(code_ref, row_ref, 4, rows // 2 - 2)
                send(pay_ref, code_ref)

        extra = [other] if two else []
        extra += [] if more is None else [more]
        return call(
            body,
            [((px, 512), BF16), ((px, 512), F32), ((8, LN), F32), ((n, rows, LN), F32, "far") if more is None else ((n, coded, LN), BF16, "far")]
            + ([((n, 4, LN), F32)] if two else []),
            [pltpu.VMEM((rows, LN), F32), pltpu.VMEM((px + 2 * grid, 2 * 768), BF16)]
            + ([] if more is None else [pltpu.VMEM((coded, LN), F32)]),
            ints, recv, counts, x, par, w, *extra,
            **kw,
        )

    def expand_stage(self, ints, recv, counts, y, par, w, params, wide, frames, edge=False, **kw):
        px, grid, n = self.px, self.grid, self.n
        rows = max(2 * wide, 4)
        code = wide > 1
        coded = 3 * wide

        def body(int_ref, recv_ref, n_ref, y_ref, par_ref, w_ref, h_ref, cst_ref, pay_ref, *refs):
            row_ref, c_ref = refs[edge : edge + 2]
            code_ref = refs[-1]
            side = int_ref[0]
            mask = region(side, px, grid)
            half_mask = 0.5 * mask
            count = n_ref[:, 2:3, :] * float(frames)
            if code:
                combine_coded(recv_ref[...], 0, params, count, cst_ref, True)
            else:
                combine(recv_ref[...], 0, params, count, cst_ref)
            mean, rs = cst_ref[0:params, :], cst_ref[params : 2 * params, :]
            scale = par_ref[0:params, :] * rs
            shift = par_ref[params : 2 * params, :] - mean * scale
            for b in range(4):
                p = b % params
                v = y_ref[:, lanes(b)] * scale[p : p + 1] + shift[p : p + 1]
                h_ref[:, lanes(b)] = gelu(v, half_mask).astype(BF16)
            if edge:
                refs[0][...] = h_ref[:, lanes(3)]
            for g in range(2):
                c_ref[:, g * 1024 : (g + 1) * 1024] = dot(h_ref[:, g * 256 : (g + 1) * 256], w_ref[...])
            moments(c_ref, row_ref, 0, 16, wide, False, mask, side_sq(side, frames))
            if code:
                encode(code_ref, row_ref, 0, wide)
            send(pay_ref, code_ref if code else row_ref)

        return call(
            body,
            [((px, 512), BF16), ((8, LN), F32), ((n, coded, LN), BF16, "far") if code else ((n, rows, LN), F32, "far")]
            + ([((px, LN), BF16, "far")] if edge else []),
            [pltpu.VMEM((rows, LN), F32), pltpu.VMEM((px, 2048), F32)]
            + ([pltpu.VMEM((coded, LN), F32)] if code else []),
            ints, recv, counts, y, par, w,
            **kw,
        )

    def fast_finish(self, ints, recv, counts, h2, h2_other, w, xf, par, wlat, pa, wa, **kw):
        px, grid, n = self.px, self.grid, self.n

        def body(
            int_ref, recv_ref, n_ref, h_ref, ho_ref, w_ref, xf_ref, par_ref, wl_ref, pa_ref, wa_ref,
            y_ref, lat_ref, cst_ref, sa_ref, pay_ref, c_ref, row_ref,
        ):
            half_mask = 0.5 * region(int_ref[0], px, grid)
            combine(recv_ref[...], 0, 1, n_ref[:, 2:3, :] * float(TF // 2), cst_ref)
            scale = par_ref[0:1, :] * cst_ref[1:2, :]
            shift = par_ref[1:2, :] - cst_ref[0:1, :] * scale
            c_ref[:, 0:256] = dot(ho_ref[...], w_ref[0:LN, 256:512])
            edge = half_mask * int_ref[1].astype(F32)
            for f in range(2):
                v = c_ref[:, lanes(f)] * scale + shift + xf_ref[:, lanes(f)].astype(F32)
                y_ref[:, lanes(f)] = jnp.where(int_ref[1] == 1, gelu(v, edge), 0.0).astype(BF16)
            for g in range(2):
                c_ref[...] = dot(h_ref[:, g * 256 : (g + 1) * 256], w_ref[...])

                def step(i, carry):
                    f = 2 + g * 8 + i
                    v = c_ref[:, lanes(i)] * scale + shift + xf_ref[:, lanes(f)].astype(F32)
                    y_ref[:, lanes(f)] = gelu(v, half_mask).astype(BF16)
                    return carry

                loop(8, step, 0)
            for t in range(2):
                at = ALPHA * t * CF
                lat_ref[:, t * LAT : (t + 1) * LAT] = dot(y_ref[:, at : at + 5 * CF], wl_ref[...]).astype(BF16)
                a = slice(t * CS_MID, (t + 1) * CS_MID)
                sa_ref[:, a] = pa_ref[:, a] + dot(lat_ref[:, t * LAT : (t + 1) * LAT], wa_ref[...])
            side = int_ref[0]
            moments(sa_ref, row_ref, 0, 4, 2, False, region(side, px, grid), side_sq(side, TS // 2))
            send(pay_ref, row_ref)

        return call(
            body,
            [((px, 18 * CF), BF16), ((px, 512), BF16), ((8, LN), F32), ((px, 512), F32), ((n, 4, LN), F32, "far")],
            [pltpu.VMEM((px, 1024), F32), pltpu.VMEM((4, LN), F32)],
            ints, recv, counts, h2, h2_other, w, xf, par, wlat, pa, wa,
            **kw,
        )

    def fast_slope(self, ints, h2, w, xf, par, cst, **kw):
        px, grid = self.px, self.grid

        def body(int_ref, h_ref, w_ref, xf_ref, par_ref, cst_ref, gp_ref, c_ref):
            half_mask = 0.5 * region(int_ref[0], px, grid)
            scale = par_ref[0:1, :] * cst_ref[1:2, :]
            shift = par_ref[1:2, :] - cst_ref[0:1, :] * scale
            for g in range(2):
                c_ref[...] = dot(h_ref[:, g * 256 : (g + 1) * 256], w_ref[...])

                def step(i, carry):
                    f = g * 8 + i
                    v = c_ref[:, lanes(i)] * scale + shift + xf_ref[:, lanes(f + 2)].astype(F32)
                    gp_ref[:, lanes(f)] = gelu_both(v, half_mask)[1]
                    return carry

                loop(8, step, 0)

        return call(body, ((px, 2048), F32), [pltpu.VMEM((px, 1024), F32)], ints, h2, w, xf, par, cst, **kw)

    def slow_start(self, xs, wa, wp, **kw):
        px = self.px

        def body(x_ref, wa_ref, wp_ref, a_ref, p_ref):
            for t in range(2):
                x = x_ref[:, t * CS : (t + 1) * CS]
                a_ref[:, t * CS_MID : (t + 1) * CS_MID] = dot(x, wa_ref[0:CS, :])
                p_ref[:, t * CS : (t + 1) * CS] = dot(x, wp_ref[0:CS, :])

        return call(body, [((px, 512), F32), ((px, 2048), F32)], [], xs, wa, wp, smem=0, **kw)

    def slow_join(self, ints, part, lat, w, params, **kw):
        px, grid = self.px, self.grid
        width = params * LN

        def body(int_ref, part_ref, lat_ref, w_ref, out_ref, row_ref):
            side = int_ref[0]
            for t in range(2):
                at = slice(t * width, (t + 1) * width)
                out_ref[:, at] = part_ref[:, at] + dot(lat_ref[:, t * LAT : (t + 1) * LAT], w_ref[...])
            moments(
                out_ref, row_ref, 0, 2 * params, params, False, region(side, px, grid), side_sq(side, TS // 2)
            )

        return call(
            body, [((px, 2 * width), F32), ((2 * params, LN), F32)], [], ints, part, lat, w, **kw
        )

    def slow_top(self, ints, recv3, recvp, counts, h2, w, sp, gs, parc, parp, **kw):
        px, grid, n = self.px, self.grid, self.n

        def body(
            int_ref, r3_ref, rp_ref, n_ref, h_ref, w_ref, sp_ref, gs_ref, pc_ref, pp_ref,
            ys_ref, ds_ref, cc_ref, cp_ref, pay_ref, row_ref, c_ref, acc_ref, k_ref,
        ):
            half_mask = 0.5 * region(int_ref[0], px, grid)
            count = n_ref[:, 2:3, :] * float(TS // 2)
            combine_coded(r3_ref[...], 0, 8, count, cc_ref)
            combine_coded(rp_ref[...], 8, 8, count, cp_ref)
            k_ref[0:8, :] = pc_ref[0:8, :] * cc_ref[8:16, :]
            k_ref[8:16, :] = pp_ref[0:8, :] * cp_ref[8:16, :]
            k_ref[16:24, :] = pc_ref[8:16, :] + pp_ref[8:16, :]
            acc_ref[...] = jnp.zeros_like(acc_ref)
            for t in range(2):
                c_ref[...] = dot(h_ref[:, t * 256 : (t + 1) * 256], w_ref[...])

                def step(b, carry):
                    at = lanes(t * 8 + b)
                    one = pl.ds(b, 1)
                    xc = c_ref[:, lanes(b)] - cc_ref[one, :]
                    xp = sp_ref[:, at] - cp_ref[one, :]
                    v = xc * k_ref[one, :] + (xp * k_ref[pl.ds(b + 8, 1), :] + k_ref[pl.ds(b + 16, 1), :])
                    y, slope = gelu_both(v, half_mask)
                    ys_ref[:, at] = y.astype(BF16)
                    d = gs_ref[:, at].astype(F32) * slope
                    ds_ref[:, at] = d
                    acc_ref[b] += rows8(d)
                    acc_ref[8 + b] += rows8(d * xc)
                    acc_ref[16 + b] += rows8(d * xp)
                    return carry

                loop(8, step, 0)
            row_ref[...] = acc_ref[...].sum(axis=1)
            row_ref[8:16, :] = row_ref[8:16, :] * cc_ref[8:16, :]
            row_ref[16:24, :] = row_ref[16:24, :] * cp_ref[8:16, :]
            send(pay_ref, row_ref)

        return call(
            body,
            [
                ((px, 2048), BF16), ((px, 2048), F32), ((16, LN), F32), ((16, LN), F32),
                ((n, 24, LN), BF16, "far"),
            ],
            [
                pltpu.VMEM((24, LN), F32), pltpu.VMEM((px, 1024), F32),
                pltpu.VMEM((24, 8, LN), F32), pltpu.VMEM((24, LN), F32),
            ],
            ints, recv3, recvp, counts, h2, w, sp, gs, parc, parp,
            **kw,
        )

    def fast_top(self, ints, dl0, dl1, dl_other, wlat, gf, gp, h2, w, cst, **kw):
        px, n = self.px, self.n

        def body(
            int_ref, d0_ref, d1_ref, do_ref, wl_ref, gf_ref, gp_ref, h_ref, w_ref, cst_ref,
            ds_ref, pay_ref, row_ref, lt_ref, c_ref, acc_ref,
        ):
            first = (1 - int_ref[1]).astype(F32)
            lt_ref[:, 0 : 3 * CF] = dot_t(d0_ref[...], wl_ref[2 * CF :, :])
            lt_ref[:, 3 * CF : 8 * CF] = dot_t(d1_ref[...], wl_ref[...])
            edge = dot_t(do_ref[...], wl_ref[0 : 2 * CF, :])
            lt_ref[:, 8 * CF : 10 * CF] = jnp.where(int_ref[1] == 0, edge, 0.0)
            acc_ref[...] = jnp.zeros_like(acc_ref)
            mean, rs = cst_ref[0:1, :], cst_ref[1:2, :]
            where = {0: 0, 1: 1, 2: 2, 6: 3, 7: 4, 8: 5, 9: 6, 10: 7, 14: 8, 15: 9}
            for g in range(2):
                c_ref[...] = dot(h_ref[:, g * 256 : (g + 1) * 256], w_ref[...])
                for i in range(8):
                    f = g * 8 + i
                    d = gf_ref[:, lanes(f)].astype(F32)
                    if f in where:
                        d = d + lt_ref[:, lanes(where[f])]
                    d = d * gp_ref[:, lanes(f)]
                    ds_ref[:, lanes(f)] = d
                    acc_ref[0] += rows8(d)
                    acc_ref[1] += rows8(d * (c_ref[:, lanes(i)] - mean))
            row_ref[...] = jnp.zeros_like(row_ref)
            row_ref[0:1, :] = acc_ref[0].sum(axis=0, keepdims=True)
            row_ref[1:2, :] = acc_ref[1].sum(axis=0, keepdims=True) * rs
            send(pay_ref, row_ref)

        return call(
            body,
            [((px, 2048), F32), ((n, 4, LN), F32, "far")],
            [
                pltpu.VMEM((4, LN), F32), pltpu.VMEM((px, 10 * CF), F32),
                pltpu.VMEM((px, 1024), F32), pltpu.VMEM((2, 8, LN), F32),
            ],
            ints, dl0, dl1, dl_other, wlat, gf, gp, h2, w, cst,
            **kw,
        )

    def expand_back(self, ints, counts, recv, ds, h2, w, cstw, parw, y, cst, par, params, wide, frames, shortcut=None, **kw):
        px, grid, n = self.px, self.grid, self.n
        fold = params == 1
        both = shortcut is not None
        srows = 3 * wide if both else 4

        def body(*refs):
            int_ref, n_ref, recv_ref, ds_ref, h_ref, w_ref, cw_ref, pw_ref, y_ref, cs_ref, par_ref = refs[:11]
            refs = refs[11:]
            if both:
                sp_ref, cp_ref, pp_ref, dp_ref = refs[:4]
                refs = refs[4:]
            dc_ref, dn_ref, sum_ref, pay_ref, row_ref, c_ref, k3_ref = refs
            mask = region(int_ref[0], px, grid)
            half_mask = 0.5 * mask
            inv_k = 1.0 / (n_ref[:, 2:3, :].sum(axis=0) * float(frames))
            sums = recv_ref[...].astype(F32).sum(axis=0)
            sum_ref[...] = sums
            a = pw_ref[0:wide, :] * cw_ref[wide : 2 * wide, :]
            k3_ref[0:wide, :] = a
            k3_ref[wide : 2 * wide, :] = a * inv_k * sums[0:wide]
            k3_ref[2 * wide : 3 * wide, :] = a * inv_k * cw_ref[wide : 2 * wide, :] * sums[wide : 2 * wide]
            if both:
                a = pp_ref[0:wide, :] * cp_ref[wide : 2 * wide, :]
                k3_ref[3 * wide : 4 * wide, :] = a
                k3_ref[4 * wide : 5 * wide, :] = a * inv_k * sums[0:wide]
                k3_ref[5 * wide : 6 * wide, :] = (
                    a * inv_k * cp_ref[wide : 2 * wide, :] * sums[2 * wide : 3 * wide]
                )
            mean, rs = cs_ref[0:params, :], cs_ref[params : 2 * params, :]
            accs = [[jnp.zeros((8, LN), F32) for _ in range(params)] for _ in range(2)]
            for g in range(2):
                c_ref[...] = dot(h_ref[:, g * 256 : (g + 1) * 256], w_ref[...])

                def step(b, carry):
                    at = lanes(g * 8 + b)
                    p = b if wide == 8 else 0
                    d = ds_ref[:, at]
                    e = (c_ref[:, lanes(b)] - cw_ref[pl.ds(p, 1), :]) * k3_ref[pl.ds(2 * wide + p, 1), :]
                    e = d * k3_ref[pl.ds(p, 1), :] - k3_ref[pl.ds(wide + p, 1), :] - e
                    dc_ref[:, at] = (e * mask).astype(BF16)
                    if both:
                        e = (sp_ref[:, at] - cp_ref[pl.ds(p, 1), :]) * k3_ref[pl.ds(5 * wide + p, 1), :]
                        e = d * k3_ref[pl.ds(3 * wide + p, 1), :] - k3_ref[pl.ds(4 * wide + p, 1), :] - e
                        dp_ref[:, at] = (e * mask).astype(BF16)
                    return carry

                loop(8, step, 0)
                dh = dot_t(dc_ref[:, g * 1024 : (g + 1) * 1024], w_ref[...])
                for half in range(2):
                    b = g * 2 + half
                    p = b % params
                    xh = (y_ref[:, lanes(b)] - mean[p : p + 1]) * rs[p : p + 1]
                    v = xh * par_ref[p : p + 1, :] + par_ref[params + p : params + p + 1, :]
                    d = dh[:, half * LN : (half + 1) * LN] * gelu_both(v, half_mask)[1]
                    dn_ref[:, lanes(b)] = d
                    accs[0][p] = accs[0][p] + rows8(d)
                    accs[1][p] = accs[1][p] + rows8(d * xh)
            row_ref[...] = jnp.zeros_like(row_ref)
            for q in range(2):
                for p in range(params):
                    row_ref[q * params + p : q * params + p + 1, :] = total(accs[q][p], fold)
            send(pay_ref, row_ref)

        outs = [((px, 2048), BF16)] if both else []
        outs += [((px, 2048), BF16), ((px, 512), F32), ((srows, LN), F32, "far"), ((n, 4, LN), F32, "far")]
        extra = list(shortcut) if both else []
        return call(
            body,
            outs,
            [pltpu.VMEM((4, LN), F32), pltpu.VMEM((px, 1024), F32), pltpu.VMEM((max(6 * wide, 8), LN), F32)],
            ints, counts, recv, ds, h2, w, cstw, parw, y, cst, par, *extra,
            **kw,
        )

    def conv_back(self, ints, counts, recv, dn, y, cst2, par2, wt, x, cst1, par1, params, frames, other=None, **kw):
        px, grid, n = self.px, self.grid, self.n
        fold = params == 1
        two = other is not None

        def body(int_ref, n_ref, recv_ref, dn_ref, y_ref, c2_ref, p2_ref, w_ref, x_ref, c1_ref, p1_ref, *refs):
            o_ref = None
            if two:
                o_ref, refs = refs[0], refs[1:]
            db_ref, dn1_ref, sum_ref, pay_ref, row_ref, pad = refs
            mask = region(int_ref[0], px, grid)
            half_mask = 0.5 * mask
            inv_k = 1.0 / (n_ref[:, 2:3, :].sum(axis=0) * float(frames))
            sums = recv_ref[...].astype(F32).sum(axis=0)
            sum_ref[...] = sums
            mean2, rs2 = c2_ref[0:params, :], c2_ref[params : 2 * params, :]
            a = p2_ref[0:params, :] * rs2
            b0 = a * inv_k * sums[0:params]
            c0 = a * inv_k * rs2 * sums[params : 2 * params]
            clear_edges(pad, px, grid)
            for b in range(4):
                p = b % params
                e = (y_ref[:, lanes(b)] - mean2[p : p + 1]) * c0[p : p + 1]
                e = (dn_ref[:, lanes(b)] * a[p : p + 1] - b0[p : p + 1] - e) * mask
                db_ref[:, lanes(b)] = e.astype(BF16)
                before, after = neighbours(e, px, grid)
                pack3(pad, b, e, after, before, px, grid)
            mean, rs = c1_ref[0:params, :], c1_ref[params : 2 * params, :]
            accs = [[jnp.zeros((8, LN), F32) for _ in range(params)] for _ in range(2)]
            for g in range(2):
                dh = None
                for i in range(3):
                    part = dot(pad[grid * i : grid * i + px, g * 768 : (g + 1) * 768], w_ref[2 - i])
                    dh = part if dh is None else dh + part
                for half in range(2):
                    b = g * 2 + half
                    p = b % params
                    xh = (pick_half(int_ref, o_ref, x_ref, b) - mean[p : p + 1]) * rs[p : p + 1]
                    v = xh * p1_ref[p : p + 1, :] + p1_ref[params + p : params + p + 1, :]
                    d = dh[:, half * LN : (half + 1) * LN] * gelu_both(v, half_mask)[1]
                    dn1_ref[:, lanes(b)] = d
                    accs[0][p] = accs[0][p] + rows8(d)
                    accs[1][p] = accs[1][p] + rows8(d * xh)
            row_ref[...] = jnp.zeros_like(row_ref)
            for q in range(2):
                for p in range(params):
                    row_ref[q * params + p : q * params + p + 1, :] = total(accs[q][p], fold)
            send(pay_ref, row_ref)

        extra = [other] if two else []
        return call(
            body,
            [((px, 512), BF16), ((px, 512), F32), ((4, LN), F32, "far"), ((n, 4, LN), F32, "far")],
            [pltpu.VMEM((4, LN), F32), pltpu.VMEM((px + 2 * grid, 2 * 768), BF16)],
            ints, counts, recv, dn, y, cst2, par2, wt, x, cst1, par1, *extra,
            **kw,
        )

    def slow_last(self, ints, counts, recv, dn, x, cst, par, dp, wa, wp, **kw):
        px, grid = self.px, self.grid

        def body(
            int_ref, n_ref, recv_ref, dn_ref, x_ref, cst_ref, par_ref, dp_ref, wa_ref, wp_ref,
            da_ref, d0_ref, d1_ref, sum_ref,
        ):
            mask = region(int_ref[0], px, grid)
            inv_k = 1.0 / (n_ref[:, 2:3, :].sum(axis=0) * float(TS // 2))
            sums = recv_ref[...].astype(F32).sum(axis=0)
            sum_ref[...] = sums
            mean, rs = cst_ref[0:2, :], cst_ref[2:4, :]
            a = par_ref[0:2, :] * rs
            b0 = a * inv_k * sums[0:2]
            c0 = a * inv_k * rs * sums[2:4]
            for b in range(4):
                p = b % 2
                e = (x_ref[:, lanes(b)] - mean[p : p + 1]) * c0[p : p + 1]
                e = (dn_ref[:, lanes(b)] * a[p : p + 1] - b0[p : p + 1] - e) * mask
                da_ref[:, lanes(b)] = e.astype(BF16)
            for t, out in ((0, d0_ref), (1, d1_ref)):
                out[...] = (
                    dot_t(da_ref[:, t * CS_MID : (t + 1) * CS_MID], wa_ref[...])
                    + dot_t(dp_ref[:, t * CS : (t + 1) * CS], wp_ref[...])
                ).astype(BF16)

        return call(
            body,
            [((px, 512), BF16), ((px, LAT), BF16), ((px, LAT), BF16), ((4, LN), F32, "far")],
            [],
            ints, counts, recv, dn, x, cst, par, dp, wa, wp,
            **kw,
        )

    def slow_input_grad(self, da, dp, wa, wp, **kw):
        px = self.px

        def body(da_ref, dp_ref, wa_ref, wp_ref, dx_ref):
            for t in range(2):
                dx_ref[:, t * CS : (t + 1) * CS] = (
                    dot_t(da_ref[:, t * CS_MID : (t + 1) * CS_MID], wa_ref[0:CS, :])
                    + dot_t(dp_ref[:, t * CS : (t + 1) * CS], wp_ref[0:CS, :])
                ).astype(BF16)

        return call(body, ((px, 2048), BF16, "far"), [], da, dp, wa, wp, smem=0, **kw)

    def fast_first_back(self, ints, counts, recv, dn_lo, dn_hi, fa_lo, fa_hi, cst, par, **kw):
        px, grid = self.px, self.grid

        def body(int_ref, n_ref, recv_ref, dl_ref, dh_ref, xl_ref, xh_ref, cst_ref, par_ref, da_ref, sum_ref):
            sums = recv_ref[...].sum(axis=0)
            sum_ref[...] = sums

            @pl.when(int_ref[1] == 1)
            def _():
                mask = region(int_ref[0], px, grid)
                inv_k = 1.0 / (n_ref[:, 2:3, :].sum(axis=0) * float(TF // 2))
                mean, rs = cst_ref[0:1, :], cst_ref[1:2, :]
                a = par_ref[0:1, :] * rs
                b0 = a * inv_k * sums[0:1]
                c0 = a * inv_k * rs * sums[1:2]
                for dn_ref, h_ref, base in ((dl_ref, xl_ref, 0), (dh_ref, xh_ref, 4)):
                    for b in range(4):
                        e = (h_ref[:, lanes(b)] - mean) * c0
                        e = (dn_ref[:, lanes(b)] * a - b0 - e) * mask
                        da_ref[:, lanes(base + b)] = e.astype(BF16)

        return call(
            body,
            [((px, 1024), BF16), ((4, LN), F32, "far")],
            [],
            ints, counts, recv, dn_lo, dn_hi, fa_lo, fa_hi, cst, par,
            **kw,
        )

    def fast_small(self, ints, da, xf, bc, bc_other, **kw):
        first = 3 * CF_MID
        rows = first + bc.shape[0]

        def body(int_ref, da_ref, x_ref, b0_ref, b1_ref, out_ref, row_ref, scratch):
            row_ref[0:first, :] = jnp.zeros((first, LN), F32)
            row_ref[first:rows, :] = b0_ref[...] + b1_ref[...]

            @pl.when(int_ref[1] == 1)
            def _():
                accs = [None] * 3
                for g in range(4):
                    lo, hi = max(8 * g - 1, 0), min(8 * g + 9, TF)
                    k0 = lo - (8 * g - 1)
                    d = dot(da_ref[:, g * 256 : (g + 1) * 256].T, x_ref[:, lo * CF : hi * CF])
                    for k in range(3):
                        for i in range(8):
                            j = i + k - k0
                            if 0 <= j < hi - lo:
                                part = d[i * CF_MID : (i + 1) * CF_MID, j * CF : (j + 1) * CF]
                                accs[k] = part if accs[k] is None else accs[k] + part
                for k in range(3):
                    tiled = jnp.concatenate([accs[k]] * 4, axis=0).T
                    row_ref[k * CF_MID : (k + 1) * CF_MID, :] = tiled_rows(scratch, tiled)

            out_ref[...] = row_ref[...].astype(BF16)

        return call(
            body,
            ((rows, LN), BF16, "far"),
            [pltpu.VMEM((rows, LN), F32), pltpu.VMEM((LN, LN), F32)],
            ints, da, xf, bc, bc_other,
            **kw,
        )

    def last(self, ints, da, ds_lo, ds_hi, band, dxs0, dxs1, **kw):
        px = self.px

        def body(int_ref, da_ref, sl_ref, sh_ref, band_ref, x0_ref, x1_ref, dx_ref, acc_ref, out_ref, sem):
            def part(g):
                at = slice(g * 1024, (g + 1) * 1024)
                return pltpu.make_async_copy(out_ref.at[:, at], dx_ref.at[:, at], sem.at[g])

            def half(ref, g):
                return pltpu.make_async_copy(ref, out_ref.at[:, g * 2048 : (g + 1) * 2048], sem.at[4 + g])

            @pl.when(int_ref[1] == 0)
            def _():
                half(x0_ref, 0).start()
                half(x1_ref, 1).start()
                for g in range(2):
                    half(x0_ref if g == 0 else x1_ref, g).wait()
                    part(2 * g).start()
                    part(2 * g + 1).start()
                for g in range(4):
                    part(g).wait()

            @pl.when(int_ref[1] == 1)
            def _():
                acc_ref[:, 0 : 10 * CF] = dot_t(da_ref[:, 0:256], band_ref[...])
                for g in range(4):
                    if g < 3:
                        p = dot_t(da_ref[:, (g + 1) * 256 : (g + 2) * 256], band_ref[...])
                        base = 8 * (g + 1) * CF
                        acc_ref[:, base : base + 2 * CF] += p[:, 0 : 2 * CF]
                        acc_ref[:, base + 2 * CF : base + 10 * CF] = p[:, 2 * CF :]
                    s_ref = sl_ref if g < 2 else sh_ref
                    for i in range(8):
                        f = 8 * g + i
                        s = s_ref[:, lanes(f % 16)] + acc_ref[:, lanes(f + 1)]
                        out_ref[:, lanes(f)] = s.astype(BF16)
                    part(g).start()
                for g in range(4):
                    part(g).wait()

        return call(
            body,
            ((px, 4096), BF16, "manual"),
            [pltpu.VMEM((px, 34 * CF), F32), pltpu.VMEM((px, 4096), BF16), pltpu.SemaphoreType.DMA((6,))],
            ints, da, ds_lo, ds_hi, band, Manual(dxs0), Manual(dxs1),
            **kw,
        )

    def halves(self, ints, x, x_other, cot, cot_other, **kw):
        px = self.px

        def body(int_ref, x_ref, xo_ref, c_ref, co_ref, xs_ref, xf_ref, gs_ref, gf_ref, sem):
            def run(pairs):
                copies = [pltpu.make_async_copy(a, b, sem.at[k]) for k, (a, b) in enumerate(pairs)]
                for c in copies:
                    c.start()
                for c in copies:
                    c.wait()

            lo, hi = slice(0, 2048), slice(2048, 4096)

            @pl.when(int_ref[1] == 0)
            def _():
                xf_ref[:, 0 : 2 * CF] = jnp.zeros((px, 2 * CF), BF16)
                run([
                    (x_ref.at[:, lo], xs_ref), (xo_ref.at[:, lo], xf_ref.at[:, 2 * CF : 18 * CF]),
                    (c_ref.at[:, lo], gs_ref), (co_ref.at[:, lo], gf_ref),
                ])

            @pl.when(int_ref[1] == 1)
            def _():
                run([
                    (xo_ref.at[:, hi], xs_ref), (x_ref.at[:, 14 * CF :], xf_ref),
                    (co_ref.at[:, hi], gs_ref), (c_ref.at[:, hi], gf_ref),
                ])

        wide = ((px, 2048), BF16)
        return call(
            body,
            [wide, ((px, 18 * CF), BF16), wide, wide],
            [pltpu.SemaphoreType.DMA((4,))],
            ints, Manual(x), Manual(x_other), Manual(cot), Manual(cot_other),
            **kw,
        )

    def out_send(self, ints, ys, yf, **kw):
        px = self.px

        def body(int_ref, ys_ref, yf_ref, out_ref):
            for path, ref, at in ((0, yf_ref, 2 * CF), (1, ys_ref, 0)):

                @pl.when(int_ref[1] == path)
                def _():
                    out_ref[...] = ref[:, at : at + 2048]

        return call(body, ((px, 2048), BF16, "far"), [], ints, ys, yf, **kw)

    def out_join(self, ints, ys, yf, other, **kw):
        px = self.px

        def body(int_ref, ys_ref, yf_ref, o_ref, out_ref):
            for path, ref, at in ((0, ys_ref, 0), (1, yf_ref, 2 * CF)):

                @pl.when(int_ref[1] == path)
                def _():
                    mine, far = path * 2048, (1 - path) * 2048
                    out_ref[:, mine : mine + 2048] = ref[:, at : at + 2048]
                    out_ref[:, far : far + 2048] = o_ref[...]

        return call(body, ((px, 4096), BF16, "far"), [], ints, ys, yf, Far(other), **kw)

    def fast_grads_bc(self, h1, db, h2, dc, **kw):
        px, grid = self.px, self.grid

        def body(h1_ref, db_ref, h2_ref, dc_ref, out_ref, pad, scratch):
            clear_edges(pad, px, grid)
            for b in range(4):
                h = h1_ref[:, lanes(b)].astype(F32)
                before, after = neighbours(h, px, grid)
                pack3(pad, b, h, before, after, px, grid)
            same = (lax.broadcasted_iota(jnp.int32, (256, 256), 0) >> 5) == (
                lax.broadcasted_iota(jnp.int32, (256, 256), 1) >> 5
            )
            for i in range(3):
                for s in range(3):
                    acc = jnp.zeros((256, 256), F32)
                    for g in range(2):
                        at = g * 768 + s * 256
                        acc = acc + dot(
                            pad[grid * i : grid * i + px, at : at + 256].T,
                            db_ref[:, g * 256 : (g + 1) * 256],
                        )
                    acc = jnp.where(same, acc, 0.0).reshape(8, CF_MID, 256).sum(axis=0)
                    at = (3 * i + s) * 8
                    out_ref[at : at + 8, :] = tiled_rows(scratch, fold32(acc))
            acc = jnp.zeros((256, 1024), F32)
            for g in range(2):
                acc = acc + dot(h2_ref[:, g * 256 : (g + 1) * 256].T, dc_ref[:, g * 1024 : (g + 1) * 1024])
            out = None
            for i in range(8):
                part = acc[i * CF_MID : (i + 1) * CF_MID, i * CF : (i + 1) * CF]
                out = part if out is None else out + part
            out_ref[72:104, :] = out
            out_ref[104:, :] = jnp.zeros((8, LN), F32)

        return call(
            body,
            ((112, LN), F32, "far"),
            [pltpu.VMEM((px + 2 * grid, 2 * 768), BF16), pltpu.VMEM((CF_MID, LN), F32)],
            h1, db, h2, dc, smem=0,
            **kw,
        )

    def grads_early(self, plan, ints, xs, lat, dp, h2, dc, **kw):
        px = self.px
        rows = plan.early

        def body(int_ref, x_ref, lat_ref, dp_ref, h2_ref, dc_ref, keep_ref, send_ref, buf, xt):
            def put(base, q, acc):
                for j in range(2):
                    buf[pl.ds(base + 2 * q + j, 256, stride=8), :] = acc[:, j * LN : (j + 1) * LN]

            for c in range(6):
                for t in range(2):
                    if c == 5:
                        x = h2_ref[:, t * 256 : (t + 1) * 256]
                    elif c == 4:
                        x = lat_ref[:, t * LAT : (t + 1) * LAT]
                    else:
                        x = x_ref[:, t * CS + c * 256 : t * CS + (c + 1) * 256]
                    xt[:, t * px : (t + 1) * px] = x.T
                source = dc_ref if c == 5 else dp_ref
                base = (ROW_SC if c == 5 else ROW_SP + c * 2048) - ROW_SC
                for q in range(4):
                    acc = None
                    for t in range(2):
                        at = t * CS + q * 256
                        part = dot(xt[:, t * px : (t + 1) * px], source[:, at : at + 256])
                        acc = part if acc is None else acc + part
                    put(base, q, acc)
            lo = 0
            hi = plan.base[1] - ROW_SC
            mine = pl.multiple_of(jnp.where(int_ref[1] == 0, lo, hi), 16)
            other = pl.multiple_of(jnp.where(int_ref[1] == 0, hi, lo), 16)
            keep_ref[...] = buf[pl.ds(mine, rows), :].astype(BF16)
            send_ref[...] = buf[pl.ds(other, rows), :].astype(BF16)

        return call(
            body,
            [((rows, LN), BF16, "far"), ((rows, LN), BF16, "far")],
            [pltpu.VMEM((ROW_SG - ROW_SC, LN), F32), pltpu.VMEM((256, 2 * px), BF16)],
            ints, xs, lat, dp, h2, dc,
            **kw,
        )

    def grads_conv(self, h1, db, **kw):
        px, grid = self.px, self.grid

        def body(h1_ref, db_ref, out_ref, buf, pad):
            clear_edges(pad, px, grid)
            for b in range(4):
                h = h1_ref[:, lanes(b)].astype(F32)
                before, after = neighbours(h, px, grid)
                pack3(pad, b, h, before, after, px, grid)
            for i in range(3):
                for s in range(3):
                    acc = None
                    for t in range(2):
                        at = t * 768 + s * 256
                        part = dot(
                            pad[grid * i : grid * i + px, at : at + 256].T,
                            db_ref[:, t * 256 : (t + 1) * 256],
                        )
                        acc = part if acc is None else acc + part
                    for j in range(2):
                        buf[pl.ds((3 * i + s) * 512 + j, 256, stride=2), :] = acc[:, j * LN : (j + 1) * LN]
            out_ref[...] = buf[...].astype(BF16)

        return call(
            body,
            ((ROW_SC - ROW_SB, LN), BF16, "far"),
            [pltpu.VMEM((ROW_SC - ROW_SB, LN), F32), pltpu.VMEM((px + 2 * grid, 2 * 768), BF16)],
            h1, db, smem=0,
            **kw,
        )

    def grads_late(self, ints, xs, lat, da, yf, dl0, dl1, **kw):
        px = self.px
        rows = ROW_SB - ROW_SA
        lat_rows = ROW_FG - ROW_LAT

        def body(int_ref, x_ref, lat_ref, da_ref, yf_ref, d0_ref, d1_ref, keep_ref, send_ref, buf):
            for c in range(5):
                acc = None
                for t in range(2):
                    if c == 4:
                        x = lat_ref[:, t * LAT : (t + 1) * LAT]
                    else:
                        x = x_ref[:, t * CS + c * 256 : t * CS + (c + 1) * 256]
                    part = dot(x.T, da_ref[:, t * CS_MID : (t + 1) * CS_MID])
                    acc = part if acc is None else acc + part
                for j in range(2):
                    buf[pl.ds(c * 512 + j, 256, stride=2), :] = acc[:, j * LN : (j + 1) * LN]
            for k in range(5):
                acc = dot(yf_ref[:, lanes(k)].T, d0_ref[...]) + dot(yf_ref[:, lanes(8 + k)].T, d1_ref[...])
                for j in range(2):
                    buf[pl.ds(rows + k * 256 + j, CF, stride=2), :] = acc[:, j * LN : (j + 1) * LN]
            mine = pl.multiple_of(jnp.where(int_ref[1] == 0, 0, rows), 16)
            other = pl.multiple_of(jnp.where(int_ref[1] == 0, rows, 0), 16)
            keep_ref[...] = buf[pl.ds(mine, rows), :].astype(BF16)
            send_ref[...] = buf[pl.ds(other, rows), :].astype(BF16)

        return call(
            body,
            [((rows, LN), BF16, "far"), ((rows, LN), BF16, "far")],
            [pltpu.VMEM((2 * rows, LN), F32)],
            ints, xs, lat, da, yf, dl0, dl1,
            **kw,
        )

    def windows(self, plan, ints, early, conv, late, **kw):
        ndp, chunk, half = self.ndp, plan.chunk, self.ndp // 2

        def body(int_ref, e0_ref, e1_ref, c0_ref, c1_ref, l0_ref, l1_ref, keep_ref, send_ref, buf):
            def add(a, b, rows):
                return a[0:rows, :].astype(F32) + b[0:rows, :].astype(F32)

            for path in range(2):

                @pl.when(int_ref[1] == path)
                def _():
                    buf[...] = jnp.zeros_like(buf)
                    base = plan.base[path]
                    if path == 0:
                        buf[ROW_SA:ROW_SB, :] = add(l0_ref, l1_ref, ROW_SB - ROW_SA)
                        buf[ROW_SB:ROW_SC, :] = add(c0_ref, c1_ref, ROW_SC - ROW_SB)
                        rest = min(plan.length - ROW_SC, plan.early)
                        buf[ROW_SC : ROW_SC + rest, :] = add(e0_ref, e1_ref, rest)
                    else:
                        rest = ROW_SG - base
                        buf[0:rest, :] = add(e0_ref, e1_ref, rest)
                        at = ROW_LAT - base
                        buf[at : at + ROW_FG - ROW_LAT, :] = add(l0_ref, l1_ref, ROW_FG - ROW_LAT)

            path = int_ref[1]
            base = jnp.where(path == 0, plan.base[0], plan.base[1])

            def stretch(place):
                j = 0
                for step in range(plan.bits):
                    bit = (place >> (plan.bits - 1 - step)) & 1
                    j = j + jnp.where(
                        path == 0, bit << plan.order[0][step], bit << plan.order[1][step]
                    )
                at = ((path * ndp + j) * plan.share) // (16 * LN) * 16 - base
                return buf[pl.ds(pl.multiple_of(at, 16), chunk), :].astype(BF16)

            def step(q, carry):
                bit = int_ref[5]
                keep_ref[q] = stretch(bit * half + q)
                send_ref[q] = stretch((1 - bit) * half + q)
                return carry

            loop(half, step, 0)

        return call(
            body,
            [((half, chunk, LN), BF16, "far")] * 2,
            [pltpu.VMEM((plan.length, LN), F32)],
            ints, *early, *conv, *late,
            **kw,
        )

    def halve(self, plan, ints, step, keep, came, **kw):
        half = keep.shape[0] // 2

        def body(int_ref, a_ref, b_ref, keep_ref, send_ref):
            bit = int_ref[5 + step]

            def one(q, carry):
                for out, at in ((keep_ref, bit * half + q), (send_ref, (1 - bit) * half + q)):
                    out[q] = (a_ref[at].astype(F32) + b_ref[at].astype(F32)).astype(BF16)
                return carry

            loop(half, one, 0)

        return call(
            body,
            [((half, plan.chunk, LN), BF16, "far")] * 2,
            [],
            ints, Far(keep), came,
            **kw,
        )

    def add(self, parts, **kw):
        def body(*refs):
            refs[-1][...] = sum(r[...].astype(F32) for r in refs[:-1]).astype(BF16)

        return call(body, (parts[0].shape, BF16, "far"), [], Far(parts[0]), *parts[1:], smem=0, **kw)

    def window(self, plan, ints, keep, came, parts, vectors, tail, **kw):
        chunk, out_rows = plan.chunk, plan.out_rows
        extra, count = parts[0].shape[0], len(parts)
        pad = extra + 8

        def body(int_ref, keep_ref, came_ref, vec_ref, tail_ref, *refs):
            out_ref, a_ref, small_ref = refs[count:]
            r0 = int_ref[2]
            row = int_ref[3]
            lane = int_ref[4]
            a_ref[...] = jnp.zeros_like(a_ref)
            total = sum(r[...].astype(F32) for r in refs[:count])
            small_ref[...] = jnp.where(int_ref[1] == 1, total, 0.0)
            for ref, start, n in (
                (vec_ref, ROW_SG, 2 * SLOW_VEC), (small_ref, ROW_FA, ROW_LAT - ROW_FA), (tail_ref, ROW_FG, 3)
            ):
                at = jnp.clip(start - r0, -n, chunk) + pad
                a_ref[pl.ds(at, n), :] += ref[0:n, :]
            a_ref[pad : pad + chunk, :] += keep_ref[0].astype(F32) + came_ref[0].astype(F32)
            one = a_ref[pl.ds(pad + row, out_rows), :]
            two = a_ref[pl.ds(pad + row + 1, out_rows), :]
            shift = (LN - lane) & (LN - 1)
            one = pltpu.roll(one, shift, 1)
            two = pltpu.roll(two, shift, 1)
            at = lax.broadcasted_iota(jnp.int32, (out_rows, LN), 1)
            out_ref[...] = jnp.where(at < LN - lane, one, two)

        return call(
            body,
            ((out_rows, LN), F32, "far"),
            [pltpu.VMEM((chunk + 2 * pad + 8, LN), F32), pltpu.VMEM((extra, LN), F32)],
            ints, keep, came, vectors, tail, *parts,
            **kw,
        )


class Plan:
    def __init__(self, ndp):
        n = 2 * ndp
        self.ndp = ndp
        self.share = VALUES // n
        self.first = [self.share * d // LN // 16 * 16 for d in range(n)]
        ends = [-(-self.share * (d + 1) // LN) for d in range(n)]
        self.chunk = -(-max(e - f for e, f in zip(ends, self.first)) // 16) * 16
        self.base = [self.first[0], self.first[ndp]]
        self.length = max(
            self.first[q * ndp + ndp - 1] + self.chunk - self.base[q] for q in range(2)
        )
        self.early = ROW_SG - self.base[1]
        self.out_rows = -(-self.share // LN)
        self.bits = ndp.bit_length() - 1
        one = list(range(self.bits))
        two = one[1:] + one[:1]
        self.order = [one, two]
        self.stages = [
            [m << b for m in range(1, 1 << min(2, self.bits - b))] for b in range(0, self.bits, 2)
        ]

    def place(self, path, j):
        at = 0
        for b in self.order[path]:
            at = 2 * at + ((j >> b) & 1)
        return at

    def route(self, mask):
        return [(q * self.ndp + j, q * self.ndp + (j ^ mask)) for q in range(2) for j in range(self.ndp)]

    def pairs(self, step):
        out = []
        for q in range(2):
            b = self.order[q][step]
            out += [(q * self.ndp + j, q * self.ndp + (j ^ (1 << b))) for j in range(self.ndp)]
        return out


def exchange(x):
    return lax.all_to_all(x, ("path", "dp"), 0, 0)


def swap(x):
    x = x.array if isinstance(x, Near) else x
    return lax.ppermute(x, "path", SWAP)


def local(
    acts, cotangent, clip_res, w_slow_a, w_slow_b, w_slow_c, w_slow_proj, slow_gain, slow_bias,
    w_fast_a, w_fast_b, w_fast_c, w_lateral, fast_gain, fast_bias,
):
    grid = acts.shape[2]
    px = grid * grid
    ndp = lax.axis_size("dp")
    net = Net(ndp, grid)
    plan = Plan(ndp)
    path, chip = lax.axis_index("path"), lax.axis_index("dp")
    core0 = path == 0
    level = clip_res[0]
    side = jnp.where(
        level == 1, grid * 5 // 8, jnp.where(level == 2, grid * 7 // 8, jnp.where(level == 3, grid, 0))
    )
    start = (path * ndp + chip) * plan.share
    r0 = start // LN // 16 * 16
    off = start - r0 * LN
    bits = [
        jnp.where(core0, chip >> plan.order[0][s], chip >> plan.order[1][s]) & 1 for s in range(plan.bits)
    ]
    ints = jnp.stack([side, path, r0, off // LN, off % LN] + bits).astype(jnp.int32)
    x = acts.reshape(px, 4096)
    cot = cotangent.reshape(px, 4096)
    sg, sb_ = slow_gain.reshape(SLOW_VEC, LN), slow_bias.reshape(SLOW_VEC, LN)

    def slow_par(a, b):
        return jnp.concatenate([sg[a:b], sb_[a:b]], axis=0)

    def fast_par(a, b):
        one = jnp.stack([fast_gain[a:b], fast_bias[a:b]])
        return jnp.tile(one, (1, LN // (b - a)))

    wlat = w_lateral.reshape(5 * CF, LAT)
    wa_lat = Far(w_slow_a, (LAT, CS_MID), (CS // LAT, 0))
    wp_lat = Far(w_slow_proj, (LAT, CS), (CS // LAT, 0))
    f1, f2, f3 = fast_par(0, 32), fast_par(32, 64), fast_par(64, 192)
    s1, s2, s3, s4 = slow_par(0, 2), slow_par(2, 4), slow_par(4, 12), slow_par(12, 20)
    wb3 = w_slow_b.reshape(3, 768, 256)
    wbt3 = w_slow_b.transpose(0, 2, 1).reshape(3, 768, 256)
    half = TF // 2

    x_other = swap(x)
    cot_other = swap(cot)

    fa_lo, fa_hi, band, pay = net.fast_first(ints, x, w_fast_a.transpose(0, 2, 1), us=3.5)
    (fb_w, fbt_w, fc_w), tok = net.fast_weights(
        w_fast_b, w_fast_b.transpose(0, 2, 1), w_fast_c, us=1.0, after=[pay], token=True
    )
    fa_other = swap(fa_lo)
    r1 = exchange(pay)
    fh1, fb, fc1, pay, r1 = net.conv_stage(
        ints, r1, r1, fa_hi, f1, fb_w, 1, half, fa_other, us=2.7, after=[tok]
    )
    (xs, xf, gs, gf), tok = net.halves(ints, x, x_other, cot, cot_other, us=2.5, after=[pay], token=True)
    r = exchange(pay)
    fh2, fc2, pay, fh2_edge = net.expand_stage(
        ints, r, r1, fb, f2, fc_w, 1, 1, half, True, us=2.6, after=[tok]
    )
    fh2_other = swap(fh2_edge)
    (pa, pp), tok = net.slow_start(xs, w_slow_a, w_slow_proj, us=3.5, after=[pay], token=True)
    r = exchange(pay)
    yf, lat, fc3, sa, pay = net.fast_finish(
        ints, r, r1, fh2, fh2_other, fc_w, xf, f3, wlat, pa, wa_lat, us=5.0, after=[tok]
    )

    (sp, sp_rows), tok = net.slow_join(ints, pp, lat, wp_lat, 8, us=3.0, after=[pay], token=True)
    r = exchange(pay)
    sh1, sb, sc1, pay = net.conv_stage(
        ints, r, r1, sa, s1, wb3, 2, TS // 2, more=sp_rows, us=3.0, after=[tok]
    )
    rp = exchange(pay)
    gp, tok = net.fast_slope(ints, fh2, fc_w, xf, f3, fc3, us=4.0, after=[pay], token=True)
    sh2, sc2, pay = net.expand_stage(ints, rp, r1, sb, s2, w_slow_c, 2, 8, TS // 2, us=3.0, after=[tok])
    r = exchange(pay)
    ys, ds, scc, scp, pay = net.slow_top(ints, r, rp, r1, sh2, w_slow_c, sp, gs, s3, s4, us=6.0)

    sent, tok = net.out_send(ints, ys, yf, us=2.0, after=[pay], token=True)
    r = exchange(pay)
    (dp, dc, dn, t3, pay), (sent,) = net.expand_back(
        ints, r1, r, ds, sh2, w_slow_c, scc, s3, sb, sc2, s2, 2, 8, TS // 2, (sp, scp, s4),
        us=6.0, after=[tok], through=[sent],
    )
    theirs = swap(sent)
    (early, early_out), tok = net.grads_early(
        plan, ints, xs, lat, dp, sh2, dc, us=6.0, after=[pay], token=True
    )
    r = exchange(pay)
    (db, dn, t2, pay), (early_out,) = net.conv_back(
        ints, r1, r, dn, sb, sc2, s2, wbt3, sa, sc1, s1, 2, TS // 2, us=3.0, after=[tok], through=[early_out]
    )
    early_in = swap(early_out)
    conv, tok = net.grads_conv(sh1, db, us=3.0, after=[pay], token=True)
    out, tok = net.out_join(ints, ys, yf, theirs, us=3.0, after=[tok], token=True)
    r = exchange(pay)
    (da, dl0, dl1, t1), (conv_out,) = net.slow_last(
        ints, r1, r, dn, sa, sc1, s1, dp, wa_lat, wp_lat, us=3.0, after=[tok], through=[conv]
    )
    dl_other = swap(dl0)
    (late, late_out), tok = net.grads_late(ints, xs, lat, da, yf, dl0, dl1, us=4.0, token=True)

    (fds, pay), (conv_out, late_out) = net.fast_top(
        ints, dl0, dl1, dl_other, wlat, gf, gp, fh2, fc_w, fc3, us=4.0, through=[conv_out, late_out]
    )
    conv_in = swap(conv_out)
    late_in = swap(late_out)
    fds_lo = swap(fds)
    (keep, there), tok = net.windows(
        plan, ints, (Far(early), early_in), (Far(conv_out), conv_in), (Far(late), late_in),
        us=6.0, after=[pay], token=True,
    )
    r = exchange(pay)
    (fdc, dn, u3, pay), (there,) = net.expand_back(
        ints, r1, r, fds, fh2, fc_w, fc3, f3, fb, fc2, f2, 1, 1, half,
        us=5.0, after=[tok], through=[there],
    )
    here = lax.ppermute(there, ("path", "dp"), plan.pairs(0))
    dxs, tok = net.slow_input_grad(da, dp, w_slow_a, w_slow_proj, us=4.0, after=[pay], token=True)
    (keep, there), tok = net.halve(plan, ints, 1, keep, here, us=3.0, after=[tok], token=True)
    r = exchange(pay)
    (fdb, dn, u2, pay), (dxs_out, there) = net.conv_back(
        ints, r1, r, dn, fb, fc2, f2, fbt_w, fa_hi, fc1, f1, 1, half, fa_other,
        us=4.0, after=[tok], through=[dxs, there],
    )
    dn_lo = swap(dn)
    here = lax.ppermute(there, ("path", "dp"), plan.pairs(1))
    bc, tok = net.fast_grads_bc(fh1, fdb, fh2, fdc, us=4.0, after=[pay], token=True)
    (keep, there), tok = net.halve(plan, ints, 2, keep, here, us=2.5, after=[tok], token=True)
    r = exchange(pay)
    (fda, u1), (bc, there) = net.fast_first_back(
        ints, r1, r, dn_lo, dn, Far(fa_lo), fa_hi, fc1, f1, us=2.5, after=[tok], through=[bc, there]
    )
    bc_other = swap(bc)
    dxs_other = swap(dxs_out)
    small = net.fast_small(ints, fda, x, bc, bc_other, us=3.0)
    here = lax.ppermute(there, ("path", "dp"), plan.pairs(2))
    for step in range(3, plan.bits):
        keep, there = net.halve(plan, ints, step, keep, here, us=2.5, after=[small])
        here = lax.ppermute(there, ("path", "dp"), plan.pairs(step))
    for k, masks in enumerate(plan.stages):
        parts = [small] + [lax.ppermute(small, ("path", "dp"), plan.route(m)) for m in masks]
        if k < len(plan.stages) - 1:
            small = net.add(parts, us=1.0, after=[keep, dxs_other, fds_lo] if k == 0 else [])
    dx = net.last(ints, fda, Far(fds_lo), fds, band, dxs_out, dxs_other, us=4.5, after=[small])

    vectors = jnp.concatenate([t1[2:4], t2[2:4], t3[8:24], t1[0:2], t2[0:2], t3[0:8], t3[0:8]], axis=0)
    tail = jnp.concatenate([u1[1, :32], u2[1, :32], u3[1], u1[0, :32], u2[0, :32], u3[0]]).reshape(3, LN)
    tail = jnp.pad(tail, ((0, 5), (0, 0)))
    flat = net.window(plan, ints, keep, here, parts, vectors, tail).reshape(-1)[: plan.share]
    return (out.reshape(acts.shape), dx.reshape(acts.shape), flat)


def solution(mesh):
    data = P("path", "dp", None, None, None)
    in_specs = (data, data, P("dp")) + (P(),) * 12
    out_specs = (data, data, P(("path", "dp")))
    return jax.shard_map(local, mesh=mesh, in_specs=in_specs, out_specs=out_specs, check_vma=False)
```

```python
import functools

import jax
import jax.numpy as jnp
from jax import lax
from jax.experimental import pallas as pl
from jax.experimental.pallas import tpu as pltpu
from jax.sharding import PartitionSpec as P

TS = 4
ALPHA = 8
CS = 1024
CS_MID = 256
CF = 128
CF_MID = 32
LAT = 256
TF = 32
LN = 128
EPS = 1e-05
GELU_C = 0.7978845608028654
GELU_A = 0.044715

F32 = jnp.float32
BF16 = jnp.bfloat16
SWAP = [(0, 1), (1, 0)]

ROW_SA = 0
ROW_SB = ROW_SA + (CS + LAT) * CS_MID // LN
ROW_SC = ROW_SB + 9 * CS_MID * CS_MID // LN
ROW_SP = ROW_SC + CS_MID * CS // LN
ROW_SG = ROW_SP + (CS + LAT) * CS // LN
SLOW_VEC = (2 * CS_MID + 2 * CS) // LN
ROW_FA = ROW_SG + 2 * SLOW_VEC
ROW_LAT = ROW_FA + (3 * CF * CF_MID + 9 * CF_MID * CF_MID + CF_MID * CF) // LN
ROW_FG = ROW_LAT + 5 * CF * LAT // LN
VALUES = 2685312


def dot(a, b):
    return lax.dot_general(a, b, (((1,), (0,)), ((), ())), preferred_element_type=F32)


def dot_t(a, b):
    return lax.dot_general(a, b, (((1,), (1,)), ((), ())), preferred_element_type=F32)


class Near:
    def __init__(self, array):
        self.array = array


class Far:
    def __init__(self, array, block=None, index=None):
        self.array = pltpu.with_memory_space_constraint(array, pltpu.HBM)
        self.block, self.index = block, index


class Manual(Far):
    def __init__(self, array, pinned=True):
        if isinstance(array, Near):
            self.array = pltpu.with_memory_space_constraint(array.array, pltpu.HBM)
        else:
            self.array = pltpu.with_memory_space_constraint(array, pltpu.HBM) if pinned else array
        self.block = None


def dot_l(a, b):
    return lax.dot_general(a, b, (((0,), (0,)), ((), ())), preferred_element_type=F32)


def call(body, outs, scratch, *args, smem=1, limit=20, us=2.0, after=(), token=False, through=()):
    one = not isinstance(outs, list)
    shapes, out_specs, specs, operands = [], [], [], []
    vmem, anywhere = pl.BlockSpec(memory_space=pltpu.VMEM), pl.BlockSpec(memory_space=pl.ANY)
    for out in [outs] if one else outs:
        place = out[2] if len(out) > 2 else "near"
        shapes.append(pltpu.HBM(out[0], out[1]))
        out_specs.append(anywhere if place == "manual" else vmem)
    if token:
        shapes.append(pltpu.HBM((8, LN), F32))
        out_specs.append(anywhere)
    for k, a in enumerate(args):
        if k < smem:
            specs.append(pl.BlockSpec(memory_space=pltpu.SMEM))
        elif isinstance(a, Manual):
            specs.append(anywhere)
        elif isinstance(a, Far) and a.block is not None:
            index = a.index
            specs.append(pl.BlockSpec(a.block, lambda i, index=index: index))
        else:
            specs.append(vmem)
        if isinstance(a, Near):
            a = pltpu.with_memory_space_constraint(a.array, pltpu.HBM)
        operands.append(a.array if isinstance(a, Far) else a)
    for a in after:
        specs.append(anywhere)
        operands.append(pltpu.with_memory_space_constraint(a, pltpu.HBM))
    aliases = {}
    for a in through:
        aliases[len(operands)] = len(shapes)
        specs.append(anywhere)
        operands.append(pltpu.with_memory_space_constraint(a, pltpu.HBM))
        shapes.append(pltpu.HBM(a.shape, a.dtype))
        out_specs.append(anywhere)
    n_in, n_out = len(args), len(shapes) - token - len(through)
    cut = any(isinstance(a, Far) and a.block is not None for a in args)

    def wrapped(*refs):
        rest = refs[n_in + len(after) + len(through) :]
        body(*refs[:n_in], *rest[:n_out], *rest[n_out + token + len(through) :])

    res = pl.pallas_call(
        wrapped,
        out_shape=shapes,
        grid=(1,) if cut else (),
        in_specs=specs,
        out_specs=out_specs,
        scratch_shapes=scratch,
        input_output_aliases=aliases,
        cost_estimate=pl.CostEstimate(flops=int(us * 1e9), bytes_accessed=0, transcendentals=0),
        compiler_params=pltpu.CompilerParams(vmem_limit_bytes=limit * 1024 * 1024),
    )(*operands)
    got = [
        Near(r) if len(out) == 2 else r for r, out in zip(res, [outs] if one else outs)
    ]
    got = got[0] if one else got
    if through:
        return got, list(res[n_out + token :])
    return (got, res[n_out]) if token else got


def lanes(index):
    if isinstance(index, int):
        return slice(index * LN, (index + 1) * LN)
    return pl.ds(pl.multiple_of(index * LN, LN), LN)


def region(side, px, grid):
    bits = grid.bit_length() - 1
    r = lax.broadcasted_iota(jnp.int32, (px, LN), 0)
    inside = jnp.logical_and((r >> bits) < side, (r & (grid - 1)) < side)
    return jnp.where(inside, 1.0, 0.0).astype(F32)


def rows8(x):
    return x.reshape(x.shape[0] // 8, 8, LN).sum(axis=0)


def total(acc, fold):
    if fold:
        acc = acc + pltpu.roll(acc, 32, 1)
        acc = acc + pltpu.roll(acc, 64, 1)
    return acc.sum(axis=0, keepdims=True)


def gelu(v, half_mask):
    t = jnp.tanh(v * (GELU_C + (GELU_C * GELU_A) * (v * v)))
    return v * (half_mask + half_mask * t)


def gelu_both(v, half_mask):
    w = GELU_C + (GELU_C * GELU_A) * (v * v)
    t = jnp.tanh(v * w)
    q = half_mask + half_mask * t
    return v * q, q * (1.0 + (v - v * t) * (3.0 * w - 2.0 * GELU_C))


def loop(n, body, init, unroll=False):
    if unroll:
        for i in range(n):
            init = body(i, init)
        return init
    return lax.fori_loop(0, n, body, init)


def moments(ref, out, row, blocks, params, fold, mask, count):
    inv = 1.0 / jnp.maximum(count, 1.0)
    for p in range(params):
        n = blocks // params

        def first(i, acc):
            return acc + rows8(ref[:, lanes(p + i * params)] * mask)

        zero = jnp.zeros((8, LN), F32)
        s = total(loop(n, first, zero, n <= 4), fold)
        mean = s * inv

        def second(i, acc):
            d = (ref[:, lanes(p + i * params)] - mean) * mask
            return acc + rows8(d * d)

        m2 = total(loop(n, second, zero, n <= 4), fold)
        out[row + p : row + p + 1, :] = s
        out[row + params + p : row + params + p + 1, :] = m2


def send(pay_ref, rows_ref):
    value = rows_ref[...].astype(pay_ref.dtype)
    for d in range(pay_ref.shape[0]):
        pay_ref[d] = value


def split(v):
    high = v.astype(BF16).astype(F32)
    return high, v - high


def encode(code_ref, rows_ref, narrow, wide):
    at = 0
    if narrow:
        high, low = split(rows_ref[0:narrow, :])
        code_ref[0:narrow, :] = high
        code_ref[narrow : 2 * narrow, :] = low
        at = 2 * narrow
    if wide:
        high, low = split(rows_ref[narrow : narrow + wide, :])
        code_ref[at : at + wide, :] = high
        code_ref[at + wide : at + 2 * wide, :] = low
        code_ref[at + 2 * wide : at + 3 * wide, :] = rows_ref[narrow + wide : narrow + 2 * wide, :]


def combine(recv, row, params, n, cst_ref):
    combine_sums(recv[:, row : row + params, :], recv[:, row + params : row + 2 * params, :], n, params, cst_ref)


def combine_coded(recv, row, params, n, cst_ref, narrow=False):
    v = recv.astype(F32)
    if narrow:
        v = v[:, 0 : 2 * params] + v[:, 2 * params : 4 * params]
        combine_sums(v[:, 0:params], v[:, params:], n, params, cst_ref)
        return
    s = v[:, row : row + params] + v[:, row + params : row + 2 * params]
    combine_sums(s, v[:, row + 2 * params : row + 3 * params], n, params, cst_ref)


def combine_sums(s, m2, n, params, cst_ref):
    k = n.sum(axis=0)
    mean = s.sum(axis=0) / k
    off = s / jnp.maximum(n, 1.0) - mean[None]
    cst_ref[0:params, :] = mean
    cst_ref[params : 2 * params, :] = lax.rsqrt((m2 + n * off * off).sum(axis=0) / k + EPS)


def pick_half(int_ref, other_ref, ref, b):
    if other_ref is None:
        return ref[:, lanes(b)]
    return jnp.where(int_ref[1] == 0, other_ref[:, lanes(b)], ref[:, lanes(b)])


def fold32(v):
    v = v[:, 0:LN] + v[:, LN:256]
    v = v + pltpu.roll(v, 32, 1)
    return v + pltpu.roll(v, 64, 1)


def tiled_rows(scratch, tiled):
    c = tiled.shape[0]
    scratch[0:c, :] = tiled
    group = lax.broadcasted_iota(jnp.int32, (c // 4, LN), 1) >> 5
    out = jnp.zeros((c // 4, LN), F32)
    for q in range(4):
        out = jnp.where(group == q, scratch[pl.ds(q, c // 4, stride=4), :], out)
    return out


def pack3(pad, b, mid, left, right, px, grid):
    g, half = b // 2, b % 2
    for slot, value in enumerate((left, mid, right)):
        at = g * 768 + slot * 256 + half * 128
        pad[grid : grid + px, at : at + LN] = value.astype(BF16)


def neighbours(h, px, grid):
    col = lax.broadcasted_iota(jnp.int32, (px, LN), 0) & (grid - 1)
    before = jnp.where(col == 0, 0.0, pltpu.roll(h, 1, 0))
    after = jnp.where(col == grid - 1, 0.0, pltpu.roll(h, px - 1, 0))
    return before, after


def clear_edges(pad, px, grid):
    zero = jnp.zeros((grid, pad.shape[1]), BF16)
    pad[0:grid, :] = zero
    pad[grid + px : grid + px + grid, :] = zero


def put_count(rows_ref, row, count):
    rows_ref[row : row + 1, :] = jnp.zeros((1, LN), F32) + count


def side_sq(side, frames):
    s = side.astype(F32)
    return s * s * frames


class Net:
    def __init__(self, ndp, grid):
        self.ndp = ndp
        self.n = 2 * ndp
        self.grid = grid
        self.px = grid * grid

    def fast_first(self, ints, xf, wa, **kw):
        px, grid, n = self.px, self.grid, self.n

        def body(int_ref, xf_ref, wa_ref, lo_ref, hi_ref, band_ref, pay_ref, row_ref, fa_ref):
            side = int_ref[0]
            row_ref[...] = jnp.zeros_like(row_ref)

            @pl.when(int_ref[1] == 1)
            def _():
                pick = jnp.where(
                    (lax.broadcasted_iota(jnp.int32, (CF_MID, 256), 1) & (CF_MID - 1))
                    == lax.broadcasted_iota(jnp.int32, (CF_MID, 256), 0),
                    1.0,
                    0.0,
                ).astype(BF16)
                wide = [dot_l(wa_ref[k], pick) for k in range(3)]
                group = lax.broadcasted_iota(jnp.int32, (CF, 256), 1) >> 5
                for j in range(10):
                    acc = jnp.zeros((CF, 256), F32)
                    for k in range(3):
                        if 0 <= j - k < 8:
                            acc = jnp.where(group == j - k, wide[k], acc)
                    band_ref[j * CF : (j + 1) * CF, :] = acc.astype(BF16)
                for g in range(4):
                    lo, hi = max(8 * g - 1, 0), min(8 * g + 9, TF)
                    k0 = lo - (8 * g - 1)
                    out = dot(
                        xf_ref[:, lo * CF : hi * CF], band_ref[k0 * CF : (k0 + hi - lo) * CF, :]
                    )
                    fa_ref[:, g * 256 : (g + 1) * 256] = out
                    target = lo_ref if g < 2 else hi_ref
                    target[:, (g % 2) * 256 : (g % 2 + 1) * 256] = out
                moments(fa_ref, row_ref, 0, 8, 1, True, region(side, px, grid), side_sq(side, TF))

            put_count(row_ref, 2, side_sq(side, 1))
            send(pay_ref, row_ref)

        return call(
            body,
            [((px, 512), F32, "far"), ((px, 512), F32), ((10 * CF, 256), BF16), ((n, 4, LN), F32, "far")],
            [pltpu.VMEM((4, LN), F32), pltpu.VMEM((px, 1024), F32)],
            ints, xf, wa,
            **kw,
        )

    def fast_weights(self, wb, wbt, wc, **kw):
        def body(wb_ref, wbt_ref, wc_ref, b_ref, bt_ref, c_ref):
            pick = jnp.where(
                (lax.broadcasted_iota(jnp.int32, (CF_MID, 256), 1) & (CF_MID - 1))
                == lax.broadcasted_iota(jnp.int32, (CF_MID, 256), 0),
                1.0,
                0.0,
            ).astype(BF16)
            same = (lax.broadcasted_iota(jnp.int32, (256, 256), 0) >> 5) == (
                lax.broadcasted_iota(jnp.int32, (256, 256), 1) >> 5
            )
            for source, target in ((wb_ref, b_ref), (wbt_ref, bt_ref)):
                for tap in range(9):
                    tiled = jnp.concatenate([dot(source[tap], pick)] * 8, axis=0)
                    target[tap // 3, (tap % 3) * 256 : (tap % 3 + 1) * 256, :] = jnp.where(
                        same, tiled, 0.0
                    ).astype(BF16)
            c_ref[...] = jnp.zeros_like(c_ref)
            for i in range(8):
                c_ref[i * CF_MID : (i + 1) * CF_MID, i * CF : (i + 1) * CF] = wc_ref[...]

        return call(
            body,
            [((3, 768, 256), BF16), ((3, 768, 256), BF16), ((256, 1024), BF16)],
            [],
            wb, wbt, wc, smem=0,
            **kw,
        )

    def conv_stage(self, ints, recv, counts, x, par, w, params, frames, other=None, more=None, **kw):
        px, grid, n, ndp = self.px, self.grid, self.n, self.ndp
        fold = params == 1
        two = other is not None
        rows = 4 + (0 if more is None else more.array.shape[0])
        coded = 8 + 3 * (rows - 4) // 2

        def body(int_ref, recv_ref, n_ref, x_ref, par_ref, w_ref, *refs):
            o_ref = None
            if two:
                o_ref, refs = refs[0], refs[1:]
            if more is not None:
                m_ref, refs = refs[0], refs[1:]
            h_ref, y_ref, cst_ref, pay_ref = refs[:4]
            row_ref, pad = refs[4 + two : 6 + two]
            code_ref = refs[-1]
            if two:
                refs[4][...] = recv_ref[...]
            side = int_ref[0]
            mask = region(side, px, grid)
            half_mask = 0.5 * mask
            if two:
                stats, count = recv_ref[ndp:], n_ref[ndp:, 2:3, :] * float(TF)
            else:
                stats, count = recv_ref[...], n_ref[:, 2:3, :] * float(frames)
            combine(stats, 0, params, count, cst_ref)
            mean, rs = cst_ref[0:params, :], cst_ref[params : 2 * params, :]
            scale = par_ref[0:params, :] * rs
            shift = par_ref[params : 2 * params, :] - mean * scale
            clear_edges(pad, px, grid)
            for b in range(4):
                p = b % params
                v = pick_half(int_ref, o_ref, x_ref, b) * scale[p : p + 1] + shift[p : p + 1]
                h = gelu(v, half_mask)
                h_ref[:, lanes(b)] = h.astype(BF16)
                before, after = neighbours(h, px, grid)
                pack3(pad, b, h, before, after, px, grid)
            for g in range(2):
                acc = None
                for i in range(3):
                    part = dot(pad[grid * i : grid * i + px, g * 768 : (g + 1) * 768], w_ref[i])
                    acc = part if acc is None else acc + part
                y_ref[:, g * 256 : (g + 1) * 256] = acc
            moments(y_ref, row_ref, 0, 4, params, fold, mask, side_sq(side, frames))
            if more is None:
                send(pay_ref, row_ref)
            else:
                row_ref[4:rows, :] = m_ref[...]
                encode(code_ref, row_ref, 4, rows // 2 - 2)
                send(pay_ref, code_ref)

        extra = [other] if two else []
        extra += [] if more is None else [more]
        return call(
            body,
            [((px, 512), BF16), ((px, 512), F32), ((8, LN), F32), ((n, rows, LN), F32, "far") if more is None else ((n, coded, LN), BF16, "far")]
            + ([((n, 4, LN), F32)] if two else []),
            [pltpu.VMEM((rows, LN), F32), pltpu.VMEM((px + 2 * grid, 2 * 768), BF16)]
            + ([] if more is None else [pltpu.VMEM((coded, LN), F32)]),
            ints, recv, counts, x, par, w, *extra,
            **kw,
        )

    def expand_stage(self, ints, recv, counts, y, par, w, params, wide, frames, edge=False, **kw):
        px, grid, n = self.px, self.grid, self.n
        rows = max(2 * wide, 4)
        code = wide > 1
        coded = 3 * wide

        def body(int_ref, recv_ref, n_ref, y_ref, par_ref, w_ref, h_ref, cst_ref, pay_ref, *refs):
            row_ref, c_ref = refs[edge : edge + 2]
            code_ref = refs[-1]
            side = int_ref[0]
            mask = region(side, px, grid)
            half_mask = 0.5 * mask
            count = n_ref[:, 2:3, :] * float(frames)
            if code:
                combine_coded(recv_ref[...], 0, params, count, cst_ref, True)
            else:
                combine(recv_ref[...], 0, params, count, cst_ref)
            mean, rs = cst_ref[0:params, :], cst_ref[params : 2 * params, :]
            scale = par_ref[0:params, :] * rs
            shift = par_ref[params : 2 * params, :] - mean * scale
            for b in range(4):
                p = b % params
                v = y_ref[:, lanes(b)] * scale[p : p + 1] + shift[p : p + 1]
                h_ref[:, lanes(b)] = gelu(v, half_mask).astype(BF16)
            if edge:
                refs[0][...] = h_ref[:, lanes(3)]
            for g in range(2):
                c_ref[:, g * 1024 : (g + 1) * 1024] = dot(h_ref[:, g * 256 : (g + 1) * 256], w_ref[...])
            moments(c_ref, row_ref, 0, 16, wide, False, mask, side_sq(side, frames))
            if code:
                encode(code_ref, row_ref, 0, wide)
            send(pay_ref, code_ref if code else row_ref)

        return call(
            body,
            [((px, 512), BF16), ((8, LN), F32), ((n, coded, LN), BF16, "far") if code else ((n, rows, LN), F32, "far")]
            + ([((px, LN), BF16, "far")] if edge else []),
            [pltpu.VMEM((rows, LN), F32), pltpu.VMEM((px, 2048), F32)]
            + ([pltpu.VMEM((coded, LN), F32)] if code else []),
            ints, recv, counts, y, par, w,
            **kw,
        )

    def fast_finish(self, ints, recv, counts, h2, h2_other, w, xf, par, wlat, pa, wa, **kw):
        px, grid, n = self.px, self.grid, self.n

        def body(
            int_ref, recv_ref, n_ref, h_ref, ho_ref, w_ref, xf_ref, par_ref, wl_ref, pa_ref, wa_ref,
            y_ref, lat_ref, cst_ref, sa_ref, pay_ref, c_ref, row_ref,
        ):
            half_mask = 0.5 * region(int_ref[0], px, grid)
            combine(recv_ref[...], 0, 1, n_ref[:, 2:3, :] * float(TF // 2), cst_ref)
            scale = par_ref[0:1, :] * cst_ref[1:2, :]
            shift = par_ref[1:2, :] - cst_ref[0:1, :] * scale
            c_ref[:, 0:256] = dot(ho_ref[...], w_ref[0:LN, 256:512])
            edge = half_mask * int_ref[1].astype(F32)
            for f in range(2):
                v = c_ref[:, lanes(f)] * scale + shift + xf_ref[:, lanes(f)].astype(F32)
                y_ref[:, lanes(f)] = jnp.where(int_ref[1] == 1, gelu(v, edge), 0.0).astype(BF16)
            for g in range(2):
                c_ref[...] = dot(h_ref[:, g * 256 : (g + 1) * 256], w_ref[...])

                def step(i, carry):
                    f = 2 + g * 8 + i
                    v = c_ref[:, lanes(i)] * scale + shift + xf_ref[:, lanes(f)].astype(F32)
                    y_ref[:, lanes(f)] = gelu(v, half_mask).astype(BF16)
                    return carry

                loop(8, step, 0)
            for t in range(2):
                at = ALPHA * t * CF
                lat_ref[:, t * LAT : (t + 1) * LAT] = dot(y_ref[:, at : at + 5 * CF], wl_ref[...]).astype(BF16)
                a = slice(t * CS_MID, (t + 1) * CS_MID)
                sa_ref[:, a] = pa_ref[:, a] + dot(lat_ref[:, t * LAT : (t + 1) * LAT], wa_ref[...])
            side = int_ref[0]
            moments(sa_ref, row_ref, 0, 4, 2, False, region(side, px, grid), side_sq(side, TS // 2))
            send(pay_ref, row_ref)

        return call(
            body,
            [((px, 18 * CF), BF16), ((px, 512), BF16), ((8, LN), F32), ((px, 512), F32), ((n, 4, LN), F32, "far")],
            [pltpu.VMEM((px, 1024), F32), pltpu.VMEM((4, LN), F32)],
            ints, recv, counts, h2, h2_other, w, xf, par, wlat, pa, wa,
            **kw,
        )

    def fast_slope(self, ints, h2, w, xf, par, cst, **kw):
        px, grid = self.px, self.grid

        def body(int_ref, h_ref, w_ref, xf_ref, par_ref, cst_ref, gp_ref, c_ref):
            half_mask = 0.5 * region(int_ref[0], px, grid)
            scale = par_ref[0:1, :] * cst_ref[1:2, :]
            shift = par_ref[1:2, :] - cst_ref[0:1, :] * scale
            for g in range(2):
                c_ref[...] = dot(h_ref[:, g * 256 : (g + 1) * 256], w_ref[...])

                def step(i, carry):
                    f = g * 8 + i
                    v = c_ref[:, lanes(i)] * scale + shift + xf_ref[:, lanes(f + 2)].astype(F32)
                    gp_ref[:, lanes(f)] = gelu_both(v, half_mask)[1]
                    return carry

                loop(8, step, 0)

        return call(body, ((px, 2048), F32), [pltpu.VMEM((px, 1024), F32)], ints, h2, w, xf, par, cst, **kw)

    def slow_start(self, xs, wa, wp, **kw):
        px = self.px

        def body(x_ref, wa_ref, wp_ref, a_ref, p_ref):
            for t in range(2):
                x = x_ref[:, t * CS : (t + 1) * CS]
                a_ref[:, t * CS_MID : (t + 1) * CS_MID] = dot(x, wa_ref[0:CS, :])
                p_ref[:, t * CS : (t + 1) * CS] = dot(x, wp_ref[0:CS, :])

        return call(body, [((px, 512), F32), ((px, 2048), F32)], [], xs, wa, wp, smem=0, **kw)

    def slow_join(self, ints, part, lat, w, params, **kw):
        px, grid = self.px, self.grid
        width = params * LN

        def body(int_ref, part_ref, lat_ref, w_ref, out_ref, row_ref):
            side = int_ref[0]
            for t in range(2):
                at = slice(t * width, (t + 1) * width)
                out_ref[:, at] = part_ref[:, at] + dot(lat_ref[:, t * LAT : (t + 1) * LAT], w_ref[...])
            moments(
                out_ref, row_ref, 0, 2 * params, params, False, region(side, px, grid), side_sq(side, TS // 2)
            )

        return call(
            body, [((px, 2 * width), F32), ((2 * params, LN), F32)], [], ints, part, lat, w, **kw
        )

    def slow_top(self, ints, recv3, recvp, counts, h2, w, sp, gs, parc, parp, **kw):
        px, grid, n = self.px, self.grid, self.n

        def body(
            int_ref, r3_ref, rp_ref, n_ref, h_ref, w_ref, sp_ref, gs_ref, pc_ref, pp_ref,
            ys_ref, ds_ref, cc_ref, cp_ref, pay_ref, row_ref, c_ref, acc_ref, k_ref,
        ):
            half_mask = 0.5 * region(int_ref[0], px, grid)
            count = n_ref[:, 2:3, :] * float(TS // 2)
            combine_coded(r3_ref[...], 0, 8, count, cc_ref)
            combine_coded(rp_ref[...], 8, 8, count, cp_ref)
            k_ref[0:8, :] = pc_ref[0:8, :] * cc_ref[8:16, :]
            k_ref[8:16, :] = pp_ref[0:8, :] * cp_ref[8:16, :]
            k_ref[16:24, :] = pc_ref[8:16, :] + pp_ref[8:16, :]
            acc_ref[...] = jnp.zeros_like(acc_ref)
            for t in range(2):
                c_ref[...] = dot(h_ref[:, t * 256 : (t + 1) * 256], w_ref[...])

                def step(b, carry):
                    at = lanes(t * 8 + b)
                    one = pl.ds(b, 1)
                    xc = c_ref[:, lanes(b)] - cc_ref[one, :]
                    xp = sp_ref[:, at] - cp_ref[one, :]
                    v = xc * k_ref[one, :] + (xp * k_ref[pl.ds(b + 8, 1), :] + k_ref[pl.ds(b + 16, 1), :])
                    y, slope = gelu_both(v, half_mask)
                    ys_ref[:, at] = y.astype(BF16)
                    d = gs_ref[:, at].astype(F32) * slope
                    ds_ref[:, at] = d
                    acc_ref[b] += rows8(d)
                    acc_ref[8 + b] += rows8(d * xc)
                    acc_ref[16 + b] += rows8(d * xp)
                    return carry

                loop(8, step, 0)
            row_ref[...] = acc_ref[...].sum(axis=1)
            row_ref[8:16, :] = row_ref[8:16, :] * cc_ref[8:16, :]
            row_ref[16:24, :] = row_ref[16:24, :] * cp_ref[8:16, :]
            send(pay_ref, row_ref)

        return call(
            body,
            [
                ((px, 2048), BF16), ((px, 2048), F32), ((16, LN), F32), ((16, LN), F32),
                ((n, 24, LN), BF16, "far"),
            ],
            [
                pltpu.VMEM((24, LN), F32), pltpu.VMEM((px, 1024), F32),
                pltpu.VMEM((24, 8, LN), F32), pltpu.VMEM((24, LN), F32),
            ],
            ints, recv3, recvp, counts, h2, w, sp, gs, parc, parp,
            **kw,
        )

    def fast_top(self, ints, dl0, dl1, dl_other, wlat, gf, gp, h2, w, cst, **kw):
        px, n = self.px, self.n

        def body(
            int_ref, d0_ref, d1_ref, do_ref, wl_ref, gf_ref, gp_ref, h_ref, w_ref, cst_ref,
            ds_ref, pay_ref, row_ref, lt_ref, c_ref, acc_ref,
        ):
            first = (1 - int_ref[1]).astype(F32)
            lt_ref[:, 0 : 3 * CF] = dot_t(d0_ref[...], wl_ref[2 * CF :, :])
            lt_ref[:, 3 * CF : 8 * CF] = dot_t(d1_ref[...], wl_ref[...])
            edge = dot_t(do_ref[...], wl_ref[0 : 2 * CF, :])
            lt_ref[:, 8 * CF : 10 * CF] = jnp.where(int_ref[1] == 0, edge, 0.0)
            acc_ref[...] = jnp.zeros_like(acc_ref)
            mean, rs = cst_ref[0:1, :], cst_ref[1:2, :]
            where = {0: 0, 1: 1, 2: 2, 6: 3, 7: 4, 8: 5, 9: 6, 10: 7, 14: 8, 15: 9}
            for g in range(2):
                c_ref[...] = dot(h_ref[:, g * 256 : (g + 1) * 256], w_ref[...])
                for i in range(8):
                    f = g * 8 + i
                    d = gf_ref[:, lanes(f)].astype(F32)
                    if f in where:
                        d = d + lt_ref[:, lanes(where[f])]
                    d = d * gp_ref[:, lanes(f)]
                    ds_ref[:, lanes(f)] = d
                    acc_ref[0] += rows8(d)
                    acc_ref[1] += rows8(d * (c_ref[:, lanes(i)] - mean))
            row_ref[...] = jnp.zeros_like(row_ref)
            row_ref[0:1, :] = acc_ref[0].sum(axis=0, keepdims=True)
            row_ref[1:2, :] = acc_ref[1].sum(axis=0, keepdims=True) * rs
            send(pay_ref, row_ref)

        return call(
            body,
            [((px, 2048), F32), ((n, 4, LN), F32, "far")],
            [
                pltpu.VMEM((4, LN), F32), pltpu.VMEM((px, 10 * CF), F32),
                pltpu.VMEM((px, 1024), F32), pltpu.VMEM((2, 8, LN), F32),
            ],
            ints, dl0, dl1, dl_other, wlat, gf, gp, h2, w, cst,
            **kw,
        )

    def expand_back(self, ints, counts, recv, ds, h2, w, cstw, parw, y, cst, par, params, wide, frames, shortcut=None, **kw):
        px, grid, n = self.px, self.grid, self.n
        fold = params == 1
        both = shortcut is not None
        srows = 3 * wide if both else 4

        def body(*refs):
            int_ref, n_ref, recv_ref, ds_ref, h_ref, w_ref, cw_ref, pw_ref, y_ref, cs_ref, par_ref = refs[:11]
            refs = refs[11:]
            if both:
                sp_ref, cp_ref, pp_ref, dp_ref = refs[:4]
                refs = refs[4:]
            dc_ref, dn_ref, sum_ref, pay_ref, row_ref, c_ref, k3_ref = refs
            mask = region(int_ref[0], px, grid)
            half_mask = 0.5 * mask
            inv_k = 1.0 / (n_ref[:, 2:3, :].sum(axis=0) * float(frames))
            sums = recv_ref[...].astype(F32).sum(axis=0)
            sum_ref[...] = sums
            a = pw_ref[0:wide, :] * cw_ref[wide : 2 * wide, :]
            k3_ref[0:wide, :] = a
            k3_ref[wide : 2 * wide, :] = a * inv_k * sums[0:wide]
            k3_ref[2 * wide : 3 * wide, :] = a * inv_k * cw_ref[wide : 2 * wide, :] * sums[wide : 2 * wide]
            if both:
                a = pp_ref[0:wide, :] * cp_ref[wide : 2 * wide, :]
                k3_ref[3 * wide : 4 * wide, :] = a
                k3_ref[4 * wide : 5 * wide, :] = a * inv_k * sums[0:wide]
                k3_ref[5 * wide : 6 * wide, :] = (
                    a * inv_k * cp_ref[wide : 2 * wide, :] * sums[2 * wide : 3 * wide]
                )
            mean, rs = cs_ref[0:params, :], cs_ref[params : 2 * params, :]
            accs = [[jnp.zeros((8, LN), F32) for _ in range(params)] for _ in range(2)]
            for g in range(2):
                c_ref[...] = dot(h_ref[:, g * 256 : (g + 1) * 256], w_ref[...])

                def step(b, carry):
                    at = lanes(g * 8 + b)
                    p = b if wide == 8 else 0
                    d = ds_ref[:, at]
                    e = (c_ref[:, lanes(b)] - cw_ref[pl.ds(p, 1), :]) * k3_ref[pl.ds(2 * wide + p, 1), :]
                    e = d * k3_ref[pl.ds(p, 1), :] - k3_ref[pl.ds(wide + p, 1), :] - e
                    dc_ref[:, at] = (e * mask).astype(BF16)
                    if both:
                        e = (sp_ref[:, at] - cp_ref[pl.ds(p, 1), :]) * k3_ref[pl.ds(5 * wide + p, 1), :]
                        e = d * k3_ref[pl.ds(3 * wide + p, 1), :] - k3_ref[pl.ds(4 * wide + p, 1), :] - e
                        dp_ref[:, at] = (e * mask).astype(BF16)
                    return carry

                loop(8, step, 0)
                dh = dot_t(dc_ref[:, g * 1024 : (g + 1) * 1024], w_ref[...])
                for half in range(2):
                    b = g * 2 + half
                    p = b % params
                    xh = (y_ref[:, lanes(b)] - mean[p : p + 1]) * rs[p : p + 1]
                    v = xh * par_ref[p : p + 1, :] + par_ref[params + p : params + p + 1, :]
                    d = dh[:, half * LN : (half + 1) * LN] * gelu_both(v, half_mask)[1]
                    dn_ref[:, lanes(b)] = d
                    accs[0][p] = accs[0][p] + rows8(d)
                    accs[1][p] = accs[1][p] + rows8(d * xh)
            row_ref[...] = jnp.zeros_like(row_ref)
            for q in range(2):
                for p in range(params):
                    row_ref[q * params + p : q * params + p + 1, :] = total(accs[q][p], fold)
            send(pay_ref, row_ref)

        outs = [((px, 2048), BF16)] if both else []
        outs += [((px, 2048), BF16), ((px, 512), F32), ((srows, LN), F32, "far"), ((n, 4, LN), F32, "far")]
        extra = list(shortcut) if both else []
        return call(
            body,
            outs,
            [pltpu.VMEM((4, LN), F32), pltpu.VMEM((px, 1024), F32), pltpu.VMEM((max(6 * wide, 8), LN), F32)],
            ints, counts, recv, ds, h2, w, cstw, parw, y, cst, par, *extra,
            **kw,
        )

    def conv_back(self, ints, counts, recv, dn, y, cst2, par2, wt, x, cst1, par1, params, frames, other=None, **kw):
        px, grid, n = self.px, self.grid, self.n
        fold = params == 1
        two = other is not None

        def body(int_ref, n_ref, recv_ref, dn_ref, y_ref, c2_ref, p2_ref, w_ref, x_ref, c1_ref, p1_ref, *refs):
            o_ref = None
            if two:
                o_ref, refs = refs[0], refs[1:]
            db_ref, dn1_ref, sum_ref, pay_ref, row_ref, pad = refs
            mask = region(int_ref[0], px, grid)
            half_mask = 0.5 * mask
            inv_k = 1.0 / (n_ref[:, 2:3, :].sum(axis=0) * float(frames))
            sums = recv_ref[...].astype(F32).sum(axis=0)
            sum_ref[...] = sums
            mean2, rs2 = c2_ref[0:params, :], c2_ref[params : 2 * params, :]
            a = p2_ref[0:params, :] * rs2
            b0 = a * inv_k * sums[0:params]
            c0 = a * inv_k * rs2 * sums[params : 2 * params]
            clear_edges(pad, px, grid)
            for b in range(4):
                p = b % params
                e = (y_ref[:, lanes(b)] - mean2[p : p + 1]) * c0[p : p + 1]
                e = (dn_ref[:, lanes(b)] * a[p : p + 1] - b0[p : p + 1] - e) * mask
                db_ref[:, lanes(b)] = e.astype(BF16)
                before, after = neighbours(e, px, grid)
                pack3(pad, b, e, after, before, px, grid)
            mean, rs = c1_ref[0:params, :], c1_ref[params : 2 * params, :]
            accs = [[jnp.zeros((8, LN), F32) for _ in range(params)] for _ in range(2)]
            for g in range(2):
                dh = None
                for i in range(3):
                    part = dot(pad[grid * i : grid * i + px, g * 768 : (g + 1) * 768], w_ref[2 - i])
                    dh = part if dh is None else dh + part
                for half in range(2):
                    b = g * 2 + half
                    p = b % params
                    xh = (pick_half(int_ref, o_ref, x_ref, b) - mean[p : p + 1]) * rs[p : p + 1]
                    v = xh * p1_ref[p : p + 1, :] + p1_ref[params + p : params + p + 1, :]
                    d = dh[:, half * LN : (half + 1) * LN] * gelu_both(v, half_mask)[1]
                    dn1_ref[:, lanes(b)] = d
                    accs[0][p] = accs[0][p] + rows8(d)
                    accs[1][p] = accs[1][p] + rows8(d * xh)
            row_ref[...] = jnp.zeros_like(row_ref)
            for q in range(2):
                for p in range(params):
                    row_ref[q * params + p : q * params + p + 1, :] = total(accs[q][p], fold)
            send(pay_ref, row_ref)

        extra = [other] if two else []
        return call(
            body,
            [((px, 512), BF16), ((px, 512), F32), ((4, LN), F32, "far"), ((n, 4, LN), F32, "far")],
            [pltpu.VMEM((4, LN), F32), pltpu.VMEM((px + 2 * grid, 2 * 768), BF16)],
            ints, counts, recv, dn, y, cst2, par2, wt, x, cst1, par1, *extra,
            **kw,
        )

    def slow_last(self, ints, counts, recv, dn, x, cst, par, dp, wa, wp, **kw):
        px, grid = self.px, self.grid

        def body(
            int_ref, n_ref, recv_ref, dn_ref, x_ref, cst_ref, par_ref, dp_ref, wa_ref, wp_ref,
            da_ref, d0_ref, d1_ref, sum_ref,
        ):
            mask = region(int_ref[0], px, grid)
            inv_k = 1.0 / (n_ref[:, 2:3, :].sum(axis=0) * float(TS // 2))
            sums = recv_ref[...].astype(F32).sum(axis=0)
            sum_ref[...] = sums
            mean, rs = cst_ref[0:2, :], cst_ref[2:4, :]
            a = par_ref[0:2, :] * rs
            b0 = a * inv_k * sums[0:2]
            c0 = a * inv_k * rs * sums[2:4]
            for b in range(4):
                p = b % 2
                e = (x_ref[:, lanes(b)] - mean[p : p + 1]) * c0[p : p + 1]
                e = (dn_ref[:, lanes(b)] * a[p : p + 1] - b0[p : p + 1] - e) * mask
                da_ref[:, lanes(b)] = e.astype(BF16)
            for t, out in ((0, d0_ref), (1, d1_ref)):
                out[...] = (
                    dot_t(da_ref[:, t * CS_MID : (t + 1) * CS_MID], wa_ref[...])
                    + dot_t(dp_ref[:, t * CS : (t + 1) * CS], wp_ref[...])
                ).astype(BF16)

        return call(
            body,
            [((px, 512), BF16), ((px, LAT), BF16), ((px, LAT), BF16), ((4, LN), F32, "far")],
            [],
            ints, counts, recv, dn, x, cst, par, dp, wa, wp,
            **kw,
        )

    def slow_input_grad(self, da, dp, wa, wp, **kw):
        px = self.px

        def body(da_ref, dp_ref, wa_ref, wp_ref, dx_ref):
            for t in range(2):
                dx_ref[:, t * CS : (t + 1) * CS] = (
                    dot_t(da_ref[:, t * CS_MID : (t + 1) * CS_MID], wa_ref[0:CS, :])
                    + dot_t(dp_ref[:, t * CS : (t + 1) * CS], wp_ref[0:CS, :])
                ).astype(BF16)

        return call(body, ((px, 2048), BF16, "far"), [], da, dp, wa, wp, smem=0, **kw)

    def fast_first_back(self, ints, counts, recv, dn_lo, dn_hi, fa_lo, fa_hi, cst, par, **kw):
        px, grid = self.px, self.grid

        def body(int_ref, n_ref, recv_ref, dl_ref, dh_ref, xl_ref, xh_ref, cst_ref, par_ref, da_ref, sum_ref):
            sums = recv_ref[...].sum(axis=0)
            sum_ref[...] = sums

            @pl.when(int_ref[1] == 1)
            def _():
                mask = region(int_ref[0], px, grid)
                inv_k = 1.0 / (n_ref[:, 2:3, :].sum(axis=0) * float(TF // 2))
                mean, rs = cst_ref[0:1, :], cst_ref[1:2, :]
                a = par_ref[0:1, :] * rs
                b0 = a * inv_k * sums[0:1]
                c0 = a * inv_k * rs * sums[1:2]
                for dn_ref, h_ref, base in ((dl_ref, xl_ref, 0), (dh_ref, xh_ref, 4)):
                    for b in range(4):
                        e = (h_ref[:, lanes(b)] - mean) * c0
                        e = (dn_ref[:, lanes(b)] * a - b0 - e) * mask
                        da_ref[:, lanes(base + b)] = e.astype(BF16)

        return call(
            body,
            [((px, 1024), BF16), ((4, LN), F32, "far")],
            [],
            ints, counts, recv, dn_lo, dn_hi, fa_lo, fa_hi, cst, par,
            **kw,
        )

    def fast_small(self, ints, da, xf, bc, bc_other, **kw):
        first = 3 * CF_MID
        rows = first + bc.shape[0]

        def body(int_ref, da_ref, x_ref, b0_ref, b1_ref, out_ref, row_ref, scratch):
            row_ref[0:first, :] = jnp.zeros((first, LN), F32)
            row_ref[first:rows, :] = b0_ref[...] + b1_ref[...]

            @pl.when(int_ref[1] == 1)
            def _():
                accs = [None] * 3
                for g in range(4):
                    lo, hi = max(8 * g - 1, 0), min(8 * g + 9, TF)
                    k0 = lo - (8 * g - 1)
                    d = dot(da_ref[:, g * 256 : (g + 1) * 256].T, x_ref[:, lo * CF : hi * CF])
                    for k in range(3):
                        for i in range(8):
                            j = i + k - k0
                            if 0 <= j < hi - lo:
                                part = d[i * CF_MID : (i + 1) * CF_MID, j * CF : (j + 1) * CF]
                                accs[k] = part if accs[k] is None else accs[k] + part
                for k in range(3):
                    tiled = jnp.concatenate([accs[k]] * 4, axis=0).T
                    row_ref[k * CF_MID : (k + 1) * CF_MID, :] = tiled_rows(scratch, tiled)

            out_ref[...] = row_ref[...].astype(BF16)

        return call(
            body,
            ((rows, LN), BF16, "far"),
            [pltpu.VMEM((rows, LN), F32), pltpu.VMEM((LN, LN), F32)],
            ints, da, xf, bc, bc_other,
            **kw,
        )

    def last(self, ints, da, ds_lo, ds_hi, band, dxs0, dxs1, **kw):
        px = self.px

        def body(int_ref, da_ref, sl_ref, sh_ref, band_ref, x0_ref, x1_ref, dx_ref, acc_ref, out_ref, sem):
            def part(g):
                at = slice(g * 1024, (g + 1) * 1024)
                return pltpu.make_async_copy(out_ref.at[:, at], dx_ref.at[:, at], sem.at[g])

            def half(ref, g):
                return pltpu.make_async_copy(ref, out_ref.at[:, g * 2048 : (g + 1) * 2048], sem.at[4 + g])

            @pl.when(int_ref[1] == 0)
            def _():
                half(x0_ref, 0).start()
                half(x1_ref, 1).start()
                for g in range(2):
                    half(x0_ref if g == 0 else x1_ref, g).wait()
                    part(2 * g).start()
                    part(2 * g + 1).start()
                for g in range(4):
                    part(g).wait()

            @pl.when(int_ref[1] == 1)
            def _():
                acc_ref[:, 0 : 10 * CF] = dot_t(da_ref[:, 0:256], band_ref[...])
                for g in range(4):
                    if g < 3:
                        p = dot_t(da_ref[:, (g + 1) * 256 : (g + 2) * 256], band_ref[...])
                        base = 8 * (g + 1) * CF
                        acc_ref[:, base : base + 2 * CF] += p[:, 0 : 2 * CF]
                        acc_ref[:, base + 2 * CF : base + 10 * CF] = p[:, 2 * CF :]
                    s_ref = sl_ref if g < 2 else sh_ref
                    for i in range(8):
                        f = 8 * g + i
                        s = s_ref[:, lanes(f % 16)] + acc_ref[:, lanes(f + 1)]
                        out_ref[:, lanes(f)] = s.astype(BF16)
                    part(g).start()
                for g in range(4):
                    part(g).wait()

        return call(
            body,
            ((px, 4096), BF16, "manual"),
            [pltpu.VMEM((px, 34 * CF), F32), pltpu.VMEM((px, 4096), BF16), pltpu.SemaphoreType.DMA((6,))],
            ints, da, ds_lo, ds_hi, band, Manual(dxs0), Manual(dxs1),
            **kw,
        )

    def halves(self, ints, x, x_other, cot, cot_other, **kw):
        px = self.px

        def body(int_ref, x_ref, xo_ref, c_ref, co_ref, xs_ref, xf_ref, gs_ref, gf_ref, sem):
            def run(pairs):
                copies = [pltpu.make_async_copy(a, b, sem.at[k]) for k, (a, b) in enumerate(pairs)]
                for c in copies:
                    c.start()
                for c in copies:
                    c.wait()

            lo, hi = slice(0, 2048), slice(2048, 4096)

            @pl.when(int_ref[1] == 0)
            def _():
                xf_ref[:, 0 : 2 * CF] = jnp.zeros((px, 2 * CF), BF16)
                run([
                    (x_ref.at[:, lo], xs_ref), (xo_ref.at[:, lo], xf_ref.at[:, 2 * CF : 18 * CF]),
                    (c_ref.at[:, lo], gs_ref), (co_ref.at[:, lo], gf_ref),
                ])

            @pl.when(int_ref[1] == 1)
            def _():
                run([
                    (xo_ref.at[:, hi], xs_ref), (x_ref.at[:, 14 * CF :], xf_ref),
                    (co_ref.at[:, hi], gs_ref), (c_ref.at[:, hi], gf_ref),
                ])

        wide = ((px, 2048), BF16)
        return call(
            body,
            [wide, ((px, 18 * CF), BF16), wide, wide],
            [pltpu.SemaphoreType.DMA((4,))],
            ints, Manual(x), Manual(x_other), Manual(cot), Manual(cot_other),
            **kw,
        )

    def out_send(self, ints, ys, yf, **kw):
        px = self.px

        def body(int_ref, ys_ref, yf_ref, out_ref):
            for path, ref, at in ((0, yf_ref, 2 * CF), (1, ys_ref, 0)):

                @pl.when(int_ref[1] == path)
                def _():
                    out_ref[...] = ref[:, at : at + 2048]

        return call(body, ((px, 2048), BF16, "far"), [], ints, ys, yf, **kw)

    def out_join(self, ints, ys, yf, other, **kw):
        px = self.px

        def body(int_ref, ys_ref, yf_ref, o_ref, out_ref):
            for path, ref, at in ((0, ys_ref, 0), (1, yf_ref, 2 * CF)):

                @pl.when(int_ref[1] == path)
                def _():
                    mine, far = path * 2048, (1 - path) * 2048
                    out_ref[:, mine : mine + 2048] = ref[:, at : at + 2048]
                    out_ref[:, far : far + 2048] = o_ref[...]

        return call(body, ((px, 4096), BF16, "far"), [], ints, ys, yf, Far(other), **kw)

    def fast_grads_bc(self, h1, db, h2, dc, **kw):
        px, grid = self.px, self.grid

        def body(h1_ref, db_ref, h2_ref, dc_ref, out_ref, pad, scratch):
            clear_edges(pad, px, grid)
            for b in range(4):
                h = h1_ref[:, lanes(b)].astype(F32)
                before, after = neighbours(h, px, grid)
                pack3(pad, b, h, before, after, px, grid)
            same = (lax.broadcasted_iota(jnp.int32, (256, 256), 0) >> 5) == (
                lax.broadcasted_iota(jnp.int32, (256, 256), 1) >> 5
            )
            for i in range(3):
                for s in range(3):
                    acc = jnp.zeros((256, 256), F32)
                    for g in range(2):
                        at = g * 768 + s * 256
                        acc = acc + dot(
                            pad[grid * i : grid * i + px, at : at + 256].T,
                            db_ref[:, g * 256 : (g + 1) * 256],
                        )
                    acc = jnp.where(same, acc, 0.0).reshape(8, CF_MID, 256).sum(axis=0)
                    at = (3 * i + s) * 8
                    out_ref[at : at + 8, :] = tiled_rows(scratch, fold32(acc))
            acc = jnp.zeros((256, 1024), F32)
            for g in range(2):
                acc = acc + dot(h2_ref[:, g * 256 : (g + 1) * 256].T, dc_ref[:, g * 1024 : (g + 1) * 1024])
            out = None
            for i in range(8):
                part = acc[i * CF_MID : (i + 1) * CF_MID, i * CF : (i + 1) * CF]
                out = part if out is None else out + part
            out_ref[72:104, :] = out
            out_ref[104:, :] = jnp.zeros((8, LN), F32)

        return call(
            body,
            ((112, LN), F32, "far"),
            [pltpu.VMEM((px + 2 * grid, 2 * 768), BF16), pltpu.VMEM((CF_MID, LN), F32)],
            h1, db, h2, dc, smem=0,
            **kw,
        )

    def grads_early(self, plan, ints, xs, lat, dp, h2, dc, **kw):
        px = self.px
        rows = plan.early

        def body(int_ref, x_ref, lat_ref, dp_ref, h2_ref, dc_ref, keep_ref, send_ref, buf, xt):
            def put(base, q, acc):
                for j in range(2):
                    buf[pl.ds(base + 2 * q + j, 256, stride=8), :] = acc[:, j * LN : (j + 1) * LN]

            for c in range(6):
                for t in range(2):
                    if c == 5:
                        x = h2_ref[:, t * 256 : (t + 1) * 256]
                    elif c == 4:
                        x = lat_ref[:, t * LAT : (t + 1) * LAT]
                    else:
                        x = x_ref[:, t * CS + c * 256 : t * CS + (c + 1) * 256]
                    xt[:, t * px : (t + 1) * px] = x.T
                source = dc_ref if c == 5 else dp_ref
                base = (ROW_SC if c == 5 else ROW_SP + c * 2048) - ROW_SC
                for q in range(4):
                    acc = None
                    for t in range(2):
                        at = t * CS + q * 256
                        part = dot(xt[:, t * px : (t + 1) * px], source[:, at : at + 256])
                        acc = part if acc is None else acc + part
                    put(base, q, acc)
            lo = 0
            hi = plan.base[1] - ROW_SC
            mine = pl.multiple_of(jnp.where(int_ref[1] == 0, lo, hi), 16)
            other = pl.multiple_of(jnp.where(int_ref[1] == 0, hi, lo), 16)
            keep_ref[...] = buf[pl.ds(mine, rows), :].astype(BF16)
            send_ref[...] = buf[pl.ds(other, rows), :].astype(BF16)

        return call(
            body,
            [((rows, LN), BF16, "far"), ((rows, LN), BF16, "far")],
            [pltpu.VMEM((ROW_SG - ROW_SC, LN), F32), pltpu.VMEM((256, 2 * px), BF16)],
            ints, xs, lat, dp, h2, dc,
            **kw,
        )

    def grads_conv(self, h1, db, **kw):
        px, grid = self.px, self.grid

        def body(h1_ref, db_ref, out_ref, buf, pad):
            clear_edges(pad, px, grid)
            for b in range(4):
                h = h1_ref[:, lanes(b)].astype(F32)
                before, after = neighbours(h, px, grid)
                pack3(pad, b, h, before, after, px, grid)
            for i in range(3):
                for s in range(3):
                    acc = None
                    for t in range(2):
                        at = t * 768 + s * 256
                        part = dot(
                            pad[grid * i : grid * i + px, at : at + 256].T,
                            db_ref[:, t * 256 : (t + 1) * 256],
                        )
                        acc = part if acc is None else acc + part
                    for j in range(2):
                        buf[pl.ds((3 * i + s) * 512 + j, 256, stride=2), :] = acc[:, j * LN : (j + 1) * LN]
            out_ref[...] = buf[...].astype(BF16)

        return call(
            body,
            ((ROW_SC - ROW_SB, LN), BF16, "far"),
            [pltpu.VMEM((ROW_SC - ROW_SB, LN), F32), pltpu.VMEM((px + 2 * grid, 2 * 768), BF16)],
            h1, db, smem=0,
            **kw,
        )

    def grads_late(self, ints, xs, lat, da, yf, dl0, dl1, **kw):
        px = self.px
        rows = ROW_SB - ROW_SA
        lat_rows = ROW_FG - ROW_LAT

        def body(int_ref, x_ref, lat_ref, da_ref, yf_ref, d0_ref, d1_ref, keep_ref, send_ref, buf):
            for c in range(5):
                acc = None
                for t in range(2):
                    if c == 4:
                        x = lat_ref[:, t * LAT : (t + 1) * LAT]
                    else:
                        x = x_ref[:, t * CS + c * 256 : t * CS + (c + 1) * 256]
                    part = dot(x.T, da_ref[:, t * CS_MID : (t + 1) * CS_MID])
                    acc = part if acc is None else acc + part
                for j in range(2):
                    buf[pl.ds(c * 512 + j, 256, stride=2), :] = acc[:, j * LN : (j + 1) * LN]
            for k in range(5):
                acc = dot(yf_ref[:, lanes(k)].T, d0_ref[...]) + dot(yf_ref[:, lanes(8 + k)].T, d1_ref[...])
                for j in range(2):
                    buf[pl.ds(rows + k * 256 + j, CF, stride=2), :] = acc[:, j * LN : (j + 1) * LN]
            mine = pl.multiple_of(jnp.where(int_ref[1] == 0, 0, rows), 16)
            other = pl.multiple_of(jnp.where(int_ref[1] == 0, rows, 0), 16)
            keep_ref[...] = buf[pl.ds(mine, rows), :].astype(BF16)
            send_ref[...] = buf[pl.ds(other, rows), :].astype(BF16)

        return call(
            body,
            [((rows, LN), BF16, "far"), ((rows, LN), BF16, "far")],
            [pltpu.VMEM((2 * rows, LN), F32)],
            ints, xs, lat, da, yf, dl0, dl1,
            **kw,
        )

    def windows(self, plan, ints, early, conv, late, **kw):
        ndp, chunk, half = self.ndp, plan.chunk, self.ndp // 2

        def body(int_ref, e0_ref, e1_ref, c0_ref, c1_ref, l0_ref, l1_ref, keep_ref, send_ref, buf):
            def add(a, b, rows):
                return a[0:rows, :].astype(F32) + b[0:rows, :].astype(F32)

            for path in range(2):

                @pl.when(int_ref[1] == path)
                def _():
                    buf[...] = jnp.zeros_like(buf)
                    base = plan.base[path]
                    if path == 0:
                        buf[ROW_SA:ROW_SB, :] = add(l0_ref, l1_ref, ROW_SB - ROW_SA)
                        buf[ROW_SB:ROW_SC, :] = add(c0_ref, c1_ref, ROW_SC - ROW_SB)
                        rest = min(plan.length - ROW_SC, plan.early)
                        buf[ROW_SC : ROW_SC + rest, :] = add(e0_ref, e1_ref, rest)
                    else:
                        rest = ROW_SG - base
                        buf[0:rest, :] = add(e0_ref, e1_ref, rest)
                        at = ROW_LAT - base
                        buf[at : at + ROW_FG - ROW_LAT, :] = add(l0_ref, l1_ref, ROW_FG - ROW_LAT)

            path = int_ref[1]
            base = jnp.where(path == 0, plan.base[0], plan.base[1])

            def stretch(place):
                j = 0
                for step in range(plan.bits):
                    bit = (place >> (plan.bits - 1 - step)) & 1
                    j = j + jnp.where(
                        path == 0, bit << plan.order[0][step], bit << plan.order[1][step]
                    )
                at = ((path * ndp + j) * plan.share) // (16 * LN) * 16 - base
                return buf[pl.ds(pl.multiple_of(at, 16), chunk), :].astype(BF16)

            def step(q, carry):
                bit = int_ref[5]
                keep_ref[q] = stretch(bit * half + q)
                send_ref[q] = stretch((1 - bit) * half + q)
                return carry

            loop(half, step, 0)

        return call(
            body,
            [((half, chunk, LN), BF16, "far")] * 2,
            [pltpu.VMEM((plan.length, LN), F32)],
            ints, *early, *conv, *late,
            **kw,
        )

    def halve(self, plan, ints, step, keep, came, **kw):
        half = keep.shape[0] // 2

        def body(int_ref, a_ref, b_ref, keep_ref, send_ref):
            bit = int_ref[5 + step]

            def one(q, carry):
                for out, at in ((keep_ref, bit * half + q), (send_ref, (1 - bit) * half + q)):
                    out[q] = (a_ref[at].astype(F32) + b_ref[at].astype(F32)).astype(BF16)
                return carry

            loop(half, one, 0)

        return call(
            body,
            [((half, plan.chunk, LN), BF16, "far")] * 2,
            [],
            ints, Far(keep), came,
            **kw,
        )

    def add(self, parts, **kw):
        def body(*refs):
            refs[-1][...] = sum(r[...].astype(F32) for r in refs[:-1]).astype(BF16)

        return call(body, (parts[0].shape, BF16, "far"), [], Far(parts[0]), *parts[1:], smem=0, **kw)

    def window(self, plan, ints, keep, came, parts, vectors, tail, **kw):
        chunk, out_rows = plan.chunk, plan.out_rows
        extra, count = parts[0].shape[0], len(parts)
        pad = extra + 8

        def body(int_ref, keep_ref, came_ref, vec_ref, tail_ref, *refs):
            out_ref, a_ref, small_ref = refs[count:]
            r0 = int_ref[2]
            row = int_ref[3]
            lane = int_ref[4]
            a_ref[...] = jnp.zeros_like(a_ref)
            total = sum(r[...].astype(F32) for r in refs[:count])
            small_ref[...] = jnp.where(int_ref[1] == 1, total, 0.0)
            for ref, start, n in (
                (vec_ref, ROW_SG, 2 * SLOW_VEC), (small_ref, ROW_FA, ROW_LAT - ROW_FA), (tail_ref, ROW_FG, 3)
            ):
                at = jnp.clip(start - r0, -n, chunk) + pad
                a_ref[pl.ds(at, n), :] += ref[0:n, :]
            a_ref[pad : pad + chunk, :] += keep_ref[0].astype(F32) + came_ref[0].astype(F32)
            one = a_ref[pl.ds(pad + row, out_rows), :]
            two = a_ref[pl.ds(pad + row + 1, out_rows), :]
            shift = (LN - lane) & (LN - 1)
            one = pltpu.roll(one, shift, 1)
            two = pltpu.roll(two, shift, 1)
            at = lax.broadcasted_iota(jnp.int32, (out_rows, LN), 1)
            out_ref[...] = jnp.where(at < LN - lane, one, two)

        return call(
            body,
            ((out_rows, LN), F32, "far"),
            [pltpu.VMEM((chunk + 2 * pad + 8, LN), F32), pltpu.VMEM((extra, LN), F32)],
            ints, keep, came, vectors, tail, *parts,
            **kw,
        )


class Plan:
    def __init__(self, ndp):
        n = 2 * ndp
        self.ndp = ndp
        self.share = VALUES // n
        self.first = [self.share * d // LN // 16 * 16 for d in range(n)]
        ends = [-(-self.share * (d + 1) // LN) for d in range(n)]
        self.chunk = -(-max(e - f for e, f in zip(ends, self.first)) // 16) * 16
        self.base = [self.first[0], self.first[ndp]]
        self.length = max(
            self.first[q * ndp + ndp - 1] + self.chunk - self.base[q] for q in range(2)
        )
        self.early = ROW_SG - self.base[1]
        self.out_rows = -(-self.share // LN)
        self.bits = ndp.bit_length() - 1
        one = list(range(self.bits))
        two = one[1:] + one[:1]
        self.order = [one, two]
        self.stages = [
            [m << b for m in range(1, 1 << min(2, self.bits - b))] for b in range(0, self.bits, 2)
        ]

    def place(self, path, j):
        at = 0
        for b in self.order[path]:
            at = 2 * at + ((j >> b) & 1)
        return at

    def route(self, mask):
        return [(q * self.ndp + j, q * self.ndp + (j ^ mask)) for q in range(2) for j in range(self.ndp)]

    def pairs(self, step):
        out = []
        for q in range(2):
            b = self.order[q][step]
            out += [(q * self.ndp + j, q * self.ndp + (j ^ (1 << b))) for j in range(self.ndp)]
        return out


def exchange(x):
    return lax.all_to_all(x, ("path", "dp"), 0, 0)


def swap(x):
    x = x.array if isinstance(x, Near) else x
    return lax.ppermute(x, "path", SWAP)


def local(
    acts, cotangent, clip_res, w_slow_a, w_slow_b, w_slow_c, w_slow_proj, slow_gain, slow_bias,
    w_fast_a, w_fast_b, w_fast_c, w_lateral, fast_gain, fast_bias,
):
    grid = acts.shape[2]
    px = grid * grid
    ndp = lax.axis_size("dp")
    net = Net(ndp, grid)
    plan = Plan(ndp)
    path, chip = lax.axis_index("path"), lax.axis_index("dp")
    core0 = path == 0
    level = clip_res[0]
    side = jnp.where(
        level == 1, grid * 5 // 8, jnp.where(level == 2, grid * 7 // 8, jnp.where(level == 3, grid, 0))
    )
    start = (path * ndp + chip) * plan.share
    r0 = start // LN // 16 * 16
    off = start - r0 * LN
    bits = [
        jnp.where(core0, chip >> plan.order[0][s], chip >> plan.order[1][s]) & 1 for s in range(plan.bits)
    ]
    ints = jnp.stack([side, path, r0, off // LN, off % LN] + bits).astype(jnp.int32)
    x = acts.reshape(px, 4096)
    cot = cotangent.reshape(px, 4096)
    sg, sb_ = slow_gain.reshape(SLOW_VEC, LN), slow_bias.reshape(SLOW_VEC, LN)

    def slow_par(a, b):
        return jnp.concatenate([sg[a:b], sb_[a:b]], axis=0)

    def fast_par(a, b):
        one = jnp.stack([fast_gain[a:b], fast_bias[a:b]])
        return jnp.tile(one, (1, LN // (b - a)))

    wlat = w_lateral.reshape(5 * CF, LAT)
    wa_lat = Far(w_slow_a, (LAT, CS_MID), (CS // LAT, 0))
    wp_lat = Far(w_slow_proj, (LAT, CS), (CS // LAT, 0))
    f1, f2, f3 = fast_par(0, 32), fast_par(32, 64), fast_par(64, 192)
    s1, s2, s3, s4 = slow_par(0, 2), slow_par(2, 4), slow_par(4, 12), slow_par(12, 20)
    wb3 = w_slow_b.reshape(3, 768, 256)
    wbt3 = w_slow_b.transpose(0, 2, 1).reshape(3, 768, 256)
    half = TF // 2

    x_other = swap(x)
    cot_other = swap(cot)

    fa_lo, fa_hi, band, pay = net.fast_first(ints, Far(x), Far(w_fast_a.transpose(0, 2, 1)), us=3.5)
    (fb_w, fbt_w, fc_w), tok = net.fast_weights(
        w_fast_b, w_fast_b.transpose(0, 2, 1), w_fast_c, us=1.0, after=[pay], token=True
    )
    fa_other = swap(fa_lo)
    r1 = exchange(pay)
    fh1, fb, fc1, pay, r1 = net.conv_stage(
        ints, r1, r1, fa_hi, f1, fb_w, 1, half, fa_other, us=2.7, after=[tok]
    )
    (xs, xf, gs, gf), tok = net.halves(ints, x, x_other, cot, cot_other, us=2.5, after=[pay], token=True)
    r = exchange(pay)
    fh2, fc2, pay, fh2_edge = net.expand_stage(
        ints, r, r1, fb, f2, fc_w, 1, 1, half, True, us=2.6, after=[tok]
    )
    fh2_other = swap(fh2_edge)
    (pa, pp), tok = net.slow_start(xs, Far(w_slow_a), Far(w_slow_proj), us=3.5, after=[pay], token=True)
    r = exchange(pay)
    yf, lat, fc3, sa, pay = net.fast_finish(
        ints, r, r1, fh2, fh2_other, fc_w, xf, f3, wlat, pa, wa_lat, us=5.0, after=[tok]
    )

    (sp, sp_rows), tok = net.slow_join(ints, pp, lat, wp_lat, 8, us=3.0, after=[pay], token=True)
    r = exchange(pay)
    sh1, sb, sc1, pay = net.conv_stage(
        ints, r, r1, sa, s1, wb3, 2, TS // 2, more=sp_rows, us=3.0, after=[tok]
    )
    rp = exchange(pay)
    gp, tok = net.fast_slope(ints, fh2, fc_w, xf, f3, fc3, us=4.0, after=[pay], token=True)
    sh2, sc2, pay = net.expand_stage(ints, rp, r1, sb, s2, w_slow_c, 2, 8, TS // 2, us=3.0, after=[tok])
    r = exchange(pay)
    ys, ds, scc, scp, pay = net.slow_top(ints, r, rp, r1, sh2, w_slow_c, sp, gs, s3, s4, us=6.0)

    sent, tok = net.out_send(ints, ys, yf, us=2.0, after=[pay], token=True)
    r = exchange(pay)
    (dp, dc, dn, t3, pay), (sent,) = net.expand_back(
        ints, r1, r, ds, sh2, w_slow_c, scc, s3, sb, sc2, s2, 2, 8, TS // 2, (sp, scp, s4),
        us=6.0, after=[tok], through=[sent],
    )
    theirs = swap(sent)
    (early, early_out), tok = net.grads_early(
        plan, ints, xs, lat, dp, sh2, dc, us=6.0, after=[pay], token=True
    )
    r = exchange(pay)
    (db, dn, t2, pay), (early_out,) = net.conv_back(
        ints, r1, r, dn, sb, sc2, s2, wbt3, sa, sc1, s1, 2, TS // 2, us=3.0, after=[tok], through=[early_out]
    )
    early_in = swap(early_out)
    conv, tok = net.grads_conv(sh1, db, us=3.0, after=[pay], token=True)
    out, tok = net.out_join(ints, ys, yf, theirs, us=3.0, after=[tok], token=True)
    r = exchange(pay)
    (da, dl0, dl1, t1), (conv_out,) = net.slow_last(
        ints, r1, r, dn, sa, sc1, s1, dp, wa_lat, wp_lat, us=3.0, after=[tok], through=[conv]
    )
    dl_other = swap(dl0)
    (late, late_out), tok = net.grads_late(ints, xs, lat, da, yf, dl0, dl1, us=4.0, token=True)

    (fds, pay), (conv_out, late_out) = net.fast_top(
        ints, dl0, dl1, dl_other, wlat, gf, gp, fh2, fc_w, fc3, us=4.0, through=[conv_out, late_out]
    )
    conv_in = swap(conv_out)
    late_in = swap(late_out)
    fds_lo = swap(fds)
    (keep, there), tok = net.windows(
        plan, ints, (Far(early), early_in), (Far(conv_out), conv_in), (Far(late), late_in),
        us=6.0, after=[pay], token=True,
    )
    r = exchange(pay)
    (fdc, dn, u3, pay), (there,) = net.expand_back(
        ints, r1, r, fds, fh2, fc_w, fc3, f3, fb, fc2, f2, 1, 1, half,
        us=5.0, after=[tok], through=[there],
    )
    here = lax.ppermute(there, ("path", "dp"), plan.pairs(0))
    dxs, tok = net.slow_input_grad(da, dp, Far(w_slow_a), Far(w_slow_proj), us=4.0, after=[pay], token=True)
    (keep, there), tok = net.halve(plan, ints, 1, keep, here, us=3.0, after=[tok], token=True)
    r = exchange(pay)
    (fdb, dn, u2, pay), (dxs_out, there) = net.conv_back(
        ints, r1, r, dn, fb, fc2, f2, fbt_w, fa_hi, fc1, f1, 1, half, fa_other,
        us=4.0, after=[tok], through=[dxs, there],
    )
    dn_lo = swap(dn)
    here = lax.ppermute(there, ("path", "dp"), plan.pairs(1))
    bc, tok = net.fast_grads_bc(fh1, fdb, fh2, fdc, us=4.0, after=[pay], token=True)
    (keep, there), tok = net.halve(plan, ints, 2, keep, here, us=2.5, after=[tok], token=True)
    r = exchange(pay)
    (fda, u1), (bc, there) = net.fast_first_back(
        ints, r1, r, dn_lo, dn, Far(fa_lo), fa_hi, fc1, f1, us=2.5, after=[tok], through=[bc, there]
    )
    bc_other = swap(bc)
    dxs_other = swap(dxs_out)
    small = net.fast_small(ints, fda, Far(x), bc, bc_other, us=3.0, after=[fds_lo])
    here = lax.ppermute(there, ("path", "dp"), plan.pairs(2))
    for step in range(3, plan.bits):
        keep, there = net.halve(plan, ints, step, keep, here, us=2.5, after=[small])
        here = lax.ppermute(there, ("path", "dp"), plan.pairs(step))
    for k, masks in enumerate(plan.stages):
        parts = [small] + [lax.ppermute(small, ("path", "dp"), plan.route(m)) for m in masks]
        if k < len(plan.stages) - 1:
            small = net.add(parts, us=1.0, after=[keep] if k == 0 else [])
    dx = net.last(ints, fda, Far(fds_lo), fds, band, dxs_out, dxs_other, us=4.5, after=[small])

    vectors = jnp.concatenate([t1[2:4], t2[2:4], t3[8:24], t1[0:2], t2[0:2], t3[0:8], t3[0:8]], axis=0)
    tail = jnp.concatenate([u1[1, :32], u2[1, :32], u3[1], u1[0, :32], u2[0, :32], u3[0]]).reshape(3, LN)
    tail = jnp.pad(tail, ((0, 5), (0, 0)))
    flat = net.window(plan, ints, keep, here, parts, vectors, tail).reshape(-1)[: plan.share]
    return (out.reshape(acts.shape), dx.reshape(acts.shape), flat)


def solution(mesh):
    data = P("path", "dp", None, None, None)
    in_specs = (data, data, P("dp")) + (P(),) * 12
    out_specs = (data, data, P(("path", "dp")))
    return jax.shard_map(local, mesh=mesh, in_specs=in_specs, out_specs=out_specs, check_vma=False)
```

```python
import functools

import jax
import jax.numpy as jnp
from jax import lax
from jax.experimental import pallas as pl
from jax.experimental.pallas import tpu as pltpu
from jax.sharding import PartitionSpec as P

TS = 4
ALPHA = 8
CS = 1024
CS_MID = 256
CF = 128
CF_MID = 32
LAT = 256
TF = 32
LN = 128
EPS = 1e-05
GELU_C = 0.7978845608028654
GELU_A = 0.044715

F32 = jnp.float32
BF16 = jnp.bfloat16
SWAP = [(0, 1), (1, 0)]

ROW_SA = 0
ROW_SB = ROW_SA + (CS + LAT) * CS_MID // LN
ROW_SC = ROW_SB + 9 * CS_MID * CS_MID // LN
ROW_SP = ROW_SC + CS_MID * CS // LN
ROW_SG = ROW_SP + (CS + LAT) * CS // LN
SLOW_VEC = (2 * CS_MID + 2 * CS) // LN
ROW_FA = ROW_SG + 2 * SLOW_VEC
ROW_LAT = ROW_FA + (3 * CF * CF_MID + 9 * CF_MID * CF_MID + CF_MID * CF) // LN
ROW_FG = ROW_LAT + 5 * CF * LAT // LN
VALUES = 2685312


def dot(a, b):
    return lax.dot_general(a, b, (((1,), (0,)), ((), ())), preferred_element_type=F32)


def dot_t(a, b):
    return lax.dot_general(a, b, (((1,), (1,)), ((), ())), preferred_element_type=F32)


class Near:
    def __init__(self, array):
        self.array = array


class Far:
    def __init__(self, array, block=None, index=None):
        self.array = pltpu.with_memory_space_constraint(array, pltpu.HBM)
        self.block, self.index = block, index


class Manual(Far):
    def __init__(self, array, pinned=True):
        if isinstance(array, Near):
            self.array = pltpu.with_memory_space_constraint(array.array, pltpu.HBM)
        else:
            self.array = pltpu.with_memory_space_constraint(array, pltpu.HBM) if pinned else array
        self.block = None


def dot_l(a, b):
    return lax.dot_general(a, b, (((0,), (0,)), ((), ())), preferred_element_type=F32)


def call(body, outs, scratch, *args, smem=1, limit=20, us=2.0, after=(), token=False, through=()):
    one = not isinstance(outs, list)
    shapes, out_specs, specs, operands = [], [], [], []
    vmem, anywhere = pl.BlockSpec(memory_space=pltpu.VMEM), pl.BlockSpec(memory_space=pl.ANY)
    for out in [outs] if one else outs:
        place = out[2] if len(out) > 2 else "near"
        shapes.append(pltpu.HBM(out[0], out[1]))
        out_specs.append(anywhere if place == "manual" else vmem)
    if token:
        shapes.append(pltpu.HBM((8, LN), F32))
        out_specs.append(anywhere)
    for k, a in enumerate(args):
        if k < smem:
            specs.append(pl.BlockSpec(memory_space=pltpu.SMEM))
        elif isinstance(a, Manual):
            specs.append(anywhere)
        elif isinstance(a, Far) and a.block is not None:
            index = a.index
            specs.append(pl.BlockSpec(a.block, lambda i, index=index: index))
        else:
            specs.append(vmem)
        if isinstance(a, Near):
            a = pltpu.with_memory_space_constraint(a.array, pltpu.HBM)
        operands.append(a.array if isinstance(a, Far) else a)
    for a in after:
        specs.append(anywhere)
        operands.append(pltpu.with_memory_space_constraint(a, pltpu.HBM))
    aliases = {}
    for a in through:
        aliases[len(operands)] = len(shapes)
        specs.append(anywhere)
        operands.append(pltpu.with_memory_space_constraint(a, pltpu.HBM))
        shapes.append(pltpu.HBM(a.shape, a.dtype))
        out_specs.append(anywhere)
    n_in, n_out = len(args), len(shapes) - token - len(through)
    cut = any(isinstance(a, Far) and a.block is not None for a in args)

    def wrapped(*refs):
        rest = refs[n_in + len(after) + len(through) :]
        body(*refs[:n_in], *rest[:n_out], *rest[n_out + token + len(through) :])

    res = pl.pallas_call(
        wrapped,
        out_shape=shapes,
        grid=(1,) if cut else (),
        in_specs=specs,
        out_specs=out_specs,
        scratch_shapes=scratch,
        input_output_aliases=aliases,
        cost_estimate=pl.CostEstimate(flops=int(us * 1e9), bytes_accessed=0, transcendentals=0),
        compiler_params=pltpu.CompilerParams(vmem_limit_bytes=limit * 1024 * 1024),
    )(*operands)
    got = [
        Near(r) if len(out) == 2 else r for r, out in zip(res, [outs] if one else outs)
    ]
    got = got[0] if one else got
    if through:
        return got, list(res[n_out + token :])
    return (got, res[n_out]) if token else got


def lanes(index):
    if isinstance(index, int):
        return slice(index * LN, (index + 1) * LN)
    return pl.ds(pl.multiple_of(index * LN, LN), LN)


def region(side, px, grid):
    bits = grid.bit_length() - 1
    r = lax.broadcasted_iota(jnp.int32, (px, LN), 0)
    inside = jnp.logical_and((r >> bits) < side, (r & (grid - 1)) < side)
    return jnp.where(inside, 1.0, 0.0).astype(F32)


def rows8(x):
    return x.reshape(x.shape[0] // 8, 8, LN).sum(axis=0)


def total(acc, fold):
    if fold:
        acc = acc + pltpu.roll(acc, 32, 1)
        acc = acc + pltpu.roll(acc, 64, 1)
    return acc.sum(axis=0, keepdims=True)


def gelu(v, half_mask):
    t = jnp.tanh(v * (GELU_C + (GELU_C * GELU_A) * (v * v)))
    return v * (half_mask + half_mask * t)


def gelu_both(v, half_mask):
    w = GELU_C + (GELU_C * GELU_A) * (v * v)
    t = jnp.tanh(v * w)
    q = half_mask + half_mask * t
    return v * q, q * (1.0 + (v - v * t) * (3.0 * w - 2.0 * GELU_C))


def loop(n, body, init, unroll=False):
    if unroll:
        for i in range(n):
            init = body(i, init)
        return init
    return lax.fori_loop(0, n, body, init)


def moments(ref, out, row, blocks, params, fold, mask, count):
    inv = 1.0 / jnp.maximum(count, 1.0)
    for p in range(params):
        n = blocks // params

        def first(i, acc):
            return acc + rows8(ref[:, lanes(p + i * params)] * mask)

        zero = jnp.zeros((8, LN), F32)
        s = total(loop(n, first, zero, n <= 4), fold)
        mean = s * inv

        def second(i, acc):
            d = (ref[:, lanes(p + i * params)] - mean) * mask
            return acc + rows8(d * d)

        m2 = total(loop(n, second, zero, n <= 4), fold)
        out[row + p : row + p + 1, :] = s
        out[row + params + p : row + params + p + 1, :] = m2


def send(pay_ref, rows_ref):
    value = rows_ref[...].astype(pay_ref.dtype)
    for d in range(pay_ref.shape[0]):
        pay_ref[d] = value


def split(v):
    high = v.astype(BF16).astype(F32)
    return high, v - high


def encode(code_ref, rows_ref, narrow, wide):
    at = 0
    if narrow:
        high, low = split(rows_ref[0:narrow, :])
        code_ref[0:narrow, :] = high
        code_ref[narrow : 2 * narrow, :] = low
        at = 2 * narrow
    if wide:
        high, low = split(rows_ref[narrow : narrow + wide, :])
        code_ref[at : at + wide, :] = high
        code_ref[at + wide : at + 2 * wide, :] = low
        code_ref[at + 2 * wide : at + 3 * wide, :] = rows_ref[narrow + wide : narrow + 2 * wide, :]


def combine(recv, row, params, n, cst_ref):
    combine_sums(recv[:, row : row + params, :], recv[:, row + params : row + 2 * params, :], n, params, cst_ref)


def combine_coded(recv, row, params, n, cst_ref, narrow=False):
    v = recv.astype(F32)
    if narrow:
        v = v[:, 0 : 2 * params] + v[:, 2 * params : 4 * params]
        combine_sums(v[:, 0:params], v[:, params:], n, params, cst_ref)
        return
    s = v[:, row : row + params] + v[:, row + params : row + 2 * params]
    combine_sums(s, v[:, row + 2 * params : row + 3 * params], n, params, cst_ref)


def combine_sums(s, m2, n, params, cst_ref):
    k = n.sum(axis=0)
    mean = s.sum(axis=0) / k
    off = s / jnp.maximum(n, 1.0) - mean[None]
    cst_ref[0:params, :] = mean
    cst_ref[params : 2 * params, :] = lax.rsqrt((m2 + n * off * off).sum(axis=0) / k + EPS)


def pick_half(int_ref, other_ref, ref, b):
    if other_ref is None:
        return ref[:, lanes(b)]
    return jnp.where(int_ref[1] == 0, other_ref[:, lanes(b)], ref[:, lanes(b)])


def fold32(v):
    v = v[:, 0:LN] + v[:, LN:256]
    v = v + pltpu.roll(v, 32, 1)
    return v + pltpu.roll(v, 64, 1)


def tiled_rows(scratch, tiled):
    c = tiled.shape[0]
    scratch[0:c, :] = tiled
    group = lax.broadcasted_iota(jnp.int32, (c // 4, LN), 1) >> 5
    out = jnp.zeros((c // 4, LN), F32)
    for q in range(4):
        out = jnp.where(group == q, scratch[pl.ds(q, c // 4, stride=4), :], out)
    return out


def pack3(pad, b, mid, left, right, px, grid):
    g, half = b // 2, b % 2
    for slot, value in enumerate((left, mid, right)):
        at = g * 768 + slot * 256 + half * 128
        pad[grid : grid + px, at : at + LN] = value.astype(BF16)


def neighbours(h, px, grid):
    col = lax.broadcasted_iota(jnp.int32, (px, LN), 0) & (grid - 1)
    before = jnp.where(col == 0, 0.0, pltpu.roll(h, 1, 0))
    after = jnp.where(col == grid - 1, 0.0, pltpu.roll(h, px - 1, 0))
    return before, after


def clear_edges(pad, px, grid):
    zero = jnp.zeros((grid, pad.shape[1]), BF16)
    pad[0:grid, :] = zero
    pad[grid + px : grid + px + grid, :] = zero


def put_count(rows_ref, row, count):
    rows_ref[row : row + 1, :] = jnp.zeros((1, LN), F32) + count


def side_sq(side, frames):
    s = side.astype(F32)
    return s * s * frames


class Net:
    def __init__(self, ndp, grid):
        self.ndp = ndp
        self.n = 2 * ndp
        self.grid = grid
        self.px = grid * grid

    def fast_first(self, ints, xf, wa, **kw):
        px, grid, n = self.px, self.grid, self.n

        def body(int_ref, xf_ref, wa_ref, lo_ref, hi_ref, band_ref, pay_ref, row_ref, fa_ref):
            side = int_ref[0]
            row_ref[...] = jnp.zeros_like(row_ref)

            @pl.when(int_ref[1] == 1)
            def _():
                pick = jnp.where(
                    (lax.broadcasted_iota(jnp.int32, (CF_MID, 256), 1) & (CF_MID - 1))
                    == lax.broadcasted_iota(jnp.int32, (CF_MID, 256), 0),
                    1.0,
                    0.0,
                ).astype(BF16)
                wide = [dot_l(wa_ref[k], pick) for k in range(3)]
                group = lax.broadcasted_iota(jnp.int32, (CF, 256), 1) >> 5
                for j in range(10):
                    acc = jnp.zeros((CF, 256), F32)
                    for k in range(3):
                        if 0 <= j - k < 8:
                            acc = jnp.where(group == j - k, wide[k], acc)
                    band_ref[j * CF : (j + 1) * CF, :] = acc.astype(BF16)
                for g in range(4):
                    lo, hi = max(8 * g - 1, 0), min(8 * g + 9, TF)
                    k0 = lo - (8 * g - 1)
                    out = dot(
                        xf_ref[:, lo * CF : hi * CF], band_ref[k0 * CF : (k0 + hi - lo) * CF, :]
                    )
                    fa_ref[:, g * 256 : (g + 1) * 256] = out
                    target = lo_ref if g < 2 else hi_ref
                    target[:, (g % 2) * 256 : (g % 2 + 1) * 256] = out
                moments(fa_ref, row_ref, 0, 8, 1, True, region(side, px, grid), side_sq(side, TF))

            put_count(row_ref, 2, side_sq(side, 1))
            send(pay_ref, row_ref)

        return call(
            body,
            [((px, 512), F32, "far"), ((px, 512), F32), ((10 * CF, 256), BF16), ((n, 4, LN), F32, "far")],
            [pltpu.VMEM((4, LN), F32), pltpu.VMEM((px, 1024), F32)],
            ints, xf, wa,
            **kw,
        )

    def fast_weights(self, wb, wbt, wc, **kw):
        def body(wb_ref, wbt_ref, wc_ref, b_ref, bt_ref, c_ref):
            pick = jnp.where(
                (lax.broadcasted_iota(jnp.int32, (CF_MID, 256), 1) & (CF_MID - 1))
                == lax.broadcasted_iota(jnp.int32, (CF_MID, 256), 0),
                1.0,
                0.0,
            ).astype(BF16)
            same = (lax.broadcasted_iota(jnp.int32, (256, 256), 0) >> 5) == (
                lax.broadcasted_iota(jnp.int32, (256, 256), 1) >> 5
            )
            for source, target in ((wb_ref, b_ref), (wbt_ref, bt_ref)):
                for tap in range(9):
                    tiled = jnp.concatenate([dot(source[tap], pick)] * 8, axis=0)
                    target[tap // 3, (tap % 3) * 256 : (tap % 3 + 1) * 256, :] = jnp.where(
                        same, tiled, 0.0
                    ).astype(BF16)
            c_ref[...] = jnp.zeros_like(c_ref)
            for i in range(8):
                c_ref[i * CF_MID : (i + 1) * CF_MID, i * CF : (i + 1) * CF] = wc_ref[...]

        return call(
            body,
            [((3, 768, 256), BF16), ((3, 768, 256), BF16), ((256, 1024), BF16)],
            [],
            wb, wbt, wc, smem=0,
            **kw,
        )

    def conv_stage(self, ints, recv, counts, x, par, w, params, frames, other=None, more=None, **kw):
        px, grid, n, ndp = self.px, self.grid, self.n, self.ndp
        fold = params == 1
        two = other is not None
        rows = 4 + (0 if more is None else more.array.shape[0])
        coded = 8 + 3 * (rows - 4) // 2

        def body(int_ref, recv_ref, n_ref, x_ref, par_ref, w_ref, *refs):
            o_ref = None
            if two:
                o_ref, refs = refs[0], refs[1:]
            if more is not None:
                m_ref, refs = refs[0], refs[1:]
            h_ref, y_ref, cst_ref, pay_ref = refs[:4]
            row_ref, pad = refs[4 + two : 6 + two]
            code_ref = refs[-1]
            if two:
                refs[4][...] = recv_ref[...]
            side = int_ref[0]
            mask = region(side, px, grid)
            half_mask = 0.5 * mask
            if two:
                stats, count = recv_ref[ndp:], n_ref[ndp:, 2:3, :] * float(TF)
            else:
                stats, count = recv_ref[...], n_ref[:, 2:3, :] * float(frames)
            combine(stats, 0, params, count, cst_ref)
            mean, rs = cst_ref[0:params, :], cst_ref[params : 2 * params, :]
            scale = par_ref[0:params, :] * rs
            shift = par_ref[params : 2 * params, :] - mean * scale
            clear_edges(pad, px, grid)
            for b in range(4):
                p = b % params
                v = pick_half(int_ref, o_ref, x_ref, b) * scale[p : p + 1] + shift[p : p + 1]
                h = gelu(v, half_mask)
                h_ref[:, lanes(b)] = h.astype(BF16)
                before, after = neighbours(h, px, grid)
                pack3(pad, b, h, before, after, px, grid)
            for g in range(2):
                acc = None
                for i in range(3):
                    part = dot(pad[grid * i : grid * i + px, g * 768 : (g + 1) * 768], w_ref[i])
                    acc = part if acc is None else acc + part
                y_ref[:, g * 256 : (g + 1) * 256] = acc
            moments(y_ref, row_ref, 0, 4, params, fold, mask, side_sq(side, frames))
            if more is None:
                send(pay_ref, row_ref)
            else:
                row_ref[4:rows, :] = m_ref[...]
                encode(code_ref, row_ref, 4, rows // 2 - 2)
                send(pay_ref, code_ref)

        extra = [other] if two else []
        extra += [] if more is None else [more]
        return call(
            body,
            [((px, 512), BF16), ((px, 512), F32), ((8, LN), F32), ((n, rows, LN), F32, "far") if more is None else ((n, coded, LN), BF16, "far")]
            + ([((n, 4, LN), F32)] if two else []),
            [pltpu.VMEM((rows, LN), F32), pltpu.VMEM((px + 2 * grid, 2 * 768), BF16)]
            + ([] if more is None else [pltpu.VMEM((coded, LN), F32)]),
            ints, recv, counts, x, par, w, *extra,
            **kw,
        )

    def expand_stage(self, ints, recv, counts, y, par, w, params, wide, frames, edge=False, **kw):
        px, grid, n = self.px, self.grid, self.n
        rows = max(2 * wide, 4)
        code = wide > 1
        coded = 3 * wide

        def body(int_ref, recv_ref, n_ref, y_ref, par_ref, w_ref, h_ref, cst_ref, pay_ref, *refs):
            row_ref, c_ref = refs[edge : edge + 2]
            code_ref = refs[-1]
            side = int_ref[0]
            mask = region(side, px, grid)
            half_mask = 0.5 * mask
            count = n_ref[:, 2:3, :] * float(frames)
            if code:
                combine_coded(recv_ref[...], 0, params, count, cst_ref, True)
            else:
                combine(recv_ref[...], 0, params, count, cst_ref)
            mean, rs = cst_ref[0:params, :], cst_ref[params : 2 * params, :]
            scale = par_ref[0:params, :] * rs
            shift = par_ref[params : 2 * params, :] - mean * scale
            for b in range(4):
                p = b % params
                v = y_ref[:, lanes(b)] * scale[p : p + 1] + shift[p : p + 1]
                h_ref[:, lanes(b)] = gelu(v, half_mask).astype(BF16)
            if edge:
                refs[0][...] = h_ref[:, lanes(3)]
            for g in range(2):
                c_ref[:, g * 1024 : (g + 1) * 1024] = dot(h_ref[:, g * 256 : (g + 1) * 256], w_ref[...])
            moments(c_ref, row_ref, 0, 16, wide, False, mask, side_sq(side, frames))
            if code:
                encode(code_ref, row_ref, 0, wide)
            send(pay_ref, code_ref if code else row_ref)

        return call(
            body,
            [((px, 512), BF16), ((8, LN), F32), ((n, coded, LN), BF16, "far") if code else ((n, rows, LN), F32, "far")]
            + ([((px, LN), BF16, "far")] if edge else []),
            [pltpu.VMEM((rows, LN), F32), pltpu.VMEM((px, 2048), F32)]
            + ([pltpu.VMEM((coded, LN), F32)] if code else []),
            ints, recv, counts, y, par, w,
            **kw,
        )

    def fast_finish(self, ints, recv, counts, h2, h2_other, w, xf, par, wlat, pa, wa, **kw):
        px, grid, n = self.px, self.grid, self.n

        def body(
            int_ref, recv_ref, n_ref, h_ref, ho_ref, w_ref, xf_ref, par_ref, wl_ref, pa_ref, wa_ref,
            y_ref, lat_ref, cst_ref, sa_ref, pay_ref, c_ref, row_ref,
        ):
            half_mask = 0.5 * region(int_ref[0], px, grid)
            combine(recv_ref[...], 0, 1, n_ref[:, 2:3, :] * float(TF // 2), cst_ref)
            scale = par_ref[0:1, :] * cst_ref[1:2, :]
            shift = par_ref[1:2, :] - cst_ref[0:1, :] * scale
            c_ref[:, 0:256] = dot(ho_ref[...], w_ref[0:LN, 256:512])
            edge = half_mask * int_ref[1].astype(F32)
            for f in range(2):
                v = c_ref[:, lanes(f)] * scale + shift + xf_ref[:, lanes(f)].astype(F32)
                y_ref[:, lanes(f)] = jnp.where(int_ref[1] == 1, gelu(v, edge), 0.0).astype(BF16)
            for g in range(2):
                c_ref[...] = dot(h_ref[:, g * 256 : (g + 1) * 256], w_ref[...])

                def step(i, carry):
                    f = 2 + g * 8 + i
                    v = c_ref[:, lanes(i)] * scale + shift + xf_ref[:, lanes(f)].astype(F32)
                    y_ref[:, lanes(f)] = gelu(v, half_mask).astype(BF16)
                    return carry

                loop(8, step, 0)
            for t in range(2):
                at = ALPHA * t * CF
                lat_ref[:, t * LAT : (t + 1) * LAT] = dot(y_ref[:, at : at + 5 * CF], wl_ref[...]).astype(BF16)
                a = slice(t * CS_MID, (t + 1) * CS_MID)
                sa_ref[:, a] = pa_ref[:, a] + dot(lat_ref[:, t * LAT : (t + 1) * LAT], wa_ref[...])
            side = int_ref[0]
            moments(sa_ref, row_ref, 0, 4, 2, False, region(side, px, grid), side_sq(side, TS // 2))
            send(pay_ref, row_ref)

        return call(
            body,
            [((px, 18 * CF), BF16), ((px, 512), BF16), ((8, LN), F32), ((px, 512), F32), ((n, 4, LN), F32, "far")],
            [pltpu.VMEM((px, 1024), F32), pltpu.VMEM((4, LN), F32)],
            ints, recv, counts, h2, h2_other, w, xf, par, wlat, pa, wa,
            **kw,
        )

    def fast_slope(self, ints, h2, w, xf, par, cst, **kw):
        px, grid = self.px, self.grid

        def body(int_ref, h_ref, w_ref, xf_ref, par_ref, cst_ref, gp_ref, c_ref):
            half_mask = 0.5 * region(int_ref[0], px, grid)
            scale = par_ref[0:1, :] * cst_ref[1:2, :]
            shift = par_ref[1:2, :] - cst_ref[0:1, :] * scale
            for g in range(2):
                c_ref[...] = dot(h_ref[:, g * 256 : (g + 1) * 256], w_ref[...])

                def step(i, carry):
                    f = g * 8 + i
                    v = c_ref[:, lanes(i)] * scale + shift + xf_ref[:, lanes(f + 2)].astype(F32)
                    gp_ref[:, lanes(f)] = gelu_both(v, half_mask)[1]
                    return carry

                loop(8, step, 0)

        return call(body, ((px, 2048), F32), [pltpu.VMEM((px, 1024), F32)], ints, h2, w, xf, par, cst, **kw)

    def slow_start(self, xs, wa, wp, **kw):
        px = self.px

        def body(x_ref, wa_ref, wp_ref, a_ref, p_ref):
            for t in range(2):
                x = x_ref[:, t * CS : (t + 1) * CS]
                a_ref[:, t * CS_MID : (t + 1) * CS_MID] = dot(x, wa_ref[0:CS, :])
                p_ref[:, t * CS : (t + 1) * CS] = dot(x, wp_ref[0:CS, :])

        return call(body, [((px, 512), F32), ((px, 2048), F32)], [], xs, wa, wp, smem=0, **kw)

    def slow_join(self, ints, part, lat, w, params, **kw):
        px, grid = self.px, self.grid
        width = params * LN

        def body(int_ref, part_ref, lat_ref, w_ref, out_ref, row_ref):
            side = int_ref[0]
            for t in range(2):
                at = slice(t * width, (t + 1) * width)
                out_ref[:, at] = part_ref[:, at] + dot(lat_ref[:, t * LAT : (t + 1) * LAT], w_ref[...])
            moments(
                out_ref, row_ref, 0, 2 * params, params, False, region(side, px, grid), side_sq(side, TS // 2)
            )

        return call(
            body, [((px, 2 * width), F32), ((2 * params, LN), F32)], [], ints, part, lat, w, **kw
        )

    def slow_top(self, ints, recv3, recvp, counts, h2, w, sp, gs, parc, parp, **kw):
        px, grid, n = self.px, self.grid, self.n

        def body(
            int_ref, r3_ref, rp_ref, n_ref, h_ref, w_ref, sp_ref, gs_ref, pc_ref, pp_ref,
            ys_ref, ds_ref, cc_ref, cp_ref, pay_ref, row_ref, c_ref, acc_ref, k_ref,
        ):
            half_mask = 0.5 * region(int_ref[0], px, grid)
            count = n_ref[:, 2:3, :] * float(TS // 2)
            combine_coded(r3_ref[...], 0, 8, count, cc_ref)
            combine_coded(rp_ref[...], 8, 8, count, cp_ref)
            k_ref[0:8, :] = pc_ref[0:8, :] * cc_ref[8:16, :]
            k_ref[8:16, :] = pp_ref[0:8, :] * cp_ref[8:16, :]
            k_ref[16:24, :] = pc_ref[8:16, :] + pp_ref[8:16, :]
            acc_ref[...] = jnp.zeros_like(acc_ref)
            for t in range(2):
                c_ref[...] = dot(h_ref[:, t * 256 : (t + 1) * 256], w_ref[...])

                def step(b, carry):
                    at = lanes(t * 8 + b)
                    one = pl.ds(b, 1)
                    xc = c_ref[:, lanes(b)] - cc_ref[one, :]
                    xp = sp_ref[:, at] - cp_ref[one, :]
                    v = xc * k_ref[one, :] + (xp * k_ref[pl.ds(b + 8, 1), :] + k_ref[pl.ds(b + 16, 1), :])
                    y, slope = gelu_both(v, half_mask)
                    ys_ref[:, at] = y.astype(BF16)
                    d = gs_ref[:, at].astype(F32) * slope
                    ds_ref[:, at] = d
                    acc_ref[b] += rows8(d)
                    acc_ref[8 + b] += rows8(d * xc)
                    acc_ref[16 + b] += rows8(d * xp)
                    return carry

                loop(8, step, 0)
            row_ref[...] = acc_ref[...].sum(axis=1)
            row_ref[8:16, :] = row_ref[8:16, :] * cc_ref[8:16, :]
            row_ref[16:24, :] = row_ref[16:24, :] * cp_ref[8:16, :]
            send(pay_ref, row_ref)

        return call(
            body,
            [
                ((px, 2048), BF16), ((px, 2048), F32), ((16, LN), F32), ((16, LN), F32),
                ((n, 24, LN), BF16, "far"),
            ],
            [
                pltpu.VMEM((24, LN), F32), pltpu.VMEM((px, 1024), F32),
                pltpu.VMEM((24, 8, LN), F32), pltpu.VMEM((24, LN), F32),
            ],
            ints, recv3, recvp, counts, h2, w, sp, gs, parc, parp,
            **kw,
        )

    def fast_top(self, ints, dl0, dl1, dl_other, wlat, gf, gp, h2, w, cst, **kw):
        px, n = self.px, self.n

        def body(
            int_ref, d0_ref, d1_ref, do_ref, wl_ref, gf_ref, gp_ref, h_ref, w_ref, cst_ref,
            ds_ref, pay_ref, row_ref, lt_ref, c_ref, acc_ref,
        ):
            first = (1 - int_ref[1]).astype(F32)
            lt_ref[:, 0 : 3 * CF] = dot_t(d0_ref[...], wl_ref[2 * CF :, :])
            lt_ref[:, 3 * CF : 8 * CF] = dot_t(d1_ref[...], wl_ref[...])
            edge = dot_t(do_ref[...], wl_ref[0 : 2 * CF, :])
            lt_ref[:, 8 * CF : 10 * CF] = jnp.where(int_ref[1] == 0, edge, 0.0)
            acc_ref[...] = jnp.zeros_like(acc_ref)
            mean, rs = cst_ref[0:1, :], cst_ref[1:2, :]
            where = {0: 0, 1: 1, 2: 2, 6: 3, 7: 4, 8: 5, 9: 6, 10: 7, 14: 8, 15: 9}
            for g in range(2):
                c_ref[...] = dot(h_ref[:, g * 256 : (g + 1) * 256], w_ref[...])
                for i in range(8):
                    f = g * 8 + i
                    d = gf_ref[:, lanes(f)].astype(F32)
                    if f in where:
                        d = d + lt_ref[:, lanes(where[f])]
                    d = d * gp_ref[:, lanes(f)]
                    ds_ref[:, lanes(f)] = d
                    acc_ref[0] += rows8(d)
                    acc_ref[1] += rows8(d * (c_ref[:, lanes(i)] - mean))
            row_ref[...] = jnp.zeros_like(row_ref)
            row_ref[0:1, :] = acc_ref[0].sum(axis=0, keepdims=True)
            row_ref[1:2, :] = acc_ref[1].sum(axis=0, keepdims=True) * rs
            send(pay_ref, row_ref)

        return call(
            body,
            [((px, 2048), F32), ((n, 4, LN), F32, "far")],
            [
                pltpu.VMEM((4, LN), F32), pltpu.VMEM((px, 10 * CF), F32),
                pltpu.VMEM((px, 1024), F32), pltpu.VMEM((2, 8, LN), F32),
            ],
            ints, dl0, dl1, dl_other, wlat, gf, gp, h2, w, cst,
            **kw,
        )

    def expand_back(self, ints, counts, recv, ds, h2, w, cstw, parw, y, cst, par, params, wide, frames, shortcut=None, **kw):
        px, grid, n = self.px, self.grid, self.n
        fold = params == 1
        both = shortcut is not None
        srows = 3 * wide if both else 4

        def body(*refs):
            int_ref, n_ref, recv_ref, ds_ref, h_ref, w_ref, cw_ref, pw_ref, y_ref, cs_ref, par_ref = refs[:11]
            refs = refs[11:]
            if both:
                sp_ref, cp_ref, pp_ref, dp_ref = refs[:4]
                refs = refs[4:]
            dc_ref, dn_ref, sum_ref, pay_ref, row_ref, c_ref, k3_ref = refs
            mask = region(int_ref[0], px, grid)
            half_mask = 0.5 * mask
            inv_k = 1.0 / (n_ref[:, 2:3, :].sum(axis=0) * float(frames))
            sums = recv_ref[...].astype(F32).sum(axis=0)
            sum_ref[...] = sums
            a = pw_ref[0:wide, :] * cw_ref[wide : 2 * wide, :]
            k3_ref[0:wide, :] = a
            k3_ref[wide : 2 * wide, :] = a * inv_k * sums[0:wide]
            k3_ref[2 * wide : 3 * wide, :] = a * inv_k * cw_ref[wide : 2 * wide, :] * sums[wide : 2 * wide]
            if both:
                a = pp_ref[0:wide, :] * cp_ref[wide : 2 * wide, :]
                k3_ref[3 * wide : 4 * wide, :] = a
                k3_ref[4 * wide : 5 * wide, :] = a * inv_k * sums[0:wide]
                k3_ref[5 * wide : 6 * wide, :] = (
                    a * inv_k * cp_ref[wide : 2 * wide, :] * sums[2 * wide : 3 * wide]
                )
            mean, rs = cs_ref[0:params, :], cs_ref[params : 2 * params, :]
            accs = [[jnp.zeros((8, LN), F32) for _ in range(params)] for _ in range(2)]
            for g in range(2):
                c_ref[...] = dot(h_ref[:, g * 256 : (g + 1) * 256], w_ref[...])

                def step(b, carry):
                    at = lanes(g * 8 + b)
                    p = b if wide == 8 else 0
                    d = ds_ref[:, at]
                    e = (c_ref[:, lanes(b)] - cw_ref[pl.ds(p, 1), :]) * k3_ref[pl.ds(2 * wide + p, 1), :]
                    e = d * k3_ref[pl.ds(p, 1), :] - k3_ref[pl.ds(wide + p, 1), :] - e
                    dc_ref[:, at] = (e * mask).astype(BF16)
                    if both:
                        e = (sp_ref[:, at] - cp_ref[pl.ds(p, 1), :]) * k3_ref[pl.ds(5 * wide + p, 1), :]
                        e = d * k3_ref[pl.ds(3 * wide + p, 1), :] - k3_ref[pl.ds(4 * wide + p, 1), :] - e
                        dp_ref[:, at] = (e * mask).astype(BF16)
                    return carry

                loop(8, step, 0)
                dh = dot_t(dc_ref[:, g * 1024 : (g + 1) * 1024], w_ref[...])
                for half in range(2):
                    b = g * 2 + half
                    p = b % params
                    xh = (y_ref[:, lanes(b)] - mean[p : p + 1]) * rs[p : p + 1]
                    v = xh * par_ref[p : p + 1, :] + par_ref[params + p : params + p + 1, :]
                    d = dh[:, half * LN : (half + 1) * LN] * gelu_both(v, half_mask)[1]
                    dn_ref[:, lanes(b)] = d
                    accs[0][p] = accs[0][p] + rows8(d)
                    accs[1][p] = accs[1][p] + rows8(d * xh)
            row_ref[...] = jnp.zeros_like(row_ref)
            for q in range(2):
                for p in range(params):
                    row_ref[q * params + p : q * params + p + 1, :] = total(accs[q][p], fold)
            send(pay_ref, row_ref)

        outs = [((px, 2048), BF16)] if both else []
        outs += [((px, 2048), BF16), ((px, 512), F32), ((srows, LN), F32, "far"), ((n, 4, LN), F32, "far")]
        extra = list(shortcut) if both else []
        return call(
            body,
            outs,
            [pltpu.VMEM((4, LN), F32), pltpu.VMEM((px, 1024), F32), pltpu.VMEM((max(6 * wide, 8), LN), F32)],
            ints, counts, recv, ds, h2, w, cstw, parw, y, cst, par, *extra,
            **kw,
        )

    def conv_back(self, ints, counts, recv, dn, y, cst2, par2, wt, x, cst1, par1, params, frames, other=None, **kw):
        px, grid, n = self.px, self.grid, self.n
        fold = params == 1
        two = other is not None

        def body(int_ref, n_ref, recv_ref, dn_ref, y_ref, c2_ref, p2_ref, w_ref, x_ref, c1_ref, p1_ref, *refs):
            o_ref = None
            if two:
                o_ref, refs = refs[0], refs[1:]
            db_ref, dn1_ref, sum_ref, pay_ref, row_ref, pad = refs
            mask = region(int_ref[0], px, grid)
            half_mask = 0.5 * mask
            inv_k = 1.0 / (n_ref[:, 2:3, :].sum(axis=0) * float(frames))
            sums = recv_ref[...].astype(F32).sum(axis=0)
            sum_ref[...] = sums
            mean2, rs2 = c2_ref[0:params, :], c2_ref[params : 2 * params, :]
            a = p2_ref[0:params, :] * rs2
            b0 = a * inv_k * sums[0:params]
            c0 = a * inv_k * rs2 * sums[params : 2 * params]
            clear_edges(pad, px, grid)
            for b in range(4):
                p = b % params
                e = (y_ref[:, lanes(b)] - mean2[p : p + 1]) * c0[p : p + 1]
                e = (dn_ref[:, lanes(b)] * a[p : p + 1] - b0[p : p + 1] - e) * mask
                db_ref[:, lanes(b)] = e.astype(BF16)
                before, after = neighbours(e, px, grid)
                pack3(pad, b, e, after, before, px, grid)
            mean, rs = c1_ref[0:params, :], c1_ref[params : 2 * params, :]
            accs = [[jnp.zeros((8, LN), F32) for _ in range(params)] for _ in range(2)]
            for g in range(2):
                dh = None
                for i in range(3):
                    part = dot(pad[grid * i : grid * i + px, g * 768 : (g + 1) * 768], w_ref[2 - i])
                    dh = part if dh is None else dh + part
                for half in range(2):
                    b = g * 2 + half
                    p = b % params
                    xh = (pick_half(int_ref, o_ref, x_ref, b) - mean[p : p + 1]) * rs[p : p + 1]
                    v = xh * p1_ref[p : p + 1, :] + p1_ref[params + p : params + p + 1, :]
                    d = dh[:, half * LN : (half + 1) * LN] * gelu_both(v, half_mask)[1]
                    dn1_ref[:, lanes(b)] = d
                    accs[0][p] = accs[0][p] + rows8(d)
                    accs[1][p] = accs[1][p] + rows8(d * xh)
            row_ref[...] = jnp.zeros_like(row_ref)
            for q in range(2):
                for p in range(params):
                    row_ref[q * params + p : q * params + p + 1, :] = total(accs[q][p], fold)
            send(pay_ref, row_ref)

        extra = [other] if two else []
        return call(
            body,
            [((px, 512), BF16), ((px, 512), F32), ((4, LN), F32, "far"), ((n, 4, LN), F32, "far")],
            [pltpu.VMEM((4, LN), F32), pltpu.VMEM((px + 2 * grid, 2 * 768), BF16)],
            ints, counts, recv, dn, y, cst2, par2, wt, x, cst1, par1, *extra,
            **kw,
        )

    def slow_last(self, ints, counts, recv, dn, x, cst, par, dp, wa, wp, **kw):
        px, grid = self.px, self.grid

        def body(
            int_ref, n_ref, recv_ref, dn_ref, x_ref, cst_ref, par_ref, dp_ref, wa_ref, wp_ref,
            da_ref, d0_ref, d1_ref, sum_ref,
        ):
            mask = region(int_ref[0], px, grid)
            inv_k = 1.0 / (n_ref[:, 2:3, :].sum(axis=0) * float(TS // 2))
            sums = recv_ref[...].astype(F32).sum(axis=0)
            sum_ref[...] = sums
            mean, rs = cst_ref[0:2, :], cst_ref[2:4, :]
            a = par_ref[0:2, :] * rs
            b0 = a * inv_k * sums[0:2]
            c0 = a * inv_k * rs * sums[2:4]
            for b in range(4):
                p = b % 2
                e = (x_ref[:, lanes(b)] - mean[p : p + 1]) * c0[p : p + 1]
                e = (dn_ref[:, lanes(b)] * a[p : p + 1] - b0[p : p + 1] - e) * mask
                da_ref[:, lanes(b)] = e.astype(BF16)
            for t, out in ((0, d0_ref), (1, d1_ref)):
                out[...] = (
                    dot_t(da_ref[:, t * CS_MID : (t + 1) * CS_MID], wa_ref[...])
                    + dot_t(dp_ref[:, t * CS : (t + 1) * CS], wp_ref[...])
                ).astype(BF16)

        return call(
            body,
            [((px, 512), BF16), ((px, LAT), BF16), ((px, LAT), BF16), ((4, LN), F32, "far")],
            [],
            ints, counts, recv, dn, x, cst, par, dp, wa, wp,
            **kw,
        )

    def slow_input_grad(self, da, dp, wa, wp, **kw):
        px = self.px

        def body(da_ref, dp_ref, wa_ref, wp_ref, dx_ref):
            for t in range(2):
                dx_ref[:, t * CS : (t + 1) * CS] = (
                    dot_t(da_ref[:, t * CS_MID : (t + 1) * CS_MID], wa_ref[0:CS, :])
                    + dot_t(dp_ref[:, t * CS : (t + 1) * CS], wp_ref[0:CS, :])
                ).astype(BF16)

        return call(body, ((px, 2048), BF16, "far"), [], da, dp, wa, wp, smem=0, **kw)

    def fast_first_back(self, ints, counts, recv, dn_lo, dn_hi, fa_lo, fa_hi, cst, par, **kw):
        px, grid = self.px, self.grid

        def body(int_ref, n_ref, recv_ref, dl_ref, dh_ref, xl_ref, xh_ref, cst_ref, par_ref, da_ref, sum_ref):
            sums = recv_ref[...].sum(axis=0)
            sum_ref[...] = sums

            @pl.when(int_ref[1] == 1)
            def _():
                mask = region(int_ref[0], px, grid)
                inv_k = 1.0 / (n_ref[:, 2:3, :].sum(axis=0) * float(TF // 2))
                mean, rs = cst_ref[0:1, :], cst_ref[1:2, :]
                a = par_ref[0:1, :] * rs
                b0 = a * inv_k * sums[0:1]
                c0 = a * inv_k * rs * sums[1:2]
                for dn_ref, h_ref, base in ((dl_ref, xl_ref, 0), (dh_ref, xh_ref, 4)):
                    for b in range(4):
                        e = (h_ref[:, lanes(b)] - mean) * c0
                        e = (dn_ref[:, lanes(b)] * a - b0 - e) * mask
                        da_ref[:, lanes(base + b)] = e.astype(BF16)

        return call(
            body,
            [((px, 1024), BF16), ((4, LN), F32, "far")],
            [],
            ints, counts, recv, dn_lo, dn_hi, fa_lo, fa_hi, cst, par,
            **kw,
        )

    def fast_small(self, ints, da, xf, bc, bc_other, **kw):
        first = 3 * CF_MID
        rows = first + bc.shape[0]

        def body(int_ref, da_ref, x_ref, b0_ref, b1_ref, out_ref, row_ref, scratch):
            row_ref[0:first, :] = jnp.zeros((first, LN), F32)
            row_ref[first:rows, :] = b0_ref[...] + b1_ref[...]

            @pl.when(int_ref[1] == 1)
            def _():
                accs = [None] * 3
                for g in range(4):
                    lo, hi = max(8 * g - 1, 0), min(8 * g + 9, TF)
                    k0 = lo - (8 * g - 1)
                    d = dot(da_ref[:, g * 256 : (g + 1) * 256].T, x_ref[:, lo * CF : hi * CF])
                    for k in range(3):
                        for i in range(8):
                            j = i + k - k0
                            if 0 <= j < hi - lo:
                                part = d[i * CF_MID : (i + 1) * CF_MID, j * CF : (j + 1) * CF]
                                accs[k] = part if accs[k] is None else accs[k] + part
                for k in range(3):
                    tiled = jnp.concatenate([accs[k]] * 4, axis=0).T
                    row_ref[k * CF_MID : (k + 1) * CF_MID, :] = tiled_rows(scratch, tiled)

            out_ref[...] = row_ref[...].astype(BF16)

        return call(
            body,
            ((rows, LN), BF16, "far"),
            [pltpu.VMEM((rows, LN), F32), pltpu.VMEM((LN, LN), F32)],
            ints, da, xf, bc, bc_other,
            **kw,
        )

    def last(self, ints, da, ds_lo, ds_hi, band, dxs0, dxs1, **kw):
        px = self.px

        def body(int_ref, da_ref, sl_ref, sh_ref, band_ref, x0_ref, x1_ref, dx_ref, acc_ref, out_ref, sem):
            def part(g):
                at = slice(g * 1024, (g + 1) * 1024)
                return pltpu.make_async_copy(out_ref.at[:, at], dx_ref.at[:, at], sem.at[g])

            def half(ref, g):
                return pltpu.make_async_copy(ref, out_ref.at[:, g * 2048 : (g + 1) * 2048], sem.at[4 + g])

            @pl.when(int_ref[1] == 0)
            def _():
                half(x0_ref, 0).start()
                half(x1_ref, 1).start()
                for g in range(2):
                    half(x0_ref if g == 0 else x1_ref, g).wait()
                    part(2 * g).start()
                    part(2 * g + 1).start()
                for g in range(4):
                    part(g).wait()

            @pl.when(int_ref[1] == 1)
            def _():
                acc_ref[:, 0 : 10 * CF] = dot_t(da_ref[:, 0:256], band_ref[...])
                for g in range(4):
                    if g < 3:
                        p = dot_t(da_ref[:, (g + 1) * 256 : (g + 2) * 256], band_ref[...])
                        base = 8 * (g + 1) * CF
                        acc_ref[:, base : base + 2 * CF] += p[:, 0 : 2 * CF]
                        acc_ref[:, base + 2 * CF : base + 10 * CF] = p[:, 2 * CF :]
                    s_ref = sl_ref if g < 2 else sh_ref
                    for i in range(8):
                        f = 8 * g + i
                        s = s_ref[:, lanes(f % 16)] + acc_ref[:, lanes(f + 1)]
                        out_ref[:, lanes(f)] = s.astype(BF16)
                    part(g).start()
                for g in range(4):
                    part(g).wait()

        return call(
            body,
            ((px, 4096), BF16, "manual"),
            [pltpu.VMEM((px, 34 * CF), F32), pltpu.VMEM((px, 4096), BF16), pltpu.SemaphoreType.DMA((6,))],
            ints, da, ds_lo, ds_hi, band, Manual(dxs0), Manual(dxs1),
            **kw,
        )

    def halves(self, ints, x, x_other, cot, cot_other, **kw):
        px = self.px

        def body(int_ref, x_ref, xo_ref, c_ref, co_ref, xs_ref, xf_ref, gs_ref, gf_ref, sem):
            def run(pairs):
                copies = [pltpu.make_async_copy(a, b, sem.at[k]) for k, (a, b) in enumerate(pairs)]
                for c in copies:
                    c.start()
                for c in copies:
                    c.wait()

            lo, hi = slice(0, 2048), slice(2048, 4096)

            @pl.when(int_ref[1] == 0)
            def _():
                xf_ref[:, 0 : 2 * CF] = jnp.zeros((px, 2 * CF), BF16)
                run([
                    (x_ref.at[:, lo], xs_ref), (xo_ref.at[:, lo], xf_ref.at[:, 2 * CF : 18 * CF]),
                    (c_ref.at[:, lo], gs_ref), (co_ref.at[:, lo], gf_ref),
                ])

            @pl.when(int_ref[1] == 1)
            def _():
                run([
                    (xo_ref.at[:, hi], xs_ref), (x_ref.at[:, 14 * CF :], xf_ref),
                    (co_ref.at[:, hi], gs_ref), (c_ref.at[:, hi], gf_ref),
                ])

        wide = ((px, 2048), BF16)
        return call(
            body,
            [wide, ((px, 18 * CF), BF16), wide, wide],
            [pltpu.SemaphoreType.DMA((4,))],
            ints, Manual(x), Manual(x_other), Manual(cot), Manual(cot_other),
            **kw,
        )

    def out_send(self, ints, ys, yf, **kw):
        px = self.px

        def body(int_ref, ys_ref, yf_ref, out_ref):
            for path, ref, at in ((0, yf_ref, 2 * CF), (1, ys_ref, 0)):

                @pl.when(int_ref[1] == path)
                def _():
                    out_ref[...] = ref[:, at : at + 2048]

        return call(body, ((px, 2048), BF16, "far"), [], ints, ys, yf, **kw)

    def out_join(self, ints, ys, yf, other, **kw):
        px = self.px

        def body(int_ref, ys_ref, yf_ref, o_ref, out_ref):
            for path, ref, at in ((0, ys_ref, 0), (1, yf_ref, 2 * CF)):

                @pl.when(int_ref[1] == path)
                def _():
                    mine, far = path * 2048, (1 - path) * 2048
                    out_ref[:, mine : mine + 2048] = ref[:, at : at + 2048]
                    out_ref[:, far : far + 2048] = o_ref[...]

        return call(body, ((px, 4096), BF16, "far"), [], ints, ys, yf, Far(other), **kw)

    def fast_grads_bc(self, h1, db, h2, dc, **kw):
        px, grid = self.px, self.grid

        def body(h1_ref, db_ref, h2_ref, dc_ref, out_ref, pad, scratch):
            clear_edges(pad, px, grid)
            for b in range(4):
                h = h1_ref[:, lanes(b)].astype(F32)
                before, after = neighbours(h, px, grid)
                pack3(pad, b, h, before, after, px, grid)
            same = (lax.broadcasted_iota(jnp.int32, (256, 256), 0) >> 5) == (
                lax.broadcasted_iota(jnp.int32, (256, 256), 1) >> 5
            )
            for i in range(3):
                for s in range(3):
                    acc = jnp.zeros((256, 256), F32)
                    for g in range(2):
                        at = g * 768 + s * 256
                        acc = acc + dot(
                            pad[grid * i : grid * i + px, at : at + 256].T,
                            db_ref[:, g * 256 : (g + 1) * 256],
                        )
                    acc = jnp.where(same, acc, 0.0).reshape(8, CF_MID, 256).sum(axis=0)
                    at = (3 * i + s) * 8
                    out_ref[at : at + 8, :] = tiled_rows(scratch, fold32(acc))
            acc = jnp.zeros((256, 1024), F32)
            for g in range(2):
                acc = acc + dot(h2_ref[:, g * 256 : (g + 1) * 256].T, dc_ref[:, g * 1024 : (g + 1) * 1024])
            out = None
            for i in range(8):
                part = acc[i * CF_MID : (i + 1) * CF_MID, i * CF : (i + 1) * CF]
                out = part if out is None else out + part
            out_ref[72:104, :] = out
            out_ref[104:, :] = jnp.zeros((8, LN), F32)

        return call(
            body,
            ((112, LN), F32, "far"),
            [pltpu.VMEM((px + 2 * grid, 2 * 768), BF16), pltpu.VMEM((CF_MID, LN), F32)],
            h1, db, h2, dc, smem=0,
            **kw,
        )

    def grads_early(self, plan, ints, xs, lat, dp, h2, dc, **kw):
        px = self.px
        rows = plan.early

        def body(int_ref, x_ref, lat_ref, dp_ref, h2_ref, dc_ref, keep_ref, send_ref, buf, xt):
            def put(base, q, acc):
                for j in range(2):
                    buf[pl.ds(base + 2 * q + j, 256, stride=8), :] = acc[:, j * LN : (j + 1) * LN]

            for c in range(6):
                for t in range(2):
                    if c == 5:
                        x = h2_ref[:, t * 256 : (t + 1) * 256]
                    elif c == 4:
                        x = lat_ref[:, t * LAT : (t + 1) * LAT]
                    else:
                        x = x_ref[:, t * CS + c * 256 : t * CS + (c + 1) * 256]
                    xt[:, t * px : (t + 1) * px] = x.T
                source = dc_ref if c == 5 else dp_ref
                base = (ROW_SC if c == 5 else ROW_SP + c * 2048) - ROW_SC
                for q in range(4):
                    acc = None
                    for t in range(2):
                        at = t * CS + q * 256
                        part = dot(xt[:, t * px : (t + 1) * px], source[:, at : at + 256])
                        acc = part if acc is None else acc + part
                    put(base, q, acc)
            lo = 0
            hi = plan.base[1] - ROW_SC
            mine = pl.multiple_of(jnp.where(int_ref[1] == 0, lo, hi), 16)
            other = pl.multiple_of(jnp.where(int_ref[1] == 0, hi, lo), 16)
            keep_ref[...] = buf[pl.ds(mine, rows), :].astype(BF16)
            send_ref[...] = buf[pl.ds(other, rows), :].astype(BF16)

        return call(
            body,
            [((rows, LN), BF16, "far"), ((rows, LN), BF16, "far")],
            [pltpu.VMEM((ROW_SG - ROW_SC, LN), F32), pltpu.VMEM((256, 2 * px), BF16)],
            ints, xs, lat, dp, h2, dc,
            **kw,
        )

    def grads_conv(self, h1, db, **kw):
        px, grid = self.px, self.grid

        def body(h1_ref, db_ref, out_ref, buf, pad):
            clear_edges(pad, px, grid)
            for b in range(4):
                h = h1_ref[:, lanes(b)].astype(F32)
                before, after = neighbours(h, px, grid)
                pack3(pad, b, h, before, after, px, grid)
            for i in range(3):
                for s in range(3):
                    acc = None
                    for t in range(2):
                        at = t * 768 + s * 256
                        part = dot(
                            pad[grid * i : grid * i + px, at : at + 256].T,
                            db_ref[:, t * 256 : (t + 1) * 256],
                        )
                        acc = part if acc is None else acc + part
                    for j in range(2):
                        buf[pl.ds((3 * i + s) * 512 + j, 256, stride=2), :] = acc[:, j * LN : (j + 1) * LN]
            out_ref[...] = buf[...].astype(BF16)

        return call(
            body,
            ((ROW_SC - ROW_SB, LN), BF16, "far"),
            [pltpu.VMEM((ROW_SC - ROW_SB, LN), F32), pltpu.VMEM((px + 2 * grid, 2 * 768), BF16)],
            h1, db, smem=0,
            **kw,
        )

    def grads_late(self, ints, xs, lat, da, yf, dl0, dl1, **kw):
        px = self.px
        rows = ROW_SB - ROW_SA
        lat_rows = ROW_FG - ROW_LAT

        def body(int_ref, x_ref, lat_ref, da_ref, yf_ref, d0_ref, d1_ref, keep_ref, send_ref, buf):
            for c in range(5):
                acc = None
                for t in range(2):
                    if c == 4:
                        x = lat_ref[:, t * LAT : (t + 1) * LAT]
                    else:
                        x = x_ref[:, t * CS + c * 256 : t * CS + (c + 1) * 256]
                    part = dot(x.T, da_ref[:, t * CS_MID : (t + 1) * CS_MID])
                    acc = part if acc is None else acc + part
                for j in range(2):
                    buf[pl.ds(c * 512 + j, 256, stride=2), :] = acc[:, j * LN : (j + 1) * LN]
            for k in range(5):
                acc = dot(yf_ref[:, lanes(k)].T, d0_ref[...]) + dot(yf_ref[:, lanes(8 + k)].T, d1_ref[...])
                for j in range(2):
                    buf[pl.ds(rows + k * 256 + j, CF, stride=2), :] = acc[:, j * LN : (j + 1) * LN]
            mine = pl.multiple_of(jnp.where(int_ref[1] == 0, 0, rows), 16)
            other = pl.multiple_of(jnp.where(int_ref[1] == 0, rows, 0), 16)
            keep_ref[...] = buf[pl.ds(mine, rows), :].astype(BF16)
            send_ref[...] = buf[pl.ds(other, rows), :].astype(BF16)

        return call(
            body,
            [((rows, LN), BF16, "far"), ((rows, LN), BF16, "far")],
            [pltpu.VMEM((2 * rows, LN), F32)],
            ints, xs, lat, da, yf, dl0, dl1,
            **kw,
        )

    def windows(self, plan, ints, early, conv, late, **kw):
        ndp, chunk, half = self.ndp, plan.chunk, self.ndp // 2

        def body(int_ref, e0_ref, e1_ref, c0_ref, c1_ref, l0_ref, l1_ref, keep_ref, send_ref, buf):
            def add(a, b, rows):
                return a[0:rows, :].astype(F32) + b[0:rows, :].astype(F32)

            for path in range(2):

                @pl.when(int_ref[1] == path)
                def _():
                    buf[...] = jnp.zeros_like(buf)
                    base = plan.base[path]
                    if path == 0:
                        buf[ROW_SA:ROW_SB, :] = add(l0_ref, l1_ref, ROW_SB - ROW_SA)
                        buf[ROW_SB:ROW_SC, :] = add(c0_ref, c1_ref, ROW_SC - ROW_SB)
                        rest = min(plan.length - ROW_SC, plan.early)
                        buf[ROW_SC : ROW_SC + rest, :] = add(e0_ref, e1_ref, rest)
                    else:
                        rest = ROW_SG - base
                        buf[0:rest, :] = add(e0_ref, e1_ref, rest)
                        at = ROW_LAT - base
                        buf[at : at + ROW_FG - ROW_LAT, :] = add(l0_ref, l1_ref, ROW_FG - ROW_LAT)

            path = int_ref[1]
            base = jnp.where(path == 0, plan.base[0], plan.base[1])

            def stretch(place):
                j = 0
                for step in range(plan.bits):
                    bit = (place >> (plan.bits - 1 - step)) & 1
                    j = j + jnp.where(
                        path == 0, bit << plan.order[0][step], bit << plan.order[1][step]
                    )
                at = ((path * ndp + j) * plan.share) // (16 * LN) * 16 - base
                return buf[pl.ds(pl.multiple_of(at, 16), chunk), :].astype(BF16)

            def step(q, carry):
                bit = int_ref[5]
                keep_ref[q] = stretch(bit * half + q)
                send_ref[q] = stretch((1 - bit) * half + q)
                return carry

            loop(half, step, 0)

        return call(
            body,
            [((half, chunk, LN), BF16, "far")] * 2,
            [pltpu.VMEM((plan.length, LN), F32)],
            ints, *early, *conv, *late,
            **kw,
        )

    def halve(self, plan, ints, step, keep, came, **kw):
        half = keep.shape[0] // 2

        def body(int_ref, a_ref, b_ref, keep_ref, send_ref):
            bit = int_ref[5 + step]

            def one(q, carry):
                for out, at in ((keep_ref, bit * half + q), (send_ref, (1 - bit) * half + q)):
                    out[q] = (a_ref[at].astype(F32) + b_ref[at].astype(F32)).astype(BF16)
                return carry

            loop(half, one, 0)

        return call(
            body,
            [((half, plan.chunk, LN), BF16, "far")] * 2,
            [],
            ints, Far(keep), came,
            **kw,
        )

    def add(self, parts, **kw):
        def body(*refs):
            refs[-1][...] = sum(r[...].astype(F32) for r in refs[:-1]).astype(BF16)

        return call(body, (parts[0].shape, BF16, "far"), [], Far(parts[0]), *parts[1:], smem=0, **kw)

    def window(self, plan, ints, keep, came, parts, vectors, tail, **kw):
        chunk, out_rows = plan.chunk, plan.out_rows
        extra, count = parts[0].shape[0], len(parts)
        pad = extra + 8

        def body(int_ref, keep_ref, came_ref, vec_ref, tail_ref, *refs):
            out_ref, a_ref, small_ref = refs[count:]
            r0 = int_ref[2]
            row = int_ref[3]
            lane = int_ref[4]
            a_ref[...] = jnp.zeros_like(a_ref)
            total = sum(r[...].astype(F32) for r in refs[:count])
            small_ref[...] = jnp.where(int_ref[1] == 1, total, 0.0)
            for ref, start, n in (
                (vec_ref, ROW_SG, 2 * SLOW_VEC), (small_ref, ROW_FA, ROW_LAT - ROW_FA), (tail_ref, ROW_FG, 3)
            ):
                at = jnp.clip(start - r0, -n, chunk) + pad
                a_ref[pl.ds(at, n), :] += ref[0:n, :]
            a_ref[pad : pad + chunk, :] += keep_ref[0].astype(F32) + came_ref[0].astype(F32)
            one = a_ref[pl.ds(pad + row, out_rows), :]
            two = a_ref[pl.ds(pad + row + 1, out_rows), :]
            shift = (LN - lane) & (LN - 1)
            one = pltpu.roll(one, shift, 1)
            two = pltpu.roll(two, shift, 1)
            at = lax.broadcasted_iota(jnp.int32, (out_rows, LN), 1)
            out_ref[...] = jnp.where(at < LN - lane, one, two)

        return call(
            body,
            ((out_rows, LN), F32, "far"),
            [pltpu.VMEM((chunk + 2 * pad + 8, LN), F32), pltpu.VMEM((extra, LN), F32)],
            ints, keep, came, vectors, tail, *parts,
            **kw,
        )


class Plan:
    def __init__(self, ndp):
        n = 2 * ndp
        self.ndp = ndp
        self.share = VALUES // n
        self.first = [self.share * d // LN // 16 * 16 for d in range(n)]
        ends = [-(-self.share * (d + 1) // LN) for d in range(n)]
        self.chunk = -(-max(e - f for e, f in zip(ends, self.first)) // 16) * 16
        self.base = [self.first[0], self.first[ndp]]
        self.length = max(
            self.first[q * ndp + ndp - 1] + self.chunk - self.base[q] for q in range(2)
        )
        self.early = ROW_SG - self.base[1]
        self.out_rows = -(-self.share // LN)
        self.bits = ndp.bit_length() - 1
        one = list(range(self.bits))
        two = one[1:] + one[:1]
        self.order = [one, two]
        self.stages = [
            [m << b for m in range(1, 1 << min(2, self.bits - b))] for b in range(0, self.bits, 2)
        ]

    def place(self, path, j):
        at = 0
        for b in self.order[path]:
            at = 2 * at + ((j >> b) & 1)
        return at

    def route(self, mask):
        return [(q * self.ndp + j, q * self.ndp + (j ^ mask)) for q in range(2) for j in range(self.ndp)]

    def pairs(self, step):
        out = []
        for q in range(2):
            b = self.order[q][step]
            out += [(q * self.ndp + j, q * self.ndp + (j ^ (1 << b))) for j in range(self.ndp)]
        return out


def exchange(x):
    return lax.all_to_all(x, ("path", "dp"), 0, 0)


def swap(x):
    x = x.array if isinstance(x, Near) else x
    return lax.ppermute(x, "path", SWAP)


def local(
    acts, cotangent, clip_res, w_slow_a, w_slow_b, w_slow_c, w_slow_proj, slow_gain, slow_bias,
    w_fast_a, w_fast_b, w_fast_c, w_lateral, fast_gain, fast_bias,
):
    grid = acts.shape[2]
    px = grid * grid
    ndp = lax.axis_size("dp")
    net = Net(ndp, grid)
    plan = Plan(ndp)
    path, chip = lax.axis_index("path"), lax.axis_index("dp")
    core0 = path == 0
    level = clip_res[0]
    side = jnp.where(
        level == 1, grid * 5 // 8, jnp.where(level == 2, grid * 7 // 8, jnp.where(level == 3, grid, 0))
    )
    start = (path * ndp + chip) * plan.share
    r0 = start // LN // 16 * 16
    off = start - r0 * LN
    bits = [
        jnp.where(core0, chip >> plan.order[0][s], chip >> plan.order[1][s]) & 1 for s in range(plan.bits)
    ]
    ints = jnp.stack([side, path, r0, off // LN, off % LN] + bits).astype(jnp.int32)
    x = acts.reshape(px, 4096)
    cot = cotangent.reshape(px, 4096)
    sg, sb_ = slow_gain.reshape(SLOW_VEC, LN), slow_bias.reshape(SLOW_VEC, LN)

    def slow_par(a, b):
        return jnp.concatenate([sg[a:b], sb_[a:b]], axis=0)

    def fast_par(a, b):
        one = jnp.stack([fast_gain[a:b], fast_bias[a:b]])
        return jnp.tile(one, (1, LN // (b - a)))

    wlat = w_lateral.reshape(5 * CF, LAT)
    wa_lat = Far(w_slow_a, (LAT, CS_MID), (CS // LAT, 0))
    wp_lat = Far(w_slow_proj, (LAT, CS), (CS // LAT, 0))
    f1, f2, f3 = fast_par(0, 32), fast_par(32, 64), fast_par(64, 192)
    s1, s2, s3, s4 = slow_par(0, 2), slow_par(2, 4), slow_par(4, 12), slow_par(12, 20)
    wb3 = w_slow_b.reshape(3, 768, 256)
    wbt3 = w_slow_b.transpose(0, 2, 1).reshape(3, 768, 256)
    half = TF // 2

    x_other = swap(x)
    cot_other = swap(cot)

    fa_lo, fa_hi, band, pay = net.fast_first(ints, Far(x), Far(w_fast_a.transpose(0, 2, 1)), us=3.5)
    (fb_w, fbt_w, fc_w), tok = net.fast_weights(
        w_fast_b, w_fast_b.transpose(0, 2, 1), w_fast_c, us=1.0, after=[pay], token=True
    )
    fa_other = swap(fa_lo)
    r1 = exchange(pay)
    fh1, fb, fc1, pay, r1 = net.conv_stage(
        ints, r1, r1, fa_hi, f1, fb_w, 1, half, fa_other, us=2.7, after=[tok]
    )
    (xs, xf, gs, gf), tok = net.halves(ints, x, x_other, cot, cot_other, us=2.5, after=[pay], token=True)
    r = exchange(pay)
    fh2, fc2, pay, fh2_edge = net.expand_stage(
        ints, r, r1, fb, f2, fc_w, 1, 1, half, True, us=2.6, after=[tok]
    )
    fh2_other = swap(fh2_edge)
    (pa, pp), tok = net.slow_start(xs, Far(w_slow_a), Far(w_slow_proj), us=3.5, after=[pay], token=True)
    r = exchange(pay)
    yf, lat, fc3, sa, pay = net.fast_finish(
        ints, r, r1, fh2, fh2_other, fc_w, xf, f3, wlat, pa, wa_lat, us=5.0, after=[tok]
    )

    (sp, sp_rows), tok = net.slow_join(ints, pp, lat, wp_lat, 8, us=3.0, after=[pay], token=True)
    r = exchange(pay)
    sh1, sb, sc1, pay = net.conv_stage(
        ints, r, r1, sa, s1, wb3, 2, TS // 2, more=sp_rows, us=3.0, after=[tok]
    )
    rp = exchange(pay)
    gp, tok = net.fast_slope(ints, fh2, fc_w, xf, f3, fc3, us=4.0, after=[pay], token=True)
    sh2, sc2, pay = net.expand_stage(ints, rp, r1, sb, s2, w_slow_c, 2, 8, TS // 2, us=3.0, after=[tok])
    r = exchange(pay)
    ys, ds, scc, scp, pay = net.slow_top(ints, r, rp, r1, sh2, w_slow_c, sp, gs, s3, s4, us=6.0)

    sent, tok = net.out_send(ints, ys, yf, us=2.0, after=[pay], token=True)
    r = exchange(pay)
    (dp, dc, dn, t3, pay), (sent,) = net.expand_back(
        ints, r1, r, ds, sh2, w_slow_c, scc, s3, sb, sc2, s2, 2, 8, TS // 2, (sp, scp, s4),
        us=6.0, after=[tok], through=[sent],
    )
    theirs = swap(sent)
    (early, early_out), tok = net.grads_early(
        plan, ints, xs, lat, dp, sh2, dc, us=6.0, after=[pay], token=True
    )
    r = exchange(pay)
    db, dn, t2, pay = net.conv_back(
        ints, r1, r, dn, sb, sc2, s2, wbt3, sa, sc1, s1, 2, TS // 2, us=3.0, after=[tok]
    )
    conv, tok = net.grads_conv(sh1, db, us=3.0, after=[pay], token=True)
    r = exchange(pay)
    (da, dl0, dl1, t1), (conv_out, early_out) = net.slow_last(
        ints, r1, r, dn, sa, sc1, s1, dp, wa_lat, wp_lat, us=3.0, after=[tok], through=[conv, early_out]
    )
    dl_other = swap(dl0)
    early_in = swap(early_out)
    (late, late_out), tok = net.grads_late(ints, xs, lat, da, yf, dl0, dl1, us=4.0, token=True)

    (fds, pay), (conv_out, late_out) = net.fast_top(
        ints, dl0, dl1, dl_other, wlat, gf, gp, fh2, fc_w, fc3, us=4.0, through=[conv_out, late_out]
    )
    conv_in = swap(conv_out)
    late_in = swap(late_out)
    fds_lo = swap(fds)
    (keep, there), tok = net.windows(
        plan, ints, (Far(early), early_in), (Far(conv_out), conv_in), (Far(late), late_in),
        us=6.0, after=[pay], token=True,
    )
    r = exchange(pay)
    (fdc, dn, u3, pay), (there,) = net.expand_back(
        ints, r1, r, fds, fh2, fc_w, fc3, f3, fb, fc2, f2, 1, 1, half,
        us=5.0, after=[tok], through=[there],
    )
    here = lax.ppermute(there, ("path", "dp"), plan.pairs(0))
    dxs, tok = net.slow_input_grad(da, dp, Far(w_slow_a), Far(w_slow_proj), us=4.0, after=[pay], token=True)
    out, tok = net.out_join(ints, ys, yf, theirs, us=3.0, after=[tok], token=True)
    (keep, there), tok = net.halve(plan, ints, 1, keep, here, us=3.0, after=[tok], token=True)
    r = exchange(pay)
    (fdb, dn, u2, pay), (dxs_out, there) = net.conv_back(
        ints, r1, r, dn, fb, fc2, f2, fbt_w, fa_hi, fc1, f1, 1, half, fa_other,
        us=4.0, after=[tok], through=[dxs, there],
    )
    dn_lo = swap(dn)
    here = lax.ppermute(there, ("path", "dp"), plan.pairs(1))
    bc, tok = net.fast_grads_bc(fh1, fdb, fh2, fdc, us=4.0, after=[pay], token=True)
    (keep, there), tok = net.halve(plan, ints, 2, keep, here, us=2.5, after=[tok], token=True)
    r = exchange(pay)
    (fda, u1), (bc, there) = net.fast_first_back(
        ints, r1, r, dn_lo, dn, Far(fa_lo), fa_hi, fc1, f1, us=2.5, after=[tok], through=[bc, there]
    )
    bc_other = swap(bc)
    dxs_other = swap(dxs_out)
    small = net.fast_small(ints, fda, Far(x), bc, bc_other, us=3.0, after=[fds_lo])
    here = lax.ppermute(there, ("path", "dp"), plan.pairs(2))
    for step in range(3, plan.bits):
        keep, there = net.halve(plan, ints, step, keep, here, us=2.5, after=[small])
        here = lax.ppermute(there, ("path", "dp"), plan.pairs(step))
    for k, masks in enumerate(plan.stages):
        parts = [small] + [lax.ppermute(small, ("path", "dp"), plan.route(m)) for m in masks]
        if k < len(plan.stages) - 1:
            small = net.add(parts, us=1.0, after=[keep] if k == 0 else [])
    dx = net.last(ints, fda, Far(fds_lo), fds, band, dxs_out, dxs_other, us=4.5, after=[small])

    vectors = jnp.concatenate([t1[2:4], t2[2:4], t3[8:24], t1[0:2], t2[0:2], t3[0:8], t3[0:8]], axis=0)
    tail = jnp.concatenate([u1[1, :32], u2[1, :32], u3[1], u1[0, :32], u2[0, :32], u3[0]]).reshape(3, LN)
    tail = jnp.pad(tail, ((0, 5), (0, 0)))
    flat = net.window(plan, ints, keep, here, parts, vectors, tail).reshape(-1)[: plan.share]
    return (out.reshape(acts.shape), dx.reshape(acts.shape), flat)


def solution(mesh):
    data = P("path", "dp", None, None, None)
    in_specs = (data, data, P("dp")) + (P(),) * 12
    out_specs = (data, data, P(("path", "dp")))
    return jax.shard_map(local, mesh=mesh, in_specs=in_specs, out_specs=out_specs, check_vma=False)
```
